128 devices in a mesh: tok: 16 (over y, z_hi, core), br: 8 (over z_lo, x).
Axes of the slice: x: 4, y: 4, z: 4 (z_hi: 2, z_lo: 2; z = z_hi * 2 + z_lo), core: 2. Of those that a mesh axis runs over, the one named last changes fastest.
Arguments:
- tokens: bfloat16 [16384, 2048], P(('tok', 'br')), may hold values from -6 to 6
- norm_gain: float32 [2048], replicated, may hold values from 0.1 to 1.9
- norm_bias: float32 [2048], replicated, may hold values from -3 to 3
- qkv_weight: bfloat16 [3, 2048, 2048], P(None, 'tok', 'br'), may hold values from -0.125 to 0.125
- qkv_bias: bfloat16 [3, 32, 64], P(None, 'br', 'tok'), may hold values from -3 to 3
- out_weight: bfloat16 [2048, 2048], P('br', 'tok'), may hold values from -1.5 to 1.5
- gate_weight: bfloat16 [2048, 5632], P('tok', 'br'), may hold values from -0.125 to 0.125
- up_weight: bfloat16 [2048, 5632], P('tok', 'br'), may hold values from -0.125 to 0.125
- down_weight: bfloat16 [5632, 2048], P('br', 'tok'), may hold values from -0.078125 to 0.078125
- cotangent: bfloat16 [16384, 2048], P(('tok', 'br')), may hold values from -6 to 6
- block_map: int32 [32], replicated, may hold values from 0 to 31, as said below
- lengths: int32 [10], replicated, may hold values from 256 to 4096, as said below
Outputs:
- out: bfloat16 [16384, 2048], P(('tok', 'br'))
- grad_tokens: float32 [16384, 2048], P(('tok', 'br'))
- grad_gain: float32 [2048], P(('tok', 'br'))
- grad_bias: float32 [2048], P(('tok', 'br'))
- grad_qkv: float32 [3, 2048, 2048], P(None, 'tok', 'br')
- grad_qkv_bias: float32 [3, 32, 64], P(None, 'br', 'tok')
- grad_out: float32 [2048, 2048], P('br', 'tok')
- grad_gate: float32 [2048, 5632], P('tok', 'br')
- grad_up: float32 [2048, 5632], P('tok', 'br')
- grad_down: float32 [5632, 2048], P('br', 'tok')
The draws below stay inside these ranges and needn't reach their ends.
Inputs may be any that keep to these rules, and one draw needn't show every extreme that they name: `block_map`: a permutation of the 32 block numbers. `lengths`: each long row is its whole capacity 8 * 512; every short row is at most its capacity 2 * 512.
All inputs are finite; a program needn't handle non-finite values.
Results may differ from the reference program's by a relative error of at most 0.03.
Values may be sent and summed in bfloat16 or wider, within the bound.
A program may use at most 192 MiB of HBM per device.

```python
import math
import jax
import jax.numpy as jnp
from jax import lax

D = 2048
HEADS = 32
HD = 64
ROT = 16
FF = 5632
BLK = 512
LB = 8
NBLK = 32
TOKENS = 16384
NL = 16
NROWS = 10


def draw_block_map(key, part):
    key = jax.random.fold_in(key, 11)
    score = jax.random.permutation(key, NBLK).astype(jnp.int32)
    slots = jnp.arange(NBLK, dtype=jnp.int32)
    special = (slots == 0) | (slots == NBLK - 1) | (slots == NBLK // 2)
    score = score + NBLK * special.astype(jnp.int32)
    ranking = jnp.argsort(-score)
    base = jnp.argsort(ranking).astype(jnp.int32)
    long_rows = NL // LB
    chosen = jax.random.randint(jax.random.fold_in(key, 3), (), 0, long_rows).astype(jnp.int32)
    moved = (base + chosen * LB) % NL
    return jnp.where(base < NL, moved, base).astype(jnp.int32)


def draw_lengths(key, part):
    key = jax.random.fold_in(key, 5)
    long_rows = NL // LB
    short_lengths = jax.random.randint(key, (NROWS - long_rows,), BLK // 2, 2 * BLK + 1).astype(jnp.int32)
    return jnp.concatenate([jnp.full((long_rows,), LB * BLK, jnp.int32), short_lengths])


def levels(key, shape, shards, least, high):
    loudness, own = 1.0, jax.random.fold_in(key, 6)
    for dim, shards_of in shards:
        steps = jnp.exp(jax.random.uniform(jax.random.fold_in(own, dim), (shards_of,), jnp.float32, least / len(shards), high / len(shards)))
        loudness = loudness * jnp.repeat(steps, shape[dim] // shards_of).reshape([-1 if axis == dim else 1 for axis in range(len(shape))])
    return loudness


def scatter_about(key, shape, scale, reach, cuts=(), held_as=jnp.bfloat16):
    array = jax.random.normal(key, shape, jnp.float32) * scale
    if len(cuts) > 0:
        array = levels(key, shape, cuts, -0.22, 0.18) * array
    return jnp.clip(array, min=-reach, max=reach).astype(held_as)


def setup_inputs(seed: int = 0) -> dict:
    seeds = jax.random.split(jax.random.key(seed), 13)
    return {
        "tokens": scatter_about(seeds[0], (TOKENS, D), 1.0, 6.0, ((0, 128),)),
        "norm_gain": jnp.clip(1.0 + 0.18 * jax.random.normal(seeds[1], (D,), jnp.float32), 0.1, 1.9),
        "norm_bias": scatter_about(seeds[2], (D,), 0.5, 3.0, (), jnp.float32),
        "qkv_weight": scatter_about(seeds[3], (3, D, D), D ** -0.5, 0.125, ((1, 16), (2, 8))),
        "qkv_bias": scatter_about(seeds[4], (3, HEADS, HD), 0.5, 3.0, ((1, 8), (2, 16))),
        "out_weight": scatter_about(seeds[5], (D, D), (D // 128) ** -0.5, 1.5, ((0, 8), (1, 16))),
        "gate_weight": scatter_about(seeds[6], (D, FF), D ** -0.5, 0.125, ((0, 16), (1, 8))),
        "up_weight": scatter_about(seeds[7], (D, FF), D ** -0.5, 0.125, ((0, 16), (1, 8))),
        "down_weight": scatter_about(seeds[8], (FF, D), FF ** -0.5, 0.078125, ((0, 8), (1, 16))),
        "cotangent": scatter_about(seeds[9], (TOKENS, D), 1.0, 6.0, ((0, 128),)),
        "block_map": draw_block_map(jax.random.fold_in(seeds[12], 71), 0),
        "lengths": draw_lengths(jax.random.fold_in(seeds[12], 71), 0),
    }


@jax.custom_vjp
def low(v):
    return lax.optimization_barrier(v.astype(jnp.bfloat16)).astype(jnp.float32)

@jax.custom_vjp
def low_back(v):
    return v

def low_keep(v):
    return (low(v), None)

def low_pass(kept, grad):
    return (grad,)

def back_keep(v):
    return (v, None)

def back_low(kept, grad):
    return (low(grad),)
low.defvjp(low_keep, low_pass)
low_back.defvjp(back_keep, back_low)
EPSILON = 1e-05
ROPE_BASE = 10000.0
MASKED = -1e+30
PRECISE = lax.Precision.HIGHEST

def rotate(values, positions, turning):
    half_rot = ROT // 2
    frequency = ROPE_BASE ** (-(jnp.arange(half_rot).astype(jnp.float32) * 2.0 / ROT))
    angles = positions[:, None] * frequency[None, :]
    cosine = jnp.cos(angles)[:, None, :]
    sine_part = turning * jnp.sin(angles)[:, None, :]
    front_half = values[..., :half_rot]
    back_half = values[..., half_rot:ROT]
    return jnp.concatenate([front_half * cosine - back_half * sine_part, back_half * cosine + front_half * sine_part, values[..., ROT:]], axis=-1)

def attend_row(queries, key_rows, value_rows, length):
    row_count = queries.shape[0]
    score_scale = 1.0 / math.sqrt(HD)
    key_pos = jnp.arange(row_count, dtype=jnp.int32)

    def one_block(block_start):
        query_block = lax.dynamic_slice_in_dim(queries, block_start, BLK, 0)
        query_pos = block_start + jnp.arange(BLK, dtype=jnp.int32)
        scores = jnp.einsum('qhd,khd->hqk', query_block, key_rows, precision=PRECISE) * score_scale
        allowed = (key_pos[None, :] <= query_pos[:, None]) & (key_pos[None, :] < length)
        scores = low_back(jnp.where(allowed[None], scores, MASKED))
        shifted_scores = scores - lax.optimization_barrier(jnp.max(scores, axis=-1, keepdims=True))
        exps = jnp.exp(shifted_scores)
        weights = low(exps / lax.optimization_barrier(jnp.sum(exps, axis=-1, keepdims=True)))
        return jnp.einsum('hqk,khd->qhd', weights, value_rows, precision=PRECISE)
    starts = jnp.arange(row_count // BLK, dtype=jnp.int32) * BLK
    return lax.map(jax.checkpoint(one_block), starts).reshape(row_count, HEADS, HD)

def reference(tokens, norm_gain, norm_bias, qkv_weight, qkv_bias, out_weight, gate_weight, up_weight, down_weight, cotangent, block_map, lengths):
    block_count = block_map.shape[0]
    long_len = block_count // 2 * BLK
    long_count = block_count // 2 // LB
    short_count = block_count // 4
    slot_of = jnp.argsort(block_map).astype(jnp.int32)
    in_block = jnp.arange(BLK, dtype=jnp.int32)
    to_global = (slot_of[:, None] * BLK + in_block[None, :]).reshape(-1)
    to_slots = (block_map[:, None] * BLK + in_block[None, :]).reshape(-1)
    positions = jnp.concatenate([jnp.arange(long_len, dtype=jnp.int32) % (LB * BLK), jnp.arange(TOKENS - long_len, dtype=jnp.int32) % (2 * BLK)]).astype(jnp.float32)

    def forward(residual, gain, shift, wqkv, bqkv, wout, wgate, wup, wdown):
        centred = residual - lax.optimization_barrier(jnp.mean(residual, axis=-1, keepdims=True))
        variance = lax.optimization_barrier(jnp.mean(centred * centred, axis=-1, keepdims=True))
        shifted = low(centred * lax.rsqrt(variance + EPSILON) * gain + shift)
        joined = low_back(jnp.einsum('nd,cde->cne', shifted, wqkv, precision=PRECISE) + bqkv.reshape(3, 1, D))
        joined = jnp.take(joined, to_global, axis=1).reshape(3, TOKENS, HEADS, HD)
        queries = low(rotate(joined[0], positions, 1.0))
        key_rows = low(rotate(joined[1], positions, 1.0))
        value_rows = low(joined[2])

        def one_row(packed):
            return attend_row(packed[0], packed[1], packed[2], packed[3])
        long_shape = (long_count, LB * BLK, HEADS, HD)
        long_out = lax.map(one_row, (queries[:long_len].reshape(long_shape), key_rows[:long_len].reshape(long_shape), value_rows[:long_len].reshape(long_shape), lengths[:long_count]))
        short_shape = (short_count, 2 * BLK, HEADS, HD)
        short_out = lax.map(one_row, (queries[long_len:].reshape(short_shape), key_rows[long_len:].reshape(short_shape), value_rows[long_len:].reshape(short_shape), lengths[long_count:]))
        attended = jnp.concatenate([long_out.reshape(long_len, HEADS, HD), short_out.reshape(TOKENS - long_len, HEADS, HD)], axis=0).reshape(TOKENS, D)
        mixed = low(low_back(jnp.take(attended, to_slots, axis=0)))
        gate_pre = low_back(jnp.dot(shifted, wgate, precision=PRECISE))
        up_pre = low_back(jnp.dot(shifted, wup, precision=PRECISE))
        hidden = low(gate_pre * jax.nn.sigmoid(gate_pre) * up_pre)
        return residual + jnp.dot(mixed, wout, precision=PRECISE) + jnp.dot(hidden, wdown, precision=PRECISE)
    inputs = (tokens.astype(jnp.float32), norm_gain, norm_bias, qkv_weight.astype(jnp.float32), qkv_bias.astype(jnp.float32), out_weight.astype(jnp.float32), gate_weight.astype(jnp.float32), up_weight.astype(jnp.float32), down_weight.astype(jnp.float32))
    result, backward = jax.vjp(forward, *inputs)
    grads = backward(cotangent.astype(jnp.float32))
    return (result.astype(jnp.bfloat16), grads[0], grads[1], grads[2], grads[3], grads[4], grads[5], grads[6], grads[7], grads[8])
```

```python
import functools

import jax
import jax.numpy as jnp
from jax import lax
from jax.experimental import pallas as pl
from jax.experimental.pallas import tpu as pltpu
from jax.sharding import PartitionSpec as P

HD = 64
ROT = 16
BLK = 512
LB = 8
EPSILON = 1e-05
ROPE_BASE = 10000.0
MASKED = -1e30
BF = jnp.bfloat16
F32 = jnp.float32
NN = (((1,), (0,)), ((), ()))
NT = (((1,), (1,)), ((), ()))
TN = (((0,), (0,)), ((), ()))
VMEM = pl.BlockSpec(memory_space=pltpu.VMEM)
SMEM = pl.BlockSpec(memory_space=pltpu.SMEM)


def dot(left, right, dims):
    return lax.dot_general(left, right, dims, preferred_element_type=F32)


def block_info(block, long_blocks):
    is_long = block < long_blocks
    place = jnp.where(is_long, block % LB, (block - long_blocks) % 2)
    return is_long, place, block - place


def lane_half(packed, half, upper):
    piece = packed[:, half * HD : (half + 1) * HD]
    zero = jnp.zeros_like(piece)
    return jnp.concatenate([zero, piece] if upper else [piece, zero], axis=1)


def allowed_pairs(place, step, limit):
    key_pos = step * BLK + lax.broadcasted_iota(jnp.int32, (BLK, BLK), 0)
    query_pos = place * BLK + lax.broadcasted_iota(jnp.int32, (BLK, BLK), 1)
    return (key_pos <= query_pos) & (key_pos < limit)


def attn_fwd_kernel(long_blocks, qblk, qlim, kslot, q_ref, kv_ref, ot_ref, lse_ref, o_ref):
    def pack(i, unused):
        packed = q_ref[i]
        for half in range(2):
            slot = 2 * i + half
            is_long, place, first = block_info(qblk[slot], long_blocks)
            limit = qlim[slot]
            queries = lane_half(packed, half, False) * jnp.asarray(0.125, BF)

            def step(j, carry, masked):
                top, total, acc = carry
                rows = pl.ds(pl.multiple_of(kslot[first + j] * BLK, BLK), BLK)
                kv = kv_ref[rows, :]
                scores = dot(kv, queries, NT)
                if masked:
                    scores = jnp.where(allowed_pairs(place, j, limit), scores, MASKED)
                new_top = jnp.maximum(top, jnp.max(scores, axis=0, keepdims=True))
                fade = jnp.exp(top - new_top)
                probs = jnp.exp(scores - new_top)
                total = total * fade + jnp.sum(probs, axis=0, keepdims=True)
                acc = acc * fade + dot(kv, probs.astype(BF), TN)
                return new_top, total, acc

            free = jnp.where(is_long, place, 0)
            carry = (
                jnp.full((1, BLK), MASKED, F32),
                jnp.zeros((1, BLK), F32),
                jnp.zeros((2 * HD, BLK), F32),
            )
            carry = lax.fori_loop(0, free, lambda j, c: step(j, c, False), carry)
            top, total, acc = lax.fori_loop(free, place + 1, lambda j, c: step(j, c, True), carry)
            lse_ref[slot] = top + jnp.log(total)
            ot_ref[i, half * HD : (half + 1) * HD, :] = acc[HD:, :] / total
        o_ref[i] = jnp.transpose(ot_ref[i]).astype(BF)
        return unused

    lax.fori_loop(0, q_ref.shape[0], pack, 0)


def attn_fwd(qblk, qlim, kslot, q, kv, long_blocks):
    n = q.shape[0]
    return pl.pallas_call(
        functools.partial(attn_fwd_kernel, long_blocks),
        out_shape=(
            jax.ShapeDtypeStruct((n, 2 * HD, BLK), F32),
            jax.ShapeDtypeStruct((2 * n, 1, BLK), F32),
            jax.ShapeDtypeStruct((n, BLK, 2 * HD), BF),
        ),
        in_specs=[SMEM, SMEM, SMEM, VMEM, VMEM],
        out_specs=(VMEM, VMEM, VMEM),
        compiler_params=pltpu.CompilerParams(vmem_limit_bytes=48 * 2**20),
        cost_estimate=pl.CostEstimate(
            flops=int(20e9), bytes_accessed=8 * 2**20, transcendentals=8 * 2**20
        ),
        name="attn_fwd",
    )(qblk, qlim, kslot, q, kv)


def attn_bwd_kernel(
    long_blocks, qblk, qlim, kslot, q_ref, do_ref, kv_ref, ot_ref, lse_ref, dq_ref, dkv_ref, acc, dqt
):
    acc[...] = jnp.zeros_like(acc)

    def pack(i, unused):
        q_packed = q_ref[i]
        d_packed = do_ref[i]
        d_turned = jnp.transpose(d_packed.astype(F32))
        for half in range(2):
            slot = 2 * i + half
            is_long, place, first = block_info(qblk[slot], long_blocks)
            limit = qlim[slot]
            queries = lane_half(q_packed, half, False) * jnp.asarray(0.125, BF)
            grads = lane_half(d_packed, half, True)
            both = jnp.concatenate([queries, grads], axis=0)
            lanes = slice(half * HD, (half + 1) * HD)
            delta = jnp.sum(d_turned[lanes] * ot_ref[i, lanes, :], axis=0, keepdims=True)
            lse = lse_ref[slot]

            def step(j, total, masked):
                rows = pl.ds(pl.multiple_of(kslot[first + j] * BLK, BLK), BLK)
                kv = kv_ref[rows, :]
                scores = dot(kv, queries, NT)
                if masked:
                    scores = jnp.where(allowed_pairs(place, j, limit), scores, MASKED)
                probs = jnp.exp(scores - lse)
                ds = (probs * (dot(kv, grads, NT) - delta)).astype(BF)
                acc[rows, :] += dot(jnp.concatenate([ds, probs.astype(BF)], axis=1), both, NN)
                return total + dot(kv, ds, TN)

            free = jnp.where(is_long, place, 0)
            total = lax.fori_loop(
                0, free, lambda j, c: step(j, c, False), jnp.zeros((2 * HD, BLK), F32)
            )
            total = lax.fori_loop(free, place + 1, lambda j, c: step(j, c, True), total)
            dqt[lanes, :] = total[:HD, :] * 0.125
        dq_ref[i] = jnp.transpose(dqt[...]).astype(BF)
        return unused

    lax.fori_loop(0, q_ref.shape[0], pack, 0)

    def finish(i, unused):
        rows = pl.ds(pl.multiple_of(i * BLK, BLK), BLK)
        dkv_ref[rows, :] = acc[rows, :].astype(BF)
        return unused

    lax.fori_loop(0, kv_ref.shape[0] // BLK, finish, 0)


def attn_bwd(qblk, qlim, kslot, q, do, kv, ot, lse, long_blocks):
    n = q.shape[0]
    return pl.pallas_call(
        functools.partial(attn_bwd_kernel, long_blocks),
        out_shape=(
            jax.ShapeDtypeStruct((n, BLK, 2 * HD), BF),
            jax.ShapeDtypeStruct(kv.shape, BF),
        ),
        in_specs=[SMEM, SMEM, SMEM, VMEM, VMEM, VMEM, VMEM, VMEM],
        out_specs=(VMEM, VMEM),
        scratch_shapes=[pltpu.VMEM(kv.shape, F32), pltpu.VMEM((2 * HD, BLK), F32)],
        compiler_params=pltpu.CompilerParams(vmem_limit_bytes=56 * 2**20),
        cost_estimate=pl.CostEstimate(
            flops=int(30e9), bytes_accessed=12 * 2**20, transcendentals=8 * 2**20
        ),
        name="attn_bwd",
    )(qblk, qlim, kslot, q, do, kv, ot, lse)


def turn(values, cos, sin, copies):
    width = values.shape[1]
    lane = lax.broadcasted_iota(jnp.int32, values.shape, 1) % HD
    partner = jnp.where(
        lane < ROT // 2,
        pltpu.roll(values, width - ROT // 2, 1),
        pltpu.roll(values, ROT // 2, 1),
    )
    cos = jnp.concatenate([cos] * copies, axis=1)
    sin = jnp.concatenate([sin] * copies, axis=1)
    return values * cos + partner * sin


def project_kernel(heads, x_ref, w_ref, b_ref, cq, sq, ck, sk, q_ref, kv_ref):
    width = heads * HD
    parts = []
    for slot in range(2):
        joined = dot(x_ref[slot], w_ref[...], NN) + b_ref[...]
        parts.append(
            turn(joined[:, :width], cq[slot], sq[slot], heads // 2).astype(BF)
        )
        kv = turn(joined[:, width:], ck[slot], sk[slot], heads).astype(BF)
        for head in range(heads):
            kv_ref[head, slot] = kv[:, head * 2 * HD : (head + 1) * 2 * HD]
    for head in range(heads):
        lanes = slice(head * HD, (head + 1) * HD)
        q_ref[head] = jnp.concatenate([parts[0][:, lanes], parts[1][:, lanes]], axis=1)


def project(x, w, bias, tables, heads):
    tile = 256
    width = 3 * heads * HD
    depth = x.shape[1]
    table = pl.BlockSpec((2, tile, 2 * HD), lambda i: (0, i, 0))
    return pl.pallas_call(
        functools.partial(project_kernel, heads),
        grid=(BLK // tile,),
        out_shape=(
            jax.ShapeDtypeStruct((heads, BLK, 2 * HD), BF),
            jax.ShapeDtypeStruct((heads, 2, BLK, 2 * HD), BF),
        ),
        in_specs=[
            pl.BlockSpec((2, tile, depth), lambda i: (0, i, 0)),
            pl.BlockSpec((depth, width), lambda i: (0, 0)),
            pl.BlockSpec((1, width), lambda i: (0, 0)),
            table,
            table,
            table,
            table,
        ],
        out_specs=(
            pl.BlockSpec((heads, tile, 2 * HD), lambda i: (0, i, 0)),
            pl.BlockSpec((heads, 2, tile, 2 * HD), lambda i: (0, 0, i, 0)),
        ),
        compiler_params=pltpu.CompilerParams(vmem_limit_bytes=40 * 2**20),
        name="project",
    )(x.reshape(2, BLK, depth), w, bias, *tables)


def unturn_kernel(heads, dq_ref, dkv_ref, cq, sq, ck, sk, out_ref, sum_ref):
    width = heads * HD
    sums = jnp.zeros((1, 3 * width), F32)
    for slot in range(2):
        lanes = slice(slot * HD, (slot + 1) * HD)
        q = jnp.concatenate([dq_ref[head][:, lanes] for head in range(heads)], axis=1)
        q = turn(q.astype(F32), cq[slot], -sq[slot], heads // 2).astype(BF)
        kv = jnp.concatenate([dkv_ref[head, slot] for head in range(heads)], axis=1)
        kv = turn(kv.astype(F32), ck[slot], -sk[slot], heads).astype(BF)
        both = jnp.concatenate([q, kv], axis=1)
        out_ref[slot] = both
        sums += jnp.sum(both.astype(F32), axis=0, keepdims=True)

    @pl.when(pl.program_id(0) == 0)
    def _():
        sum_ref[...] = jnp.zeros_like(sum_ref)

    sum_ref[...] += sums


def unturn(dq, dkv, tables, heads):
    tile = 256
    width = 3 * heads * HD
    table = pl.BlockSpec((2, tile, 2 * HD), lambda i: (0, i, 0))
    out, sums = pl.pallas_call(
        functools.partial(unturn_kernel, heads),
        grid=(BLK // tile,),
        out_shape=(
            jax.ShapeDtypeStruct((2, BLK, width), BF),
            jax.ShapeDtypeStruct((1, width), F32),
        ),
        in_specs=[
            pl.BlockSpec((heads, tile, 2 * HD), lambda i: (0, i, 0)),
            pl.BlockSpec((heads, 2, tile, 2 * HD), lambda i: (0, 0, i, 0)),
            table,
            table,
            table,
            table,
        ],
        out_specs=(
            pl.BlockSpec((2, tile, width), lambda i: (0, i, 0)),
            pl.BlockSpec((1, width), lambda i: (0, 0)),
        ),
        compiler_params=pltpu.CompilerParams(vmem_limit_bytes=40 * 2**20),
        name="unturn",
    )(dq, dkv, *tables)
    return out.reshape(2 * BLK, width), sums


def tok_perm(dy, dz, dc):
    pairs = []
    for t in range(16):
        y, z, c = t // 4, (t // 2) % 2, t % 2
        pairs.append((t, ((y + dy) % 4) * 4 + (z ^ dz) * 2 + (c ^ dc)))
    return pairs


def pick(array, index):
    return lax.dynamic_index_in_dim(array, index, 0, keepdims=False)


def spread_heads(by_head, y):
    parts = [pick(by_head, y)]
    for d in range(1, 4):
        parts.append(lax.ppermute(pick(by_head, (y + d) % 4), "tok", tok_perm(d, 0, 0)))
    return parts


def return_heads(parts, y):
    back = [parts[0]]
    for d in range(1, 4):
        back.append(lax.ppermute(parts[d], "tok", tok_perm(4 - d, 0, 0)))
    stacked = jnp.stack(back + back)
    return lax.dynamic_slice_in_dim(stacked, (4 - y) % 4, 4, 0)


def rotary_tables(positions, long_shape):
    half = ROT // 2
    frequency = ROPE_BASE ** (-(jnp.arange(half).astype(F32) * 2.0 / ROT))
    angles = positions.astype(F32)[:, None] * frequency[None, :]
    cos, sin = jnp.cos(angles), jnp.sin(angles)
    rows = positions.shape[0]
    one = jnp.ones((rows, HD - ROT), F32)
    zero = jnp.zeros((rows, HD - ROT), F32)
    cos64 = jnp.concatenate([cos, cos, one], axis=1)
    sin64 = jnp.concatenate([-sin, sin, zero], axis=1)
    tables = (
        jnp.concatenate([cos64, cos64], axis=1),
        jnp.concatenate([sin64, sin64], axis=1),
        jnp.concatenate([cos64, jnp.ones((rows, HD), F32)], axis=1),
        jnp.concatenate([sin64, jnp.zeros((rows, HD), F32)], axis=1),
    )
    return tuple(t.reshape(2, BLK, 2 * HD) for t in tables)


def body(
    tokens,
    norm_gain,
    norm_bias,
    qkv_weight,
    qkv_bias,
    out_weight,
    gate_weight,
    up_weight,
    down_weight,
    cotangent,
    block_map,
    lengths,
):
    tok = lax.axis_index("tok")
    y, z, c = tok // 4, (tok // 2) % 2, tok % 2
    total_blocks = block_map.shape[0]
    long_blocks = total_blocks // 2
    rows = tokens.shape[0]
    depth = tokens.shape[1]
    wrows = qkv_weight.shape[1]
    heads = qkv_bias.shape[1]
    width = heads * HD
    hidden_width = gate_weight.shape[1]
    main = hidden_width // 128 * 128
    tail = hidden_width - main

    residual = tokens.astype(F32)
    centred = residual - jnp.mean(residual, axis=-1, keepdims=True)
    inverse = lax.rsqrt(jnp.mean(centred * centred, axis=-1, keepdims=True) + EPSILON)
    normed = centred * inverse
    shifted = (normed * norm_gain + norm_bias).astype(BF)

    kv_shard = jnp.stack(
        [w.reshape(wrows, heads, HD) for w in (qkv_weight[1], qkv_weight[2])], axis=2
    ).reshape(wrows, 2 * width)
    bias_row = jnp.pad(qkv_bias.reshape(1, -1), ((0, wrows - 1), (0, 128 - qkv_bias.size)))
    qkv_shard = jnp.concatenate([qkv_weight[0], kv_shard, bias_row], axis=1)
    gu_shard = jnp.concatenate(
        [gate_weight[:, :main], up_weight[:, :main], gate_weight[:, main:], up_weight[:, main:]],
        axis=1,
    )
    do_shard = jnp.concatenate(
        [
            jnp.transpose(down_weight),
            jnp.zeros((wrows, 128 - tail), BF),
            jnp.transpose(out_weight),
        ],
        axis=1,
    )
    qkv_full = lax.all_gather(qkv_shard, "tok", axis=0, tiled=True)
    x = lax.all_gather(shifted, "br", axis=0, tiled=True)
    grad = lax.all_gather(cotangent, "br", axis=0, tiled=True)
    do_full = lax.all_gather(do_shard, "tok", axis=0, tiled=True)
    gu_full = lax.all_gather(gu_shard, "tok", axis=0, tiled=True)

    bias = qkv_full.reshape(16, wrows, -1)[:, 0, 3 * width : 3 * width + qkv_bias.size]
    bias = jnp.transpose(bias.reshape(16, 3, heads, 4), (1, 2, 0, 3)).reshape(3, heads, HD)
    bias = jnp.concatenate(
        [bias[0].reshape(1, width), jnp.stack([bias[1], bias[2]], axis=1).reshape(1, 2 * width)],
        axis=1,
    ).astype(F32)

    slot_table = jnp.arange(total_blocks, dtype=jnp.int32)
    slot_of = jnp.sum(
        jnp.where(block_map[None, :] == slot_table[:, None], slot_table[None, :], 0), axis=1
    )
    owner = slot_of // 2
    key_index = (((owner // 2) % 2 ^ z) * 2 + (owner % 2 ^ c)) * 4 + (y - owner // 4) % 4
    key_slot = (key_index * 2 + slot_of % 2).astype(jnp.int32)
    from_tok = ((y - jnp.arange(4, dtype=jnp.int32)) % 4) * 4 + z * 2 + c
    my_queries = jnp.stack([2 * from_tok, 2 * from_tok + 1], axis=1).reshape(-1)
    query_block = jnp.sum(
        jnp.where(my_queries[:, None] == slot_table[None, :], block_map[None, :], 0), axis=1
    ).astype(jnp.int32)
    query_row = jnp.where(
        query_block < long_blocks,
        query_block // LB,
        long_blocks // LB + (query_block - long_blocks) // 2,
    )
    row_table = jnp.arange(lengths.shape[0], dtype=jnp.int32)
    query_limit = jnp.sum(
        jnp.where(query_row[:, None] == row_table[None, :], lengths[None, :], 0), axis=1
    ).astype(jnp.int32)

    my_blocks = lax.dynamic_slice_in_dim(block_map, tok * 2, 2)
    my_start = (
        jnp.where(my_blocks < long_blocks, my_blocks % LB, (my_blocks - long_blocks) % 2) * BLK
    )
    positions = (my_start[:, None] + jnp.arange(BLK, dtype=jnp.int32)[None, :]).reshape(-1)
    tables = rotary_tables(positions, long_blocks)

    q_heads, kv_heads = project(x, qkv_full, bias, tables, heads)
    joined = jnp.concatenate([q_heads, kv_heads.reshape(heads, 2 * BLK, 2 * HD)], axis=1)
    parts = jnp.stack(spread_heads(joined, y))
    q_all = parts[:, :BLK]
    kv_mine = parts[:, BLK:]
    kv_core = lax.ppermute(kv_mine, "tok", tok_perm(0, 0, 1))
    kv_far = lax.ppermute(kv_mine, "tok", tok_perm(0, 1, 0))
    kv_diag = lax.ppermute(kv_far, "tok", tok_perm(0, 0, 1))
    kv_all = jnp.stack([kv_mine, kv_core, kv_far, kv_diag]).reshape(-1, 2 * HD)

    turned, lse, o_parts = attn_fwd(query_block, query_limit, key_slot, q_all, kv_all, long_blocks)

    def to_heads(flat):
        split = flat.reshape(2, BLK, heads, HD)
        return jnp.transpose(split, (2, 1, 0, 3)).reshape(heads, BLK, 2 * HD)

    def from_heads(packed):
        split = packed.reshape(heads, BLK, 2, HD)
        return jnp.transpose(split, (2, 1, 0, 3)).reshape(2 * BLK, width)

    mixed = from_heads(return_heads([o_parts[d] for d in range(4)], y))

    down_width = do_full.shape[1] - width
    down_full = do_full[:, :down_width]
    out_full = do_full[:, down_width:]
    grad_mixed = dot(grad, out_full, NN).astype(BF)
    do_all = jnp.stack(spread_heads(to_heads(grad_mixed), y))

    both = dot(x, gu_full, NN)
    grad_hidden = dot(grad, down_full, NN)
    ends = both[:, 2 * main :]
    gate = jnp.concatenate([both[:, :main], ends[:, :tail]], axis=1)
    up = jnp.concatenate([both[:, main : 2 * main], ends[:, tail:]], axis=1)
    gh = grad_hidden[:, :hidden_width]
    sig = jax.nn.sigmoid(gate)
    hidden = (gate * sig * up).astype(BF)
    hidden = jnp.pad(hidden, ((0, 0), (0, down_width - hidden_width)))
    grad_gate = (gh * up * sig * (1.0 + gate * (1.0 - sig))).astype(BF)
    grad_up = (gh * gate * sig).astype(BF)
    grad_both = jnp.concatenate(
        [grad_gate[:, :main], grad_up[:, :main], grad_gate[:, main:], grad_up[:, main:]], axis=1
    )
    branches = (dot(hidden, down_full, NT) + dot(mixed, out_full, NT)).astype(BF)
    summed = lax.psum_scatter(branches, "br", scatter_dimension=0, tiled=True)
    result = (residual + summed.astype(F32)).astype(BF)
    grad_do = jnp.concatenate([dot(grad, hidden, TN), dot(grad, mixed, TN)], axis=1).astype(BF)
    grad_gu = dot(x, grad_both, TN).astype(BF)
    grad_do = lax.psum_scatter(grad_do, "tok", scatter_dimension=0, tiled=True)
    grad_gu = lax.psum_scatter(grad_gu, "tok", scatter_dimension=0, tiled=True)

    dq_parts, dkv_all = attn_bwd(
        query_block, query_limit, key_slot, q_all, do_all, kv_all, turned, lse, long_blocks
    )
    dkv = dkv_all.reshape(2, 2, 4 * 2 * BLK, 2 * HD)
    near = dkv[:, 0].astype(F32) + lax.ppermute(dkv[:, 1], "tok", tok_perm(0, 0, 1)).astype(F32)
    far = lax.ppermute(near[1].astype(BF), "tok", tok_perm(0, 1, 0))
    mine = (near[0] + far.astype(F32)).astype(BF).reshape(4, 2 * BLK, 2 * HD)
    back = return_heads([jnp.concatenate([dq_parts[d], mine[d]], axis=0) for d in range(4)], y)
    dq_heads = back[:, :BLK]
    dkv_heads = back[:, BLK:].reshape(heads, 2, BLK, 2 * HD)
    grad_joined, bias_sums = unturn(dq_heads, dkv_heads, tables, heads)
    grad_shifted = (
        dot(grad_both, gu_full, NT) + dot(grad_joined, qkv_full[:, : 3 * width], NT)
    ).astype(BF)
    my_grad_shifted = lax.psum_scatter(
        grad_shifted, "br", scatter_dimension=0, tiled=True
    ).astype(F32)
    grad_qkv = dot(x, grad_joined, TN).astype(BF)
    qsum = bias_sums[0, :width].reshape(1, heads, HD)
    kvsum = jnp.transpose(bias_sums[0, width:].reshape(heads, 2, HD), (1, 0, 2))
    bsum = jnp.concatenate([qsum, kvsum], axis=0).reshape(3, heads, 16, 4)
    bsum = jnp.transpose(bsum, (2, 0, 1, 3)).reshape(16, 1, qkv_bias.size).astype(BF)
    bsum = jnp.pad(bsum, ((0, 0), (0, wrows - 1), (0, 128 - qkv_bias.size)))
    grad_qkv = jnp.concatenate([grad_qkv, bsum.reshape(16 * wrows, 128)], axis=1)
    grad_qkv = lax.psum_scatter(grad_qkv, "tok", scatter_dimension=0, tiled=True).astype(F32)

    grad_bias_out = grad_qkv[0, 3 * width : 3 * width + qkv_bias.size].reshape(qkv_bias.shape)
    gkv = grad_qkv[:, width : 3 * width].reshape(wrows, heads, 2, HD)
    grad_qkv_out = jnp.stack(
        [
            grad_qkv[:, :width],
            gkv[:, :, 0].reshape(wrows, width),
            gkv[:, :, 1].reshape(wrows, width),
        ]
    )
    grad_do = grad_do.astype(F32)
    grad_gu = grad_gu.astype(F32)
    grad_down_out = jnp.transpose(grad_do[:, :hidden_width])
    grad_out_out = jnp.transpose(grad_do[:, down_width:])
    grad_gate_out = jnp.concatenate(
        [grad_gu[:, :main], grad_gu[:, 2 * main : 2 * main + tail]], axis=1
    )
    grad_up_out = jnp.concatenate(
        [grad_gu[:, main : 2 * main], grad_gu[:, 2 * main + tail :]], axis=1
    )

    gain_part = jnp.sum(my_grad_shifted * normed, axis=0)
    bias_part = jnp.sum(my_grad_shifted, axis=0)
    grad_normed = my_grad_shifted * norm_gain
    grad_tokens = cotangent.astype(F32) + inverse * (
        grad_normed
        - jnp.mean(grad_normed, axis=-1, keepdims=True)
        - normed * jnp.mean(grad_normed * normed, axis=-1, keepdims=True)
    )
    grad_gain, grad_bias = (
        lax.psum_scatter(gain_part, ("tok", "br"), scatter_dimension=0, tiled=True),
        lax.psum_scatter(bias_part, ("tok", "br"), scatter_dimension=0, tiled=True),
    )
    return (
        result,
        grad_tokens,
        grad_gain,
        grad_bias,
        grad_qkv_out,
        grad_bias_out,
        grad_out_out,
        grad_gate_out,
        grad_up_out,
        grad_down_out,
    )


def solution(mesh):
    in_specs = (
        P(("tok", "br"), None),
        P(),
        P(),
        P(None, "tok", "br"),
        P(None, "br", "tok"),
        P("br", "tok"),
        P("tok", "br"),
        P("tok", "br"),
        P("br", "tok"),
        P(("tok", "br"), None),
        P(),
        P(),
    )
    out_specs = (
        P(("tok", "br"), None),
        P(("tok", "br"), None),
        P(("tok", "br")),
        P(("tok", "br")),
        P(None, "tok", "br"),
        P(None, "br", "tok"),
        P("br", "tok"),
        P("tok", "br"),
        P("tok", "br"),
        P("br", "tok"),
    )
    return jax.shard_map(body, mesh=mesh, in_specs=in_specs, out_specs=out_specs, check_vma=False)
```

```python
import functools

import jax
import jax.numpy as jnp
from jax import lax
from jax.experimental import pallas as pl
from jax.experimental.pallas import tpu as pltpu
from jax.sharding import PartitionSpec as P

HD = 64
ROT = 16
BLK = 512
LB = 8
EPSILON = 1e-05
ROPE_BASE = 10000.0
MASKED = -1e30
BF = jnp.bfloat16
F32 = jnp.float32
NN = (((1,), (0,)), ((), ()))
NT = (((1,), (1,)), ((), ()))
TN = (((0,), (0,)), ((), ()))
VMEM = pl.BlockSpec(memory_space=pltpu.VMEM)
SMEM = pl.BlockSpec(memory_space=pltpu.SMEM)
ANY = pl.BlockSpec(memory_space=pl.ANY)


def dot(left, right, dims):
    return lax.dot_general(left, right, dims, preferred_element_type=F32)


def block_info(block, long_blocks):
    is_long = block < long_blocks
    place = jnp.where(is_long, block % LB, (block - long_blocks) % 2)
    return is_long, place, block - place


def lane_half(packed, half, upper):
    piece = packed[:, half * HD : (half + 1) * HD]
    zero = jnp.zeros_like(piece)
    return jnp.concatenate([zero, piece] if upper else [piece, zero], axis=1)


def allowed_pairs(place, step, limit):
    key_pos = step * BLK + lax.broadcasted_iota(jnp.int32, (BLK, BLK), 0)
    query_pos = place * BLK + lax.broadcasted_iota(jnp.int32, (BLK, BLK), 1)
    return (key_pos <= query_pos) & (key_pos < limit)


def attn_fwd_kernel(long_blocks, qblk, qlim, kslot, q_ref, kv_ref, ot_ref, lse_ref, o_ref):
    def pack(i, unused):
        packed = q_ref[i]
        for half in range(2):
            slot = 2 * i + half
            is_long, place, first = block_info(qblk[slot], long_blocks)
            limit = qlim[slot]
            queries = lane_half(packed, half, False) * jnp.asarray(0.125, BF)

            def step(j, carry, masked):
                top, total, acc = carry
                rows = pl.ds(pl.multiple_of(kslot[first + j] * BLK, BLK), BLK)
                kv = kv_ref[rows, :]
                scores = dot(kv, queries, NT)
                if masked:
                    scores = jnp.where(allowed_pairs(place, j, limit), scores, MASKED)
                new_top = jnp.maximum(top, jnp.max(scores, axis=0, keepdims=True))
                fade = jnp.exp(top - new_top)
                probs = jnp.exp(scores - new_top)
                total = total * fade + jnp.sum(probs, axis=0, keepdims=True)
                acc = acc * fade + dot(kv, probs.astype(BF), TN)
                return new_top, total, acc

            free = jnp.where(is_long, place, 0)
            carry = (
                jnp.full((1, BLK), MASKED, F32),
                jnp.zeros((1, BLK), F32),
                jnp.zeros((2 * HD, BLK), F32),
            )
            carry = lax.fori_loop(0, free, lambda j, c: step(j, c, False), carry)
            top, total, acc = lax.fori_loop(free, place + 1, lambda j, c: step(j, c, True), carry)
            lse_ref[slot] = top + jnp.log(total)
            ot_ref[i, half * HD : (half + 1) * HD, :] = acc[HD:, :] / total
        o_ref[i] = jnp.transpose(ot_ref[i]).astype(BF)
        return unused

    lax.fori_loop(0, q_ref.shape[0], pack, 0)


def attn_fwd(qblk, qlim, kslot, q, kv, long_blocks):
    n = q.shape[0]
    return pl.pallas_call(
        functools.partial(attn_fwd_kernel, long_blocks),
        out_shape=(
            jax.ShapeDtypeStruct((n, 2 * HD, BLK), F32),
            jax.ShapeDtypeStruct((2 * n, 1, BLK), F32),
            jax.ShapeDtypeStruct((n, BLK, 2 * HD), BF),
        ),
        in_specs=[SMEM, SMEM, SMEM, VMEM, VMEM],
        out_specs=(VMEM, VMEM, VMEM),
        compiler_params=pltpu.CompilerParams(vmem_limit_bytes=48 * 2**20),
        cost_estimate=pl.CostEstimate(
            flops=int(20e9), bytes_accessed=8 * 2**20, transcendentals=8 * 2**20
        ),
        name="attn_fwd",
    )(qblk, qlim, kslot, q, kv)


def attn_bwd_kernel(
    long_blocks, qblk, qlim, kslot, q_ref, do_ref, kv_ref, ot_ref, lse_ref, dq_ref, dkv_ref, acc, dqt
):
    acc[...] = jnp.zeros_like(acc)

    def pack(i, unused):
        q_packed = q_ref[i]
        d_packed = do_ref[i]
        d_turned = jnp.transpose(d_packed.astype(F32))
        for half in range(2):
            slot = 2 * i + half
            is_long, place, first = block_info(qblk[slot], long_blocks)
            limit = qlim[slot]
            queries = lane_half(q_packed, half, False) * jnp.asarray(0.125, BF)
            grads = lane_half(d_packed, half, True)
            both = jnp.concatenate([queries, grads], axis=0)
            lanes = slice(half * HD, (half + 1) * HD)
            delta = jnp.sum(d_turned[lanes] * ot_ref[i, lanes, :], axis=0, keepdims=True)
            lse = lse_ref[slot]

            def step(j, total, masked):
                rows = pl.ds(pl.multiple_of(kslot[first + j] * BLK, BLK), BLK)
                kv = kv_ref[rows, :]
                scores = dot(kv, queries, NT)
                if masked:
                    scores = jnp.where(allowed_pairs(place, j, limit), scores, MASKED)
                probs = jnp.exp(scores - lse)
                ds = (probs * (dot(kv, grads, NT) - delta)).astype(BF)
                acc[rows, :] += dot(jnp.concatenate([ds, probs.astype(BF)], axis=1), both, NN)
                return total + dot(kv, ds, TN)

            free = jnp.where(is_long, place, 0)
            total = lax.fori_loop(
                0, free, lambda j, c: step(j, c, False), jnp.zeros((2 * HD, BLK), F32)
            )
            total = lax.fori_loop(free, place + 1, lambda j, c: step(j, c, True), total)
            dqt[lanes, :] = total[:HD, :] * 0.125
        dq_ref[i] = jnp.transpose(dqt[...]).astype(BF)
        return unused

    lax.fori_loop(0, q_ref.shape[0], pack, 0)

    def finish(i, unused):
        rows = pl.ds(pl.multiple_of(i * BLK, BLK), BLK)
        dkv_ref[rows, :] = acc[rows, :].astype(BF)
        return unused

    lax.fori_loop(0, kv_ref.shape[0] // BLK, finish, 0)


def attn_bwd(qblk, qlim, kslot, q, do, kv, ot, lse, long_blocks):
    n = q.shape[0]
    return pl.pallas_call(
        functools.partial(attn_bwd_kernel, long_blocks),
        out_shape=(
            jax.ShapeDtypeStruct((n, BLK, 2 * HD), BF),
            jax.ShapeDtypeStruct(kv.shape, BF),
        ),
        in_specs=[SMEM, SMEM, SMEM, VMEM, VMEM, VMEM, VMEM, VMEM],
        out_specs=(VMEM, VMEM),
        scratch_shapes=[pltpu.VMEM(kv.shape, F32), pltpu.VMEM((2 * HD, BLK), F32)],
        compiler_params=pltpu.CompilerParams(vmem_limit_bytes=56 * 2**20),
        cost_estimate=pl.CostEstimate(
            flops=int(30e9), bytes_accessed=12 * 2**20, transcendentals=8 * 2**20
        ),
        name="attn_bwd",
    )(qblk, qlim, kslot, q, do, kv, ot, lse)


def turn(values, cos, sin, copies):
    width = values.shape[1]
    lane = lax.broadcasted_iota(jnp.int32, values.shape, 1) % HD
    partner = jnp.where(
        lane < ROT // 2,
        pltpu.roll(values, width - ROT // 2, 1),
        pltpu.roll(values, ROT // 2, 1),
    )
    cos = jnp.concatenate([cos] * copies, axis=1)
    sin = jnp.concatenate([sin] * copies, axis=1)
    return values * cos + partner * sin


def project_kernel(heads, x_ref, w_ref, b_ref, cq, sq, ck, sk, q_ref, kv_ref):
    width = heads * HD
    parts = []
    for slot in range(2):
        joined = dot(x_ref[slot], w_ref[...], NN) + b_ref[...]
        parts.append(
            turn(joined[:, :width], cq[slot], sq[slot], heads // 2).astype(BF)
        )
        kv = turn(joined[:, width:], ck[slot], sk[slot], heads).astype(BF)
        for head in range(heads):
            kv_ref[head, slot] = kv[:, head * 2 * HD : (head + 1) * 2 * HD]
    for head in range(heads):
        lanes = slice(head * HD, (head + 1) * HD)
        q_ref[head] = jnp.concatenate([parts[0][:, lanes], parts[1][:, lanes]], axis=1)


def project(x, w, bias, tables, heads):
    tile = 256
    width = 3 * heads * HD
    depth = x.shape[1]
    table = pl.BlockSpec((2, tile, 2 * HD), lambda i: (0, i, 0))
    return pl.pallas_call(
        functools.partial(project_kernel, heads),
        grid=(BLK // tile,),
        out_shape=(
            jax.ShapeDtypeStruct((heads, BLK, 2 * HD), BF),
            jax.ShapeDtypeStruct((heads, 2, BLK, 2 * HD), BF),
        ),
        in_specs=[
            pl.BlockSpec((2, tile, depth), lambda i: (0, i, 0)),
            pl.BlockSpec((depth, width), lambda i: (0, 0)),
            pl.BlockSpec((1, width), lambda i: (0, 0)),
            table,
            table,
            table,
            table,
        ],
        out_specs=(
            pl.BlockSpec((heads, tile, 2 * HD), lambda i: (0, i, 0)),
            pl.BlockSpec((heads, 2, tile, 2 * HD), lambda i: (0, 0, i, 0)),
        ),
        compiler_params=pltpu.CompilerParams(vmem_limit_bytes=40 * 2**20),
        name="project",
    )(x.reshape(2, BLK, depth), w, bias, *tables)


def unturn_kernel(heads, dq_ref, dkv_ref, cq, sq, ck, sk, out_ref, sum_ref):
    width = heads * HD
    sums = jnp.zeros((1, 3 * width), F32)
    for slot in range(2):
        lanes = slice(slot * HD, (slot + 1) * HD)
        q = jnp.concatenate([dq_ref[head][:, lanes] for head in range(heads)], axis=1)
        q = turn(q.astype(F32), cq[slot], -sq[slot], heads // 2).astype(BF)
        kv = jnp.concatenate([dkv_ref[head, slot] for head in range(heads)], axis=1)
        kv = turn(kv.astype(F32), ck[slot], -sk[slot], heads).astype(BF)
        both = jnp.concatenate([q, kv], axis=1)
        out_ref[slot] = both
        sums += jnp.sum(both.astype(F32), axis=0, keepdims=True)

    @pl.when(pl.program_id(0) == 0)
    def _():
        sum_ref[...] = jnp.zeros_like(sum_ref)

    sum_ref[...] += sums


def unturn(dq, dkv, tables, heads):
    tile = 256
    width = 3 * heads * HD
    table = pl.BlockSpec((2, tile, 2 * HD), lambda i: (0, i, 0))
    out, sums = pl.pallas_call(
        functools.partial(unturn_kernel, heads),
        grid=(BLK // tile,),
        out_shape=(
            jax.ShapeDtypeStruct((2, BLK, width), BF),
            jax.ShapeDtypeStruct((1, width), F32),
        ),
        in_specs=[
            pl.BlockSpec((heads, tile, 2 * HD), lambda i: (0, i, 0)),
            pl.BlockSpec((heads, 2, tile, 2 * HD), lambda i: (0, 0, i, 0)),
            table,
            table,
            table,
            table,
        ],
        out_specs=(
            pl.BlockSpec((2, tile, width), lambda i: (0, i, 0)),
            pl.BlockSpec((1, width), lambda i: (0, 0)),
        ),
        compiler_params=pltpu.CompilerParams(vmem_limit_bytes=40 * 2**20),
        name="unturn",
    )(dq, dkv, *tables)
    return out.reshape(2 * BLK, width), sums


def coords():
    tok, br = lax.axis_index("tok"), lax.axis_index("br")
    return tok // 4, (tok // 2) % 2, tok % 2, br // 4, br % 4


def peer(dy=0, dz=0, dc=0, dl=0, dx=0):
    y, z, c, l, x = coords()
    tok = ((y + dy) % 4) * 4 + ((z + dz) % 2) * 2 + (c + dc) % 2
    return tok, ((l + dl) % 2) * 4 + (x + dx) % 4


class Links:
    def __init__(self, send_sems, recv_sems, local_sems):
        self.sems = (send_sems, recv_sems, local_sems)
        self.sent, self.locals = [], []

    def greet(self, partners):
        barrier = pltpu.get_barrier_semaphore()
        for offsets in partners:
            pl.semaphore_signal(
                barrier, inc=1, device_id=peer(**offsets), device_id_type=pl.DeviceIdType.MESH
            )
        pl.semaphore_wait(barrier, len(partners))

    def copy(self, number, source, target, offsets):
        return pltpu.make_async_remote_copy(
            src_ref=source,
            dst_ref=target,
            send_sem=self.sems[0].at[number],
            recv_sem=self.sems[1].at[number],
            device_id=peer(**offsets),
            device_id_type=pl.DeviceIdType.MESH,
        )

    def send(self, source, target, **offsets):
        copy = self.copy(len(self.sent), source, target, offsets)
        copy.start()
        self.sent.append(copy)
        return len(self.sent) - 1, offsets

    def arrived(self, ticket, place):
        self.copy(ticket[0], place, place, ticket[1]).wait_recv()

    def local(self, source, target):
        copy = pltpu.make_async_copy(source, target, self.sems[2].at[len(self.locals)])
        copy.start()
        self.locals.append([copy, True])
        return len(self.locals) - 1

    def settle(self, number):
        copy, pending = self.locals[number]
        if pending:
            copy.wait()
        self.locals[number][1] = False

    def close(self):
        for number in range(len(self.locals)):
            self.settle(number)
        for copy in self.sent:
            copy.wait_send()


def in_turn(tasks):
    tasks = list(tasks)
    while tasks:
        for task in list(tasks):
            try:
                next(task)
            except StopIteration:
                tasks.remove(task)


def ring_four(links, own, place, axis, landed):
    right = links.send(own, place(0, None), **{axis: 1})
    left = links.send(own, place(0, None), **{axis: -1})
    yield
    links.arrived(right, place(-1, None))
    on_right = links.send(place(-1, 0), place(-1, 0), **{axis: 1})
    landed(-1)
    yield
    links.arrived(left, place(1, None))
    on_left = links.send(place(1, 1), place(1, 1), **{axis: -1})
    landed(1)
    yield
    links.arrived(on_right, place(2, 0))
    links.arrived(on_left, place(2, 1))
    landed(2)


def half_of(ref, part):
    if part is None:
        return ref
    rows = ref.shape[0] // 2
    return ref.at[pl.ds(part * rows, rows)]


def gather_br(links, own, whole):
    unused_y, unused_z, unused_c, l, x = coords()

    def place(dl):
        return lambda dx, part: half_of(whole.at[(l + dl) % 2, (x + dx) % 4], part)

    links.local(own, place(0)(0, None))
    across = links.send(own, place(0)(0, None), dl=1)
    near = ring_four(links, own, place(0), "dx", lambda d: None)
    next(near)
    yield
    links.arrived(across, place(1)(0, None))
    far = ring_four(links, place(1)(0, None), place(1), "dx", lambda d: None)
    next(far)
    for unused in near:
        yield
    for unused in far:
        yield


def gather_tok(links, own, whole):
    y, z, c, unused_l, unused_x = coords()
    passed = []

    def place(dz, dc=0):
        return lambda dy, part: half_of(
            whole.at[(y + dy) % 4, (z + dz) % 2, (c + dc) % 2], part
        )

    def passer(dz):
        def landed(dy):
            ref = place(dz)(dy, None)
            passed.append((links.send(ref, ref, dc=1), place(dz, 1)(dy, None)))

        return landed

    links.local(own, place(0)(0, None))
    across = links.send(own, place(0)(0, None), dz=1)
    near = ring_four(links, own, place(0), "dy", passer(0))
    next(near)
    passed.append((links.send(own, place(0)(0, None), dc=1), place(0, 1)(0, None)))
    yield
    links.arrived(across, place(1)(0, None))
    far = ring_four(links, place(1)(0, None), place(1), "dy", passer(1))
    next(far)
    passer(1)(0)
    for unused in near:
        yield
    for unused in far:
        yield
    for ticket, ref in passed:
        links.arrived(ticket, ref)


def spread_heads(links, joined, queries, pairs):
    y, z, c, unused_l, unused_x = coords()
    rows = queries.shape[1]
    keys = pl.ds(rows, joined.shape[1] - rows)
    links.local(joined.at[y, pl.ds(0, rows)], queries.at[y])
    links.local(joined.at[y, keys], pairs.at[y, z, c])
    order = (1, 3, 2)
    direct = [
        links.send(joined.at[(y + d) % 4, keys], pairs.at[y, z, c], dy=d) for d in order
    ]
    across = [links.send(joined.at[y, keys], pairs.at[y, z, c], dz=1)]
    passed = [(links.send(joined.at[y, keys], pairs.at[y, z, c], dc=1), 0, 0)]
    asked = [
        links.send(joined.at[(y + d) % 4, pl.ds(0, rows)], queries.at[y], dy=d) for d in order
    ]
    yield

    def far(i):
        dy = 0 if i == 0 else -order[i - 1]
        ref = pairs.at[(y + dy) % 4, 1 - z, c]
        links.arrived(across[i], ref)
        passed.append((links.send(ref, ref, dc=1), dy, 1))

    for i, d in enumerate(order):
        ref = pairs.at[(y - d) % 4, z, c]
        links.arrived(direct[i], ref)
        across.append(links.send(ref, ref, dz=1))
        passed.append((links.send(ref, ref, dc=1), -d, 0))
        yield
        far(i)
        yield
    far(3)
    yield
    for i, d in enumerate(order):
        links.arrived(asked[i], queries.at[(y - d) % 4])
    for ticket, dy, dz in passed:
        links.arrived(ticket, pairs.at[(y + dy) % 4, (z + dz) % 2, 1 - c])


def add_up(target, sources, rows, finish):
    chunk = 16

    def step(i, unused):
        here = pl.ds(pl.multiple_of(i * chunk, chunk), chunk)
        total = sources[0][here, :].astype(F32)
        for source in sources[1:]:
            total = total + source[here, :].astype(F32)
        target[here, :] = finish(total, here).astype(target.dtype)
        return unused

    lax.fori_loop(0, rows // chunk, step, 0)


def plain(total, here):
    return total


def reduce_heads(links, grads, dq, dq_home, grads_home, mine, near, far, total):
    y, z, c, unused_l, unused_x = coords()
    order = (1, 3, 2, 0)
    held, from_core = {}, {}
    for dz in (1, 0):
        for d in order:
            place = ((y + d) % 4, (z + dz) % 2)
            from_core[d, dz] = links.send(
                grads.at[place[0], place[1], 1 - c], near.at[place[0], place[1]], dc=1
            )
            held[d, dz] = links.local(
                grads.at[place[0], place[1], c], mine.at[place[0], place[1]]
            )
    asked = [links.send(dq.at[(y + d) % 4], dq_home.at[y], dy=d) for d in order[:3]]
    links.local(dq.at[y], dq_home.at[y])
    yield
    rows = mine.shape[2]
    across = {}
    for d in order:
        here = (y + d) % 4
        links.arrived(from_core[d, 1], near.at[here, 1 - z])
        links.settle(held[d, 1])
        add_up(
            mine.at[here, 1 - z], [mine.at[here, 1 - z], near.at[here, 1 - z]], rows, plain
        )
        across[d] = links.send(mine.at[here, 1 - z], far.at[here], dz=1)
        yield
    home = {}
    for d in order:
        here = (y + d) % 4
        links.arrived(from_core[d, 0], near.at[here, z])
        links.settle(held[d, 0])
        links.arrived(across[d], far.at[here])
        add_up(
            total.at[here], [mine.at[here, z], near.at[here, z], far.at[here]], rows, plain
        )
        if d:
            home[d] = links.send(total.at[here], grads_home.at[y], dy=d)
        else:
            links.local(total.at[here], grads_home.at[y])
        yield
    for i, d in enumerate(order[:3]):
        links.arrived(asked[i], dq_home.at[(y - d) % 4])
        links.arrived(home[d], grads_home.at[(y - d) % 4])


def reduce_br(links, parts, own, near, out, far, target, finish):
    unused_y, unused_z, unused_c, l, x = coords()
    order = (1, 3, 2)
    tickets = {}
    held = {}
    for dl in (1, 0):
        there = (l + dl) % 2
        held[dl] = links.local(parts.at[there, x], own.at[there])
        for i, d in enumerate(order):
            tickets[dl, i] = links.send(
                parts.at[there, (x + d) % 4], near.at[i, there], dx=d
            )
    yield
    rows = out.shape[0]
    for i in range(3):
        links.arrived(tickets[1, i], near.at[i, 1 - l])
        yield
    links.settle(held[1])
    add_up(out, [own.at[1 - l]] + [near.at[i, 1 - l] for i in range(3)], rows, plain)
    across = links.send(out, far, dl=1)
    yield
    for i in range(3):
        links.arrived(tickets[0, i], near.at[i, l])
        yield
    links.settle(held[0])
    links.arrived(across, far)
    add_up(
        target, [own.at[l]] + [near.at[i, l] for i in range(3)] + [far], rows, finish
    )


def reduce_tok(links, parts, mine, near, side, out, far, target):
    y, z, c, unused_l, unused_x = coords()
    order = (1, 3, 2)
    tickets, held = {}, {}
    for d in order + (0,):
        here = (y + d) % 4
        tickets[d] = links.send(parts.at[here, :, 1 - c], near.at[here], dc=1)
        held[d] = links.local(parts.at[here, :, c], mine.at[here])
    yield
    rows = out.shape[0]
    sent = {}
    for i, d in enumerate(order + (0,)):
        here = (y + d) % 4
        links.arrived(tickets[d], near.at[here])
        links.settle(held[d])
        for k in range(2):
            add_up(mine.at[here, k], [mine.at[here, k], near.at[here, k]], rows, plain)
        if d:
            sent[i] = links.send(mine.at[here], side.at[i], dy=d)
        yield
    for i in range(3):
        links.arrived(sent[i], side.at[i])
        yield
    add_up(out, [mine.at[y, 1 - z]] + [side.at[i, 1 - z] for i in range(3)], rows, plain)
    across = links.send(out, far, dz=1)
    yield
    links.arrived(across, far)
    add_up(target, [mine.at[y, z]] + [side.at[i, z] for i in range(3)] + [far], rows, plain)


BR_NEAR = [dict(dl=1), dict(dx=1), dict(dx=-1)]
BR_ALL = BR_NEAR + [dict(dx=2)]
TOK_NEAR = [dict(dz=1), dict(dc=1), dict(dy=1), dict(dy=-1)]
TOK_ALL = TOK_NEAR + [dict(dy=2)]


def comm_call(kernel, name, number, args, outs, scratch=(), in_vmem=(), out_vmem=(), copies=48):
    return pl.pallas_call(
        kernel,
        out_shape=tuple(outs),
        in_specs=[VMEM if i in in_vmem else ANY for i in range(len(args))],
        out_specs=tuple(VMEM if i in out_vmem else ANY for i in range(len(outs))),
        scratch_shapes=list(scratch)
        + [
            pltpu.SemaphoreType.DMA((copies,)),
            pltpu.SemaphoreType.DMA((copies,)),
            pltpu.SemaphoreType.DMA((16,)),
        ],
        compiler_params=pltpu.CompilerParams(
            collective_id=number, has_side_effects=True, vmem_limit_bytes=48 * 2**20
        ),
        name=name,
    )(*args)


def start_kernel(s_ref, w_ref, x_out, w_out, *sems):
    links = Links(*sems)
    links.greet(BR_NEAR + TOK_NEAR)
    in_turn([gather_br(links, s_ref, x_out), gather_tok(links, w_ref, w_out)])
    links.close()


def start(shifted, weights):
    rows, depth = shifted.shape
    wrows, cols = weights.shape
    return comm_call(
        start_kernel,
        "start",
        0,
        (shifted, weights),
        (
            jax.ShapeDtypeStruct((2, 4, rows, depth), BF),
            jax.ShapeDtypeStruct((4, 2, 2, wrows, cols), BF),
        ),
    )


def heads_kernel(joined, cot, queries, pairs, grad_out, *sems):
    links = Links(*sems)
    links.greet(BR_NEAR + TOK_ALL)
    in_turn([spread_heads(links, joined, queries, pairs), gather_br(links, cot, grad_out)])
    links.close()


def heads_out(joined, cot):
    rows, depth = cot.shape
    heads, span, lanes = joined.shape
    return comm_call(
        heads_kernel,
        "heads_out",
        1,
        (joined, cot),
        (
            jax.ShapeDtypeStruct((4, BLK, lanes), BF),
            jax.ShapeDtypeStruct((4, 2, 2, span - BLK, lanes), BF),
            jax.ShapeDtypeStruct((2, 4, rows, depth), BF),
        ),
    )


def home_kernel(grads, dq, branches, tokens, dq_home, grads_home, result, *rest):
    mine, near, far, total, own, side, out, cross = rest[:8]
    links = Links(*rest[8:])
    links.greet(BR_ALL + TOK_ALL)

    def finish(value, here):
        return value + tokens[here, :].astype(F32)

    in_turn(
        [
            reduce_heads(links, grads, dq, dq_home, grads_home, mine, near, far, total),
            reduce_br(links, branches, own, side, out, cross, result, finish),
        ]
    )
    links.close()


def heads_home(grads, dq, branches, tokens):
    rows, depth = tokens.shape
    span, lanes = grads.shape[3:]
    return comm_call(
        home_kernel,
        "heads_home",
        2,
        (grads, dq, branches, tokens),
        (
            jax.ShapeDtypeStruct(dq.shape, BF),
            jax.ShapeDtypeStruct((4, span, lanes), BF),
            jax.ShapeDtypeStruct((rows, depth), BF),
        ),
        scratch=[
            pltpu.VMEM((4, 2, span, lanes), BF),
            pltpu.VMEM((4, 2, span, lanes), BF),
            pltpu.VMEM((4, span, lanes), BF),
            pltpu.VMEM((4, span, lanes), BF),
            pltpu.VMEM((2, rows, depth), BF),
            pltpu.VMEM((3, 2, rows, depth), BF),
            pltpu.VMEM((rows, depth), BF),
            pltpu.VMEM((rows, depth), BF),
        ],
        in_vmem=(3,),
        out_vmem=(2,),
    )


def last_kernel(grads, weights, shifted, mine_out, *rest):
    own, side, out, cross, mine, near, edge, wout, wcross = rest[:9]
    links = Links(*rest[9:])
    links.greet(BR_ALL + TOK_ALL)
    in_turn(
        [
            reduce_tok(links, weights, mine, near, edge, wout, wcross, mine_out),
            reduce_br(links, grads, own, side, out, cross, shifted, plain),
        ]
    )
    links.close()


def last_sums(grads, weights):
    rows, depth = grads.shape[2:]
    wrows, cols = weights.shape[3:]
    return comm_call(
        last_kernel,
        "last_sums",
        3,
        (grads, weights),
        (
            jax.ShapeDtypeStruct((rows, depth), F32),
            jax.ShapeDtypeStruct((wrows, cols), F32),
        ),
        scratch=[
            pltpu.VMEM((2, rows, depth), BF),
            pltpu.VMEM((3, 2, rows, depth), BF),
            pltpu.VMEM((rows, depth), BF),
            pltpu.VMEM((rows, depth), BF),
            pltpu.VMEM((4, 2, wrows, cols), BF),
            pltpu.VMEM((4, 2, wrows, cols), BF),
            pltpu.VMEM((3, 2, wrows, cols), BF),
            pltpu.VMEM((wrows, cols), BF),
            pltpu.VMEM((wrows, cols), BF),
        ],
        out_vmem=(0, 1),
    )


def sides_kernel(parts, result, here, side, *sems):
    y, z, c, l, x = coords()
    links = Links(*sems)
    near = [dict(dl=i // 4, dx=i % 4) for i in range(1, 8)]
    wide = [dict(dy=i // 4, dz=(i // 2) % 2, dc=i % 2) for i in range(1, 16)]
    links.greet(near + wide)
    tickets = []
    for i, o in enumerate(near):
        there = ((l + o["dl"]) % 2) * 4 + (x + o["dx"]) % 4
        tickets.append(links.send(parts.at[there], here.at[i], **o))
    total = parts[l * 4 + x]
    for i, ticket in enumerate(tickets):
        links.arrived(ticket, here.at[i])
        total = total + here[i]
    here[7] = total
    tickets = [links.send(here.at[7], side.at[i], **o) for i, o in enumerate(wide)]
    for i, ticket in enumerate(tickets):
        links.arrived(ticket, side.at[i])
        total = total + side[i]
    result[...] = total
    links.close()


def sum_sides(parts):
    return comm_call(
        sides_kernel,
        "sum_sides",
        4,
        (parts,),
        (jax.ShapeDtypeStruct(parts.shape[1:], F32),),
        scratch=[pltpu.VMEM(parts.shape, F32), pltpu.VMEM((15,) + parts.shape[1:], F32)],
        in_vmem=(0,),
        out_vmem=(0,),
    )[0]


def tok_perm(dy):
    return [(t, ((t // 4 + dy) % 4) * 4 + t % 4) for t in range(16)]


def swap_heads(parts, y):
    back = [lax.dynamic_index_in_dim(parts, y, 0, keepdims=False)]
    for d in (3, 2, 1):
        piece = lax.dynamic_index_in_dim(parts, (y + d) % 4, 0, keepdims=False)
        back.append(lax.ppermute(piece, "tok", tok_perm(d)))
    stacked = jnp.stack(back + back)
    return lax.dynamic_slice_in_dim(stacked, (4 - y) % 4, 4, 0)


def rotary_tables(positions, long_shape):
    half = ROT // 2
    frequency = ROPE_BASE ** (-(jnp.arange(half).astype(F32) * 2.0 / ROT))
    angles = positions.astype(F32)[:, None] * frequency[None, :]
    cos, sin = jnp.cos(angles), jnp.sin(angles)
    rows = positions.shape[0]
    one = jnp.ones((rows, HD - ROT), F32)
    zero = jnp.zeros((rows, HD - ROT), F32)
    cos64 = jnp.concatenate([cos, cos, one], axis=1)
    sin64 = jnp.concatenate([-sin, sin, zero], axis=1)
    tables = (
        jnp.concatenate([cos64, cos64], axis=1),
        jnp.concatenate([sin64, sin64], axis=1),
        jnp.concatenate([cos64, jnp.ones((rows, HD), F32)], axis=1),
        jnp.concatenate([sin64, jnp.zeros((rows, HD), F32)], axis=1),
    )
    return tuple(t.reshape(2, BLK, 2 * HD) for t in tables)


def body(
    tokens,
    norm_gain,
    norm_bias,
    qkv_weight,
    qkv_bias,
    out_weight,
    gate_weight,
    up_weight,
    down_weight,
    cotangent,
    block_map,
    lengths,
):
    tok = lax.axis_index("tok")
    y, z, c = tok // 4, (tok // 2) % 2, tok % 2
    total_blocks = block_map.shape[0]
    long_blocks = total_blocks // 2
    rows = tokens.shape[0]
    depth = tokens.shape[1]
    wrows = qkv_weight.shape[1]
    heads = qkv_bias.shape[1]
    width = heads * HD
    hidden_width = gate_weight.shape[1]
    main = hidden_width // 128 * 128
    tail = hidden_width - main

    residual = tokens.astype(F32)
    centred = residual - jnp.mean(residual, axis=-1, keepdims=True)
    inverse = lax.rsqrt(jnp.mean(centred * centred, axis=-1, keepdims=True) + EPSILON)
    normed = centred * inverse
    shifted = (normed * norm_gain + norm_bias).astype(BF)

    kv_shard = jnp.stack(
        [w.reshape(wrows, heads, HD) for w in (qkv_weight[1], qkv_weight[2])], axis=2
    ).reshape(wrows, 2 * width)
    bias_row = jnp.pad(qkv_bias.reshape(1, -1), ((0, wrows - 1), (0, 128 - qkv_bias.size)))
    qkv_shard = jnp.concatenate([qkv_weight[0], kv_shard, bias_row], axis=1)
    ff_shard = jnp.concatenate(
        [
            gate_weight[:, :main],
            up_weight[:, :main],
            gate_weight[:, main:],
            up_weight[:, main:],
            jnp.transpose(down_weight),
            jnp.zeros((wrows, 128 - tail), BF),
            jnp.transpose(out_weight),
        ],
        axis=1,
    )
    both_width = 2 * hidden_width
    down_width = main + 128
    ff_full = lax.all_gather(ff_shard, "tok", axis=0, tiled=True)
    gu_full = ff_full[:, :both_width]
    down_full = ff_full[:, both_width : both_width + down_width]
    out_full = ff_full[:, both_width + down_width :]
    x, qkv_full = start(shifted, qkv_shard)
    x = x.reshape(2 * BLK, depth)
    qkv_full = qkv_full.reshape(16 * wrows, -1)

    bias = qkv_full.reshape(16, wrows, -1)[:, 0, 3 * width : 3 * width + qkv_bias.size]
    bias = jnp.transpose(bias.reshape(16, 3, heads, 4), (1, 2, 0, 3)).reshape(3, heads, HD)
    bias = jnp.concatenate(
        [bias[0].reshape(1, width), jnp.stack([bias[1], bias[2]], axis=1).reshape(1, 2 * width)],
        axis=1,
    ).astype(F32)

    slot_table = jnp.arange(total_blocks, dtype=jnp.int32)
    slot_of = jnp.sum(
        jnp.where(block_map[None, :] == slot_table[:, None], slot_table[None, :], 0), axis=1
    )
    key_slot = slot_of.astype(jnp.int32)
    from_tok = jnp.arange(4, dtype=jnp.int32) * 4 + z * 2 + c
    my_queries = jnp.stack([2 * from_tok, 2 * from_tok + 1], axis=1).reshape(-1)
    query_block = jnp.sum(
        jnp.where(my_queries[:, None] == slot_table[None, :], block_map[None, :], 0), axis=1
    ).astype(jnp.int32)
    query_row = jnp.where(
        query_block < long_blocks,
        query_block // LB,
        long_blocks // LB + (query_block - long_blocks) // 2,
    )
    row_table = jnp.arange(lengths.shape[0], dtype=jnp.int32)
    query_limit = jnp.sum(
        jnp.where(query_row[:, None] == row_table[None, :], lengths[None, :], 0), axis=1
    ).astype(jnp.int32)

    my_blocks = lax.dynamic_slice_in_dim(block_map, tok * 2, 2)
    my_start = (
        jnp.where(my_blocks < long_blocks, my_blocks % LB, (my_blocks - long_blocks) % 2) * BLK
    )
    positions = (my_start[:, None] + jnp.arange(BLK, dtype=jnp.int32)[None, :]).reshape(-1)
    tables = rotary_tables(positions, long_blocks)

    q_heads, kv_heads = project(x, qkv_full, bias, tables, heads)
    joined = jnp.concatenate([q_heads, kv_heads.reshape(heads, 2 * BLK, 2 * HD)], axis=1)
    q_all, kv_all, grad = heads_out(joined, cotangent)
    grad = grad.reshape(2 * BLK, depth)
    kv_all = kv_all.reshape(-1, 2 * HD)

    turned, lse, o_parts = attn_fwd(query_block, query_limit, key_slot, q_all, kv_all, long_blocks)

    def to_heads(flat):
        split = flat.reshape(2, BLK, heads, HD)
        return jnp.transpose(split, (2, 1, 0, 3)).reshape(heads, BLK, 2 * HD)

    def from_heads(packed):
        split = packed.reshape(heads, BLK, 2, HD)
        return jnp.transpose(split, (2, 1, 0, 3)).reshape(2 * BLK, width)

    mixed = from_heads(swap_heads(o_parts, y))

    grad_mixed = dot(grad, out_full, NN).astype(BF)
    do_all = swap_heads(to_heads(grad_mixed), y)

    both = dot(x, gu_full, NN)
    grad_hidden = dot(grad, down_full, NN)
    ends = both[:, 2 * main :]
    gate = jnp.concatenate([both[:, :main], ends[:, :tail]], axis=1)
    up = jnp.concatenate([both[:, main : 2 * main], ends[:, tail:]], axis=1)
    gh = grad_hidden[:, :hidden_width]
    sig = jax.nn.sigmoid(gate)
    hidden = (gate * sig * up).astype(BF)
    hidden = jnp.pad(hidden, ((0, 0), (0, down_width - hidden_width)))
    grad_gate = (gh * up * sig * (1.0 + gate * (1.0 - sig))).astype(BF)
    grad_up = (gh * gate * sig).astype(BF)
    grad_both = jnp.concatenate(
        [grad_gate[:, :main], grad_up[:, :main], grad_gate[:, main:], grad_up[:, main:]], axis=1
    )
    branches = (dot(hidden, down_full, NT) + dot(mixed, out_full, NT)).astype(BF)
    grad_ff = jnp.concatenate(
        [
            dot(x, grad_both, TN).astype(BF),
            dot(grad, hidden, TN).astype(BF),
            dot(grad, mixed, TN).astype(BF),
        ],
        axis=1,
    )
    grad_ff = lax.psum_scatter(grad_ff, "tok", scatter_dimension=0, tiled=True)

    dq_parts, dkv_all = attn_bwd(
        query_block, query_limit, key_slot, q_all, do_all, kv_all, turned, lse, long_blocks
    )
    dq_heads, dkv_heads, result = heads_home(
        dkv_all.reshape(4, 2, 2, 2 * BLK, 2 * HD),
        dq_parts,
        branches.reshape(2, 4, rows, depth),
        tokens,
    )
    dkv_heads = dkv_heads.reshape(heads, 2, BLK, 2 * HD)
    grad_joined, bias_sums = unturn(dq_heads, dkv_heads, tables, heads)
    grad_shifted = (
        dot(grad_both, gu_full, NT) + dot(grad_joined, qkv_full[:, : 3 * width], NT)
    ).astype(BF)
    grad_qkv = dot(x, grad_joined, TN).astype(BF)
    qsum = bias_sums[0, :width].reshape(1, heads, HD)
    kvsum = jnp.transpose(bias_sums[0, width:].reshape(heads, 2, HD), (1, 0, 2))
    bsum = jnp.concatenate([qsum, kvsum], axis=0).reshape(3, heads, 16, 4)
    bsum = jnp.transpose(bsum, (2, 0, 1, 3)).reshape(16, 1, qkv_bias.size).astype(BF)
    bsum = jnp.pad(bsum, ((0, 0), (0, wrows - 1), (0, 128 - qkv_bias.size)))
    grad_qkv = jnp.concatenate([grad_qkv, bsum.reshape(16 * wrows, 128)], axis=1)
    my_grad_shifted, grad_qkv = last_sums(
        grad_shifted.reshape(2, 4, rows, depth), grad_qkv.reshape(4, 2, 2, wrows, -1)
    )

    grad_bias_out = grad_qkv[0, 3 * width : 3 * width + qkv_bias.size].reshape(qkv_bias.shape)
    gkv = grad_qkv[:, width : 3 * width].reshape(wrows, heads, 2, HD)
    grad_qkv_out = jnp.stack(
        [
            grad_qkv[:, :width],
            gkv[:, :, 0].reshape(wrows, width),
            gkv[:, :, 1].reshape(wrows, width),
        ]
    )
    grad_ff = grad_ff.astype(F32)
    ends = grad_ff[:, 2 * main : both_width]
    grad_gate_out = jnp.concatenate([grad_ff[:, :main], ends[:, :tail]], axis=1)
    grad_up_out = jnp.concatenate([grad_ff[:, main : 2 * main], ends[:, tail:]], axis=1)
    grad_down_out = jnp.transpose(grad_ff[:, both_width : both_width + hidden_width])
    grad_out_out = jnp.transpose(grad_ff[:, both_width + down_width :])

    gain_part = jnp.sum(my_grad_shifted * normed, axis=0)
    bias_part = jnp.sum(my_grad_shifted, axis=0)
    grad_normed = my_grad_shifted * norm_gain
    grad_tokens = cotangent.astype(F32) + inverse * (
        grad_normed
        - jnp.mean(grad_normed, axis=-1, keepdims=True)
        - normed * jnp.mean(grad_normed * normed, axis=-1, keepdims=True)
    )
    sides = jnp.stack([gain_part, bias_part]).reshape(2, 16, 8, 16)
    sides = jnp.transpose(sides, (2, 0, 1, 3)).reshape(8, 2, 256)
    sides = sum_sides(jnp.pad(sides, ((0, 0), (0, 6), (0, 0))))
    sides = lax.dynamic_slice_in_dim(sides[:2].reshape(2, 16, 16), tok, 1, 1)[:, 0]
    grad_gain, grad_bias = sides[0], sides[1]
    return (
        result,
        grad_tokens,
        grad_gain,
        grad_bias,
        grad_qkv_out,
        grad_bias_out,
        grad_out_out,
        grad_gate_out,
        grad_up_out,
        grad_down_out,
    )


def solution(mesh):
    in_specs = (
        P(("tok", "br"), None),
        P(),
        P(),
        P(None, "tok", "br"),
        P(None, "br", "tok"),
        P("br", "tok"),
        P("tok", "br"),
        P("tok", "br"),
        P("br", "tok"),
        P(("tok", "br"), None),
        P(),
        P(),
    )
    out_specs = (
        P(("tok", "br"), None),
        P(("tok", "br"), None),
        P(("tok", "br")),
        P(("tok", "br")),
        P(None, "tok", "br"),
        P(None, "br", "tok"),
        P("br", "tok"),
        P("tok", "br"),
        P("tok", "br"),
        P("br", "tok"),
    )
    return jax.shard_map(body, mesh=mesh, in_specs=in_specs, out_specs=out_specs, check_vma=False)
```

```python
import functools

import jax
import jax.numpy as jnp
import numpy as np
from jax import lax
from jax.experimental import pallas as pl
from jax.experimental.pallas import tpu as pltpu
from jax.sharding import PartitionSpec as P

HD = 64
ROT = 16
BLK = 512
LB = 8
EPSILON = 1e-05
ROPE_BASE = 10000.0
MASKED = -1e30
BF = jnp.bfloat16
F32 = jnp.float32
NN = (((1,), (0,)), ((), ()))
NT = (((1,), (1,)), ((), ()))
TN = (((0,), (0,)), ((), ()))
VMEM = pl.BlockSpec(memory_space=pltpu.VMEM)
SMEM = pl.BlockSpec(memory_space=pltpu.SMEM)
ANY = pl.BlockSpec(memory_space=pl.ANY)


def dot(left, right, dims):
    return lax.dot_general(left, right, dims, preferred_element_type=F32)


def block_info(block, long_blocks):
    is_long = block < long_blocks
    place = jnp.where(is_long, block % LB, (block - long_blocks) % 2)
    return is_long, place, block - place


def lane_half(packed, half, upper):
    piece = packed[:, half * HD : (half + 1) * HD]
    zero = jnp.zeros_like(piece)
    return jnp.concatenate([zero, piece] if upper else [piece, zero], axis=1)


def allowed_pairs(place, step, limit):
    key_pos = step * BLK + lax.broadcasted_iota(jnp.int32, (BLK, BLK), 0)
    query_pos = place * BLK + lax.broadcasted_iota(jnp.int32, (BLK, BLK), 1)
    return (key_pos <= query_pos) & (key_pos < limit)


def attn_fwd_kernel(long_blocks, qblk, qlim, kslot, q_ref, kv_ref, ot_ref, lse_ref, o_ref):
    def pack(i, unused):
        packed = q_ref[i]
        for half in range(2):
            slot = 2 * i + half
            is_long, place, first = block_info(qblk[slot], long_blocks)
            limit = qlim[slot]
            queries = lane_half(packed, half, False) * jnp.asarray(0.125, BF)

            def step(j, carry, masked):
                top, total, acc = carry
                rows = pl.ds(pl.multiple_of(kslot[first + j] * BLK, BLK), BLK)
                kv = kv_ref[rows, :]
                scores = dot(kv, queries, NT)
                if masked:
                    scores = jnp.where(allowed_pairs(place, j, limit), scores, MASKED)
                new_top = jnp.maximum(top, jnp.max(scores, axis=0, keepdims=True))
                fade = jnp.exp(top - new_top)
                probs = jnp.exp(scores - new_top)
                total = total * fade + jnp.sum(probs, axis=0, keepdims=True)
                acc = acc * fade + dot(kv, probs.astype(BF), TN)
                return new_top, total, acc

            free = jnp.where(is_long, place, 0)
            carry = (
                jnp.full((1, BLK), MASKED, F32),
                jnp.zeros((1, BLK), F32),
                jnp.zeros((2 * HD, BLK), F32),
            )
            carry = lax.fori_loop(0, free, lambda j, c: step(j, c, False), carry)
            top, total, acc = lax.fori_loop(free, place + 1, lambda j, c: step(j, c, True), carry)
            lse_ref[slot] = top + jnp.log(total)
            ot_ref[i, half * HD : (half + 1) * HD, :] = acc[HD:, :] / total
        o_ref[i] = jnp.transpose(ot_ref[i]).astype(BF)
        return unused

    lax.fori_loop(0, q_ref.shape[0], pack, 0)


def attn_fwd(qblk, qlim, kslot, q, kv, long_blocks):
    n = q.shape[0]
    return pl.pallas_call(
        functools.partial(attn_fwd_kernel, long_blocks),
        out_shape=(
            jax.ShapeDtypeStruct((n, 2 * HD, BLK), F32),
            jax.ShapeDtypeStruct((2 * n, 1, BLK), F32),
            jax.ShapeDtypeStruct((n, BLK, 2 * HD), BF),
        ),
        in_specs=[SMEM, SMEM, SMEM, VMEM, VMEM],
        out_specs=(VMEM, VMEM, VMEM),
        compiler_params=pltpu.CompilerParams(vmem_limit_bytes=48 * 2**20),
        cost_estimate=pl.CostEstimate(
            flops=int(20e9), bytes_accessed=8 * 2**20, transcendentals=8 * 2**20
        ),
        name="attn_fwd",
    )(qblk, qlim, kslot, q, kv)


def attn_bwd_kernel(
    long_blocks, qblk, qlim, kslot, q_ref, do_ref, kv_ref, ot_ref, lse_ref, dq_ref, dkv_ref, acc, dqt
):
    acc[...] = jnp.zeros_like(acc)

    def pack(i, unused):
        q_packed = q_ref[i]
        d_packed = do_ref[i]
        d_turned = jnp.transpose(d_packed.astype(F32))
        for half in range(2):
            slot = 2 * i + half
            is_long, place, first = block_info(qblk[slot], long_blocks)
            limit = qlim[slot]
            queries = lane_half(q_packed, half, False) * jnp.asarray(0.125, BF)
            grads = lane_half(d_packed, half, True)
            both = jnp.concatenate([queries, grads], axis=0)
            lanes = slice(half * HD, (half + 1) * HD)
            delta = jnp.sum(d_turned[lanes] * ot_ref[i, lanes, :], axis=0, keepdims=True)
            lse = lse_ref[slot]

            def step(j, total, masked):
                rows = pl.ds(pl.multiple_of(kslot[first + j] * BLK, BLK), BLK)
                kv = kv_ref[rows, :]
                scores = dot(kv, queries, NT)
                if masked:
                    scores = jnp.where(allowed_pairs(place, j, limit), scores, MASKED)
                probs = jnp.exp(scores - lse)
                ds = (probs * (dot(kv, grads, NT) - delta)).astype(BF)
                acc[rows, :] += dot(jnp.concatenate([ds, probs.astype(BF)], axis=1), both, NN)
                return total + dot(kv, ds, TN)

            free = jnp.where(is_long, place, 0)
            total = lax.fori_loop(
                0, free, lambda j, c: step(j, c, False), jnp.zeros((2 * HD, BLK), F32)
            )
            total = lax.fori_loop(free, place + 1, lambda j, c: step(j, c, True), total)
            dqt[lanes, :] = total[:HD, :] * 0.125
        dq_ref[i] = jnp.transpose(dqt[...]).astype(BF)
        return unused

    lax.fori_loop(0, q_ref.shape[0], pack, 0)

    def finish(i, unused):
        rows = pl.ds(pl.multiple_of(i * BLK, BLK), BLK)
        dkv_ref[rows, :] = acc[rows, :].astype(BF)
        return unused

    lax.fori_loop(0, kv_ref.shape[0] // BLK, finish, 0)


def attn_bwd(qblk, qlim, kslot, q, do, kv, ot, lse, long_blocks):
    n = q.shape[0]
    return pl.pallas_call(
        functools.partial(attn_bwd_kernel, long_blocks),
        out_shape=(
            jax.ShapeDtypeStruct((n, BLK, 2 * HD), BF),
            jax.ShapeDtypeStruct(kv.shape, BF),
        ),
        in_specs=[SMEM, SMEM, SMEM, VMEM, VMEM, VMEM, VMEM, VMEM],
        out_specs=(VMEM, VMEM),
        scratch_shapes=[pltpu.VMEM(kv.shape, F32), pltpu.VMEM((2 * HD, BLK), F32)],
        compiler_params=pltpu.CompilerParams(vmem_limit_bytes=56 * 2**20),
        cost_estimate=pl.CostEstimate(
            flops=int(30e9), bytes_accessed=12 * 2**20, transcendentals=8 * 2**20
        ),
        name="attn_bwd",
    )(qblk, qlim, kslot, q, do, kv, ot, lse)


def turn(values, table, copies, paired, sign):
    width = values.shape[1]
    lane = lax.broadcasted_iota(jnp.int32, values.shape, 1) % HD
    partner = jnp.where(
        lane < ROT // 2,
        pltpu.roll(values, width - ROT // 2, 1),
        pltpu.roll(values, ROT // 2, 1),
    )
    cos, sin = table[:, :HD], sign * table[:, HD:]
    cos = jnp.concatenate([cos, jnp.ones_like(cos) if paired else cos], axis=1)
    sin = jnp.concatenate([sin, jnp.zeros_like(sin) if paired else sin], axis=1)
    cos = jnp.concatenate([cos] * copies, axis=1)
    sin = jnp.concatenate([sin] * copies, axis=1)
    return values * cos + partner * sin


def project_kernel(heads, places, x_ref, w_ref, b_ref, t0_ref, t1_ref, q_ref, kv_ref):
    width = heads * HD
    parts = []
    for slot, table in enumerate((t0_ref[...], t1_ref[...])):
        joined = dot(x_ref[slot], w_ref[...], NN) + b_ref[...]
        parts.append(turn(joined[:, :width], table, heads // 2, False, 1.0).astype(BF))
        kv = turn(joined[:, width:], table, heads, True, 1.0).astype(BF)
        for head in range(heads):
            kv_ref[head, slot] = kv[:, head * 2 * HD : (head + 1) * 2 * HD]
    for head in range(heads):
        lanes = slice(head * HD, (head + 1) * HD)
        q_ref[head] = jnp.concatenate([parts[0][:, lanes], parts[1][:, lanes]], axis=1)


def table_specs(tile):
    return [
        pl.BlockSpec((None, tile, 2 * HD), lambda i, places: (places[0], i, 0)),
        pl.BlockSpec((None, tile, 2 * HD), lambda i, places: (places[1], i, 0)),
    ]


def project(places, x, w, bias, table, heads):
    tile = 256
    width = 3 * heads * HD
    depth = x.shape[1]
    return pl.pallas_call(
        functools.partial(project_kernel, heads),
        grid_spec=pltpu.PrefetchScalarGridSpec(
            num_scalar_prefetch=1,
            grid=(BLK // tile,),
            in_specs=[
                pl.BlockSpec((2, tile, depth), lambda i, places: (0, i, 0)),
                pl.BlockSpec((depth, width), lambda i, places: (0, 0)),
                pl.BlockSpec((1, width), lambda i, places: (0, 0)),
            ]
            + table_specs(tile),
            out_specs=(
                pl.BlockSpec((heads, tile, 2 * HD), lambda i, places: (0, i, 0)),
                pl.BlockSpec((heads, 2, tile, 2 * HD), lambda i, places: (0, 0, i, 0)),
            ),
        ),
        out_shape=(
            jax.ShapeDtypeStruct((heads, BLK, 2 * HD), BF),
            jax.ShapeDtypeStruct((heads, 2, BLK, 2 * HD), BF),
        ),
        compiler_params=pltpu.CompilerParams(vmem_limit_bytes=40 * 2**20),
        name="project",
    )(places, x.reshape(2, BLK, depth), w, bias, table, table)


def unturn_kernel(heads, places, dq_ref, dkv_ref, t0_ref, t1_ref, out_ref, sum_ref):
    width = heads * HD
    sums = jnp.zeros((1, 3 * width), F32)
    for slot, table in enumerate((t0_ref[...], t1_ref[...])):
        lanes = slice(slot * HD, (slot + 1) * HD)
        q = jnp.concatenate([dq_ref[head][:, lanes] for head in range(heads)], axis=1)
        q = turn(q.astype(F32), table, heads // 2, False, -1.0).astype(BF)
        kv = jnp.concatenate([dkv_ref[head, slot] for head in range(heads)], axis=1)
        kv = turn(kv.astype(F32), table, heads, True, -1.0).astype(BF)
        both = jnp.concatenate([q, kv], axis=1)
        out_ref[slot] = both
        sums += jnp.sum(both.astype(F32), axis=0, keepdims=True)

    @pl.when(pl.program_id(0) == 0)
    def _():
        sum_ref[...] = jnp.zeros_like(sum_ref)

    sum_ref[...] += sums


def unturn(places, dq, dkv, table, heads):
    tile = 256
    width = 3 * heads * HD
    out, sums = pl.pallas_call(
        functools.partial(unturn_kernel, heads),
        grid_spec=pltpu.PrefetchScalarGridSpec(
            num_scalar_prefetch=1,
            grid=(BLK // tile,),
            in_specs=[
                pl.BlockSpec((heads, tile, 2 * HD), lambda i, places: (0, i, 0)),
                pl.BlockSpec((heads, 2, tile, 2 * HD), lambda i, places: (0, 0, i, 0)),
            ]
            + table_specs(tile),
            out_specs=(
                pl.BlockSpec((2, tile, width), lambda i, places: (0, i, 0)),
                pl.BlockSpec((1, width), lambda i, places: (0, 0)),
            ),
        ),
        out_shape=(
            jax.ShapeDtypeStruct((2, BLK, width), BF),
            jax.ShapeDtypeStruct((1, width), F32),
        ),
        compiler_params=pltpu.CompilerParams(vmem_limit_bytes=40 * 2**20),
        name="unturn",
    )(places, dq, dkv, table, table)
    return out.reshape(2 * BLK, width), sums


def mixed_grad_kernel(heads, g_ref, w0_ref, w1_ref, out_ref):
    weights = jnp.concatenate([w0_ref[...], w1_ref[...]], axis=1)
    parts = [dot(g_ref[slot], weights, NN).astype(BF) for slot in range(2)]
    for head in range(heads):
        lanes = slice(head * HD, (head + 1) * HD)
        out_ref[head] = jnp.concatenate([parts[0][:, lanes], parts[1][:, lanes]], axis=1)


def mixed_grad(g, weights, first, heads):
    tile = 256
    depth = g.shape[2]
    block = first // 128
    return pl.pallas_call(
        functools.partial(mixed_grad_kernel, heads),
        grid=(BLK // tile,),
        out_shape=jax.ShapeDtypeStruct((heads, BLK, 2 * HD), BF),
        in_specs=[
            pl.BlockSpec((2, tile, depth), lambda i: (0, i, 0)),
            pl.BlockSpec((depth, 128), lambda i: (0, block)),
            pl.BlockSpec((depth, 128), lambda i: (0, block + 1)),
        ],
        out_specs=pl.BlockSpec((heads, tile, 2 * HD), lambda i: (0, i, 0)),
        compiler_params=pltpu.CompilerParams(vmem_limit_bytes=40 * 2**20),
        name="mixed_grad",
    )(g, weights, weights)


def ff_kernel(
    heads, main, both, down, order, x_ref, g_ref, o_ref, w_ref, a_ref, h_ref, s_ref, *outs
):
    rows, depth = x_ref.shape[1:]
    x = x_ref[...].reshape(2 * rows, depth)
    g = g_ref[...].reshape(2 * rows, depth)
    gate_up = dot(x, w_ref[:, :both], NN)
    gh = dot(g, w_ref[:, both : both + down], NN)
    ends = gate_up[:, 2 * main :]
    gate = jnp.concatenate([gate_up[:, :main], ends], axis=1)
    up = jnp.concatenate([gate_up[:, main : 2 * main], pltpu.roll(ends, HD, 1)], axis=1)
    sig = jax.nn.sigmoid(gate)
    silu = gate * sig
    hidden = (silu * up).astype(BF)
    d_gate = gh * up * sig * (1.0 + gate * (1.0 - sig))
    d_up = gh * silu
    tail = d_gate[:, main:] + pltpu.roll(d_up[:, main:], HD, 1)
    grads = jnp.concatenate(
        [d_gate[:, :main].astype(BF), d_up[:, :main].astype(BF), tail.astype(BF)], axis=1
    )
    mixed = [
        jnp.concatenate(
            [o_ref[head][:, slot * HD : (slot + 1) * HD] for head in range(heads)], axis=1
        )
        for slot in range(2)
    ]
    held = jnp.concatenate([hidden, jnp.concatenate(mixed, axis=0)], axis=1)
    a_ref[...] = grads.reshape(2, rows, both)
    h_ref[...] = held.reshape(2, rows, -1)
    s_ref[...] = dot(grads, w_ref[:, :both], NT).astype(BF).reshape(2, rows, depth)
    branches = dot(held, w_ref[:, both:], NT).astype(BF).reshape(2, rows, depth)
    for i, out in enumerate(outs):

        @pl.when(pl.program_id(0) == i)
        def _():
            out[...] = branches


def feed_forward(order, x, g, o, w, heads, main, both, down):
    depth, cols = w.shape
    rows = BLK // 4
    kept = cols - both

    def tile(lanes, lead=2):
        return pl.BlockSpec((lead, rows, lanes), lambda i, order: (0, order[i], 0))

    part = pl.BlockSpec((2, rows, depth), lambda i, order: (0, 0, 0))
    return pl.pallas_call(
        functools.partial(ff_kernel, heads, main, both, down),
        grid_spec=pltpu.PrefetchScalarGridSpec(
            num_scalar_prefetch=1,
            grid=(4,),
            in_specs=[
                tile(depth),
                tile(depth),
                tile(2 * HD, heads),
                pl.BlockSpec(
                    (depth, cols), lambda i, order: (0, 0), pipeline_mode=pl.Buffered(1)
                ),
            ],
            out_specs=(tile(both), tile(kept), tile(depth)) + (part,) * 4,
        ),
        out_shape=(
            jax.ShapeDtypeStruct((2, BLK, both), BF),
            jax.ShapeDtypeStruct((2, BLK, kept), BF),
            jax.ShapeDtypeStruct((2, BLK, depth), BF),
        )
        + (jax.ShapeDtypeStruct((2, rows, depth), BF),) * 4,
        compiler_params=pltpu.CompilerParams(vmem_limit_bytes=60 * 2**20),
        cost_estimate=pl.CostEstimate(
            flops=int(19e9), bytes_accessed=30 * 2**20, transcendentals=2**20
        ),
        name="feed_forward",
    )(order, x, g, o, w)


def ff_weights_kernel(x_ref, g_ref, a_ref, h_ref, out_ref):
    both = a_ref.shape[1]
    out_ref[:, :both] = dot(x_ref[...], a_ref[...], TN).astype(BF)
    out_ref[:, both:] = dot(g_ref[...], h_ref[...], TN).astype(BF)


def ff_weights(x, g, a, h):
    rows, depth = x.shape
    tile = 256
    cols = a.shape[1] + h.shape[1]
    strip = pl.BlockSpec((rows, tile), lambda i: (0, i))
    return pl.pallas_call(
        ff_weights_kernel,
        grid=(depth // tile,),
        out_shape=jax.ShapeDtypeStruct((depth, cols), BF),
        in_specs=[
            strip,
            strip,
            pl.BlockSpec(a.shape, lambda i: (0, 0), pipeline_mode=pl.Buffered(1)),
            pl.BlockSpec(h.shape, lambda i: (0, 0), pipeline_mode=pl.Buffered(1)),
        ],
        out_specs=pl.BlockSpec((tile, cols), lambda i: (i, 0)),
        compiler_params=pltpu.CompilerParams(vmem_limit_bytes=48 * 2**20),
        cost_estimate=pl.CostEstimate(
            flops=int(10e9), bytes_accessed=24 * 2**20, transcendentals=0
        ),
        name="ff_weights",
    )(x, g, a, h)


def coords():
    tok, br = lax.axis_index("tok"), lax.axis_index("br")
    return tok // 4, (tok // 2) % 2, tok % 2, br // 4, br % 4


def peer(dy=0, dz=0, dc=0, dl=0, dx=0):
    y, z, c, l, x = coords()
    tok = ((y + dy) % 4) * 4 + ((z + dz) % 2) * 2 + (c + dc) % 2
    return tok, ((l + dl) % 2) * 4 + (x + dx) % 4


class Links:
    def __init__(self, send_sems, recv_sems, local_sems):
        self.sems = (send_sems, recv_sems, local_sems)
        self.sent, self.locals = [], []

    def greet(self, partners):
        barrier = pltpu.get_barrier_semaphore()
        for offsets in partners:
            pl.semaphore_signal(
                barrier, inc=1, device_id=peer(**offsets), device_id_type=pl.DeviceIdType.MESH
            )
        pl.semaphore_wait(barrier, len(partners))

    def copy(self, number, source, target, offsets):
        return pltpu.make_async_remote_copy(
            src_ref=source,
            dst_ref=target,
            send_sem=self.sems[0].at[number],
            recv_sem=self.sems[1].at[number],
            device_id=peer(**offsets),
            device_id_type=pl.DeviceIdType.MESH,
        )

    def send(self, source, target, **offsets):
        copy = self.copy(len(self.sent), source, target, offsets)
        copy.start()
        self.sent.append(copy)
        return len(self.sent) - 1, offsets

    def arrived(self, ticket, place):
        self.copy(ticket[0], place, place, ticket[1]).wait_recv()

    def local(self, source, target):
        copy = pltpu.make_async_copy(source, target, self.sems[2].at[len(self.locals)])
        copy.start()
        self.locals.append([copy, True])
        return len(self.locals) - 1

    def settle(self, number):
        copy, pending = self.locals[number]
        if pending:
            copy.wait()
        self.locals[number][1] = False

    def close(self):
        for number in range(len(self.locals)):
            self.settle(number)
        for copy in self.sent:
            copy.wait_send()


def in_turn(tasks):
    tasks = list(tasks)
    while tasks:
        for task in list(tasks):
            try:
                next(task)
            except StopIteration:
                tasks.remove(task)


def ring_four(links, own, place, axis, landed):
    right = links.send(own, place(0, None), **{axis: 1})
    left = links.send(own, place(0, None), **{axis: -1})
    yield
    links.arrived(right, place(-1, None))
    on_right = links.send(place(-1, 0), place(-1, 0), **{axis: 1})
    landed(-1)
    yield
    links.arrived(left, place(1, None))
    on_left = links.send(place(1, 1), place(1, 1), **{axis: -1})
    landed(1)
    yield
    links.arrived(on_right, place(2, 0))
    links.arrived(on_left, place(2, 1))
    landed(2)


def half_of(ref, part):
    if part is None:
        return ref
    rows = ref.shape[0] // 2
    return ref.at[pl.ds(part * rows, rows)]


def gather_br(links, own, whole):
    unused_y, unused_z, unused_c, l, x = coords()

    def place(dl):
        return lambda dx, part: half_of(whole.at[(l + dl) % 2, (x + dx) % 4], part)

    links.local(own, place(0)(0, None))
    across = links.send(own, place(0)(0, None), dl=1)
    near = ring_four(links, own, place(0), "dx", lambda d: None)
    next(near)
    yield
    links.arrived(across, place(1)(0, None))
    far = ring_four(links, place(1)(0, None), place(1), "dx", lambda d: None)
    next(far)
    for unused in near:
        yield
    for unused in far:
        yield


def gather_tok(links, own, whole):
    y, z, c, unused_l, unused_x = coords()
    passed = []

    def place(dz, dc=0):
        return lambda dy, part: half_of(
            whole.at[(y + dy) % 4, (z + dz) % 2, (c + dc) % 2], part
        )

    def passer(dz):
        def landed(dy):
            ref = place(dz)(dy, None)
            passed.append((links.send(ref, ref, dc=1), place(dz, 1)(dy, None)))

        return landed

    links.local(own, place(0)(0, None))
    across = links.send(own, place(0)(0, None), dz=1)
    near = ring_four(links, own, place(0), "dy", passer(0))
    next(near)
    passed.append((links.send(own, place(0)(0, None), dc=1), place(0, 1)(0, None)))
    yield
    links.arrived(across, place(1)(0, None))
    far = ring_four(links, place(1)(0, None), place(1), "dy", passer(1))
    next(far)
    passer(1)(0)
    for unused in near:
        yield
    for unused in far:
        yield
    for ticket, ref in passed:
        links.arrived(ticket, ref)


def spread_heads(links, joined, queries, pairs):
    y, z, c, unused_l, unused_x = coords()
    rows = queries.shape[1]
    keys = pl.ds(rows, joined.shape[1] - rows)
    links.local(joined.at[y, pl.ds(0, rows)], queries.at[y])
    links.local(joined.at[y, keys], pairs.at[y, z, c])
    order = (1, 3, 2)
    direct = [
        links.send(joined.at[(y + d) % 4, keys], pairs.at[y, z, c], dy=d) for d in order
    ]
    across = [links.send(joined.at[y, keys], pairs.at[y, z, c], dz=1)]
    passed = [(links.send(joined.at[y, keys], pairs.at[y, z, c], dc=1), 0, 0)]
    asked = [
        links.send(joined.at[(y + d) % 4, pl.ds(0, rows)], queries.at[y], dy=d) for d in order
    ]
    yield

    def far(i):
        dy = 0 if i == 0 else -order[i - 1]
        ref = pairs.at[(y + dy) % 4, 1 - z, c]
        links.arrived(across[i], ref)
        passed.append((links.send(ref, ref, dc=1), dy, 1))

    for i, d in enumerate(order):
        ref = pairs.at[(y - d) % 4, z, c]
        links.arrived(direct[i], ref)
        across.append(links.send(ref, ref, dz=1))
        passed.append((links.send(ref, ref, dc=1), -d, 0))
        yield
        far(i)
        yield
    far(3)
    yield
    for i, d in enumerate(order):
        links.arrived(asked[i], queries.at[(y - d) % 4])
    for ticket, dy, dz in passed:
        links.arrived(ticket, pairs.at[(y + dy) % 4, (z + dz) % 2, 1 - c])


def add_up(target, sources, rows, finish):
    chunk = 16

    def step(i, unused):
        here = pl.ds(pl.multiple_of(i * chunk, chunk), chunk)
        total = sources[0][here, :].astype(F32)
        for source in sources[1:]:
            total = total + source[here, :].astype(F32)
        target[here, :] = finish(total, here).astype(target.dtype)
        return unused

    lax.fori_loop(0, rows // chunk, step, 0)


def plain(total, here):
    return total


def reduce_heads(links, grads, dq, dq_home, grads_home, mine, near, far, total):
    y, z, c, unused_l, unused_x = coords()
    order = (1, 3, 2, 0)
    held, from_core = {}, {}
    for dz in (1, 0):
        for d in order:
            place = ((y + d) % 4, (z + dz) % 2)
            from_core[d, dz] = links.send(
                grads.at[place[0], place[1], 1 - c], near.at[place[0], place[1]], dc=1
            )
            held[d, dz] = links.local(
                grads.at[place[0], place[1], c], mine.at[place[0], place[1]]
            )
    asked = [links.send(dq.at[(y + d) % 4], dq_home.at[y], dy=d) for d in order[:3]]
    links.local(dq.at[y], dq_home.at[y])
    yield
    rows = mine.shape[2]
    across = {}
    for d in order:
        here = (y + d) % 4
        links.arrived(from_core[d, 1], near.at[here, 1 - z])
        links.settle(held[d, 1])
        add_up(
            mine.at[here, 1 - z], [mine.at[here, 1 - z], near.at[here, 1 - z]], rows, plain
        )
        across[d] = links.send(mine.at[here, 1 - z], far.at[here], dz=1)
        yield
    home = {}
    for d in order:
        here = (y + d) % 4
        links.arrived(from_core[d, 0], near.at[here, z])
        links.settle(held[d, 0])
        links.arrived(across[d], far.at[here])
        add_up(
            total.at[here], [mine.at[here, z], near.at[here, z], far.at[here]], rows, plain
        )
        if d:
            home[d] = links.send(total.at[here], grads_home.at[y], dy=d)
        else:
            links.local(total.at[here], grads_home.at[y])
        yield
    for i, d in enumerate(order[:3]):
        links.arrived(asked[i], dq_home.at[(y - d) % 4])
        links.arrived(home[d], grads_home.at[(y - d) % 4])


def reduce_br(links, parts, own, near, out, far, target, finish):
    unused_y, unused_z, unused_c, l, x = coords()
    order = (1, 3, 2)
    tickets = {}
    held = {}
    for dl in (1, 0):
        there = (l + dl) % 2
        held[dl] = links.local(parts.at[there, x], own.at[there])
        for i, d in enumerate(order):
            tickets[dl, i] = links.send(
                parts.at[there, (x + d) % 4], near.at[i, there], dx=d
            )
    yield
    rows = out.shape[0]
    for i in range(3):
        links.arrived(tickets[1, i], near.at[i, 1 - l])
        yield
    links.settle(held[1])
    add_up(out, [own.at[1 - l]] + [near.at[i, 1 - l] for i in range(3)], rows, plain)
    across = links.send(out, far, dl=1)
    yield
    for i in range(3):
        links.arrived(tickets[0, i], near.at[i, l])
        yield
    links.settle(held[0])
    links.arrived(across, far)
    add_up(
        target, [own.at[l]] + [near.at[i, l] for i in range(3)] + [far], rows, finish
    )


def reduce_tok(links, parts, mine, near, side, out, far, target):
    y, z, c, unused_l, unused_x = coords()
    order = (1, 3, 2)
    tickets, held = {}, {}
    for d in order + (0,):
        here = (y + d) % 4
        tickets[d] = links.send(parts.at[here, :, 1 - c], near.at[here], dc=1)
        held[d] = links.local(parts.at[here, :, c], mine.at[here])
    yield
    rows = out.shape[0]
    sent = {}
    for i, d in enumerate(order + (0,)):
        here = (y + d) % 4
        links.arrived(tickets[d], near.at[here])
        links.settle(held[d])
        for k in range(2):
            add_up(mine.at[here, k], [mine.at[here, k], near.at[here, k]], rows, plain)
        if d:
            sent[i] = links.send(mine.at[here], side.at[i], dy=d)
        yield
    for i in range(3):
        links.arrived(sent[i], side.at[i])
        yield
    add_up(out, [mine.at[y, 1 - z]] + [side.at[i, 1 - z] for i in range(3)], rows, plain)
    across = links.send(out, far, dz=1)
    yield
    links.arrived(across, far)
    add_up(target, [mine.at[y, z]] + [side.at[i, z] for i in range(3)] + [far], rows, plain)


BR_NEAR = [dict(dl=1), dict(dx=1), dict(dx=-1)]
BR_ALL = BR_NEAR + [dict(dx=2)]
TOK_NEAR = [dict(dz=1), dict(dc=1), dict(dy=1), dict(dy=-1)]
TOK_ALL = TOK_NEAR + [dict(dy=2)]


def comm_call(kernel, name, number, args, outs, scratch=(), in_vmem=(), out_vmem=(), copies=48):
    return pl.pallas_call(
        kernel,
        out_shape=tuple(outs),
        in_specs=[VMEM if i in in_vmem else ANY for i in range(len(args))],
        out_specs=tuple(VMEM if i in out_vmem else ANY for i in range(len(outs))),
        scratch_shapes=list(scratch)
        + [
            pltpu.SemaphoreType.DMA((copies,)),
            pltpu.SemaphoreType.DMA((copies,)),
            pltpu.SemaphoreType.DMA((16,)),
        ],
        compiler_params=pltpu.CompilerParams(
            collective_id=number, has_side_effects=True, vmem_limit_bytes=48 * 2**20
        ),
        name=name,
    )(*args)


def start_kernel(s_ref, w_ref, x_out, w_out, *sems):
    links = Links(*sems)
    links.greet(BR_NEAR + TOK_NEAR)
    in_turn([gather_br(links, s_ref, x_out), gather_tok(links, w_ref, w_out)])
    links.close()


def start(shifted, weights):
    rows, depth = shifted.shape
    wrows, cols = weights.shape
    return comm_call(
        start_kernel,
        "start",
        0,
        (shifted, weights),
        (
            jax.ShapeDtypeStruct((2, 4, rows, depth), BF),
            jax.ShapeDtypeStruct((4, 2, 2, wrows, cols), BF),
        ),
    )


def heads_kernel(joined, cot, queries, pairs, grad_out, *sems):
    links = Links(*sems)
    links.greet(BR_NEAR + TOK_ALL)
    in_turn([spread_heads(links, joined, queries, pairs), gather_br(links, cot, grad_out)])
    links.close()


def heads_out(joined, cot):
    rows, depth = cot.shape
    heads, span, lanes = joined.shape
    return comm_call(
        heads_kernel,
        "heads_out",
        1,
        (joined, cot),
        (
            jax.ShapeDtypeStruct((4, BLK, lanes), BF),
            jax.ShapeDtypeStruct((4, 2, 2, span - BLK, lanes), BF),
            jax.ShapeDtypeStruct((2, 4, rows, depth), BF),
        ),
    )


def home_kernel(grads, dq, dq_home, grads_home, mine, near, far, total, *sems):
    links = Links(*sems)
    links.greet(TOK_ALL)
    in_turn([reduce_heads(links, grads, dq, dq_home, grads_home, mine, near, far, total)])
    links.close()


def heads_home(grads, dq):
    span, lanes = grads.shape[3:]
    return comm_call(
        home_kernel,
        "heads_home",
        2,
        (grads, dq),
        (
            jax.ShapeDtypeStruct(dq.shape, BF),
            jax.ShapeDtypeStruct((4, span, lanes), BF),
        ),
        scratch=[
            pltpu.VMEM((4, 2, span, lanes), BF),
            pltpu.VMEM((4, 2, span, lanes), BF),
            pltpu.VMEM((4, span, lanes), BF),
            pltpu.VMEM((4, span, lanes), BF),
        ],
    )


def last_kernel(grads, weights, shifted, mine_out, *rest):
    own, side, out, cross, mine, near, edge, wout, wcross = rest[:9]
    links = Links(*rest[9:])
    links.greet(BR_ALL + TOK_ALL)
    in_turn(
        [
            reduce_tok(links, weights, mine, near, edge, wout, wcross, mine_out),
            reduce_br(links, grads, own, side, out, cross, shifted, plain),
        ]
    )
    links.close()


def last_sums(grads, weights):
    rows, depth = grads.shape[2:]
    wrows, cols = weights.shape[3:]
    return comm_call(
        last_kernel,
        "last_sums",
        3,
        (grads, weights),
        (
            jax.ShapeDtypeStruct((rows, depth), F32),
            jax.ShapeDtypeStruct((wrows, cols), F32),
        ),
        scratch=[
            pltpu.VMEM((2, rows, depth), BF),
            pltpu.VMEM((3, 2, rows, depth), BF),
            pltpu.VMEM((rows, depth), BF),
            pltpu.VMEM((rows, depth), BF),
            pltpu.VMEM((4, 2, wrows, cols), BF),
            pltpu.VMEM((4, 2, wrows, cols), BF),
            pltpu.VMEM((3, 2, wrows, cols), BF),
            pltpu.VMEM((wrows, cols), BF),
            pltpu.VMEM((wrows, cols), BF),
        ],
        out_vmem=(0, 1),
    )


def sides_kernel(parts, result, here, side, *sems):
    y, z, c, l, x = coords()
    links = Links(*sems)
    near = [dict(dl=i // 4, dx=i % 4) for i in range(1, 8)]
    wide = [dict(dy=i // 4, dz=(i // 2) % 2, dc=i % 2) for i in range(1, 16)]
    links.greet(near + wide)
    tickets = []
    for i, o in enumerate(near):
        there = ((l + o["dl"]) % 2) * 4 + (x + o["dx"]) % 4
        tickets.append(links.send(parts.at[there], here.at[i], **o))
    total = parts[l * 4 + x]
    for i, ticket in enumerate(tickets):
        links.arrived(ticket, here.at[i])
        total = total + here[i]
    here[7] = total
    tickets = [links.send(here.at[7], side.at[i], **o) for i, o in enumerate(wide)]
    for i, ticket in enumerate(tickets):
        links.arrived(ticket, side.at[i])
        total = total + side[i]
    result[...] = total
    links.close()


def sum_sides(parts):
    return comm_call(
        sides_kernel,
        "sum_sides",
        4,
        (parts,),
        (jax.ShapeDtypeStruct(parts.shape[1:], F32),),
        scratch=[pltpu.VMEM(parts.shape, F32), pltpu.VMEM((15,) + parts.shape[1:], F32)],
        in_vmem=(0,),
        out_vmem=(0,),
    )[0]


def tok_perm(dy):
    return [(t, ((t // 4 + dy) % 4) * 4 + t % 4) for t in range(16)]


def br_perm(dl, dx):
    return [(b, (b // 4 ^ dl) * 4 + (b + dx) % 4) for b in range(8)]


def swap_heads(parts, y):
    back = [lax.dynamic_index_in_dim(parts, y, 0, keepdims=False)]
    for d in (3, 2, 1):
        piece = lax.dynamic_index_in_dim(parts, (y + d) % 4, 0, keepdims=False)
        back.append(lax.ppermute(piece, "tok", tok_perm(d)))
    stacked = jnp.stack(back + back)
    return lax.dynamic_slice_in_dim(stacked, (4 - y) % 4, 4, 0)


def rotary_table():
    half = ROT // 2
    frequency = (ROPE_BASE ** (-(np.arange(half) * 2.0 / ROT))).astype(np.float32)
    angles = np.arange(LB * BLK, dtype=np.float32)[:, None] * frequency[None, :]
    cos, sin = np.cos(angles), np.sin(angles)
    one = np.ones((LB * BLK, HD - ROT), np.float32)
    table = np.concatenate([cos, cos, one, -sin, sin, 0.0 * one], axis=1)
    return table.astype(np.float32).reshape(LB, BLK, 2 * HD)


def body(
    tokens,
    norm_gain,
    norm_bias,
    qkv_weight,
    qkv_bias,
    out_weight,
    gate_weight,
    up_weight,
    down_weight,
    cotangent,
    block_map,
    lengths,
):
    tok = lax.axis_index("tok")
    y, z, c = tok // 4, (tok // 2) % 2, tok % 2
    total_blocks = block_map.shape[0]
    long_blocks = total_blocks // 2
    rows = tokens.shape[0]
    depth = tokens.shape[1]
    wrows = qkv_weight.shape[1]
    heads = qkv_bias.shape[1]
    width = heads * HD
    hidden_width = gate_weight.shape[1]
    main = hidden_width // 128 * 128
    tail = hidden_width - main

    residual = tokens.astype(F32)
    centred = residual - jnp.mean(residual, axis=-1, keepdims=True)
    inverse = lax.rsqrt(jnp.mean(centred * centred, axis=-1, keepdims=True) + EPSILON)
    normed = centred * inverse
    shifted = (normed * norm_gain + norm_bias).astype(BF)

    kv_shard = jnp.stack(
        [w.reshape(wrows, heads, HD) for w in (qkv_weight[1], qkv_weight[2])], axis=2
    ).reshape(wrows, 2 * width)
    bias_row = jnp.pad(qkv_bias.reshape(1, -1), ((0, wrows - 1), (0, 128 - qkv_bias.size)))
    qkv_shard = jnp.concatenate([qkv_weight[0], kv_shard, bias_row], axis=1)
    ff_shard = jnp.concatenate(
        [
            gate_weight[:, :main],
            up_weight[:, :main],
            gate_weight[:, main:],
            up_weight[:, main:],
            jnp.transpose(down_weight),
            jnp.zeros((wrows, 128 - tail), BF),
            jnp.transpose(out_weight),
        ],
        axis=1,
    )
    both_width = 2 * hidden_width
    down_width = main + 128
    ff_full = lax.all_gather(ff_shard, "tok", axis=0, tiled=True)
    x, qkv_full = start(shifted, qkv_shard)
    x = x.reshape(2 * BLK, depth)
    qkv_full = qkv_full.reshape(16 * wrows, -1)

    bias = qkv_full.reshape(16, wrows, -1)[:, 0, 3 * width : 3 * width + qkv_bias.size]
    bias = jnp.transpose(bias.reshape(16, 3, heads, 4), (1, 2, 0, 3)).reshape(3, heads, HD)
    bias = jnp.concatenate(
        [bias[0].reshape(1, width), jnp.stack([bias[1], bias[2]], axis=1).reshape(1, 2 * width)],
        axis=1,
    ).astype(F32)

    slot_table = jnp.arange(total_blocks, dtype=jnp.int32)
    slot_of = jnp.sum(
        jnp.where(block_map[None, :] == slot_table[:, None], slot_table[None, :], 0), axis=1
    )
    key_slot = slot_of.astype(jnp.int32)
    from_tok = jnp.arange(4, dtype=jnp.int32) * 4 + z * 2 + c
    my_queries = jnp.stack([2 * from_tok, 2 * from_tok + 1], axis=1).reshape(-1)
    query_block = jnp.sum(
        jnp.where(my_queries[:, None] == slot_table[None, :], block_map[None, :], 0), axis=1
    ).astype(jnp.int32)
    query_row = jnp.where(
        query_block < long_blocks,
        query_block // LB,
        long_blocks // LB + (query_block - long_blocks) // 2,
    )
    row_table = jnp.arange(lengths.shape[0], dtype=jnp.int32)
    query_limit = jnp.sum(
        jnp.where(query_row[:, None] == row_table[None, :], lengths[None, :], 0), axis=1
    ).astype(jnp.int32)

    my_blocks = lax.dynamic_slice_in_dim(block_map, tok * 2, 2)
    places = jnp.where(my_blocks < long_blocks, my_blocks % LB, (my_blocks - long_blocks) % 2)
    table = jnp.asarray(rotary_table())

    q_heads, kv_heads = project(places, x, qkv_full, bias, table, heads)
    joined = jnp.concatenate([q_heads, kv_heads.reshape(heads, 2 * BLK, 2 * HD)], axis=1)
    q_all, kv_all, grad = heads_out(joined, cotangent)
    kv_all = kv_all.reshape(-1, 2 * HD)

    turned, lse, o_parts = attn_fwd(query_block, query_limit, key_slot, q_all, kv_all, long_blocks)

    o_heads = swap_heads(o_parts, y)
    grad = grad.reshape(2, BLK, depth)
    do_heads = mixed_grad(grad, ff_full, both_width + down_width, heads)
    o_heads, do_heads = lax.optimization_barrier((o_heads, do_heads))
    do_all = swap_heads(do_heads, y)

    br = lax.axis_index("br")
    l, xi = br // 4, br % 4
    order = ((xi + jnp.array([1, 3, 2, 0], jnp.int32)) % 4).astype(jnp.int32)
    grad_both, held, grad_x, *branches = feed_forward(
        order,
        x.reshape(2, BLK, depth),
        grad,
        o_heads,
        ff_full,
        heads,
        main,
        both_width,
        down_width,
    )
    moved = [
        lax.ppermute(branches[i], "br", br_perm(0, d)) for i, d in enumerate((1, 3, 2))
    ]
    grad_ff = ff_weights(
        x,
        grad.reshape(2 * BLK, depth),
        grad_both.reshape(2 * BLK, -1),
        held.reshape(2 * BLK, -1),
    )
    grad_ff = lax.psum_scatter(grad_ff, "tok", scatter_dimension=0, tiled=True)

    dq_parts, dkv_all = attn_bwd(
        query_block, query_limit, key_slot, q_all, do_all, kv_all, turned, lse, long_blocks
    )
    summed = branches[3].astype(F32)
    for piece in moved:
        summed = summed + piece.astype(F32)
    summed, dq_parts = lax.optimization_barrier((summed, dq_parts))
    across = lax.dynamic_index_in_dim(summed.astype(BF), 1 - l, 0, keepdims=False)
    across = lax.ppermute(across, "br", br_perm(1, 0))
    dq_heads, dkv_heads = heads_home(
        dkv_all.reshape(4, 2, 2, 2 * BLK, 2 * HD),
        dq_parts,
    )
    dkv_heads = dkv_heads.reshape(heads, 2, BLK, 2 * HD)
    grad_joined, bias_sums = unturn(places, dq_heads, dkv_heads, table, heads)
    grad_shifted = (
        grad_x.reshape(2 * BLK, depth).astype(F32)
        + dot(grad_joined, qkv_full[:, : 3 * width], NT)
    ).astype(BF)
    grad_qkv = dot(x, grad_joined, TN).astype(BF)
    qsum = bias_sums[0, :width].reshape(1, heads, HD)
    kvsum = jnp.transpose(bias_sums[0, width:].reshape(heads, 2, HD), (1, 0, 2))
    bsum = jnp.concatenate([qsum, kvsum], axis=0).reshape(3, heads, 16, 4)
    bsum = jnp.transpose(bsum, (2, 0, 1, 3)).reshape(16, 1, qkv_bias.size).astype(BF)
    bsum = jnp.pad(bsum, ((0, 0), (0, wrows - 1), (0, 128 - qkv_bias.size)))
    grad_qkv = jnp.concatenate([grad_qkv, bsum.reshape(16 * wrows, 128)], axis=1)
    across, grad_shifted = lax.optimization_barrier((across, grad_shifted))
    summed = lax.dynamic_index_in_dim(summed, l, 0, keepdims=False) + across.astype(F32)
    result = (residual + summed).astype(BF)
    my_grad_shifted, grad_qkv = last_sums(
        grad_shifted.reshape(2, 4, rows, depth), grad_qkv.reshape(4, 2, 2, wrows, -1)
    )

    grad_bias_out = grad_qkv[0, 3 * width : 3 * width + qkv_bias.size].reshape(qkv_bias.shape)
    gkv = grad_qkv[:, width : 3 * width].reshape(wrows, heads, 2, HD)
    grad_qkv_out = jnp.stack(
        [
            grad_qkv[:, :width],
            gkv[:, :, 0].reshape(wrows, width),
            gkv[:, :, 1].reshape(wrows, width),
        ]
    )
    grad_ff = grad_ff.astype(F32)
    ends = grad_ff[:, 2 * main : both_width]
    grad_gate_out = jnp.concatenate([grad_ff[:, :main], ends[:, :tail]], axis=1)
    grad_up_out = jnp.concatenate([grad_ff[:, main : 2 * main], ends[:, tail:]], axis=1)
    grad_down_out = jnp.transpose(grad_ff[:, both_width : both_width + hidden_width])
    grad_out_out = jnp.transpose(grad_ff[:, both_width + down_width :])

    gain_part = jnp.sum(my_grad_shifted * normed, axis=0)
    bias_part = jnp.sum(my_grad_shifted, axis=0)
    grad_normed = my_grad_shifted * norm_gain
    grad_tokens = cotangent.astype(F32) + inverse * (
        grad_normed
        - jnp.mean(grad_normed, axis=-1, keepdims=True)
        - normed * jnp.mean(grad_normed * normed, axis=-1, keepdims=True)
    )
    sides = jnp.stack([gain_part, bias_part]).reshape(2, 16, 8, 16)
    sides = jnp.transpose(sides, (2, 0, 1, 3)).reshape(8, 2, 256)
    sides = sum_sides(jnp.pad(sides, ((0, 0), (0, 6), (0, 0))))
    sides = lax.dynamic_slice_in_dim(sides[:2].reshape(2, 16, 16), tok, 1, 1)[:, 0]
    grad_gain, grad_bias = sides[0], sides[1]
    return (
        result,
        grad_tokens,
        grad_gain,
        grad_bias,
        grad_qkv_out,
        grad_bias_out,
        grad_out_out,
        grad_gate_out,
        grad_up_out,
        grad_down_out,
    )


def solution(mesh):
    in_specs = (
        P(("tok", "br"), None),
        P(),
        P(),
        P(None, "tok", "br"),
        P(None, "br", "tok"),
        P("br", "tok"),
        P("tok", "br"),
        P("tok", "br"),
        P("br", "tok"),
        P(("tok", "br"), None),
        P(),
        P(),
    )
    out_specs = (
        P(("tok", "br"), None),
        P(("tok", "br"), None),
        P(("tok", "br")),
        P(("tok", "br")),
        P(None, "tok", "br"),
        P(None, "br", "tok"),
        P("br", "tok"),
        P("tok", "br"),
        P("tok", "br"),
        P("br", "tok"),
    )
    return jax.shard_map(body, mesh=mesh, in_specs=in_specs, out_specs=out_specs, check_vma=False)
```

```python
import functools

import jax
import jax.numpy as jnp
import numpy as np
from jax import lax
from jax.experimental import pallas as pl
from jax.experimental.pallas import tpu as pltpu
from jax.sharding import PartitionSpec as P

HD = 64
ROT = 16
BLK = 512
LB = 8
EPSILON = 1e-05
ROPE_BASE = 10000.0
MASKED = -1e30
BF = jnp.bfloat16
F32 = jnp.float32
NN = (((1,), (0,)), ((), ()))
NT = (((1,), (1,)), ((), ()))
TN = (((0,), (0,)), ((), ()))
VMEM = pl.BlockSpec(memory_space=pltpu.VMEM)
SMEM = pl.BlockSpec(memory_space=pltpu.SMEM)
ANY = pl.BlockSpec(memory_space=pl.ANY)
SMALL = pl.CostEstimate(flops=1000, bytes_accessed=1000, transcendentals=0)


def dot(left, right, dims):
    return lax.dot_general(left, right, dims, preferred_element_type=F32)


def block_info(block, long_blocks):
    is_long = block < long_blocks
    place = jnp.where(is_long, block % LB, (block - long_blocks) % 2)
    return is_long, place, block - place


def lane_half(packed, half, upper):
    piece = packed[:, half * HD : (half + 1) * HD]
    zero = jnp.zeros_like(piece)
    return jnp.concatenate([zero, piece] if upper else [piece, zero], axis=1)


def allowed_pairs(place, step, limit):
    key_pos = step * BLK + lax.broadcasted_iota(jnp.int32, (BLK, BLK), 0)
    query_pos = place * BLK + lax.broadcasted_iota(jnp.int32, (BLK, BLK), 1)
    return (key_pos <= query_pos) & (key_pos < limit)


def attn_fwd_kernel(long_blocks, qblk, qlim, kslot, q_ref, kv_ref, ot_ref, lse_ref, o_ref):
    def pack(i, unused):
        packed = q_ref[i, 0]
        for half in range(2):
            slot = 2 * i + half
            is_long, place, first = block_info(qblk[slot], long_blocks)
            limit = qlim[slot]
            queries = lane_half(packed, half, False) * jnp.asarray(0.125, BF)

            def step(j, carry, masked):
                top, total, acc = carry
                rows = pl.ds(pl.multiple_of(kslot[first + j] * BLK, BLK), BLK)
                kv = kv_ref[rows, :]
                scores = dot(kv, queries, NT)
                if masked:
                    scores = jnp.where(allowed_pairs(place, j, limit), scores, MASKED)
                new_top = jnp.maximum(top, jnp.max(scores, axis=0, keepdims=True))
                fade = jnp.exp(top - new_top)
                probs = jnp.exp(scores - new_top)
                total = total * fade + jnp.sum(probs, axis=0, keepdims=True)
                acc = acc * fade + dot(kv, probs.astype(BF), TN)
                return new_top, total, acc

            free = jnp.where(is_long, place, 0)
            carry = (
                jnp.full((1, BLK), MASKED, F32),
                jnp.zeros((1, BLK), F32),
                jnp.zeros((2 * HD, BLK), F32),
            )
            carry = lax.fori_loop(0, free, lambda j, c: step(j, c, False), carry)
            top, total, acc = lax.fori_loop(free, place + 1, lambda j, c: step(j, c, True), carry)
            lse_ref[slot] = top + jnp.log(total)
            ot_ref[i, half * HD : (half + 1) * HD, :] = acc[HD:, :] / total
        o_ref[i] = jnp.transpose(ot_ref[i]).astype(BF)
        return unused

    lax.fori_loop(0, q_ref.shape[0], pack, 0)


def attn_fwd(qblk, qlim, kslot, q, kv, long_blocks):
    n = q.shape[0]
    return pl.pallas_call(
        functools.partial(attn_fwd_kernel, long_blocks),
        out_shape=(
            jax.ShapeDtypeStruct((n, 2 * HD, BLK), F32),
            jax.ShapeDtypeStruct((2 * n, 1, BLK), F32),
            jax.ShapeDtypeStruct((n, BLK, 2 * HD), BF),
        ),
        in_specs=[SMEM, SMEM, SMEM, VMEM, VMEM],
        out_specs=(VMEM, VMEM, VMEM),
        compiler_params=pltpu.CompilerParams(vmem_limit_bytes=60 * 2**20),
        cost_estimate=SMALL,
        name="attn_fwd",
    )(qblk, qlim, kslot, q, kv)


def attn_bwd_kernel(
    long_blocks, qblk, qlim, kslot, q_ref, kv_ref, ot_ref, lse_ref, dq_ref, dkv_ref, acc, dqt
):
    acc[...] = jnp.zeros_like(acc)

    def pack(i, unused):
        q_packed = q_ref[i, 0]
        d_packed = q_ref[i, 1]
        d_turned = jnp.transpose(d_packed.astype(F32))
        for half in range(2):
            slot = 2 * i + half
            is_long, place, first = block_info(qblk[slot], long_blocks)
            limit = qlim[slot]
            queries = lane_half(q_packed, half, False) * jnp.asarray(0.125, BF)
            grads = lane_half(d_packed, half, True)
            both = jnp.concatenate([queries, grads], axis=0)
            lanes = slice(half * HD, (half + 1) * HD)
            delta = jnp.sum(d_turned[lanes] * ot_ref[i, lanes, :], axis=0, keepdims=True)
            lse = lse_ref[slot]

            def step(j, total, masked):
                rows = pl.ds(pl.multiple_of(kslot[first + j] * BLK, BLK), BLK)
                kv = kv_ref[rows, :]
                scores = dot(kv, queries, NT)
                if masked:
                    scores = jnp.where(allowed_pairs(place, j, limit), scores, MASKED)
                probs = jnp.exp(scores - lse)
                ds = (probs * (dot(kv, grads, NT) - delta)).astype(BF)
                acc[rows, :] += dot(jnp.concatenate([ds, probs.astype(BF)], axis=1), both, NN)
                return total + dot(kv, ds, TN)

            free = jnp.where(is_long, place, 0)
            total = lax.fori_loop(
                0, free, lambda j, c: step(j, c, False), jnp.zeros((2 * HD, BLK), F32)
            )
            total = lax.fori_loop(free, place + 1, lambda j, c: step(j, c, True), total)
            dqt[lanes, :] = total[:HD, :] * 0.125
        dq_ref[i] = jnp.transpose(dqt[...]).astype(BF)
        return unused

    lax.fori_loop(0, q_ref.shape[0], pack, 0)

    def finish(i, unused):
        rows = pl.ds(pl.multiple_of(i * BLK, BLK), BLK)
        dkv_ref[rows, :] = acc[rows, :].astype(BF)
        return unused

    lax.fori_loop(0, kv_ref.shape[0] // BLK, finish, 0)


def attn_bwd(qblk, qlim, kslot, q, kv, ot, lse, long_blocks):
    n = q.shape[0]
    return pl.pallas_call(
        functools.partial(attn_bwd_kernel, long_blocks),
        out_shape=(
            jax.ShapeDtypeStruct((n, BLK, 2 * HD), BF),
            jax.ShapeDtypeStruct(kv.shape, BF),
        ),
        in_specs=[SMEM, SMEM, SMEM, VMEM, VMEM, VMEM, VMEM],
        out_specs=(VMEM, VMEM),
        scratch_shapes=[pltpu.VMEM(kv.shape, F32), pltpu.VMEM((2 * HD, BLK), F32)],
        compiler_params=pltpu.CompilerParams(vmem_limit_bytes=60 * 2**20),
        cost_estimate=SMALL,
        name="attn_bwd",
    )(qblk, qlim, kslot, q, kv, ot, lse)


def turn(values, table, copies, paired, sign):
    width = values.shape[1]
    lane = lax.broadcasted_iota(jnp.int32, values.shape, 1) % HD
    partner = jnp.where(
        lane < ROT // 2,
        pltpu.roll(values, width - ROT // 2, 1),
        pltpu.roll(values, ROT // 2, 1),
    )
    cos, sin = table[:, :HD], sign * table[:, HD:]
    cos = jnp.concatenate([cos, jnp.ones_like(cos) if paired else cos], axis=1)
    sin = jnp.concatenate([sin, jnp.zeros_like(sin) if paired else sin], axis=1)
    cos = jnp.concatenate([cos] * copies, axis=1)
    sin = jnp.concatenate([sin] * copies, axis=1)
    return values * cos + partner * sin


def project_kernel(
    heads, places, x_ref, g_ref, w_ref, b_ref, wo_ref, t0_ref, t1_ref, out_ref
):
    width = heads * HD
    rows = w_ref.shape[0] // 16
    corner = b_ref[:8, :].astype(F32)
    for t in range(1, 16):
        corner = corner + b_ref[t * rows : t * rows + 8, :].astype(F32)
    bias = jnp.concatenate([corner[r : r + 1] for r in range(3 * width // 128)], axis=1)
    parts, grads = [], []
    tile, depth = x_ref.shape[1:]
    products = dot(x_ref[...].reshape(2 * tile, depth), w_ref[...], NN) + bias
    mixed = dot(g_ref[...].reshape(2 * tile, depth), wo_ref[...], NN).astype(BF)
    for slot, table in enumerate((t0_ref[...], t1_ref[...])):
        joined = products[slot * tile : (slot + 1) * tile]
        parts.append(turn(joined[:, :width], table, heads // 2, False, 1.0).astype(BF))
        grads.append(mixed[slot * tile : (slot + 1) * tile])
        kv = turn(joined[:, width:], table, heads, True, 1.0).astype(BF)
        for head in range(heads):
            out_ref[head, 2 + slot] = kv[:, head * 2 * HD : (head + 1) * 2 * HD]
    for head in range(heads):
        lanes = slice(head * HD, (head + 1) * HD)
        for i, pair in enumerate((parts, grads)):
            out_ref[head, i] = jnp.concatenate([pair[0][:, lanes], pair[1][:, lanes]], axis=1)


def project(places, x, g, w, ff, table, heads):
    tile = 256
    width = 3 * heads * HD
    depth = x.shape[2]
    rows = pl.BlockSpec((2, tile, depth), lambda i, places: (0, i, 0))
    return pl.pallas_call(
        functools.partial(project_kernel, heads),
        grid_spec=pltpu.PrefetchScalarGridSpec(
            num_scalar_prefetch=1,
            grid=(BLK // tile,),
            in_specs=[
                rows,
                rows,
                pl.BlockSpec((depth, width), lambda i, places: (0, 0)),
                pl.BlockSpec((depth, 128), lambda i, places: (0, width // 128)),
                pl.BlockSpec((depth, heads * HD), lambda i, places: (0, 3)),
                pl.BlockSpec((None, tile, 2 * HD), lambda i, places: (places[0], i, 0)),
                pl.BlockSpec((None, tile, 2 * HD), lambda i, places: (places[1], i, 0)),
            ],
            out_specs=pl.BlockSpec((heads, 4, tile, 2 * HD), lambda i, places: (0, 0, i, 0)),
        ),
        out_shape=jax.ShapeDtypeStruct((heads, 4, BLK, 2 * HD), BF),
        compiler_params=pltpu.CompilerParams(vmem_limit_bytes=60 * 2**20),
        cost_estimate=SMALL,
        name="project",
    )(places, x, g, w, w, ff, table, table)


def join_kernel(
    heads,
    places,
    dq_ref,
    dkv_ref,
    t0_ref,
    t1_ref,
    x_ref,
    g_ref,
    m_ref,
    w_ref,
    s_ref,
    out_ref,
    gs_ref,
    gj,
    sums,
):
    width = heads * HD

    @pl.when(pl.program_id(0) == 0)
    def _():
        total = jnp.zeros((1, 3 * width), F32)
        for slot, table in enumerate((t0_ref, t1_ref)):
            for half in range(2):
                rows = slice(half * BLK // 2, (half + 1) * BLK // 2)
                lanes = slice(slot * HD, (slot + 1) * HD)
                q = jnp.concatenate([dq_ref[h, rows, lanes] for h in range(heads)], axis=1)
                q = turn(q.astype(F32), table[rows, :], heads // 2, False, -1.0).astype(BF)
                kv = jnp.concatenate([dkv_ref[h, slot, rows] for h in range(heads)], axis=1)
                kv = turn(kv.astype(F32), table[rows, :], heads, True, -1.0).astype(BF)
                here = slice(slot * BLK + rows.start, slot * BLK + rows.stop)
                gj[here, :width] = q
                gj[here, width:] = kv
                total += jnp.sum(
                    jnp.concatenate([q, kv], axis=1).astype(F32), axis=0, keepdims=True
                )
        corner = [total[:, r * 128 : (r + 1) * 128] for r in range(3 * width // 128)]
        corner = jnp.concatenate(corner + [jnp.zeros((2, 128), F32)], axis=0)
        sums[...] = corner

    both = gj[...]
    tile, cols = out_ref.shape
    out_ref[:, : 3 * width] = dot(x_ref[...], both, TN).astype(BF)
    out_ref[:, 3 * width : 4 * width] = dot(g_ref[...], m_ref[...], TN).astype(BF)
    zero = jnp.zeros((120, 128), F32)
    block = jnp.concatenate([sums[...], zero] * (tile // 128), axis=0)
    out_ref[:, 4 * width :] = block.astype(BF)
    gs_ref[...] = (s_ref[...].astype(F32) + dot(both, w_ref[...], NT)).astype(BF)


def join(places, dq, dkv, table, x, g, mixed, w, partial_grad, heads):
    tile = 512
    width = 3 * heads * HD
    rows, depth = x.shape
    cols = width + heads * HD + 128
    strip = pl.BlockSpec((rows, tile), lambda i, places: (0, i))
    return pl.pallas_call(
        functools.partial(join_kernel, heads),
        grid_spec=pltpu.PrefetchScalarGridSpec(
            num_scalar_prefetch=1,
            grid=(depth // tile,),
            in_specs=[
                pl.BlockSpec(dq.shape, lambda i, places: (0, 0, 0)),
                pl.BlockSpec(dkv.shape, lambda i, places: (0, 0, 0, 0)),
                pl.BlockSpec((None, BLK, 2 * HD), lambda i, places: (places[0], 0, 0)),
                pl.BlockSpec((None, BLK, 2 * HD), lambda i, places: (places[1], 0, 0)),
                strip,
                strip,
                pl.BlockSpec(mixed.shape, lambda i, places: (0, 0)),
                pl.BlockSpec((tile, width), lambda i, places: (i, 0)),
                strip,
            ],
            out_specs=(pl.BlockSpec((tile, cols), lambda i, places: (i, 0)), strip),
            scratch_shapes=[pltpu.VMEM((rows, width), BF), pltpu.VMEM((8, 128), F32)],
        ),
        out_shape=(
            jax.ShapeDtypeStruct((depth, cols), BF),
            jax.ShapeDtypeStruct((rows, depth), BF),
        ),
        compiler_params=pltpu.CompilerParams(vmem_limit_bytes=60 * 2**20),
        cost_estimate=SMALL,
        name="join",
    )(places, dq, dkv, table, table, x, g, mixed, w, partial_grad)


def ff_part(main, down, first, x, g, w_ref, h_ref, s_ref, pause):
    rows, depth = x.shape[1:]
    x = x.reshape(2 * rows, depth)
    g = g.reshape(2 * rows, depth)
    gate_up = dot(x, w_ref[:, first:], NN)
    pause(0)
    gh = dot(g, w_ref[:, :down], NN)
    ends = gate_up[:, 2 * main :]
    gate = jnp.concatenate([gate_up[:, :main], ends], axis=1)
    up = jnp.concatenate([gate_up[:, main : 2 * main], pltpu.roll(ends, HD, 1)], axis=1)
    sig = jax.nn.sigmoid(gate)
    silu = gate * sig
    hidden = (silu * up).astype(BF)
    d_gate = gh * up * sig * (1.0 + gate * (1.0 - sig))
    d_up = gh * silu
    tail = d_gate[:, main:] + pltpu.roll(d_up[:, main:], HD, 1)
    grads = jnp.concatenate(
        [d_gate[:, :main].astype(BF), d_up[:, :main].astype(BF), tail.astype(BF)], axis=1
    )
    h_ref[...] = hidden.reshape(h_ref.shape)
    pause(1)
    s_ref[...] = dot(grads, w_ref[:, first:], NT).astype(BF).reshape(s_ref.shape)
    return grads, hidden


def branches_kernel(heads, h_ref, o_ref, w_ref, mixed_ref, out_ref):
    rows = h_ref.shape[1]
    mixed = [
        jnp.concatenate(
            [o_ref[head][:, slot * HD : (slot + 1) * HD] for head in range(heads)], axis=1
        )
        for slot in range(2)
    ]
    hidden = h_ref[...].reshape(2 * rows, -1)
    mixed = jnp.concatenate(mixed, axis=0)
    held = jnp.concatenate([hidden, mixed], axis=1)
    mixed_ref[...] = mixed.reshape(mixed_ref.shape)
    out_ref[...] = dot(held, w_ref[...], NT).astype(BF).reshape(out_ref.shape)


def add_branches(hidden, o, w, heads):
    depth = w.shape[0]
    rows = BLK // 2
    kept = hidden.shape[2] + heads * HD

    def tile(lanes, lead=2):
        return pl.BlockSpec((lead, rows, lanes), lambda i: (0, i, 0))

    return pl.pallas_call(
        functools.partial(branches_kernel, heads),
        grid=(2,),
        in_specs=[
            tile(hidden.shape[2]),
            tile(2 * HD, heads),
            pl.BlockSpec((depth, kept), lambda i: (0, 0)),
        ],
        out_specs=(tile(heads * HD), tile(depth)),
        out_shape=(
            jax.ShapeDtypeStruct((2, BLK, heads * HD), BF),
            jax.ShapeDtypeStruct((2, BLK, depth), BF),
        ),
        compiler_params=pltpu.CompilerParams(vmem_limit_bytes=60 * 2**20),
        cost_estimate=SMALL,
        name="add_branches",
    )(hidden, o, w)


def coords():
    tok, br = lax.axis_index("tok"), lax.axis_index("br")
    return tok // 4, (tok // 2) % 2, tok % 2, br // 4, br % 4


def peer(dy=0, dz=0, dc=0, dl=0, dx=0):
    y, z, c, l, x = coords()
    tok = ((y + dy) % 4) * 4 + ((z + dz) % 2) * 2 + (c + dc) % 2
    return tok, ((l + dl) % 2) * 4 + (x + dx) % 4


class Links:
    def __init__(self, send_sems, recv_sems, local_sems):
        self.sems = (send_sems, recv_sems, local_sems)
        self.sent, self.locals = [], []

    def greet(self, partners):
        barrier = pltpu.get_barrier_semaphore()
        for offsets in partners:
            pl.semaphore_signal(
                barrier, inc=1, device_id=peer(**offsets), device_id_type=pl.DeviceIdType.MESH
            )
        pl.semaphore_wait(barrier, len(partners))

    def copy(self, number, source, target, offsets):
        return pltpu.make_async_remote_copy(
            src_ref=source,
            dst_ref=target,
            send_sem=self.sems[0].at[number],
            recv_sem=self.sems[1].at[number],
            device_id=peer(**offsets),
            device_id_type=pl.DeviceIdType.MESH,
        )

    def send(self, source, target, **offsets):
        copy = self.copy(len(self.sent), source, target, offsets)
        copy.start()
        self.sent.append(copy)
        return len(self.sent) - 1, offsets

    def arrived(self, ticket, place):
        self.copy(ticket[0], place, place, ticket[1]).wait_recv()

    def local(self, source, target):
        copy = pltpu.make_async_copy(source, target, self.sems[2].at[len(self.locals)])
        copy.start()
        self.locals.append([copy, True])
        return len(self.locals) - 1

    def settle(self, number):
        copy, pending = self.locals[number]
        if pending:
            copy.wait()
        self.locals[number][1] = False

    def close(self):
        for number in range(len(self.locals)):
            self.settle(number)
        for copy in self.sent:
            copy.wait_send()


def in_turn(tasks):
    tasks = list(tasks)
    while tasks:
        for task in list(tasks):
            try:
                next(task)
            except StopIteration:
                tasks.remove(task)


def ring_four(links, own, place, axis, landed):
    right = links.send(own, place(0, None), **{axis: 1})
    left = links.send(own, place(0, None), **{axis: -1})
    yield
    links.arrived(right, place(-1, None))
    on_right = links.send(place(-1, 0), place(-1, 0), **{axis: 1})
    landed(-1)
    yield
    links.arrived(left, place(1, None))
    on_left = links.send(place(1, 1), place(1, 1), **{axis: -1})
    landed(1)
    yield
    links.arrived(on_right, place(2, 0))
    links.arrived(on_left, place(2, 1))
    landed(2)


def half_of(ref, part):
    if part is None:
        return ref
    rows = ref.shape[0] // 2
    return ref.at[pl.ds(part * rows, rows)]


def gather_br(links, own, whole):
    unused_y, unused_z, unused_c, l, x = coords()

    def place(dl):
        return lambda dx, part: half_of(whole.at[(l + dl) % 2, (x + dx) % 4], part)

    links.local(own, place(0)(0, None))
    across = links.send(own, place(0)(0, None), dl=1)
    near = ring_four(links, own, place(0), "dx", lambda d: None)
    next(near)
    yield
    links.arrived(across, place(1)(0, None))
    far = ring_four(links, place(1)(0, None), place(1), "dx", lambda d: None)
    next(far)
    for unused in near:
        yield
    for unused in far:
        yield


def gather_tok(links, own, whole):
    y, z, c, unused_l, unused_x = coords()
    passed = []

    def place(dz, dc=0):
        return lambda dy, part: half_of(
            whole.at[(y + dy) % 4, (z + dz) % 2, (c + dc) % 2], part
        )

    def passer(dz):
        def landed(dy):
            ref = place(dz)(dy, None)
            passed.append((links.send(ref, ref, dc=1), place(dz, 1)(dy, None)))

        return landed

    links.local(own, place(0)(0, None))
    across = links.send(own, place(0)(0, None), dz=1)
    near = ring_four(links, own, place(0), "dy", passer(0))
    next(near)
    passed.append((links.send(own, place(0)(0, None), dc=1), place(0, 1)(0, None)))
    yield
    links.arrived(across, place(1)(0, None))
    far = ring_four(links, place(1)(0, None), place(1), "dy", passer(1))
    next(far)
    passer(1)(0)
    for unused in near:
        yield
    for unused in far:
        yield
    for ticket, ref in passed:
        links.arrived(ticket, ref)


def add_up(target, sources, rows, finish):
    chunk = 16

    def step(i, unused):
        here = pl.ds(pl.multiple_of(i * chunk, chunk), chunk)
        total = sources[0][here, :].astype(F32)
        for source in sources[1:]:
            total = total + source[here, :].astype(F32)
        target[here, :] = finish(total, here).astype(target.dtype)
        return unused

    lax.fori_loop(0, rows // chunk, step, 0)


def plain(total, here):
    return total


def reduce_heads(links, grads, dq, dq_home, grads_home, mine, near, far, total):
    y, z, c, unused_l, unused_x = coords()
    order = (1, 3, 2, 0)
    held, from_core = {}, {}
    for dz in (1, 0):
        for d in order:
            place = ((y + d) % 4, (z + dz) % 2)
            from_core[d, dz] = links.send(
                grads.at[place[0], place[1], 1 - c], near.at[place[0], place[1]], dc=1
            )
            held[d, dz] = links.local(
                grads.at[place[0], place[1], c], mine.at[place[0], place[1]]
            )
    asked = [links.send(dq.at[(y + d) % 4], dq_home.at[y], dy=d) for d in order[:3]]
    links.local(dq.at[y], dq_home.at[y])
    yield
    rows = mine.shape[2]
    across = {}
    for d in order:
        here = (y + d) % 4
        links.arrived(from_core[d, 1], near.at[here, 1 - z])
        links.settle(held[d, 1])
        add_up(
            mine.at[here, 1 - z], [mine.at[here, 1 - z], near.at[here, 1 - z]], rows, plain
        )
        across[d] = links.send(mine.at[here, 1 - z], far.at[here], dz=1)
        yield
    home = {}
    for d in order:
        here = (y + d) % 4
        links.arrived(from_core[d, 0], near.at[here, z])
        links.settle(held[d, 0])
        links.arrived(across[d], far.at[here])
        add_up(
            total.at[here], [mine.at[here, z], near.at[here, z], far.at[here]], rows, plain
        )
        if d:
            home[d] = links.send(total.at[here], grads_home.at[y], dy=d)
        else:
            links.local(total.at[here], grads_home.at[y])
        yield
    for i, d in enumerate(order[:3]):
        links.arrived(asked[i], dq_home.at[(y - d) % 4])
        links.arrived(home[d], grads_home.at[(y - d) % 4])


def reduce_br(links, parts, own, near, out, far, target, finish):
    unused_y, unused_z, unused_c, l, x = coords()
    order = (1, 3, 2)
    tickets = {}
    held = {}
    for dl in (1, 0):
        there = (l + dl) % 2
        held[dl] = links.local(parts.at[there, x], own.at[there])
        for i, d in enumerate(order):
            tickets[dl, i] = links.send(
                parts.at[there, (x + d) % 4], near.at[i, there], dx=d
            )
    yield
    rows = out.shape[0]
    for i in range(3):
        links.arrived(tickets[1, i], near.at[i, 1 - l])
        yield
    links.settle(held[1])
    add_up(out, [own.at[1 - l]] + [near.at[i, 1 - l] for i in range(3)], rows, plain)
    across = links.send(out, far, dl=1)
    yield
    for i in range(3):
        links.arrived(tickets[0, i], near.at[i, l])
        yield
    links.settle(held[0])
    links.arrived(across, far)
    add_up(
        target, [own.at[l]] + [near.at[i, l] for i in range(3)] + [far], rows, finish
    )


def reduce_tok(links, parts, mine, near, side, out, far, target):
    y, z, c, unused_l, unused_x = coords()
    order = (1, 3, 2)
    tickets, held = {}, {}
    for d in order + (0,):
        here = (y + d) % 4
        tickets[d] = links.send(parts.at[here, :, 1 - c], near.at[here], dc=1)
        held[d] = links.local(parts.at[here, :, c], mine.at[here])
    yield
    rows = out.shape[0]
    sent = {}
    for i, d in enumerate(order + (0,)):
        here = (y + d) % 4
        links.arrived(tickets[d], near.at[here])
        links.settle(held[d])
        for k in range(2):
            add_up(mine.at[here, k], [mine.at[here, k], near.at[here, k]], rows, plain)
        if d:
            sent[i] = links.send(mine.at[here], side.at[i], dy=d)
        yield
    for i in range(3):
        links.arrived(sent[i], side.at[i])
        yield
    add_up(out, [mine.at[y, 1 - z]] + [side.at[i, 1 - z] for i in range(3)], rows, plain)
    across = links.send(out, far, dz=1)
    yield
    links.arrived(across, far)
    add_up(target, [mine.at[y, z]] + [side.at[i, z] for i in range(3)] + [far], rows, plain)


BR_NEAR = [dict(dl=1), dict(dx=1), dict(dx=-1)]
BR_ALL = BR_NEAR + [dict(dx=2)]
TOK_NEAR = [dict(dz=1), dict(dc=1), dict(dy=1), dict(dy=-1)]
TOK_ALL = TOK_NEAR + [dict(dy=2)]


def comm_call(kernel, name, number, args, outs, scratch=(), in_vmem=(), out_vmem=(), copies=48):
    return pl.pallas_call(
        kernel,
        out_shape=tuple(outs),
        in_specs=[VMEM if i in in_vmem else ANY for i in range(len(args))],
        out_specs=tuple(VMEM if i in out_vmem else ANY for i in range(len(outs))),
        scratch_shapes=list(scratch)
        + [
            pltpu.SemaphoreType.DMA((copies,)),
            pltpu.SemaphoreType.DMA((copies,)),
            pltpu.SemaphoreType.DMA((16,)),
        ],
        compiler_params=pltpu.CompilerParams(
            collective_id=number, has_side_effects=True, vmem_limit_bytes=60 * 2**20
        ),
        cost_estimate=SMALL,
        name=name,
    )(*args)


def start_kernel(s_ref, c_ref, w_ref, f_ref, x_out, g_out, w_out, f_out, *sems):
    links = Links(*sems)
    links.greet(BR_NEAR + TOK_NEAR)
    in_turn(
        [
            gather_br(links, s_ref, x_out),
            gather_tok(links, w_ref, w_out),
            gather_tok(links, f_ref, f_out),
            gather_br(links, c_ref, g_out),
        ]
    )
    links.close()


def start(shifted, cot, weights, ff):
    rows, depth = shifted.shape
    wrows = weights.shape[0]
    whole = jax.ShapeDtypeStruct((2, 4, rows, depth), BF)
    return comm_call(
        start_kernel,
        "start",
        0,
        (shifted, cot, weights, ff),
        (
            whole,
            whole,
            jax.ShapeDtypeStruct((4, 2, 2, wrows, weights.shape[1]), BF),
            jax.ShapeDtypeStruct((4, 2, 2, wrows, ff.shape[1]), BF),
        ),
        copies=64,
    )


def ff_heads_kernel(
    main,
    down,
    first,
    x_ref,
    g_ref,
    x_strip,
    g_strip,
    w_ref,
    joined,
    h_ref,
    s_ref,
    grad_ref,
    asked,
    pairs,
    held,
    held_hidden,
    *sems,
):
    y, z, c, unused_l, unused_x = coords()
    step = pl.program_id(0)
    links = Links(*sems)
    order = (1, 3, 2)
    front, back = pl.ds(0, 2), pl.ds(2, 2)

    def pair(dy, dz=0, dc=0):
        return pairs.at[(y + dy) % 4, (z + dz) % 2, (c + dc) % 2]

    kept = [
        pltpu.make_async_copy(joined.at[y, front], asked.at[y], sems[2].at[0]),
        pltpu.make_async_copy(joined.at[y, back], pair(0), sems[2].at[1]),
    ]
    number = iter(range(64))

    def plan(source, target, lands, **offsets):
        n = next(number)
        return links.copy(n, source, target, offsets), links.copy(n, lands, lands, offsets)

    keys = [
        plan(joined.at[(y + d) % 4, back], pair(0), pair(-d), dy=d) for d in order
    ]
    rest = [
        plan(joined.at[(y + d) % 4, front], asked.at[y], asked.at[(y - d) % 4], dy=d)
        for d in order
    ]
    mine = joined.at[y, back]
    far = [plan(mine, pair(0), pair(0, 1), dz=1)]
    near = [plan(mine, pair(0), pair(0, 0, 1), dc=1)]
    for d in order:
        far.append(plan(pair(-d), pair(-d), pair(-d, 1), dz=1))
        near.append(plan(pair(-d), pair(-d), pair(-d, 0, 1), dc=1))
    diagonal = [plan(pair(-d, 1), pair(-d, 1), pair(-d, 1, 1), dc=1) for d in (0,) + order]

    def relay(i):
        keys[i][1].wait_recv()
        far[i + 1][0].start()
        near[i + 1][0].start()

    def cross(i):
        far[i][1].wait_recv()
        diagonal[i][0].start()

    @pl.when(step == 0)
    def _():
        links.greet(TOK_ALL)
        for copy in kept:
            copy.start()
        for copy, unused in [keys[0], far[0], keys[1], near[0], keys[2]] + rest:
            copy.start()

    def pause(point):
        @pl.when(step == 0)
        def _():
            if point == 0:
                relay(0)
                relay(1)
            else:
                relay(2)

        @pl.when(step == 1)
        def _():
            if point == 0:
                cross(0)
            else:
                cross(1)

    for i in range(2, 4):

        @pl.when(step == i + 1)
        def _():
            cross(i)

    rows = x_ref.shape[1]

    @pl.when(step < 2)
    def _():
        grads, hidden = ff_part(
            main, down, first, x_ref[...], g_ref[...], w_ref, h_ref, s_ref, pause
        )
        here = pl.ds(pl.multiple_of(step * rows, rows), rows)
        held[:, here, :] = grads.reshape(2, rows, -1)
        held_hidden[:, here, :] = hidden.reshape(2, rows, -1)

    @pl.when(step >= 2)
    def _():
        grads = held[...].reshape(-1, held.shape[2])
        hidden = held_hidden[...].reshape(-1, down)
        grad_ref[:, :down] = dot(g_strip[...], hidden, TN).astype(BF)
        grad_ref[:, down:] = dot(x_strip[...], grads, TN).astype(BF)

    @pl.when(step == pl.num_programs(0) - 1)
    def _():
        for copy in kept:
            copy.wait()
        for unused, landed in rest + near + diagonal:
            landed.wait_recv()
        for copy, unused in keys + rest + far + near + diagonal:
            copy.wait_send()


def ff_heads(x, g, w, joined, main, down, first):
    depth, cols = w.shape
    heads, unused, span, lanes = joined.shape
    rows = BLK // 2
    both = cols - first
    strip = 512

    def tile(width):
        return pl.BlockSpec((2, rows, width), lambda i: (0, jnp.minimum(i, 1), 0))

    return pl.pallas_call(
        functools.partial(ff_heads_kernel, main, down, first),
        grid=(2 + depth // strip,),
        in_specs=[
            tile(depth),
            tile(depth),
            pl.BlockSpec((2 * BLK, strip), lambda i: (0, jnp.maximum(i - 2, 0))),
            pl.BlockSpec((2 * BLK, strip), lambda i: (0, jnp.maximum(i - 2, 0))),
            pl.BlockSpec((depth, cols), lambda i: (0, 0), pipeline_mode=pl.Buffered(1)),
            ANY,
        ],
        out_specs=(
            tile(down),
            tile(depth),
            pl.BlockSpec((strip, both + down), lambda i: (jnp.maximum(i - 2, 0), 0)),
            ANY,
            ANY,
        ),
        out_shape=(
            jax.ShapeDtypeStruct((2, BLK, down), BF),
            jax.ShapeDtypeStruct((2, BLK, depth), BF),
            jax.ShapeDtypeStruct((depth, both + down), BF),
            jax.ShapeDtypeStruct((4, 2, span, lanes), BF),
            jax.ShapeDtypeStruct((4, 2, 2, 2, span, lanes), BF),
        ),
        scratch_shapes=[
            pltpu.VMEM((2, BLK, both), BF),
            pltpu.VMEM((2, BLK, down), BF),
            pltpu.SemaphoreType.DMA((32,)),
            pltpu.SemaphoreType.DMA((32,)),
            pltpu.SemaphoreType.DMA((2,)),
        ],
        compiler_params=pltpu.CompilerParams(
            collective_id=1, has_side_effects=True, vmem_limit_bytes=60 * 2**20
        ),
        cost_estimate=SMALL,
        name="ff_heads",
    )(x, g, x.reshape(2 * BLK, depth), g.reshape(2 * BLK, depth), w, joined)


def home_kernel(grads, dq, branches, tokens, dq_home, grads_home, result, *rest):
    mine, near, far, total, own, side, out, cross = rest[:8]
    links = Links(*rest[8:])
    links.greet(BR_ALL + TOK_ALL)

    def finish(value, here):
        return value + tokens[here, :].astype(F32)

    in_turn(
        [
            reduce_heads(links, grads, dq, dq_home, grads_home, mine, near, far, total),
            reduce_br(links, branches, own, side, out, cross, result, finish),
        ]
    )
    links.close()


def heads_home(grads, dq, branches, tokens):
    rows, depth = tokens.shape
    span, lanes = grads.shape[3:]
    return comm_call(
        home_kernel,
        "heads_home",
        2,
        (grads, dq, branches, tokens),
        (
            jax.ShapeDtypeStruct(dq.shape, BF),
            jax.ShapeDtypeStruct((4, span, lanes), BF),
            jax.ShapeDtypeStruct((rows, depth), BF),
        ),
        scratch=[
            pltpu.VMEM((4, 2, span, lanes), BF),
            pltpu.VMEM((4, 2, span, lanes), BF),
            pltpu.VMEM((4, span, lanes), BF),
            pltpu.VMEM((4, span, lanes), BF),
            pltpu.VMEM((2, rows, depth), BF),
            pltpu.VMEM((3, 2, rows, depth), BF),
            pltpu.VMEM((rows, depth), BF),
            pltpu.VMEM((rows, depth), BF),
        ],
        in_vmem=(3,),
        out_vmem=(2,),
    )


def turn_back(grads, tokens, cot, gain, parts, result):
    rows, depth = tokens.shape
    chunk = 16

    def normal(here):
        value = tokens[here, :].astype(F32)
        value = value - jnp.mean(value, axis=-1, keepdims=True)
        scale = lax.rsqrt(jnp.mean(value * value, axis=-1, keepdims=True) + EPSILON)
        return value * scale, scale

    def rows_at(i):
        return pl.ds(pl.multiple_of(i * chunk, chunk), chunk)

    def sums(i, carry):
        here = rows_at(i)
        grad = grads[here, :]
        up = grad * normal(here)[0]
        return carry[0] + up.reshape(2, 8, depth).sum(0), carry[1] + grad.reshape(
            2, 8, depth
        ).sum(0)

    zero = jnp.zeros((8, depth), F32)
    found = lax.fori_loop(0, rows // chunk, sums, (zero, zero))
    for k in range(2):
        line = jnp.sum(found[k], axis=0, keepdims=True)
        parts[16 * k : 16 * (k + 1), :] = jnp.concatenate(
            [line[:, t * 128 : (t + 1) * 128] for t in range(depth // 128)], axis=0
        )
    yield

    def back(i, unused):
        here = rows_at(i)
        normed, scale = normal(here)
        grad = grads[here, :] * gain[...]
        grad = grad - jnp.mean(grad, axis=-1, keepdims=True)
        grad = grad - normed * jnp.mean(grad * normed, axis=-1, keepdims=True)
        result[here, :] = cot[here, :].astype(F32) + scale * grad
        return unused

    lax.fori_loop(0, rows // chunk, back, 0)


BR_PEERS = [dict(dl=i // 4, dx=i % 4) for i in range(1, 8)]
TOK_PEERS = [dict(dy=i // 4, dz=(i // 2) % 2, dc=i % 2) for i in range(1, 16)]


def last_kernel(
    heads, grads, weights, tokens, cot, gain, result, qkv_out, out_out, bias_out, sides, *rest
):
    own, side, out, cross, mine, near, edge, wout, wcross, summed, wsum = rest[:11]
    parts, parts_in, lines, lines_in = rest[11:15]
    links = Links(*rest[15:])
    links.greet(BR_PEERS + TOK_PEERS)
    y, z, c, l, x = coords()
    in_turn(
        [
            reduce_tok(links, weights, mine, near, edge, wout, wcross, wsum),
            reduce_br(links, grads, own, side, out, cross, summed, plain),
        ]
    )
    through = turn_back(summed, tokens, cot, gain, parts, result)
    next(through)
    tickets = [links.send(parts, parts_in.at[i], **o) for i, o in enumerate(BR_PEERS)]
    for unused in through:
        pass
    total = parts[...]
    for i, ticket in enumerate(tickets):
        links.arrived(ticket, parts_in.at[i])
        total = total + parts_in[i]
    lines[...] = jnp.zeros_like(lines)
    for t in range(16):
        lines[t, 0:2, :] = jnp.concatenate([total[t : t + 1], total[16 + t : 17 + t]], axis=0)
    tickets = []
    for i, o in enumerate(TOK_PEERS):
        there = ((y + o["dy"]) % 4) * 4 + ((z + o["dz"]) % 2) * 2 + (c + o["dc"]) % 2
        tickets.append(links.send(lines.at[there], lines_in.at[i], **o))
    width = heads * HD
    qkv_out[0] = wsum[:, :width]
    for k in range(2):
        qkv_out[1 + k] = jnp.concatenate(
            [
                wsum[:, width + (2 * h + k) * HD : width + (2 * h + k + 1) * HD]
                for h in range(heads)
            ],
            axis=1,
        )
    out_out[...] = jnp.transpose(wsum[:, 3 * width : 4 * width])
    bias_out[...] = wsum[:8, 4 * width :]
    total = lines[y * 4 + z * 2 + c]
    for i, ticket in enumerate(tickets):
        links.arrived(ticket, lines_in.at[i])
        total = total + lines_in[i]
    sides[...] = total
    links.close()


def last_sums(grads, weights, tokens, cot, gain, heads):
    rows, depth = grads.shape[2:]
    wrows, cols = weights.shape[3:]
    return comm_call(
        functools.partial(last_kernel, heads),
        "last_sums",
        3,
        (grads, weights, tokens, cot, gain),
        (
            jax.ShapeDtypeStruct((rows, depth), F32),
            jax.ShapeDtypeStruct((3, wrows, heads * HD), F32),
            jax.ShapeDtypeStruct((heads * HD, wrows), F32),
            jax.ShapeDtypeStruct((8, 128), F32),
            jax.ShapeDtypeStruct((8, 128), F32),
        ),
        scratch=[
            pltpu.VMEM((2, rows, depth), BF),
            pltpu.VMEM((3, 2, rows, depth), BF),
            pltpu.VMEM((rows, depth), BF),
            pltpu.VMEM((rows, depth), BF),
            pltpu.VMEM((4, 2, wrows, cols), BF),
            pltpu.VMEM((4, 2, wrows, cols), BF),
            pltpu.VMEM((3, 2, wrows, cols), BF),
            pltpu.VMEM((wrows, cols), BF),
            pltpu.VMEM((wrows, cols), BF),
            pltpu.VMEM((rows, depth), F32),
            pltpu.VMEM((wrows, cols), F32),
            pltpu.VMEM((32, 128), F32),
            pltpu.VMEM((7, 32, 128), F32),
            pltpu.VMEM((16, 8, 128), F32),
            pltpu.VMEM((15, 8, 128), F32),
        ],
        in_vmem=(2, 3, 4),
        out_vmem=(0, 1, 2, 3, 4),
        copies=64,
    )


def tok_perm(dy):
    return [(t, ((t // 4 + dy) % 4) * 4 + t % 4) for t in range(16)]


def swap_heads(parts, y):
    back = [lax.dynamic_index_in_dim(parts, y, 0, keepdims=False)]
    for d in (3, 2, 1):
        piece = lax.dynamic_index_in_dim(parts, (y + d) % 4, 0, keepdims=False)
        back.append(lax.ppermute(piece, "tok", tok_perm(d)))
    stacked = jnp.stack(back + back)
    return lax.dynamic_slice_in_dim(stacked, (4 - y) % 4, 4, 0)


def rotary_table():
    half = ROT // 2
    frequency = (ROPE_BASE ** (-(np.arange(half) * 2.0 / ROT))).astype(np.float32)
    angles = np.arange(LB * BLK, dtype=np.float32)[:, None] * frequency[None, :]
    cos, sin = np.cos(angles), np.sin(angles)
    one = np.ones((LB * BLK, HD - ROT), np.float32)
    table = np.concatenate([cos, cos, one, -sin, sin, 0.0 * one], axis=1)
    return table.astype(np.float32).reshape(LB, BLK, 2 * HD)


def body(
    tokens,
    norm_gain,
    norm_bias,
    qkv_weight,
    qkv_bias,
    out_weight,
    gate_weight,
    up_weight,
    down_weight,
    cotangent,
    block_map,
    lengths,
):
    tok = lax.axis_index("tok")
    y, z, c = tok // 4, (tok // 2) % 2, tok % 2
    total_blocks = block_map.shape[0]
    long_blocks = total_blocks // 2
    rows = tokens.shape[0]
    depth = tokens.shape[1]
    wrows = qkv_weight.shape[1]
    heads = qkv_bias.shape[1]
    width = heads * HD
    hidden_width = gate_weight.shape[1]
    main = hidden_width // 128 * 128
    tail = hidden_width - main

    residual = tokens.astype(F32)
    centred = residual - jnp.mean(residual, axis=-1, keepdims=True)
    inverse = lax.rsqrt(jnp.mean(centred * centred, axis=-1, keepdims=True) + EPSILON)
    normed = centred * inverse
    shifted = (normed * norm_gain + norm_bias).astype(BF)

    kv_shard = jnp.stack(
        [w.reshape(wrows, heads, HD) for w in (qkv_weight[1], qkv_weight[2])], axis=2
    ).reshape(wrows, 2 * width)
    per = qkv_bias.shape[2]
    lane_tok = jnp.arange(HD, dtype=jnp.int32) // per
    bias_lanes = jnp.where(lane_tok == tok, jnp.tile(qkv_bias, (1, 1, HD // per)), 0)
    bias_rows = jnp.concatenate(
        [
            bias_lanes[0].reshape(-1),
            jnp.stack([bias_lanes[1], bias_lanes[2]], axis=1).reshape(-1),
        ]
    ).reshape(-1, 128)
    bias_row = jnp.pad(bias_rows, ((0, wrows - bias_rows.shape[0]), (0, 0)))
    qkv_shard = jnp.concatenate([qkv_weight[0], kv_shard, bias_row], axis=1)
    ff_shard = jnp.concatenate(
        [
            jnp.transpose(down_weight),
            jnp.zeros((wrows, 128 - tail), BF),
            jnp.transpose(out_weight),
            gate_weight[:, :main],
            up_weight[:, :main],
            gate_weight[:, main:],
            up_weight[:, main:],
        ],
        axis=1,
    )
    down_width = main + 128
    first = down_width + width
    x, grad, qkv_full, ff_full = start(shifted, cotangent, qkv_shard, ff_shard)
    x = x.reshape(2, BLK, depth)
    grad = grad.reshape(2, BLK, depth)
    qkv_full = qkv_full.reshape(16 * wrows, -1)
    ff_full = ff_full.reshape(16 * wrows, -1)

    slot_table = jnp.arange(total_blocks, dtype=jnp.int32)
    slot_of = jnp.sum(
        jnp.where(block_map[None, :] == slot_table[:, None], slot_table[None, :], 0), axis=1
    )
    key_slot = slot_of.astype(jnp.int32)
    from_tok = jnp.arange(4, dtype=jnp.int32) * 4 + z * 2 + c
    my_queries = jnp.stack([2 * from_tok, 2 * from_tok + 1], axis=1).reshape(-1)
    query_block = jnp.sum(
        jnp.where(my_queries[:, None] == slot_table[None, :], block_map[None, :], 0), axis=1
    ).astype(jnp.int32)
    query_row = jnp.where(
        query_block < long_blocks,
        query_block // LB,
        long_blocks // LB + (query_block - long_blocks) // 2,
    )
    row_table = jnp.arange(lengths.shape[0], dtype=jnp.int32)
    query_limit = jnp.sum(
        jnp.where(query_row[:, None] == row_table[None, :], lengths[None, :], 0), axis=1
    ).astype(jnp.int32)

    my_blocks = lax.dynamic_slice_in_dim(block_map, tok * 2, 2)
    places = jnp.where(my_blocks < long_blocks, my_blocks % LB, (my_blocks - long_blocks) % 2)
    table = jnp.asarray(rotary_table())

    joined = project(places, x, grad, qkv_full, ff_full, table, heads)
    hidden, grad_x, grad_ff, qd_all, kv_all = ff_heads(
        x, grad, ff_full, joined, main, down_width, first
    )
    kv_all = kv_all.reshape(-1, 2 * HD)
    x = x.reshape(2 * BLK, depth)
    grad = grad.reshape(2 * BLK, depth)
    grad_ff = lax.psum_scatter(grad_ff, "tok", scatter_dimension=0, tiled=True)

    turned, lse, o_parts = attn_fwd(query_block, query_limit, key_slot, qd_all, kv_all, long_blocks)
    o_heads = swap_heads(o_parts, y)
    dq_parts, dkv_all = attn_bwd(
        query_block, query_limit, key_slot, qd_all, kv_all, turned, lse, long_blocks
    )
    o_heads, dq_parts = lax.optimization_barrier((o_heads, dq_parts))
    mixed, branches = add_branches(hidden, o_heads, ff_full, heads)
    dq_heads, dkv_heads, result = heads_home(
        dkv_all.reshape(4, 2, 2, 2 * BLK, 2 * HD),
        dq_parts,
        branches.reshape(2, 4, rows, depth),
        tokens,
    )
    grad_ff, dq_heads = lax.optimization_barrier((grad_ff, dq_heads))
    grad_qkv, grad_shifted = join(
        places,
        dq_heads,
        dkv_heads.reshape(heads, 2, BLK, 2 * HD),
        table,
        x,
        grad,
        mixed.reshape(2 * BLK, width),
        qkv_full,
        grad_x.reshape(2 * BLK, depth),
        heads,
    )
    grad_tokens, grad_qkv, grad_out_out, bias_sums, sides = last_sums(
        grad_shifted.reshape(2, 4, rows, depth),
        grad_qkv.reshape(4, 2, 2, wrows, -1),
        tokens,
        cotangent,
        norm_gain.reshape(1, depth),
        heads,
    )
    bias_sums = bias_sums[: 3 * width // 128].reshape(-1)
    bias_sums = jnp.concatenate(
        [
            bias_sums[:width].reshape(1, heads, HD),
            jnp.transpose(bias_sums[width:].reshape(heads, 2, HD), (1, 0, 2)),
        ]
    )
    grad_bias_out = lax.dynamic_slice_in_dim(bias_sums, tok * per, per, 2)
    grad_ff = grad_ff.astype(F32)
    grad_down_out = jnp.transpose(grad_ff[:, :hidden_width])
    grad_gu = grad_ff[:, down_width:]
    ends = grad_gu[:, 2 * main :]
    grad_gate_out = jnp.concatenate([grad_gu[:, :main], ends[:, :tail]], axis=1)
    grad_up_out = jnp.concatenate([grad_gu[:, main : 2 * main], ends[:, tail:]], axis=1)

    sides = lax.dynamic_slice_in_dim(sides[:2], lax.axis_index("br") * 16, 16, 1)
    return (
        result,
        grad_tokens,
        sides[0],
        sides[1],
        grad_qkv,
        grad_bias_out,
        grad_out_out,
        grad_gate_out,
        grad_up_out,
        grad_down_out,
    )


def solution(mesh):
    in_specs = (
        P(("tok", "br"), None),
        P(),
        P(),
        P(None, "tok", "br"),
        P(None, "br", "tok"),
        P("br", "tok"),
        P("tok", "br"),
        P("tok", "br"),
        P("br", "tok"),
        P(("tok", "br"), None),
        P(),
        P(),
    )
    out_specs = (
        P(("tok", "br"), None),
        P(("tok", "br"), None),
        P(("tok", "br")),
        P(("tok", "br")),
        P(None, "tok", "br"),
        P(None, "br", "tok"),
        P("br", "tok"),
        P("tok", "br"),
        P("tok", "br"),
        P("br", "tok"),
    )
    return jax.shard_map(body, mesh=mesh, in_specs=in_specs, out_specs=out_specs, check_vma=False)
```

```python
import functools

import jax
import jax.numpy as jnp
import numpy as np
from jax import lax
from jax.experimental import pallas as pl
from jax.experimental.pallas import tpu as pltpu
from jax.sharding import PartitionSpec as P

HD = 64
ROT = 16
BLK = 512
LB = 8
EPSILON = 1e-05
ROPE_BASE = 10000.0
MASKED = -1e30
BF = jnp.bfloat16
F32 = jnp.float32
NN = (((1,), (0,)), ((), ()))
NT = (((1,), (1,)), ((), ()))
TN = (((0,), (0,)), ((), ()))
VMEM = pl.BlockSpec(memory_space=pltpu.VMEM)
SMEM = pl.BlockSpec(memory_space=pltpu.SMEM)
ANY = pl.BlockSpec(memory_space=pl.ANY)
SMALL = pl.CostEstimate(flops=1000, bytes_accessed=1000, transcendentals=0)


def dot(left, right, dims):
    return lax.dot_general(left, right, dims, preferred_element_type=F32)


def block_info(block, long_blocks):
    is_long = block < long_blocks
    place = jnp.where(is_long, block % LB, (block - long_blocks) % 2)
    return is_long, place, block - place


def lane_half(packed, half, upper):
    piece = packed[:, half * HD : (half + 1) * HD]
    zero = jnp.zeros_like(piece)
    return jnp.concatenate([zero, piece] if upper else [piece, zero], axis=1)


def allowed_pairs(place, step, limit):
    key_pos = step * BLK + lax.broadcasted_iota(jnp.int32, (BLK, BLK), 0)
    query_pos = place * BLK + lax.broadcasted_iota(jnp.int32, (BLK, BLK), 1)
    return (key_pos <= query_pos) & (key_pos < limit)


def attn_fwd_kernel(long_blocks, qblk, qlim, kslot, q_ref, kv_ref, ot_ref, lse_ref, o_ref):
    def pack(i, unused):
        packed = q_ref[i, 0]
        for half in range(2):
            slot = 2 * i + half
            is_long, place, first = block_info(qblk[slot], long_blocks)
            limit = qlim[slot]
            queries = lane_half(packed, half, False) * jnp.asarray(0.125, BF)

            def step(j, carry, masked):
                top, total, acc = carry
                rows = pl.ds(pl.multiple_of(kslot[first + j] * BLK, BLK), BLK)
                kv = kv_ref[rows, :]
                scores = dot(kv, queries, NT)
                if masked:
                    scores = jnp.where(allowed_pairs(place, j, limit), scores, MASKED)
                new_top = jnp.maximum(top, jnp.max(scores, axis=0, keepdims=True))
                fade = jnp.exp(top - new_top)
                probs = jnp.exp(scores - new_top)
                total = total * fade + jnp.sum(probs, axis=0, keepdims=True)
                acc = acc * fade + dot(kv, probs.astype(BF), TN)
                return new_top, total, acc

            free = jnp.where(is_long, place, 0)
            carry = (
                jnp.full((1, BLK), MASKED, F32),
                jnp.zeros((1, BLK), F32),
                jnp.zeros((2 * HD, BLK), F32),
            )
            carry = lax.fori_loop(0, free, lambda j, c: step(j, c, False), carry)
            top, total, acc = lax.fori_loop(free, place + 1, lambda j, c: step(j, c, True), carry)
            lse_ref[slot] = top + jnp.log(total)
            ot_ref[i, half * HD : (half + 1) * HD, :] = acc[HD:, :] / total
        o_ref[i] = jnp.transpose(ot_ref[i]).astype(BF)
        return unused

    lax.fori_loop(0, q_ref.shape[0], pack, 0)


def attn_fwd(qblk, qlim, kslot, q, kv, long_blocks):
    n = q.shape[0]
    return pl.pallas_call(
        functools.partial(attn_fwd_kernel, long_blocks),
        out_shape=(
            jax.ShapeDtypeStruct((n, 2 * HD, BLK), F32),
            jax.ShapeDtypeStruct((2 * n, 1, BLK), F32),
            jax.ShapeDtypeStruct((n, BLK, 2 * HD), BF),
        ),
        in_specs=[SMEM, SMEM, SMEM, VMEM, VMEM],
        out_specs=(VMEM, VMEM, VMEM),
        compiler_params=pltpu.CompilerParams(vmem_limit_bytes=60 * 2**20),
        cost_estimate=SMALL,
        name="attn_fwd",
    )(qblk, qlim, kslot, q, kv)


def attn_bwd_kernel(
    long_blocks, qblk, qlim, kslot, q_ref, kv_ref, ot_ref, lse_ref, dq_ref, dkv_ref, acc, dqt
):
    acc[...] = jnp.zeros_like(acc)

    def pack(i, unused):
        q_packed = q_ref[i, 0]
        d_packed = q_ref[i, 1]
        d_turned = jnp.transpose(d_packed.astype(F32))
        for half in range(2):
            slot = 2 * i + half
            is_long, place, first = block_info(qblk[slot], long_blocks)
            limit = qlim[slot]
            queries = lane_half(q_packed, half, False) * jnp.asarray(0.125, BF)
            grads = lane_half(d_packed, half, True)
            both = jnp.concatenate([queries, grads], axis=0)
            lanes = slice(half * HD, (half + 1) * HD)
            delta = jnp.sum(d_turned[lanes] * ot_ref[i, lanes, :], axis=0, keepdims=True)
            lse = lse_ref[slot]

            def step(j, total, masked):
                rows = pl.ds(pl.multiple_of(kslot[first + j] * BLK, BLK), BLK)
                kv = kv_ref[rows, :]
                scores = dot(kv, queries, NT)
                if masked:
                    scores = jnp.where(allowed_pairs(place, j, limit), scores, MASKED)
                probs = jnp.exp(scores - lse)
                ds = (probs * (dot(kv, grads, NT) - delta)).astype(BF)
                acc[rows, :] += dot(jnp.concatenate([ds, probs.astype(BF)], axis=1), both, NN)
                return total + dot(kv, ds, TN)

            free = jnp.where(is_long, place, 0)
            total = lax.fori_loop(
                0, free, lambda j, c: step(j, c, False), jnp.zeros((2 * HD, BLK), F32)
            )
            total = lax.fori_loop(free, place + 1, lambda j, c: step(j, c, True), total)
            dqt[lanes, :] = total[:HD, :] * 0.125
        dq_ref[i] = jnp.transpose(dqt[...]).astype(BF)
        return unused

    lax.fori_loop(0, q_ref.shape[0], pack, 0)

    def finish(i, unused):
        rows = pl.ds(pl.multiple_of(i * BLK, BLK), BLK)
        dkv_ref[rows, :] = acc[rows, :].astype(BF)
        return unused

    lax.fori_loop(0, kv_ref.shape[0] // BLK, finish, 0)


def attn_bwd(qblk, qlim, kslot, q, kv, ot, lse, long_blocks):
    n = q.shape[0]
    return pl.pallas_call(
        functools.partial(attn_bwd_kernel, long_blocks),
        out_shape=(
            jax.ShapeDtypeStruct((n, BLK, 2 * HD), BF),
            jax.ShapeDtypeStruct(kv.shape, BF),
        ),
        in_specs=[SMEM, SMEM, SMEM, VMEM, VMEM, VMEM, VMEM],
        out_specs=(VMEM, VMEM),
        scratch_shapes=[pltpu.VMEM(kv.shape, F32), pltpu.VMEM((2 * HD, BLK), F32)],
        compiler_params=pltpu.CompilerParams(vmem_limit_bytes=60 * 2**20),
        cost_estimate=SMALL,
        name="attn_bwd",
    )(qblk, qlim, kslot, q, kv, ot, lse)


def turn(values, table, copies, paired, sign):
    width = values.shape[1]
    lane = lax.broadcasted_iota(jnp.int32, values.shape, 1) % HD
    partner = jnp.where(
        lane < ROT // 2,
        pltpu.roll(values, width - ROT // 2, 1),
        pltpu.roll(values, ROT // 2, 1),
    )
    cos, sin = table[:, :HD], sign * table[:, HD:]
    cos = jnp.concatenate([cos, jnp.ones_like(cos) if paired else cos], axis=1)
    sin = jnp.concatenate([sin, jnp.zeros_like(sin) if paired else sin], axis=1)
    cos = jnp.concatenate([cos] * copies, axis=1)
    sin = jnp.concatenate([sin] * copies, axis=1)
    return values * cos + partner * sin


def project_kernel(
    heads, places, x_ref, g_ref, w_ref, b_ref, wo_ref, t0_ref, t1_ref, out_ref
):
    width = heads * HD
    rows = w_ref.shape[0] // 16
    corner = b_ref[:8, :].astype(F32)
    for t in range(1, 16):
        corner = corner + b_ref[t * rows : t * rows + 8, :].astype(F32)
    bias = jnp.concatenate([corner[r : r + 1] for r in range(3 * width // 128)], axis=1)
    parts, grads = [], []
    tile, depth = x_ref.shape[1:]
    products = dot(x_ref[...].reshape(2 * tile, depth), w_ref[...], NN) + bias
    mixed = dot(g_ref[...].reshape(2 * tile, depth), wo_ref[...], NN).astype(BF)
    for slot, table in enumerate((t0_ref[...], t1_ref[...])):
        joined = products[slot * tile : (slot + 1) * tile]
        parts.append(turn(joined[:, :width], table, heads // 2, False, 1.0).astype(BF))
        grads.append(mixed[slot * tile : (slot + 1) * tile])
        kv = turn(joined[:, width:], table, heads, True, 1.0).astype(BF)
        for head in range(heads):
            out_ref[head, 2 + slot] = kv[:, head * 2 * HD : (head + 1) * 2 * HD]
    for head in range(heads):
        lanes = slice(head * HD, (head + 1) * HD)
        for i, pair in enumerate((parts, grads)):
            out_ref[head, i] = jnp.concatenate([pair[0][:, lanes], pair[1][:, lanes]], axis=1)


def project(places, x, g, w, ff, table, heads):
    tile = 256
    width = 3 * heads * HD
    depth = x.shape[2]
    rows = pl.BlockSpec((2, tile, depth), lambda i, places: (0, i, 0))
    return pl.pallas_call(
        functools.partial(project_kernel, heads),
        grid_spec=pltpu.PrefetchScalarGridSpec(
            num_scalar_prefetch=1,
            grid=(BLK // tile,),
            in_specs=[
                rows,
                rows,
                pl.BlockSpec((depth, width), lambda i, places: (0, 0)),
                pl.BlockSpec((depth, 128), lambda i, places: (0, width // 128)),
                pl.BlockSpec((depth, heads * HD), lambda i, places: (0, 3)),
                pl.BlockSpec((None, tile, 2 * HD), lambda i, places: (places[0], i, 0)),
                pl.BlockSpec((None, tile, 2 * HD), lambda i, places: (places[1], i, 0)),
            ],
            out_specs=pl.BlockSpec((heads, 4, tile, 2 * HD), lambda i, places: (0, 0, i, 0)),
        ),
        out_shape=jax.ShapeDtypeStruct((heads, 4, BLK, 2 * HD), BF),
        compiler_params=pltpu.CompilerParams(vmem_limit_bytes=60 * 2**20),
        cost_estimate=SMALL,
        name="project",
    )(places, x, g, w, w, ff, table, table)


def ff_part(main, down, first, x, g, w_ref, h_ref, s_ref, pause):
    rows, depth = x.shape[1:]
    x = x.reshape(2 * rows, depth)
    g = g.reshape(2 * rows, depth)
    gate_up = dot(x, w_ref[:, first:], NN)
    pause(0)
    gh = dot(g, w_ref[:, :down], NN)
    ends = gate_up[:, 2 * main :]
    gate = jnp.concatenate([gate_up[:, :main], ends], axis=1)
    up = jnp.concatenate([gate_up[:, main : 2 * main], pltpu.roll(ends, HD, 1)], axis=1)
    sig = jax.nn.sigmoid(gate)
    silu = gate * sig
    hidden = (silu * up).astype(BF)
    d_gate = gh * up * sig * (1.0 + gate * (1.0 - sig))
    d_up = gh * silu
    tail = d_gate[:, main:] + pltpu.roll(d_up[:, main:], HD, 1)
    grads = jnp.concatenate(
        [d_gate[:, :main].astype(BF), d_up[:, :main].astype(BF), tail.astype(BF)], axis=1
    )
    h_ref[...] = hidden.reshape(h_ref.shape)
    pause(1)
    s_ref[...] = dot(grads, w_ref[:, first:], NT).astype(BF).reshape(s_ref.shape)
    return grads, hidden


def coords():
    tok, br = lax.axis_index("tok"), lax.axis_index("br")
    return tok // 4, (tok // 2) % 2, tok % 2, br // 4, br % 4


def peer(dy=0, dz=0, dc=0, dl=0, dx=0):
    y, z, c, l, x = coords()
    tok = ((y + dy) % 4) * 4 + ((z + dz) % 2) * 2 + (c + dc) % 2
    return tok, ((l + dl) % 2) * 4 + (x + dx) % 4


class Links:
    def __init__(self, send_sems, recv_sems, local_sems):
        self.sems = (send_sems, recv_sems, local_sems)
        self.sent, self.locals = [], []

    def greet(self, partners):
        barrier = pltpu.get_barrier_semaphore()
        for offsets in partners:
            pl.semaphore_signal(
                barrier, inc=1, device_id=peer(**offsets), device_id_type=pl.DeviceIdType.MESH
            )
        pl.semaphore_wait(barrier, len(partners))

    def copy(self, number, source, target, offsets):
        return pltpu.make_async_remote_copy(
            src_ref=source,
            dst_ref=target,
            send_sem=self.sems[0].at[number],
            recv_sem=self.sems[1].at[number],
            device_id=peer(**offsets),
            device_id_type=pl.DeviceIdType.MESH,
        )

    def send(self, source, target, **offsets):
        copy = self.copy(len(self.sent), source, target, offsets)
        copy.start()
        self.sent.append(copy)
        return len(self.sent) - 1, offsets

    def arrived(self, ticket, place):
        self.copy(ticket[0], place, place, ticket[1]).wait_recv()

    def local(self, source, target):
        copy = pltpu.make_async_copy(source, target, self.sems[2].at[len(self.locals)])
        copy.start()
        self.locals.append([copy, True])
        return len(self.locals) - 1

    def settle(self, number):
        copy, pending = self.locals[number]
        if pending:
            copy.wait()
        self.locals[number][1] = False

    def close(self):
        for number in range(len(self.locals)):
            self.settle(number)
        for copy in self.sent:
            copy.wait_send()


def in_turn(tasks):
    tasks = list(tasks)
    while tasks:
        for task in list(tasks):
            try:
                next(task)
            except StopIteration:
                tasks.remove(task)


def ring_four(links, own, place, axis, landed):
    right = links.send(own, place(0, None), **{axis: 1})
    left = links.send(own, place(0, None), **{axis: -1})
    yield
    links.arrived(right, place(-1, None))
    on_right = links.send(place(-1, 0), place(-1, 0), **{axis: 1})
    landed(-1)
    yield
    links.arrived(left, place(1, None))
    on_left = links.send(place(1, 1), place(1, 1), **{axis: -1})
    landed(1)
    yield
    links.arrived(on_right, place(2, 0))
    links.arrived(on_left, place(2, 1))
    landed(2)


def half_of(ref, part):
    if part is None:
        return ref
    rows = ref.shape[0] // 2
    return ref.at[pl.ds(part * rows, rows)]


def gather_br(links, own, whole):
    unused_y, unused_z, unused_c, l, x = coords()

    def place(dl):
        return lambda dx, part: half_of(whole.at[(l + dl) % 2, (x + dx) % 4], part)

    links.local(own, place(0)(0, None))
    across = links.send(own, place(0)(0, None), dl=1)
    near = ring_four(links, own, place(0), "dx", lambda d: None)
    next(near)
    yield
    links.arrived(across, place(1)(0, None))
    far = ring_four(links, place(1)(0, None), place(1), "dx", lambda d: None)
    next(far)
    for unused in near:
        yield
    for unused in far:
        yield


def gather_tok(links, own, whole):
    y, z, c, unused_l, unused_x = coords()
    passed = []

    def place(dz, dc=0):
        return lambda dy, part: half_of(
            whole.at[(y + dy) % 4, (z + dz) % 2, (c + dc) % 2], part
        )

    def passer(dz):
        def landed(dy):
            ref = place(dz)(dy, None)
            passed.append((links.send(ref, ref, dc=1), place(dz, 1)(dy, None)))

        return landed

    links.local(own, place(0)(0, None))
    across = links.send(own, place(0)(0, None), dz=1)
    near = ring_four(links, own, place(0), "dy", passer(0))
    next(near)
    passed.append((links.send(own, place(0)(0, None), dc=1), place(0, 1)(0, None)))
    yield
    links.arrived(across, place(1)(0, None))
    far = ring_four(links, place(1)(0, None), place(1), "dy", passer(1))
    next(far)
    passer(1)(0)
    for unused in near:
        yield
    for unused in far:
        yield
    for ticket, ref in passed:
        links.arrived(ticket, ref)


def add_up(target, sources, rows, finish):
    chunk = 16

    def step(i, unused):
        here = pl.ds(pl.multiple_of(i * chunk, chunk), chunk)
        total = sources[0][here, :].astype(F32)
        for source in sources[1:]:
            total = total + source[here, :].astype(F32)
        target[here, :] = finish(total, here).astype(target.dtype)
        return unused

    lax.fori_loop(0, rows // chunk, step, 0)


def plain(total, here):
    return total


def reduce_heads(links, grads, dq, dq_home, grads_home, mine, near, far, total):
    y, z, c, unused_l, unused_x = coords()
    order = (1, 3, 2, 0)
    held, from_core = {}, {}
    for dz in (1, 0):
        for d in order:
            place = ((y + d) % 4, (z + dz) % 2)
            from_core[d, dz] = links.send(
                grads.at[place[0], place[1], 1 - c], near.at[place[0], place[1]], dc=1
            )
            held[d, dz] = links.local(
                grads.at[place[0], place[1], c], mine.at[place[0], place[1]]
            )
    asked = [links.send(dq.at[(y + d) % 4], dq_home.at[y], dy=d) for d in order[:3]]
    links.local(dq.at[y], dq_home.at[y])
    yield
    rows = mine.shape[2]
    across = {}
    for d in order:
        here = (y + d) % 4
        links.arrived(from_core[d, 1], near.at[here, 1 - z])
        links.settle(held[d, 1])
        add_up(
            mine.at[here, 1 - z], [mine.at[here, 1 - z], near.at[here, 1 - z]], rows, plain
        )
        across[d] = links.send(mine.at[here, 1 - z], far.at[here], dz=1)
        yield
    home = {}
    for d in order:
        here = (y + d) % 4
        links.arrived(from_core[d, 0], near.at[here, z])
        links.settle(held[d, 0])
        links.arrived(across[d], far.at[here])
        add_up(
            total.at[here], [mine.at[here, z], near.at[here, z], far.at[here]], rows, plain
        )
        if d:
            home[d] = links.send(total.at[here], grads_home.at[y], dy=d)
        else:
            links.local(total.at[here], grads_home.at[y])
        yield
    for i, d in enumerate(order[:3]):
        links.arrived(asked[i], dq_home.at[(y - d) % 4])
        links.arrived(home[d], grads_home.at[(y - d) % 4])


class ScatterSpace:
    names = ("pieces", "near", "out", "far", "across", "sums", "side")

    def __init__(self, refs):
        for name, ref in zip(self.names, refs):
            setattr(self, name, ref)

    @staticmethod
    def shapes(rows, depth):
        half = depth // 2
        sizes = (
            (2, 4, rows, depth),
            (3, 2, rows, half),
            (rows, half),
            (rows, half),
            (4, rows, half),
            (4, rows, half),
            (3, rows, half),
        )
        return [pltpu.VMEM(size, BF) for size in sizes]


def scatter_br(links, make, space, target, finish):
    unused_y, unused_z, unused_c, l, x = coords()
    rows, half = space.out.shape
    first, second = pl.ds(0, half), pl.ds(half, half)
    order = (1, 3, 2, 0)
    direct, folded, onward = {}, {}, {}
    for i, d in enumerate(order):
        there = (x + d) % 4
        make(there)
        if d:
            for dl in (1, 0):
                to = (l + dl) % 2
                direct[dl, i] = links.send(
                    space.pieces.at[to, there, :, first], space.near.at[i, to], dx=d
                )
        folded[d] = links.send(
            space.pieces.at[1 - l, there, :, second], space.across.at[there], dl=1
        )
        yield
    for i in range(3):
        links.arrived(direct[1, i], space.near.at[i, 1 - l])
        yield
    mine = space.pieces.at[1 - l, x, :, first]
    add_up(space.out, [mine] + [space.near.at[i, 1 - l] for i in range(3)], rows, plain)
    over = links.send(space.out, space.far, dl=1)
    for i, d in enumerate(order):
        there = (x + d) % 4
        links.arrived(folded[d], space.across.at[there])
        own = space.pieces.at[l, there, :, second]
        add_up(space.sums.at[there], [own, space.across.at[there]], rows, plain)
        if d:
            onward[i] = links.send(space.sums.at[there], space.side.at[i], dx=d)
        yield
    for i in range(3):
        links.arrived(direct[0, i], space.near.at[i, l])
    yield
    links.arrived(over, space.far)
    sources = [space.pieces.at[l, x, :, first]] + [space.near.at[i, l] for i in range(3)]
    add_up(target.at[:, first], sources + [space.far], rows, finish(0))
    yield
    for i in range(3):
        links.arrived(onward[i], space.side.at[i])
    sources = [space.sums.at[x]] + [space.side.at[i] for i in range(3)]
    add_up(target.at[:, second], sources, rows, finish(half))


def reduce_tok(links, make, parts, near, side, out, far, target):
    y, z, c, unused_l, unused_x = coords()
    order = (1, 3, 2, 0)
    tickets = {}
    for d in order:
        here = (y + d) % 4
        make(here)
        tickets[d] = links.send(parts.at[here, :, 1 - c], near.at[here], dc=1)
        yield
    rows = out.shape[0]
    sent = {}
    for i, d in enumerate(order):
        here = (y + d) % 4
        links.arrived(tickets[d], near.at[here])
        for k in range(2):
            own = parts.at[here, k, c]
            add_up(own, [own, near.at[here, k]], rows, plain)
        if d:
            sent[i] = links.send(parts.at[here, :, c], side.at[i], dy=d)
        yield
    for i in range(3):
        links.arrived(sent[i], side.at[i])
        yield
    add_up(out, [parts.at[y, 1 - z, c]] + [side.at[i, 1 - z] for i in range(3)], rows, plain)
    across = links.send(out, far, dz=1)
    yield
    links.arrived(across, far)
    add_up(target, [parts.at[y, z, c]] + [side.at[i, z] for i in range(3)] + [far], rows, plain)


BR_NEAR = [dict(dl=1), dict(dx=1), dict(dx=-1)]
BR_ALL = BR_NEAR + [dict(dx=2)]
TOK_NEAR = [dict(dz=1), dict(dc=1), dict(dy=1), dict(dy=-1)]
TOK_ALL = TOK_NEAR + [dict(dy=2)]


def comm_call(kernel, name, number, args, outs, scratch=(), in_vmem=(), out_vmem=(), copies=48):
    return pl.pallas_call(
        kernel,
        out_shape=tuple(outs),
        in_specs=[VMEM if i in in_vmem else ANY for i in range(len(args))],
        out_specs=tuple(VMEM if i in out_vmem else ANY for i in range(len(outs))),
        scratch_shapes=list(scratch)
        + [
            pltpu.SemaphoreType.DMA((copies,)),
            pltpu.SemaphoreType.DMA((copies,)),
            pltpu.SemaphoreType.DMA((16,)),
        ],
        compiler_params=pltpu.CompilerParams(
            collective_id=number, has_side_effects=True, vmem_limit_bytes=60 * 2**20
        ),
        cost_estimate=SMALL,
        name=name,
    )(*args)


def start_kernel(s_ref, c_ref, w_ref, f_ref, x_out, g_out, w_out, f_out, *sems):
    links = Links(*sems)
    links.greet(BR_NEAR + TOK_NEAR)
    in_turn(
        [
            gather_br(links, s_ref, x_out),
            gather_tok(links, w_ref, w_out),
            gather_tok(links, f_ref, f_out),
            gather_br(links, c_ref, g_out),
        ]
    )
    links.close()


def start(shifted, cot, weights, ff):
    rows, depth = shifted.shape
    wrows = weights.shape[0]
    whole = jax.ShapeDtypeStruct((2, 4, rows, depth), BF)
    return comm_call(
        start_kernel,
        "start",
        0,
        (shifted, cot, weights, ff),
        (
            whole,
            whole,
            jax.ShapeDtypeStruct((4, 2, 2, wrows, weights.shape[1]), BF),
            jax.ShapeDtypeStruct((4, 2, 2, wrows, ff.shape[1]), BF),
        ),
        copies=64,
    )


def ff_heads_kernel(
    main,
    down,
    first,
    x_ref,
    g_ref,
    x_strip,
    g_strip,
    w_ref,
    joined,
    h_ref,
    s_ref,
    grad_ref,
    asked,
    pairs,
    held,
    held_hidden,
    *sems,
):
    y, z, c, unused_l, unused_x = coords()
    step = pl.program_id(0)
    links = Links(*sems)
    order = (1, 3, 2)
    front, back = pl.ds(0, 2), pl.ds(2, 2)

    def pair(dy, dz=0, dc=0):
        return pairs.at[(y + dy) % 4, (z + dz) % 2, (c + dc) % 2]

    kept = [
        pltpu.make_async_copy(joined.at[y, front], asked.at[y], sems[2].at[0]),
        pltpu.make_async_copy(joined.at[y, back], pair(0), sems[2].at[1]),
    ]
    number = iter(range(64))

    def plan(source, target, lands, **offsets):
        n = next(number)
        return links.copy(n, source, target, offsets), links.copy(n, lands, lands, offsets)

    keys = [
        plan(joined.at[(y + d) % 4, back], pair(0), pair(-d), dy=d) for d in order
    ]
    rest = [
        plan(joined.at[(y + d) % 4, front], asked.at[y], asked.at[(y - d) % 4], dy=d)
        for d in order
    ]
    mine = joined.at[y, back]
    far = [plan(mine, pair(0), pair(0, 1), dz=1)]
    near = [plan(mine, pair(0), pair(0, 0, 1), dc=1)]
    for d in order:
        far.append(plan(pair(-d), pair(-d), pair(-d, 1), dz=1))
        near.append(plan(pair(-d), pair(-d), pair(-d, 0, 1), dc=1))
    diagonal = [plan(pair(-d, 1), pair(-d, 1), pair(-d, 1, 1), dc=1) for d in (0,) + order]

    def relay(i):
        keys[i][1].wait_recv()
        far[i + 1][0].start()
        near[i + 1][0].start()

    def cross(i):
        far[i][1].wait_recv()
        diagonal[i][0].start()

    @pl.when(step == 0)
    def _():
        links.greet(TOK_ALL)
        for copy in kept:
            copy.start()
        for copy, unused in [keys[0], keys[1], keys[2], far[0], near[0]]:
            copy.start()

    def pause(point):
        @pl.when(step == 0)
        def _():
            if point == 0:
                relay(0)
                relay(1)
            else:
                relay(2)
                for copy, unused in rest:
                    copy.start()

        @pl.when(step == 1)
        def _():
            if point == 0:
                cross(0)
            else:
                cross(1)

    for i in range(2, 4):

        @pl.when(step == i + 1)
        def _():
            cross(i)

    rows = x_ref.shape[1]

    @pl.when(step < 2)
    def _():
        grads, hidden = ff_part(
            main, down, first, x_ref[...], g_ref[...], w_ref, h_ref, s_ref, pause
        )
        here = pl.ds(pl.multiple_of(step * rows, rows), rows)
        held[:, here, :] = grads.reshape(2, rows, -1)
        held_hidden[:, here, :] = hidden.reshape(2, rows, -1)

    @pl.when(step >= 2)
    def _():
        grads = held[...].reshape(-1, held.shape[2])
        hidden = held_hidden[...].reshape(-1, down)
        grad_ref[:, :down] = dot(g_strip[...], hidden, TN).astype(BF)
        grad_ref[:, down:] = dot(x_strip[...], grads, TN).astype(BF)

    @pl.when(step == pl.num_programs(0) - 1)
    def _():
        for copy in kept:
            copy.wait()
        for unused, landed in rest + near + diagonal:
            landed.wait_recv()
        for copy, unused in keys + rest + far + near + diagonal:
            copy.wait_send()


def ff_heads(x, g, w, joined, main, down, first):
    depth, cols = w.shape
    heads, unused, span, lanes = joined.shape
    rows = BLK // 2
    both = cols - first
    strip = 512

    def tile(width):
        return pl.BlockSpec((2, rows, width), lambda i: (0, jnp.minimum(i, 1), 0))

    return pl.pallas_call(
        functools.partial(ff_heads_kernel, main, down, first),
        grid=(2 + depth // strip,),
        in_specs=[
            tile(depth),
            tile(depth),
            pl.BlockSpec((2 * BLK, strip), lambda i: (0, jnp.maximum(i - 2, 0))),
            pl.BlockSpec((2 * BLK, strip), lambda i: (0, jnp.maximum(i - 2, 0))),
            pl.BlockSpec((depth, cols), lambda i: (0, 0), pipeline_mode=pl.Buffered(1)),
            ANY,
        ],
        out_specs=(
            tile(down),
            tile(depth),
            pl.BlockSpec((strip, both + down), lambda i: (jnp.maximum(i - 2, 0), 0)),
            ANY,
            ANY,
        ),
        out_shape=(
            jax.ShapeDtypeStruct((2, BLK, down), BF),
            jax.ShapeDtypeStruct((2, BLK, depth), BF),
            jax.ShapeDtypeStruct((depth, both + down), BF),
            jax.ShapeDtypeStruct((4, 2, span, lanes), BF),
            jax.ShapeDtypeStruct((4, 2, 2, 2, span, lanes), BF),
        ),
        scratch_shapes=[
            pltpu.VMEM((2, BLK, both), BF),
            pltpu.VMEM((2, BLK, down), BF),
            pltpu.SemaphoreType.DMA((32,)),
            pltpu.SemaphoreType.DMA((32,)),
            pltpu.SemaphoreType.DMA((2,)),
        ],
        compiler_params=pltpu.CompilerParams(
            collective_id=1, has_side_effects=True, vmem_limit_bytes=60 * 2**20
        ),
        cost_estimate=SMALL,
        name="ff_heads",
    )(x, g, x.reshape(2 * BLK, depth), g.reshape(2 * BLK, depth), w, joined)


def home_kernel(
    heads,
    grads,
    dq,
    o_parts,
    hidden,
    weights,
    tokens,
    dq_home,
    grads_home,
    mixed_out,
    result,
    *rest,
):
    mine, near, far, total, held_w, held_h, held_o = rest[:7]
    space = ScatterSpace(rest[7:14])
    links = Links(*rest[14:])
    y, unused_z, unused_c, unused_l, unused_x = coords()
    rows, depth = tokens.shape
    kept = held_w.shape[1]
    links.greet(BR_ALL + TOK_ALL)
    loads = [
        links.local(o_parts.at[y], held_o.at[y]),
        links.local(hidden, held_h),
        links.local(weights.at[:, pl.ds(0, kept)], held_w),
    ]
    returned = [
        (d, links.send(o_parts.at[(y + d) % 4], held_o.at[y], dy=d)) for d in (1, 3, 2)
    ]

    def make(there):
        here = pl.ds(pl.multiple_of(there * rows, rows), rows)
        mixed = [
            jnp.concatenate(
                [held_o[head, here, slot * HD : (slot + 1) * HD] for head in range(heads)],
                axis=1,
            )
            for slot in range(2)
        ]
        for slot in range(2):
            mixed_out[slot, here, :] = mixed[slot]
        both = jnp.concatenate(
            [held_h[:, here, :].reshape(2 * rows, -1), jnp.concatenate(mixed, axis=0)], axis=1
        )
        branches = dot(both, held_w[...], NT).astype(BF)
        for slot in range(2):
            space.pieces[slot, there] = branches[slot * rows : (slot + 1) * rows]

    def finish(column):
        def add(value, here):
            return value + tokens[here, column : column + value.shape[1]].astype(F32)

        return add

    def output():
        yield
        for d, ticket in returned:
            links.arrived(ticket, held_o.at[(y - d) % 4])
        for load in loads:
            links.settle(load)
        yield from scatter_br(links, make, space, result, finish)

    in_turn(
        [
            reduce_heads(links, grads, dq, dq_home, grads_home, mine, near, far, total),
            output(),
        ]
    )
    links.close()


def heads_home(grads, dq, o_parts, hidden, weights, tokens, heads):
    rows, depth = tokens.shape
    span, lanes = grads.shape[3:]
    width = heads * HD
    kept = hidden.shape[2] + width
    return comm_call(
        functools.partial(home_kernel, heads),
        "heads_home",
        2,
        (grads, dq, o_parts, hidden, weights, tokens),
        (
            jax.ShapeDtypeStruct(dq.shape, BF),
            jax.ShapeDtypeStruct((4, span, lanes), BF),
            jax.ShapeDtypeStruct((2, BLK, width), BF),
            jax.ShapeDtypeStruct((rows, depth), BF),
        ),
        scratch=[
            pltpu.VMEM((4, 2, span, lanes), BF),
            pltpu.VMEM((4, 2, span, lanes), BF),
            pltpu.VMEM((4, span, lanes), BF),
            pltpu.VMEM((4, span, lanes), BF),
            pltpu.VMEM((depth, kept), BF),
            pltpu.VMEM(hidden.shape, BF),
            pltpu.VMEM(o_parts.shape, BF),
        ]
        + ScatterSpace.shapes(rows, depth),
        in_vmem=(5,),
        out_vmem=(2, 3),
        copies=64,
    )


def normal_rows(tokens, normed, scales):
    rows = tokens.shape[0]
    chunk = 16

    def step(i, unused):
        here = pl.ds(pl.multiple_of(i * chunk, chunk), chunk)
        value = tokens[here, :].astype(F32)
        value = value - jnp.mean(value, axis=-1, keepdims=True)
        scale = lax.rsqrt(jnp.mean(value * value, axis=-1, keepdims=True) + EPSILON)
        normed[here, :] = value * scale
        scales[here, :] = jnp.broadcast_to(scale, (chunk, 128))
        return unused

    lax.fori_loop(0, rows // chunk, step, 0)


def turn_back(grads, normed, scales, cot, gain, parts, result):
    rows, depth = normed.shape
    chunk = 16

    def rows_at(i):
        return pl.ds(pl.multiple_of(i * chunk, chunk), chunk)

    def sums(i, carry):
        here = rows_at(i)
        grad = grads[here, :]
        up = (grad * normed[here, :]).reshape(2, 8, depth)
        return carry[0] + up.sum(0), carry[1] + grad.reshape(2, 8, depth).sum(0)

    zero = jnp.zeros((8, depth), F32)
    found = lax.fori_loop(0, rows // chunk, sums, (zero, zero))
    for k in range(2):
        line = jnp.sum(found[k], axis=0, keepdims=True)
        parts[16 * k : 16 * (k + 1), :] = jnp.concatenate(
            [line[:, t * 128 : (t + 1) * 128] for t in range(depth // 128)], axis=0
        )
    yield

    def back(i, unused):
        here = rows_at(i)
        line = normed[here, :]
        grad = grads[here, :] * gain[...]
        slope = jnp.mean(grad * line, axis=-1, keepdims=True)
        grad = grad - jnp.mean(grad, axis=-1, keepdims=True) - line * slope
        result[here, :] = cot[here, :].astype(F32) + scales[here, :1] * grad
        return unused

    lax.fori_loop(0, rows // chunk, back, 0)


BR_PEERS = [dict(dl=i // 4, dx=i % 4) for i in range(1, 8)]
TOK_PEERS = [dict(dy=i // 4, dz=(i // 2) % 2, dc=i % 2) for i in range(1, 16)]


def last_kernel(
    heads,
    dq,
    dkv,
    table,
    x_in,
    g_in,
    m_in,
    w_in,
    s_in,
    tokens,
    cot,
    gain,
    result,
    qkv_out,
    out_out,
    bias_out,
    sides,
    *rest,
):
    held_q, held_kv, held_t, held_x, held_g, held_m, held_w, held_s, gj = rest[:9]
    parts, near, side, out, far, wsum, summed, normed, scales = rest[9:18]
    lines, lines_in, last, last_in = rest[18:22]
    space = ScatterSpace(rest[22:29])
    links = Links(*rest[29:])
    y, z, c, l, x = coords()
    links.greet(BR_PEERS + TOK_PEERS)
    width = heads * HD
    rows, depth = tokens.shape
    first = [
        links.local(dq, held_q),
        links.local(dkv, held_kv),
        links.local(table, held_t),
    ]
    second = [
        links.local(x_in, held_x),
        links.local(g_in, held_g),
        links.local(m_in, held_m),
    ]
    third = [links.local(w_in.at[:, pl.ds(0, 3 * width)], held_w), links.local(s_in, held_s)]
    for load in first:
        links.settle(load)
    total = jnp.zeros((1, 3 * width), F32)
    for slot in range(2):
        for half in range(2):
            here = slice(half * BLK // 2, (half + 1) * BLK // 2)
            lanes = slice(slot * HD, (slot + 1) * HD)
            turns = held_t[slot, here, :]
            q = jnp.concatenate([held_q[h, here, lanes] for h in range(heads)], axis=1)
            q = turn(q.astype(F32), turns, heads // 2, False, -1.0).astype(BF)
            kv = jnp.concatenate([held_kv[h, slot, here] for h in range(heads)], axis=1)
            kv = turn(kv.astype(F32), turns, heads, True, -1.0).astype(BF)
            both = jnp.concatenate([q, kv], axis=1)
            gj[slot, here, :] = both
            total += jnp.sum(both.astype(F32), axis=0, keepdims=True)
    corner = [total[:, r * 128 : (r + 1) * 128] for r in range(3 * width // 128)]
    corner = jnp.concatenate(corner + [jnp.zeros((122, 128), F32)], axis=0).astype(BF)
    for load in second:
        links.settle(load)
    wrows = parts.shape[3]
    strip = 4 * wrows

    def weights_of(there):
        here = pl.ds(pl.multiple_of(there * strip, strip), strip)
        qkv = dot(held_x[:, here], gj[...].reshape(2 * BLK, 3 * width), TN).astype(BF)
        outs = dot(held_g[:, here], held_m[...], TN).astype(BF)
        for k in range(4):
            at = slice(k * wrows, (k + 1) * wrows)
            parts[there, k // 2, k % 2, :, : 3 * width] = qkv[at]
            parts[there, k // 2, k % 2, :, 3 * width : 4 * width] = outs[at]
            parts[there, k // 2, k % 2, :, 4 * width :] = corner

    def rows_of(there):
        if third:
            for load in third:
                links.settle(load)
            third.clear()
        here = pl.ds(pl.multiple_of(there * rows, rows), rows)
        both = gj[:, here, :].reshape(2 * rows, 3 * width)
        grads = dot(both, held_w[...], NT)
        for slot in range(2):
            value = grads[slot * rows : (slot + 1) * rows] + held_s[slot, here, :].astype(F32)
            space.pieces[slot, there] = value.astype(BF)

    def aside():
        for unused in range(5):
            yield
        normal_rows(tokens, normed, scales)

    in_turn(
        [
            reduce_tok(links, weights_of, parts, near, side, out, far, wsum),
            scatter_br(links, rows_of, space, summed, lambda column: plain),
            aside(),
        ]
    )
    through = turn_back(summed, normed, scales, cot, gain, lines, result)
    next(through)
    tickets = [links.send(lines, lines_in.at[i], **o) for i, o in enumerate(BR_PEERS)]
    for unused in through:
        pass
    total = lines[...]
    for i, ticket in enumerate(tickets):
        links.arrived(ticket, lines_in.at[i])
        total = total + lines_in[i]
    last[...] = jnp.zeros_like(last)
    for t in range(16):
        last[t, 0:2, :] = jnp.concatenate([total[t : t + 1], total[16 + t : 17 + t]], axis=0)
    tickets = []
    for i, o in enumerate(TOK_PEERS):
        there = ((y + o["dy"]) % 4) * 4 + ((z + o["dz"]) % 2) * 2 + (c + o["dc"]) % 2
        tickets.append(links.send(last.at[there], last_in.at[i], **o))
    qkv_out[0] = wsum[:, :width]
    for k in range(2):
        qkv_out[1 + k] = jnp.concatenate(
            [
                wsum[:, width + (2 * h + k) * HD : width + (2 * h + k + 1) * HD]
                for h in range(heads)
            ],
            axis=1,
        )
    out_out[...] = jnp.transpose(wsum[:, 3 * width : 4 * width])
    bias_out[...] = wsum[:8, 4 * width :]
    total = last[y * 4 + z * 2 + c]
    for i, ticket in enumerate(tickets):
        links.arrived(ticket, last_in.at[i])
        total = total + last_in[i]
    sides[...] = total
    links.close()


def last_sums(dq, dkv, table, x, g, mixed, w, partial_grad, tokens, cot, gain, heads):
    rows, depth = tokens.shape
    wrows = depth // 16
    width = heads * HD
    cols = 4 * width + 128
    return comm_call(
        functools.partial(last_kernel, heads),
        "last_sums",
        3,
        (dq, dkv, table, x, g, mixed, w, partial_grad, tokens, cot, gain),
        (
            jax.ShapeDtypeStruct((rows, depth), F32),
            jax.ShapeDtypeStruct((3, wrows, width), F32),
            jax.ShapeDtypeStruct((width, wrows), F32),
            jax.ShapeDtypeStruct((8, 128), F32),
            jax.ShapeDtypeStruct((8, 128), F32),
        ),
        scratch=[
            pltpu.VMEM(dq.shape, BF),
            pltpu.VMEM(dkv.shape, BF),
            pltpu.VMEM(table.shape, F32),
            pltpu.VMEM(x.shape, BF),
            pltpu.VMEM(g.shape, BF),
            pltpu.VMEM(mixed.shape, BF),
            pltpu.VMEM((depth, 3 * width), BF),
            pltpu.VMEM(partial_grad.shape, BF),
            pltpu.VMEM((2, BLK, 3 * width), BF),
            pltpu.VMEM((4, 2, 2, wrows, cols), BF),
            pltpu.VMEM((4, 2, wrows, cols), BF),
            pltpu.VMEM((3, 2, wrows, cols), BF),
            pltpu.VMEM((wrows, cols), BF),
            pltpu.VMEM((wrows, cols), BF),
            pltpu.VMEM((wrows, cols), F32),
            pltpu.VMEM((rows, depth), F32),
            pltpu.VMEM((rows, depth), F32),
            pltpu.VMEM((rows, 128), F32),
            pltpu.VMEM((32, 128), F32),
            pltpu.VMEM((7, 32, 128), F32),
            pltpu.VMEM((16, 8, 128), F32),
            pltpu.VMEM((15, 8, 128), F32),
        ]
        + ScatterSpace.shapes(rows, depth),
        in_vmem=(8, 9, 10),
        out_vmem=(0, 1, 2, 3, 4),
        copies=80,
    )


def rotary_table():
    half = ROT // 2
    frequency = (ROPE_BASE ** (-(np.arange(half) * 2.0 / ROT))).astype(np.float32)
    angles = np.arange(LB * BLK, dtype=np.float32)[:, None] * frequency[None, :]
    cos, sin = np.cos(angles), np.sin(angles)
    one = np.ones((LB * BLK, HD - ROT), np.float32)
    table = np.concatenate([cos, cos, one, -sin, sin, 0.0 * one], axis=1)
    return table.astype(np.float32).reshape(LB, BLK, 2 * HD)


def body(
    tokens,
    norm_gain,
    norm_bias,
    qkv_weight,
    qkv_bias,
    out_weight,
    gate_weight,
    up_weight,
    down_weight,
    cotangent,
    block_map,
    lengths,
):
    tok = lax.axis_index("tok")
    y, z, c = tok // 4, (tok // 2) % 2, tok % 2
    total_blocks = block_map.shape[0]
    long_blocks = total_blocks // 2
    rows = tokens.shape[0]
    depth = tokens.shape[1]
    wrows = qkv_weight.shape[1]
    heads = qkv_bias.shape[1]
    width = heads * HD
    hidden_width = gate_weight.shape[1]
    main = hidden_width // 128 * 128
    tail = hidden_width - main

    residual = tokens.astype(F32)
    centred = residual - jnp.mean(residual, axis=-1, keepdims=True)
    inverse = lax.rsqrt(jnp.mean(centred * centred, axis=-1, keepdims=True) + EPSILON)
    normed = centred * inverse
    shifted = (normed * norm_gain + norm_bias).astype(BF)

    kv_shard = jnp.stack(
        [w.reshape(wrows, heads, HD) for w in (qkv_weight[1], qkv_weight[2])], axis=2
    ).reshape(wrows, 2 * width)
    per = qkv_bias.shape[2]
    lane_tok = jnp.arange(HD, dtype=jnp.int32) // per
    bias_lanes = jnp.where(lane_tok == tok, jnp.tile(qkv_bias, (1, 1, HD // per)), 0)
    bias_rows = jnp.concatenate(
        [
            bias_lanes[0].reshape(-1),
            jnp.stack([bias_lanes[1], bias_lanes[2]], axis=1).reshape(-1),
        ]
    ).reshape(-1, 128)
    bias_row = jnp.pad(bias_rows, ((0, wrows - bias_rows.shape[0]), (0, 0)))
    qkv_shard = jnp.concatenate([qkv_weight[0], kv_shard, bias_row], axis=1)
    ff_shard = jnp.concatenate(
        [
            jnp.transpose(down_weight),
            jnp.zeros((wrows, 128 - tail), BF),
            jnp.transpose(out_weight),
            gate_weight[:, :main],
            up_weight[:, :main],
            gate_weight[:, main:],
            up_weight[:, main:],
        ],
        axis=1,
    )
    down_width = main + 128
    first = down_width + width
    x, grad, qkv_full, ff_full = start(shifted, cotangent, qkv_shard, ff_shard)
    x = x.reshape(2, BLK, depth)
    grad = grad.reshape(2, BLK, depth)
    qkv_full = qkv_full.reshape(16 * wrows, -1)
    ff_full = ff_full.reshape(16 * wrows, -1)

    slot_table = jnp.arange(total_blocks, dtype=jnp.int32)
    slot_of = jnp.sum(
        jnp.where(block_map[None, :] == slot_table[:, None], slot_table[None, :], 0), axis=1
    )
    key_slot = slot_of.astype(jnp.int32)
    from_tok = jnp.arange(4, dtype=jnp.int32) * 4 + z * 2 + c
    my_queries = jnp.stack([2 * from_tok, 2 * from_tok + 1], axis=1).reshape(-1)
    query_block = jnp.sum(
        jnp.where(my_queries[:, None] == slot_table[None, :], block_map[None, :], 0), axis=1
    ).astype(jnp.int32)
    query_row = jnp.where(
        query_block < long_blocks,
        query_block // LB,
        long_blocks // LB + (query_block - long_blocks) // 2,
    )
    row_table = jnp.arange(lengths.shape[0], dtype=jnp.int32)
    query_limit = jnp.sum(
        jnp.where(query_row[:, None] == row_table[None, :], lengths[None, :], 0), axis=1
    ).astype(jnp.int32)

    my_blocks = lax.dynamic_slice_in_dim(block_map, tok * 2, 2)
    places = jnp.where(my_blocks < long_blocks, my_blocks % LB, (my_blocks - long_blocks) % 2)
    table = jnp.asarray(rotary_table())

    joined = project(places, x, grad, qkv_full, ff_full, table, heads)
    hidden, grad_x, grad_ff, qd_all, kv_all = ff_heads(
        x, grad, ff_full, joined, main, down_width, first
    )
    kv_all = kv_all.reshape(-1, 2 * HD)
    x = x.reshape(2 * BLK, depth)
    grad = grad.reshape(2 * BLK, depth)
    grad_ff = lax.psum_scatter(grad_ff, "tok", scatter_dimension=0, tiled=True)

    turned, lse, o_parts = attn_fwd(query_block, query_limit, key_slot, qd_all, kv_all, long_blocks)
    dq_parts, dkv_all = attn_bwd(
        query_block, query_limit, key_slot, qd_all, kv_all, turned, lse, long_blocks
    )
    dq_heads, dkv_heads, mixed, result = heads_home(
        dkv_all.reshape(4, 2, 2, 2 * BLK, 2 * HD), dq_parts, o_parts, hidden, ff_full, tokens, heads
    )
    grad_ff, dq_heads = lax.optimization_barrier((grad_ff, dq_heads))
    turns = jnp.stack([lax.dynamic_index_in_dim(table, places[i], 0, False) for i in range(2)])
    grad_tokens, grad_qkv, grad_out_out, bias_sums, sides = last_sums(
        dq_heads,
        dkv_heads.reshape(heads, 2, BLK, 2 * HD),
        turns,
        x,
        grad,
        mixed.reshape(2 * BLK, width),
        qkv_full,
        grad_x,
        tokens,
        cotangent,
        norm_gain.reshape(1, depth),
        heads,
    )
    bias_sums = bias_sums[: 3 * width // 128].reshape(-1)
    bias_sums = jnp.concatenate(
        [
            bias_sums[:width].reshape(1, heads, HD),
            jnp.transpose(bias_sums[width:].reshape(heads, 2, HD), (1, 0, 2)),
        ]
    )
    grad_bias_out = lax.dynamic_slice_in_dim(bias_sums, tok * per, per, 2)
    grad_ff = grad_ff.astype(F32)
    grad_down_out = jnp.transpose(grad_ff[:, :hidden_width])
    grad_gu = grad_ff[:, down_width:]
    ends = grad_gu[:, 2 * main :]
    grad_gate_out = jnp.concatenate([grad_gu[:, :main], ends[:, :tail]], axis=1)
    grad_up_out = jnp.concatenate([grad_gu[:, main : 2 * main], ends[:, tail:]], axis=1)

    sides = lax.dynamic_slice_in_dim(sides[:2], lax.axis_index("br") * 16, 16, 1)
    return (
        result,
        grad_tokens,
        sides[0],
        sides[1],
        grad_qkv,
        grad_bias_out,
        grad_out_out,
        grad_gate_out,
        grad_up_out,
        grad_down_out,
    )


def solution(mesh):
    in_specs = (
        P(("tok", "br"), None),
        P(),
        P(),
        P(None, "tok", "br"),
        P(None, "br", "tok"),
        P("br", "tok"),
        P("tok", "br"),
        P("tok", "br"),
        P("br", "tok"),
        P(("tok", "br"), None),
        P(),
        P(),
    )
    out_specs = (
        P(("tok", "br"), None),
        P(("tok", "br"), None),
        P(("tok", "br")),
        P(("tok", "br")),
        P(None, "tok", "br"),
        P(None, "br", "tok"),
        P("br", "tok"),
        P("tok", "br"),
        P("tok", "br"),
        P("br", "tok"),
    )
    return jax.shard_map(body, mesh=mesh, in_specs=in_specs, out_specs=out_specs, check_vma=False)
```

```python
import functools

import jax
import jax.numpy as jnp
import numpy as np
from jax import lax
from jax.experimental import pallas as pl
from jax.experimental.pallas import tpu as pltpu
from jax.sharding import PartitionSpec as P

HD = 64
ROT = 16
BLK = 512
LB = 8
EPSILON = 1e-05
ROPE_BASE = 10000.0
MASKED = -1e30
BF = jnp.bfloat16
F32 = jnp.float32
NN = (((1,), (0,)), ((), ()))
NT = (((1,), (1,)), ((), ()))
TN = (((0,), (0,)), ((), ()))
VMEM = pl.BlockSpec(memory_space=pltpu.VMEM)
SMEM = pl.BlockSpec(memory_space=pltpu.SMEM)
ANY = pl.BlockSpec(memory_space=pl.ANY)
SMALL = pl.CostEstimate(flops=1000, bytes_accessed=1000, transcendentals=0)


def dot(left, right, dims):
    return lax.dot_general(left, right, dims, preferred_element_type=F32)


def block_info(block, long_blocks):
    is_long = block < long_blocks
    place = jnp.where(is_long, block % LB, (block - long_blocks) % 2)
    return is_long, place, block - place


def lane_half(packed, half, upper):
    piece = packed[:, half * HD : (half + 1) * HD]
    zero = jnp.zeros_like(piece)
    return jnp.concatenate([zero, piece] if upper else [piece, zero], axis=1)


def allowed_pairs(place, step, limit):
    key_pos = step * BLK + lax.broadcasted_iota(jnp.int32, (BLK, BLK), 0)
    query_pos = place * BLK + lax.broadcasted_iota(jnp.int32, (BLK, BLK), 1)
    return (key_pos <= query_pos) & (key_pos < limit)


def attn_fwd_kernel(long_blocks, qblk, qlim, kslot, q_ref, kv_ref, ot_ref, lse_ref, o_ref):
    def pack(i, unused):
        packed = q_ref[i, 0]
        for half in range(2):
            slot = 2 * i + half
            is_long, place, first = block_info(qblk[slot], long_blocks)
            limit = qlim[slot]
            queries = lane_half(packed, half, False) * jnp.asarray(0.125, BF)

            def step(j, carry, masked):
                top, total, acc = carry
                rows = pl.ds(pl.multiple_of(kslot[first + j] * BLK, BLK), BLK)
                kv = kv_ref[rows, :]
                scores = dot(kv, queries, NT)
                if masked:
                    scores = jnp.where(allowed_pairs(place, j, limit), scores, MASKED)
                new_top = jnp.maximum(top, jnp.max(scores, axis=0, keepdims=True))
                fade = jnp.exp(top - new_top)
                probs = jnp.exp(scores - new_top)
                total = total * fade + jnp.sum(probs, axis=0, keepdims=True)
                acc = acc * fade + dot(kv, probs.astype(BF), TN)
                return new_top, total, acc

            free = jnp.where(is_long, place, 0)
            carry = (
                jnp.full((1, BLK), MASKED, F32),
                jnp.zeros((1, BLK), F32),
                jnp.zeros((2 * HD, BLK), F32),
            )
            carry = lax.fori_loop(0, free, lambda j, c: step(j, c, False), carry)
            top, total, acc = lax.fori_loop(free, place + 1, lambda j, c: step(j, c, True), carry)
            lse_ref[slot] = top + jnp.log(total)
            ot_ref[i, half * HD : (half + 1) * HD, :] = acc[HD:, :] / total
        o_ref[i] = jnp.transpose(ot_ref[i]).astype(BF)
        return unused

    lax.fori_loop(0, q_ref.shape[0], pack, 0)


def attn_fwd(qblk, qlim, kslot, q, kv, long_blocks):
    n = q.shape[0]
    return pl.pallas_call(
        functools.partial(attn_fwd_kernel, long_blocks),
        out_shape=(
            jax.ShapeDtypeStruct((n, 2 * HD, BLK), F32),
            jax.ShapeDtypeStruct((2 * n, 1, BLK), F32),
            jax.ShapeDtypeStruct((n, BLK, 2 * HD), BF),
        ),
        in_specs=[SMEM, SMEM, SMEM, VMEM, VMEM],
        out_specs=(VMEM, VMEM, VMEM),
        compiler_params=pltpu.CompilerParams(vmem_limit_bytes=60 * 2**20),
        cost_estimate=SMALL,
        name="attn_fwd",
    )(qblk, qlim, kslot, q, kv)


def attn_bwd_kernel(
    long_blocks, qblk, qlim, kslot, q_ref, kv_ref, ot_ref, lse_ref, dq_ref, dkv_ref, acc, dqt
):
    acc[...] = jnp.zeros_like(acc)

    def pack(i, unused):
        q_packed = q_ref[i, 0]
        d_packed = q_ref[i, 1]
        d_turned = jnp.transpose(d_packed.astype(F32))
        for half in range(2):
            slot = 2 * i + half
            is_long, place, first = block_info(qblk[slot], long_blocks)
            limit = qlim[slot]
            queries = lane_half(q_packed, half, False) * jnp.asarray(0.125, BF)
            grads = lane_half(d_packed, half, True)
            both = jnp.concatenate([queries, grads], axis=0)
            lanes = slice(half * HD, (half + 1) * HD)
            delta = jnp.sum(d_turned[lanes] * ot_ref[i, lanes, :], axis=0, keepdims=True)
            lse = lse_ref[slot]

            def step(j, total, masked):
                rows = pl.ds(pl.multiple_of(kslot[first + j] * BLK, BLK), BLK)
                kv = kv_ref[rows, :]
                scores = dot(kv, queries, NT)
                if masked:
                    scores = jnp.where(allowed_pairs(place, j, limit), scores, MASKED)
                probs = jnp.exp(scores - lse)
                ds = (probs * (dot(kv, grads, NT) - delta)).astype(BF)
                acc[rows, :] += dot(jnp.concatenate([ds, probs.astype(BF)], axis=1), both, NN)
                return total + dot(kv, ds, TN)

            free = jnp.where(is_long, place, 0)
            total = lax.fori_loop(
                0, free, lambda j, c: step(j, c, False), jnp.zeros((2 * HD, BLK), F32)
            )
            total = lax.fori_loop(free, place + 1, lambda j, c: step(j, c, True), total)
            dqt[lanes, :] = total[:HD, :] * 0.125
        dq_ref[i] = jnp.transpose(dqt[...]).astype(BF)
        return unused

    lax.fori_loop(0, q_ref.shape[0], pack, 0)

    def finish(i, unused):
        rows = pl.ds(pl.multiple_of(i * BLK, BLK), BLK)
        dkv_ref[rows, :] = acc[rows, :].astype(BF)
        return unused

    lax.fori_loop(0, kv_ref.shape[0] // BLK, finish, 0)


def attn_bwd(qblk, qlim, kslot, q, kv, ot, lse, long_blocks):
    n = q.shape[0]
    return pl.pallas_call(
        functools.partial(attn_bwd_kernel, long_blocks),
        out_shape=(
            jax.ShapeDtypeStruct((n, BLK, 2 * HD), BF),
            jax.ShapeDtypeStruct(kv.shape, BF),
        ),
        in_specs=[SMEM, SMEM, SMEM, VMEM, VMEM, VMEM, VMEM],
        out_specs=(VMEM, VMEM),
        scratch_shapes=[pltpu.VMEM(kv.shape, F32), pltpu.VMEM((2 * HD, BLK), F32)],
        compiler_params=pltpu.CompilerParams(vmem_limit_bytes=60 * 2**20),
        cost_estimate=SMALL,
        name="attn_bwd",
    )(qblk, qlim, kslot, q, kv, ot, lse)


def turn(values, table, copies, paired, sign):
    width = values.shape[1]
    lane = lax.broadcasted_iota(jnp.int32, values.shape, 1) % HD
    partner = jnp.where(
        lane < ROT // 2,
        pltpu.roll(values, width - ROT // 2, 1),
        pltpu.roll(values, ROT // 2, 1),
    )
    cos, sin = table[:, :HD], sign * table[:, HD:]
    cos = jnp.concatenate([cos, jnp.ones_like(cos) if paired else cos], axis=1)
    sin = jnp.concatenate([sin, jnp.zeros_like(sin) if paired else sin], axis=1)
    cos = jnp.concatenate([cos] * copies, axis=1)
    sin = jnp.concatenate([sin] * copies, axis=1)
    return values * cos + partner * sin


def ff_part(main, down, first, x, g, w_ref, h_ref, s_ref, mixed_grad, pause):
    rows, depth = x.shape[1:]
    x = x.reshape(2 * rows, depth)
    g = g.reshape(2 * rows, depth)
    gate_up = dot(x, w_ref[:, first:], NN)
    pause(0)
    gh = dot(g, w_ref[:, :first], NN)
    mixed_grad(gh[:, down:].astype(BF))
    gh = gh[:, :down]
    ends = gate_up[:, 2 * main :]
    gate = jnp.concatenate([gate_up[:, :main], ends], axis=1)
    up = jnp.concatenate([gate_up[:, main : 2 * main], pltpu.roll(ends, HD, 1)], axis=1)
    sig = jax.nn.sigmoid(gate)
    silu = gate * sig
    hidden = (silu * up).astype(BF)
    d_gate = gh * up * sig * (1.0 + gate * (1.0 - sig))
    d_up = gh * silu
    tail = d_gate[:, main:] + pltpu.roll(d_up[:, main:], HD, 1)
    grads = jnp.concatenate(
        [d_gate[:, :main].astype(BF), d_up[:, :main].astype(BF), tail.astype(BF)], axis=1
    )
    h_ref[...] = hidden.reshape(h_ref.shape)
    pause(1)
    s_ref[...] = dot(grads, w_ref[:, first:], NT).astype(BF).reshape(s_ref.shape)
    return grads, hidden


def coords():
    tok, br = lax.axis_index("tok"), lax.axis_index("br")
    return tok // 4, (tok // 2) % 2, tok % 2, br // 4, br % 4


def peer(dy=0, dz=0, dc=0, dl=0, dx=0):
    y, z, c, l, x = coords()
    tok = ((y + dy) % 4) * 4 + ((z + dz) % 2) * 2 + (c + dc) % 2
    return tok, ((l + dl) % 2) * 4 + (x + dx) % 4


class Links:
    def __init__(self, send_sems, recv_sems, local_sems):
        self.sems = (send_sems, recv_sems, local_sems)
        self.sent, self.locals = [], []

    def greet(self, partners):
        barrier = pltpu.get_barrier_semaphore()
        for offsets in partners:
            pl.semaphore_signal(
                barrier, inc=1, device_id=peer(**offsets), device_id_type=pl.DeviceIdType.MESH
            )
        pl.semaphore_wait(barrier, len(partners))

    def copy(self, number, source, target, offsets):
        return pltpu.make_async_remote_copy(
            src_ref=source,
            dst_ref=target,
            send_sem=self.sems[0].at[number],
            recv_sem=self.sems[1].at[number],
            device_id=peer(**offsets),
            device_id_type=pl.DeviceIdType.MESH,
        )

    def send(self, source, target, **offsets):
        copy = self.copy(len(self.sent), source, target, offsets)
        copy.start()
        self.sent.append(copy)
        return len(self.sent) - 1, offsets

    def arrived(self, ticket, place):
        self.copy(ticket[0], place, place, ticket[1]).wait_recv()

    def local(self, source, target):
        copy = pltpu.make_async_copy(source, target, self.sems[2].at[len(self.locals)])
        copy.start()
        self.locals.append([copy, True])
        return len(self.locals) - 1

    def settle(self, number):
        copy, pending = self.locals[number]
        if pending:
            copy.wait()
        self.locals[number][1] = False

    def close(self):
        for number in range(len(self.locals)):
            self.settle(number)
        for copy in self.sent:
            copy.wait_send()


def in_turn(tasks):
    tasks = list(tasks)
    while tasks:
        for task in list(tasks):
            try:
                next(task)
            except StopIteration:
                tasks.remove(task)


def ring_four(links, own, place, axis, landed):
    right = links.send(own, place(0, None), **{axis: 1})
    left = links.send(own, place(0, None), **{axis: -1})
    yield
    links.arrived(right, place(-1, None))
    on_right = links.send(place(-1, 0), place(-1, 0), **{axis: 1})
    landed(-1)
    yield
    links.arrived(left, place(1, None))
    on_left = links.send(place(1, 1), place(1, 1), **{axis: -1})
    landed(1)
    yield
    links.arrived(on_right, place(2, 0))
    links.arrived(on_left, place(2, 1))
    landed(2)


def half_of(ref, part):
    if part is None:
        return ref
    rows = ref.shape[0] // 2
    return ref.at[pl.ds(part * rows, rows)]


def gather_br(links, own, whole):
    unused_y, unused_z, unused_c, l, x = coords()

    def place(dl):
        return lambda dx, part: half_of(whole.at[(l + dl) % 2, (x + dx) % 4], part)

    kept = links.local(own, place(0)(0, None))
    across = links.send(own, place(0)(0, None), dl=1)
    near = ring_four(links, own, place(0), "dx", lambda d: None)
    next(near)
    yield
    links.arrived(across, place(1)(0, None))
    far = ring_four(links, place(1)(0, None), place(1), "dx", lambda d: None)
    next(far)
    for unused in near:
        yield
    for unused in far:
        yield
    links.settle(kept)


def gather_tok(links, own, whole):
    y, z, c, unused_l, unused_x = coords()
    passed = []

    def place(dz, dc=0):
        return lambda dy, part: half_of(
            whole.at[(y + dy) % 4, (z + dz) % 2, (c + dc) % 2], part
        )

    def passer(dz):
        def landed(dy):
            ref = place(dz)(dy, None)
            passed.append((links.send(ref, ref, dc=1), place(dz, 1)(dy, None)))

        return landed

    kept = links.local(own, place(0)(0, None))
    across = links.send(own, place(0)(0, None), dz=1)
    near = ring_four(links, own, place(0), "dy", passer(0))
    next(near)
    passed.append((links.send(own, place(0)(0, None), dc=1), place(0, 1)(0, None)))
    yield
    links.arrived(across, place(1)(0, None))
    far = ring_four(links, place(1)(0, None), place(1), "dy", passer(1))
    next(far)
    passer(1)(0)
    for unused in near:
        yield
    for unused in far:
        yield
    links.settle(kept)
    for ticket, ref in passed:
        links.arrived(ticket, ref)


def add_up(target, sources, rows, finish):
    chunk = 16

    def step(i, unused):
        here = pl.ds(pl.multiple_of(i * chunk, chunk), chunk)
        total = sources[0][here, :].astype(F32)
        for source in sources[1:]:
            total = total + source[here, :].astype(F32)
        target[here, :] = finish(total, here).astype(target.dtype)
        return unused

    lax.fori_loop(0, rows // chunk, step, 0)


def plain(total, here):
    return total


def reduce_heads(links, grads, dq, dq_home, grads_home, mine, near, far, total):
    y, z, c, unused_l, unused_x = coords()
    order = (1, 3, 2, 0)
    held, from_core = {}, {}
    for dz in (1, 0):
        for d in order:
            place = ((y + d) % 4, (z + dz) % 2)
            from_core[d, dz] = links.send(
                grads.at[place[0], place[1], 1 - c], near.at[place[0], place[1]], dc=1
            )
            held[d, dz] = links.local(
                grads.at[place[0], place[1], c], mine.at[place[0], place[1]]
            )
    asked = [links.send(dq.at[(y + d) % 4], dq_home.at[y], dy=d) for d in order[:3]]
    links.local(dq.at[y], dq_home.at[y])
    yield
    rows = mine.shape[2]
    across = {}
    for d in order:
        here = (y + d) % 4
        links.arrived(from_core[d, 1], near.at[here, 1 - z])
        links.settle(held[d, 1])
        add_up(
            mine.at[here, 1 - z], [mine.at[here, 1 - z], near.at[here, 1 - z]], rows, plain
        )
        across[d] = links.send(mine.at[here, 1 - z], far.at[here], dz=1)
        yield
    home = {}
    for d in order:
        here = (y + d) % 4
        links.arrived(from_core[d, 0], near.at[here, z])
        links.settle(held[d, 0])
        links.arrived(across[d], far.at[here])
        add_up(
            total.at[here], [mine.at[here, z], near.at[here, z], far.at[here]], rows, plain
        )
        if d:
            home[d] = links.send(total.at[here], grads_home.at[y], dy=d)
        else:
            links.local(total.at[here], grads_home.at[y])
        yield
    for i, d in enumerate(order[:3]):
        links.arrived(asked[i], dq_home.at[(y - d) % 4])
        links.arrived(home[d], grads_home.at[(y - d) % 4])


class ScatterSpace:
    names = ("pieces", "near", "out", "far", "across", "sums", "side")

    def __init__(self, refs):
        for name, ref in zip(self.names, refs):
            setattr(self, name, ref)

    @staticmethod
    def shapes(rows, depth, half):
        if half == depth:
            sizes = ((2, 4, rows, depth), (3, 2, rows, depth), (rows, depth), (rows, depth))
            return [pltpu.VMEM(size, BF) for size in sizes]
        assert 2 * half == depth
        sizes = (
            (2, 4, rows, depth),
            (3, 2, rows, half),
            (rows, half),
            (rows, half),
            (4, rows, half),
            (4, rows, half),
            (3, rows, half),
        )
        return [pltpu.VMEM(size, BF) for size in sizes]


def scatter_br(links, make, space, target, finish):
    unused_y, unused_z, unused_c, l, x = coords()
    rows, half = space.out.shape
    split = half < target.shape[1]
    first, second = pl.ds(0, half), pl.ds(half, half)
    order = (1, 3, 2, 0)
    direct, folded, onward = {}, {}, {}
    for i, d in enumerate(order):
        there = (x + d) % 4
        make(there)
        if d:
            for dl in (1, 0):
                to = (l + dl) % 2
                direct[dl, i] = links.send(
                    space.pieces.at[to, there, :, first], space.near.at[i, to], dx=d
                )
        if split:
            folded[d] = links.send(
                space.pieces.at[1 - l, there, :, second], space.across.at[there], dl=1
            )
        yield
    for i in range(3):
        links.arrived(direct[1, i], space.near.at[i, 1 - l])
        yield
    mine = space.pieces.at[1 - l, x, :, first]
    add_up(space.out, [mine] + [space.near.at[i, 1 - l] for i in range(3)], rows, plain)
    over = links.send(space.out, space.far, dl=1)
    for i, d in enumerate(order if split else ()):
        there = (x + d) % 4
        links.arrived(folded[d], space.across.at[there])
        own = space.pieces.at[l, there, :, second]
        add_up(space.sums.at[there], [own, space.across.at[there]], rows, plain)
        if d:
            onward[i] = links.send(space.sums.at[there], space.side.at[i], dx=d)
        yield
    for i in range(3):
        links.arrived(direct[0, i], space.near.at[i, l])
    yield
    links.arrived(over, space.far)
    sources = [space.pieces.at[l, x, :, first]] + [space.near.at[i, l] for i in range(3)]
    add_up(target.at[:, first], sources + [space.far], rows, finish(0))
    if not split:
        return
    yield
    for i in range(3):
        links.arrived(onward[i], space.side.at[i])
    sources = [space.sums.at[x]] + [space.side.at[i] for i in range(3)]
    add_up(target.at[:, second], sources, rows, finish(half))


def reduce_tok(links, make, parts, near, side, out, far, target):
    y, z, c, unused_l, unused_x = coords()
    order = (1, 3, 2, 0)
    tickets = {}
    for d in order:
        here = (y + d) % 4
        make(here)
        tickets[d] = links.send(parts.at[here, :, 1 - c], near.at[here], dc=1)
        yield
    rows = out.shape[0]
    sent = {}
    for i, d in enumerate(order):
        here = (y + d) % 4
        links.arrived(tickets[d], near.at[here])
        for k in range(2):
            own = parts.at[here, k, c]
            add_up(own, [own, near.at[here, k]], rows, plain)
        if d:
            sent[i] = links.send(parts.at[here, :, c], side.at[i], dy=d)
        yield
    for i in range(3):
        links.arrived(sent[i], side.at[i])
        yield
    add_up(out, [parts.at[y, 1 - z, c]] + [side.at[i, 1 - z] for i in range(3)], rows, plain)
    across = links.send(out, far, dz=1)
    yield
    links.arrived(across, far)
    add_up(target, [parts.at[y, z, c]] + [side.at[i, z] for i in range(3)] + [far], rows, plain)


BR_NEAR = [dict(dl=1), dict(dx=1), dict(dx=-1)]
BR_ALL = BR_NEAR + [dict(dx=2)]
TOK_NEAR = [dict(dz=1), dict(dc=1), dict(dy=1), dict(dy=-1)]
TOK_ALL = TOK_NEAR + [dict(dy=2)]


def comm_call(
    kernel, name, number, args, outs, scratch=(), in_vmem=(), out_vmem=(), in_smem=(), copies=48
):
    return pl.pallas_call(
        kernel,
        out_shape=tuple(outs),
        in_specs=[
            VMEM if i in in_vmem else SMEM if i in in_smem else ANY for i in range(len(args))
        ],
        out_specs=tuple(VMEM if i in out_vmem else ANY for i in range(len(outs))),
        scratch_shapes=list(scratch)
        + [
            pltpu.SemaphoreType.DMA((copies,)),
            pltpu.SemaphoreType.DMA((copies,)),
            pltpu.SemaphoreType.DMA((16,)),
        ],
        compiler_params=pltpu.CompilerParams(
            collective_id=number, has_side_effects=True, vmem_limit_bytes=60 * 2**20
        ),
        cost_estimate=SMALL,
        name=name,
    )(*args)


def table_rows(table, block_map, slot, long_blocks):
    block = block_map[lax.axis_index("tok") * 2 + slot]
    place = jnp.where(block < long_blocks, block % LB, (block - long_blocks) % 2)
    return table[place]


def shift_rows(tokens, gain, bias, shifted):
    rows = tokens.shape[0]
    chunk = 16

    def step(i, unused):
        here = pl.ds(pl.multiple_of(i * chunk, chunk), chunk)
        value = tokens[here, :].astype(F32)
        value = value - jnp.mean(value, axis=-1, keepdims=True)
        scale = lax.rsqrt(jnp.mean(value * value, axis=-1, keepdims=True) + EPSILON)
        shifted[here, :] = (value * scale * gain[...] + bias[...]).astype(BF)
        return unused

    lax.fori_loop(0, rows // chunk, step, 0)


def turned(block):
    return jnp.transpose(block.astype(F32)).astype(BF)


def bias_places(heads, per):
    width = heads * HD
    places = np.zeros((128, 3 * width), np.float32)
    for column in range(3 * width):
        if column < width:
            part, head, lane = 0, column // HD, column % HD
        else:
            pair, lane = divmod(column - width, HD)
            part, head = 1 + pair % 2, pair // 2
        places[(part * heads + head) * per + lane % per, column] = 1.0
    return places


def start_kernel(
    heads,
    main,
    block_map,
    tokens,
    gain,
    bias,
    cot,
    qkv,
    qkv_bias,
    places,
    gate,
    up,
    down,
    out,
    table,
    x_out,
    g_out,
    w_out,
    f_out,
    kv_mine,
    q_heads,
    *rest,
):
    shifted, qkv_shard, ff_shard, held_x, held_w, pairs, queries, held_t = rest[:8]
    links = Links(*rest[8:])
    y, z, c, unused_l, unused_x = coords()
    width = heads * HD
    links.greet(BR_NEAR + TOK_ALL)
    rotary = links.local(table, held_t)
    shift_rows(tokens, gain, bias, shifted)
    rows, depth = tokens.shape
    kv = []
    for head in range(heads):
        lanes = slice(head * HD, (head + 1) * HD)
        kv += [qkv[1, :, lanes], qkv[2, :, lanes]]
    qkv_shard[:, : 3 * width] = jnp.concatenate([qkv[0]] + kv, axis=1)
    line = dot(qkv_bias[...], places[...], NN)
    lane = lax.broadcasted_iota(jnp.int32, line.shape, 1) % HD
    line = jnp.where(lane // (HD // 16) == lax.axis_index("tok"), line, 0.0)[:1]
    lines = [line[:, r * 128 : (r + 1) * 128] for r in range(3 * width // 128)]
    zero = jnp.zeros((qkv_shard.shape[0] - len(lines), 128), F32)
    qkv_shard[:, 3 * width :] = jnp.concatenate(lines + [zero], axis=0).astype(BF)

    def project(half):
        tile = 2 * rows
        here = slice(half * tile, (half + 1) * tile)
        span = held_x[:, 2 * half : 2 * half + 2].reshape(2 * tile, depth)
        corner = held_w[0, 0, 0, :8, 3 * width :].astype(F32)
        for t in range(1, 16):
            corner = corner + held_w[t // 4, t // 2 % 2, t % 2, :8, 3 * width :].astype(F32)
        added = jnp.concatenate([corner[r : r + 1] for r in range(len(lines))], axis=1)
        products = dot(span, held_w[...].reshape(depth, -1)[:, : 3 * width], NN) + added
        parts = []
        for slot in range(2):
            turns = table_rows(held_t, block_map, slot, 2 * LB)[here]
            joined = products[slot * tile : (slot + 1) * tile]
            parts.append(turn(joined[:, :width], turns, heads // 2, False, 1.0).astype(BF))
            kv = turn(joined[:, width:], turns, heads, True, 1.0).astype(BF)
            for head in range(heads):
                pairs[head, slot, here, :] = kv[:, head * 2 * HD : (head + 1) * 2 * HD]
        for head in range(heads):
            lanes = slice(head * HD, (head + 1) * HD)
            queries[head, here, :] = jnp.concatenate(
                [parts[0][:, lanes], parts[1][:, lanes]], axis=1
            )

    def attention():
        tasks = [gather_br(links, shifted, held_x), gather_tok(links, qkv_shard, held_w)]
        while tasks:
            for task in list(tasks):
                try:
                    next(task)
                except StopIteration:
                    tasks.remove(task)
            yield
        links.local(held_x, x_out)
        links.local(held_w, w_out)
        links.settle(rotary)
        for half in range(2):
            project(half)
        sent = [
            (d, links.send(pairs.at[(y + d) % 4], kv_mine.at[y], dy=d)) for d in (1, 3, 2)
        ]
        links.local(pairs.at[y], kv_mine.at[y])
        links.local(queries, q_heads)
        for unused in range(12):
            yield
        for d, ticket in sent:
            links.arrived(ticket, kv_mine.at[(y - d) % 4])

    def feed_forward():
        ff_shard[:, :main] = turned(down[:main, :])
        tail = down.shape[0] - main
        ends = jnp.concatenate([down[main:, :], jnp.zeros((128 - tail, rows), BF)], axis=0)
        ff_shard[:, main : main + 128] = turned(ends)
        at = main + 128
        ff_shard[:, at : at + width] = turned(out[...])
        at += width
        ff_shard[:, at : at + main] = turned(gate[:main, :])
        ff_shard[:, at + main : at + 2 * main] = turned(up[:main, :])
        ends = jnp.concatenate([gate[main:, :], up[main:, :]], axis=0)
        ff_shard[:, at + 2 * main :] = turned(ends)
        yield
        yield from gather_tok(links, ff_shard, f_out)

    def gradient():
        for unused in range(3):
            yield
        yield from gather_br(links, cot, g_out)

    in_turn([attention(), feed_forward(), gradient()])
    links.close()


def start(
    block_map, tokens, gain, bias, cot, qkv, qkv_bias, gate, up, down, out, table, heads, main
):
    rows, depth = tokens.shape
    wrows = qkv.shape[1]
    width = heads * HD
    cols = main + 128 + width + 2 * gate.shape[0]
    whole = jax.ShapeDtypeStruct((2, 4, rows, depth), BF)
    places = jnp.asarray(bias_places(heads, qkv_bias.shape[2]))
    flat = jnp.pad(qkv_bias.reshape(1, -1).astype(F32), ((0, 7), (0, 128 - qkv_bias.size)))
    args = (block_map, tokens, gain, bias, cot, qkv, flat, places, gate, up, down, out, table)
    copies = 72
    shapes = (
        whole,
        whole,
        jax.ShapeDtypeStruct((4, 2, 2, wrows, 3 * width + 128), BF),
        jax.ShapeDtypeStruct((4, 2, 2, wrows, cols), BF),
        jax.ShapeDtypeStruct((heads, 2, BLK, 2 * HD), BF),
        jax.ShapeDtypeStruct((heads, BLK, 2 * HD), BF),
    )
    specs = [SMEM] + [VMEM] * (len(args) - 1)
    specs[4] = specs[12] = ANY
    return pl.pallas_call(
        functools.partial(start_kernel, heads, main),
        out_shape=shapes,
        in_specs=specs,
        out_specs=(ANY,) * len(shapes),
        scratch_shapes=[
            pltpu.VMEM((rows, depth), BF),
            pltpu.VMEM((wrows, 3 * width + 128), BF),
            pltpu.VMEM((wrows, cols), BF),
            pltpu.VMEM(whole.shape, BF),
            pltpu.VMEM(shapes[2].shape, BF),
            pltpu.VMEM(shapes[4].shape, BF),
            pltpu.VMEM(shapes[5].shape, BF),
            pltpu.VMEM(table.shape, F32),
            pltpu.SemaphoreType.DMA((copies,)),
            pltpu.SemaphoreType.DMA((copies,)),
            pltpu.SemaphoreType.DMA((16,)),
        ],
        compiler_params=pltpu.CompilerParams(
            collective_id=0, has_side_effects=True, vmem_limit_bytes=60 * 2**20
        ),
        cost_estimate=SMALL,
        name="start",
    )(*args)


def ff_heads_kernel(
    main,
    down,
    first,
    x_ref,
    g_ref,
    x_strip,
    g_strip,
    weights,
    kv_mine,
    q_heads,
    h_ref,
    s_ref,
    grad_ref,
    asked,
    pairs,
    w_ref,
    held,
    held_hidden,
    outs,
    *sems,
):
    y, z, c, unused_l, unused_x = coords()
    step = pl.program_id(0)
    final = pl.num_programs(0) - 1
    links = Links(*sems)
    order = (1, 3, 2)
    rows = x_ref.shape[1]

    load = pltpu.make_async_copy(weights, w_ref, sems[2].at[0])
    kept = [
        pltpu.make_async_copy(kv_mine, pairs.at[:, z, c], sems[2].at[1]),
        pltpu.make_async_copy(q_heads.at[y], asked.at[y, 0], sems[2].at[2]),
    ]
    kept_out = pltpu.make_async_copy(outs.at[y], asked.at[y, 1], sems[2].at[3])
    number = iter(range(64))

    def plan(source, target, lands, **offsets):
        n = next(number)
        return links.copy(n, source, target, offsets), links.copy(n, lands, lands, offsets)

    def swap(source, k):
        return [
            plan(source.at[(y + d) % 4], asked.at[y, k], asked.at[(y - d) % 4, k], dy=d)
            for d in order
        ]

    far = [plan(kv_mine.at[i], pairs.at[i, z, c], pairs.at[i, 1 - z, c], dz=1) for i in range(4)]
    near = [plan(kv_mine.at[i], pairs.at[i, z, c], pairs.at[i, z, 1 - c], dc=1) for i in range(4)]
    diagonal = [
        plan(pairs.at[i, 1 - z, c], pairs.at[i, 1 - z, c], pairs.at[i, 1 - z, 1 - c], dc=1)
        for i in range(4)
    ]
    asked_q, asked_o = swap(q_heads, 0), swap(outs, 1)

    def cross(i):
        far[i][1].wait_recv()
        diagonal[i][0].start()

    @pl.when(step == 0)
    def _():
        load.start()
        links.greet([dict(dz=1), dict(dc=1), dict(dy=1), dict(dy=2), dict(dy=3)])
        for copy, unused in far + near + asked_q:
            copy.start()
        for copy in kept:
            copy.start()
        load.wait()

    def pause(point):
        @pl.when(step == 1)
        def _():
            cross(point)

    for i in range(2, 4):

        @pl.when(step == i + 1)
        def _():
            cross(i)

    here = pl.ds(pl.multiple_of(jnp.minimum(step, 1) * rows, rows), rows)

    def mixed_grad(value):
        for head in range(outs.shape[0]):
            lanes = slice(head * HD, (head + 1) * HD)
            outs[head, here, :] = jnp.concatenate(
                [value[:rows, lanes], value[rows:, lanes]], axis=1
            )

    @pl.when(step < 2)
    def _():
        grads, hidden = ff_part(
            main, down, first, x_ref[...], g_ref[...], w_ref, h_ref, s_ref, mixed_grad, pause
        )
        held[:, here, :] = grads.reshape(2, rows, -1)
        held_hidden[:, here, :] = hidden.reshape(2, rows, -1)

    @pl.when(step == 1)
    def _():
        for copy, unused in asked_o:
            copy.start()
        kept_out.start()

    @pl.when(step >= 2)
    def _():
        grads = held[...].reshape(-1, held.shape[2])
        hidden = held_hidden[...].reshape(-1, down)
        grad_ref[:, :down] = dot(g_strip[...], hidden, TN).astype(BF)
        grad_ref[:, down:] = dot(x_strip[...], grads, TN).astype(BF)

    @pl.when(step == final)
    def _():
        for copy in kept + [kept_out]:
            copy.wait()
        for unused, landed in near + diagonal + asked_q + asked_o:
            landed.wait_recv()
        for copy, unused in far + near + diagonal + asked_q + asked_o:
            copy.wait_send()


def ff_heads(x, g, w, kv_mine, q_heads, main, down, first):
    depth, cols = w.shape
    heads, unused, span, lanes = kv_mine.shape
    rows = BLK // 2
    both = cols - first
    strip = 512

    def tile(width):
        return pl.BlockSpec((2, rows, width), lambda i: (0, jnp.minimum(i, 1), 0))

    return pl.pallas_call(
        functools.partial(ff_heads_kernel, main, down, first),
        grid=(2 + depth // strip,),
        in_specs=[
            tile(depth),
            tile(depth),
            pl.BlockSpec((2 * BLK, strip), lambda i: (0, jnp.maximum(i - 2, 0))),
            pl.BlockSpec((2 * BLK, strip), lambda i: (0, jnp.maximum(i - 2, 0))),
            ANY,
            ANY,
            ANY,
        ],
        out_specs=(
            tile(down),
            tile(depth),
            pl.BlockSpec((strip, both + down), lambda i: (jnp.maximum(i - 2, 0), 0)),
            ANY,
            ANY,
        ),
        out_shape=(
            jax.ShapeDtypeStruct((2, BLK, down), BF),
            jax.ShapeDtypeStruct((2, BLK, depth), BF),
            jax.ShapeDtypeStruct((depth, both + down), BF),
            jax.ShapeDtypeStruct((4, 2, span, lanes), BF),
            jax.ShapeDtypeStruct((4, 2, 2, 2, span, lanes), BF),
        ),
        scratch_shapes=[
            pltpu.VMEM((depth, cols), BF),
            pltpu.VMEM((2, BLK, both), BF),
            pltpu.VMEM((2, BLK, down), BF),
            pltpu.VMEM(q_heads.shape, BF),
            pltpu.SemaphoreType.DMA((32,)),
            pltpu.SemaphoreType.DMA((32,)),
            pltpu.SemaphoreType.DMA((4,)),
        ],
        compiler_params=pltpu.CompilerParams(
            collective_id=1, has_side_effects=True, vmem_limit_bytes=60 * 2**20
        ),
        cost_estimate=SMALL,
        name="ff_heads",
    )(x, g, x.reshape(2 * BLK, depth), g.reshape(2 * BLK, depth), w, kv_mine, q_heads)


def home_kernel(
    heads,
    grads,
    dq,
    o_parts,
    hidden,
    weights,
    tokens,
    dq_home,
    grads_home,
    mixed_out,
    result,
    *rest,
):
    mine, near, far, total, held_w, held_h, held_o = rest[:7]
    space = ScatterSpace(rest[7:11])
    links = Links(*rest[11:])
    y, unused_z, unused_c, unused_l, unused_x = coords()
    rows, depth = tokens.shape
    kept = held_w.shape[1]
    links.greet(BR_ALL + TOK_ALL)
    loads = [
        links.local(o_parts.at[y], held_o.at[y]),
        links.local(hidden, held_h),
        links.local(weights.at[:, pl.ds(0, kept)], held_w),
    ]
    returned = [
        (d, links.send(o_parts.at[(y + d) % 4], held_o.at[y], dy=d)) for d in (1, 3, 2)
    ]

    def make(there):
        here = pl.ds(pl.multiple_of(there * rows, rows), rows)
        mixed = [
            jnp.concatenate(
                [held_o[head, here, slot * HD : (slot + 1) * HD] for head in range(heads)],
                axis=1,
            )
            for slot in range(2)
        ]
        for slot in range(2):
            mixed_out[slot, here, :] = mixed[slot]
        both = jnp.concatenate(
            [held_h[:, here, :].reshape(2 * rows, -1), jnp.concatenate(mixed, axis=0)], axis=1
        )
        branches = dot(both, held_w[...], NT).astype(BF)
        for slot in range(2):
            space.pieces[slot, there] = branches[slot * rows : (slot + 1) * rows]

    def finish(column):
        def add(value, here):
            return value + tokens[here, column : column + value.shape[1]].astype(F32)

        return add

    def output():
        yield
        for d, ticket in returned:
            links.arrived(ticket, held_o.at[(y - d) % 4])
        for load in loads:
            links.settle(load)
        yield from scatter_br(links, make, space, result, finish)

    in_turn(
        [
            reduce_heads(links, grads, dq, dq_home, grads_home, mine, near, far, total),
            output(),
        ]
    )
    links.close()


def heads_home(grads, dq, o_parts, hidden, weights, tokens, heads):
    rows, depth = tokens.shape
    span, lanes = grads.shape[3:]
    width = heads * HD
    kept = hidden.shape[2] + width
    return comm_call(
        functools.partial(home_kernel, heads),
        "heads_home",
        2,
        (grads, dq, o_parts, hidden, weights, tokens),
        (
            jax.ShapeDtypeStruct(dq.shape, BF),
            jax.ShapeDtypeStruct((4, span, lanes), BF),
            jax.ShapeDtypeStruct((2, BLK, width), BF),
            jax.ShapeDtypeStruct((rows, depth), BF),
        ),
        scratch=[
            pltpu.VMEM((4, 2, span, lanes), BF),
            pltpu.VMEM((4, 2, span, lanes), BF),
            pltpu.VMEM((4, span, lanes), BF),
            pltpu.VMEM((4, span, lanes), BF),
            pltpu.VMEM((depth, kept), BF),
            pltpu.VMEM(hidden.shape, BF),
            pltpu.VMEM(o_parts.shape, BF),
        ]
        + ScatterSpace.shapes(rows, depth, depth),
        in_vmem=(5,),
        out_vmem=(2, 3),
        copies=64,
    )


def normal_rows(tokens, normed, scales):
    rows = tokens.shape[0]
    chunk = 16

    def step(i, unused):
        here = pl.ds(pl.multiple_of(i * chunk, chunk), chunk)
        value = tokens[here, :].astype(F32)
        value = value - jnp.mean(value, axis=-1, keepdims=True)
        scale = lax.rsqrt(jnp.mean(value * value, axis=-1, keepdims=True) + EPSILON)
        normed[here, :] = value * scale
        scales[here, :] = jnp.broadcast_to(scale, (chunk, 128))
        return unused

    lax.fori_loop(0, rows // chunk, step, 0)


def turn_back(grads, normed, scales, cot, gain, parts, result):
    rows, depth = normed.shape
    chunk = 16

    def rows_at(i):
        return pl.ds(pl.multiple_of(i * chunk, chunk), chunk)

    def sums(i, carry):
        here = rows_at(i)
        grad = grads[here, :]
        up = (grad * normed[here, :]).reshape(2, 8, depth)
        return carry[0] + up.sum(0), carry[1] + grad.reshape(2, 8, depth).sum(0)

    zero = jnp.zeros((8, depth), F32)
    found = lax.fori_loop(0, rows // chunk, sums, (zero, zero))
    for k in range(2):
        line = jnp.sum(found[k], axis=0, keepdims=True)
        parts[16 * k : 16 * (k + 1), :] = jnp.concatenate(
            [line[:, t * 128 : (t + 1) * 128] for t in range(depth // 128)], axis=0
        )
    yield

    def back(i, unused):
        here = rows_at(i)
        line = normed[here, :]
        grad = grads[here, :] * gain[...]
        slope = jnp.mean(grad * line, axis=-1, keepdims=True)
        grad = grad - jnp.mean(grad, axis=-1, keepdims=True) - line * slope
        result[here, :] = cot[here, :].astype(F32) + scales[here, :1] * grad
        return unused

    lax.fori_loop(0, rows // chunk, back, 0)


BR_PEERS = [dict(dl=i // 4, dx=i % 4) for i in range(1, 8)]
TOK_PEERS = [dict(dy=i // 4, dz=(i // 2) % 2, dc=i % 2) for i in range(1, 16)]


def last_kernel(
    heads,
    dq,
    dkv,
    table,
    x_in,
    g_in,
    m_in,
    w_in,
    s_in,
    tokens,
    cot,
    gain,
    block_map,
    result,
    qkv_out,
    out_out,
    bias_out,
    sides,
    *rest,
):
    held_q, held_kv, held_t, held_x, held_g, held_m, held_w, held_s, gj = rest[:9]
    parts, near, side, out, far, wsum, summed, normed, scales = rest[9:18]
    lines, lines_in, last, last_in = rest[18:22]
    space = ScatterSpace(rest[22:29])
    links = Links(*rest[29:])
    y, z, c, l, x = coords()
    links.greet(BR_PEERS + TOK_PEERS)
    width = heads * HD
    rows, depth = tokens.shape
    first = [
        links.local(dq, held_q),
        links.local(dkv, held_kv),
        links.local(table, held_t),
    ]
    second = [
        links.local(x_in, held_x),
        links.local(g_in, held_g),
        links.local(m_in, held_m),
    ]
    third = [links.local(w_in.at[:, pl.ds(0, 3 * width)], held_w), links.local(s_in, held_s)]
    for load in first:
        links.settle(load)
    total = jnp.zeros((1, 3 * width), F32)
    for slot in range(2):
        for half in range(2):
            here = slice(half * BLK // 2, (half + 1) * BLK // 2)
            lanes = slice(slot * HD, (slot + 1) * HD)
            turns = table_rows(held_t, block_map, slot, 2 * LB)[here]
            q = jnp.concatenate([held_q[h, here, lanes] for h in range(heads)], axis=1)
            q = turn(q.astype(F32), turns, heads // 2, False, -1.0).astype(BF)
            kv = jnp.concatenate([held_kv[h, slot, here] for h in range(heads)], axis=1)
            kv = turn(kv.astype(F32), turns, heads, True, -1.0).astype(BF)
            both = jnp.concatenate([q, kv], axis=1)
            gj[slot, here, :] = both
            total += jnp.sum(both.astype(F32), axis=0, keepdims=True)
    corner = [total[:, r * 128 : (r + 1) * 128] for r in range(3 * width // 128)]
    corner = jnp.concatenate(corner + [jnp.zeros((122, 128), F32)], axis=0).astype(BF)
    for load in second:
        links.settle(load)
    wrows = parts.shape[3]
    strip = 4 * wrows

    def weights_of(there):
        here = pl.ds(pl.multiple_of(there * strip, strip), strip)
        qkv = dot(held_x[:, here], gj[...].reshape(2 * BLK, 3 * width), TN).astype(BF)
        outs = dot(held_g[:, here], held_m[...], TN).astype(BF)
        for k in range(4):
            at = slice(k * wrows, (k + 1) * wrows)
            parts[there, k // 2, k % 2, :, : 3 * width] = qkv[at]
            parts[there, k // 2, k % 2, :, 3 * width : 4 * width] = outs[at]
            parts[there, k // 2, k % 2, :, 4 * width :] = corner

    def rows_of(there):
        if third:
            for load in third:
                links.settle(load)
            third.clear()
        here = pl.ds(pl.multiple_of(there * rows, rows), rows)
        both = gj[:, here, :].reshape(2 * rows, 3 * width)
        grads = dot(both, held_w[...], NT)
        for slot in range(2):
            value = grads[slot * rows : (slot + 1) * rows] + held_s[slot, here, :].astype(F32)
            space.pieces[slot, there] = value.astype(BF)

    def aside():
        for unused in range(5):
            yield
        normal_rows(tokens, normed, scales)

    in_turn(
        [
            reduce_tok(links, weights_of, parts, near, side, out, far, wsum),
            scatter_br(links, rows_of, space, summed, lambda column: plain),
            aside(),
        ]
    )
    through = turn_back(summed, normed, scales, cot, gain, lines, result)
    next(through)
    tickets = [links.send(lines, lines_in.at[i], **o) for i, o in enumerate(BR_PEERS)]
    for unused in through:
        pass
    total = lines[...]
    for i, ticket in enumerate(tickets):
        links.arrived(ticket, lines_in.at[i])
        total = total + lines_in[i]
    last[...] = jnp.zeros_like(last)
    for t in range(16):
        last[t, 0:2, :] = jnp.concatenate([total[t : t + 1], total[16 + t : 17 + t]], axis=0)
    tickets = []
    for i, o in enumerate(TOK_PEERS):
        there = ((y + o["dy"]) % 4) * 4 + ((z + o["dz"]) % 2) * 2 + (c + o["dc"]) % 2
        tickets.append(links.send(last.at[there], last_in.at[i], **o))
    qkv_out[0] = wsum[:, :width]
    for k in range(2):
        qkv_out[1 + k] = jnp.concatenate(
            [
                wsum[:, width + (2 * h + k) * HD : width + (2 * h + k + 1) * HD]
                for h in range(heads)
            ],
            axis=1,
        )
    out_out[...] = jnp.transpose(wsum[:, 3 * width : 4 * width])
    bias_out[...] = wsum[:8, 4 * width :]
    total = last[y * 4 + z * 2 + c]
    for i, ticket in enumerate(tickets):
        links.arrived(ticket, last_in.at[i])
        total = total + last_in[i]
    sides[...] = total
    links.close()


def last_sums(
    dq, dkv, table, x, g, mixed, w, partial_grad, tokens, cot, gain, block_map, heads
):
    rows, depth = tokens.shape
    wrows = depth // 16
    width = heads * HD
    cols = 4 * width + 128
    return comm_call(
        functools.partial(last_kernel, heads),
        "last_sums",
        3,
        (dq, dkv, table, x, g, mixed, w, partial_grad, tokens, cot, gain, block_map),
        (
            jax.ShapeDtypeStruct((rows, depth), F32),
            jax.ShapeDtypeStruct((3, wrows, width), F32),
            jax.ShapeDtypeStruct((width, wrows), F32),
            jax.ShapeDtypeStruct((8, 128), F32),
            jax.ShapeDtypeStruct((8, 128), F32),
        ),
        scratch=[
            pltpu.VMEM(dq.shape, BF),
            pltpu.VMEM(dkv.shape, BF),
            pltpu.VMEM(table.shape, F32),
            pltpu.VMEM(x.shape, BF),
            pltpu.VMEM(g.shape, BF),
            pltpu.VMEM(mixed.shape, BF),
            pltpu.VMEM((depth, 3 * width), BF),
            pltpu.VMEM(partial_grad.shape, BF),
            pltpu.VMEM((2, BLK, 3 * width), BF),
            pltpu.VMEM((4, 2, 2, wrows, cols), BF),
            pltpu.VMEM((4, 2, wrows, cols), BF),
            pltpu.VMEM((3, 2, wrows, cols), BF),
            pltpu.VMEM((wrows, cols), BF),
            pltpu.VMEM((wrows, cols), BF),
            pltpu.VMEM((wrows, cols), F32),
            pltpu.VMEM((rows, depth), F32),
            pltpu.VMEM((rows, depth), F32),
            pltpu.VMEM((rows, 128), F32),
            pltpu.VMEM((32, 128), F32),
            pltpu.VMEM((7, 32, 128), F32),
            pltpu.VMEM((16, 8, 128), F32),
            pltpu.VMEM((15, 8, 128), F32),
        ]
        + ScatterSpace.shapes(rows, depth, depth // 2),
        in_vmem=(8, 9, 10),
        in_smem=(11,),
        out_vmem=(0, 1, 2, 3, 4),
        copies=80,
    )


def unpack_kernel(main, grads, down, gate, up):
    def lines(start, count):
        return jnp.transpose(grads[:, start : start + count].astype(F32))

    tail = down.shape[0] - main
    down[:main, :] = lines(0, main)
    down[main:, :] = lines(main, 128)[:tail]
    at = main + 128
    gate[:main, :] = lines(at, main)
    up[:main, :] = lines(at + main, main)
    ends = lines(at + 2 * main, 128)
    gate[main:, :] = ends[:tail]
    up[main:, :] = ends[tail:]


def unpack(grads, main, hidden_width):
    shape = jax.ShapeDtypeStruct((hidden_width, grads.shape[0]), F32)
    return pl.pallas_call(
        functools.partial(unpack_kernel, main),
        out_shape=(shape,) * 3,
        in_specs=[VMEM],
        out_specs=(VMEM,) * 3,
        cost_estimate=SMALL,
        name="unpack",
    )(grads)


def rotary_table():
    half = ROT // 2
    frequency = (ROPE_BASE ** (-(np.arange(half) * 2.0 / ROT))).astype(np.float32)
    angles = np.arange(LB * BLK, dtype=np.float32)[:, None] * frequency[None, :]
    cos, sin = np.cos(angles), np.sin(angles)
    one = np.ones((LB * BLK, HD - ROT), np.float32)
    table = np.concatenate([cos, cos, one, -sin, sin, 0.0 * one], axis=1)
    return table.astype(np.float32).reshape(LB, BLK, 2 * HD)


def body(
    tokens,
    norm_gain,
    norm_bias,
    qkv_weight,
    qkv_bias,
    out_weight,
    gate_weight,
    up_weight,
    down_weight,
    cotangent,
    block_map,
    lengths,
):
    tok = lax.axis_index("tok")
    y, z, c = tok // 4, (tok // 2) % 2, tok % 2
    total_blocks = block_map.shape[0]
    long_blocks = total_blocks // 2
    rows = tokens.shape[0]
    depth = tokens.shape[1]
    wrows = qkv_weight.shape[1]
    heads = qkv_bias.shape[1]
    width = heads * HD
    hidden_width = gate_weight.shape[1]
    main = hidden_width // 128 * 128
    tail = hidden_width - main

    down_width = main + 128
    first = down_width + width
    table = jnp.asarray(rotary_table())
    x, grad, qkv_full, ff_full, kv_mine, q_heads = start(
        block_map,
        tokens,
        norm_gain.reshape(1, depth),
        norm_bias.reshape(1, depth),
        cotangent,
        qkv_weight,
        qkv_bias,
        jnp.transpose(gate_weight),
        jnp.transpose(up_weight),
        down_weight,
        out_weight,
        table,
        heads,
        main,
    )
    x = x.reshape(2, BLK, depth)
    grad = grad.reshape(2, BLK, depth)
    qkv_full = qkv_full.reshape(16 * wrows, -1)
    ff_full = ff_full.reshape(16 * wrows, -1)

    slot_table = jnp.arange(total_blocks, dtype=jnp.int32)
    slot_of = jnp.sum(
        jnp.where(block_map[None, :] == slot_table[:, None], slot_table[None, :], 0), axis=1
    )
    key_slot = slot_of.astype(jnp.int32)
    from_tok = jnp.arange(4, dtype=jnp.int32) * 4 + z * 2 + c
    my_queries = jnp.stack([2 * from_tok, 2 * from_tok + 1], axis=1).reshape(-1)
    query_block = jnp.sum(
        jnp.where(my_queries[:, None] == slot_table[None, :], block_map[None, :], 0), axis=1
    ).astype(jnp.int32)
    query_row = jnp.where(
        query_block < long_blocks,
        query_block // LB,
        long_blocks // LB + (query_block - long_blocks) // 2,
    )
    row_table = jnp.arange(lengths.shape[0], dtype=jnp.int32)
    query_limit = jnp.sum(
        jnp.where(query_row[:, None] == row_table[None, :], lengths[None, :], 0), axis=1
    ).astype(jnp.int32)

    hidden, grad_x, grad_ff, qd_all, kv_all = ff_heads(
        x, grad, ff_full, kv_mine, q_heads, main, down_width, first
    )
    kv_all = kv_all.reshape(-1, 2 * HD)
    x = x.reshape(2 * BLK, depth)
    grad = grad.reshape(2 * BLK, depth)
    grad_ff = lax.psum_scatter(grad_ff, "tok", scatter_dimension=0, tiled=True)

    turned, lse, o_parts = attn_fwd(query_block, query_limit, key_slot, qd_all, kv_all, long_blocks)
    dq_parts, dkv_all = attn_bwd(
        query_block, query_limit, key_slot, qd_all, kv_all, turned, lse, long_blocks
    )
    dq_heads, dkv_heads, mixed, result = heads_home(
        dkv_all.reshape(4, 2, 2, 2 * BLK, 2 * HD), dq_parts, o_parts, hidden, ff_full, tokens, heads
    )
    grad_ff, dq_heads = lax.optimization_barrier((grad_ff, dq_heads))
    grad_tokens, grad_qkv, grad_out_out, bias_sums, sides = last_sums(
        dq_heads,
        dkv_heads.reshape(heads, 2, BLK, 2 * HD),
        table,
        x,
        grad,
        mixed.reshape(2 * BLK, width),
        qkv_full,
        grad_x,
        tokens,
        cotangent,
        norm_gain.reshape(1, depth),
        block_map,
        heads,
    )
    bias_sums = bias_sums[: 3 * width // 128].reshape(-1)
    bias_sums = jnp.concatenate(
        [
            bias_sums[:width].reshape(1, heads, HD),
            jnp.transpose(bias_sums[width:].reshape(heads, 2, HD), (1, 0, 2)),
        ]
    )
    grad_bias_out = lax.dynamic_slice_in_dim(
        bias_sums, tok * qkv_bias.shape[2], qkv_bias.shape[2], 2
    )
    grad_down, grad_gate, grad_up = unpack(grad_ff, main, hidden_width)

    sides = lax.dynamic_slice_in_dim(sides[:2], lax.axis_index("br") * 16, 16, 1)
    return (
        result,
        grad_tokens,
        sides[0],
        sides[1],
        grad_qkv,
        grad_bias_out,
        grad_out_out,
        jnp.transpose(grad_gate),
        jnp.transpose(grad_up),
        grad_down,
    )


def solution(mesh):
    in_specs = (
        P(("tok", "br"), None),
        P(),
        P(),
        P(None, "tok", "br"),
        P(None, "br", "tok"),
        P("br", "tok"),
        P("tok", "br"),
        P("tok", "br"),
        P("br", "tok"),
        P(("tok", "br"), None),
        P(),
        P(),
    )
    out_specs = (
        P(("tok", "br"), None),
        P(("tok", "br"), None),
        P(("tok", "br")),
        P(("tok", "br")),
        P(None, "tok", "br"),
        P(None, "br", "tok"),
        P("br", "tok"),
        P("tok", "br"),
        P("tok", "br"),
        P("br", "tok"),
    )
    return jax.shard_map(body, mesh=mesh, in_specs=in_specs, out_specs=out_specs, check_vma=False)
```

```python
import functools

import jax
import jax.numpy as jnp
import numpy as np
from jax import lax
from jax.experimental import pallas as pl
from jax.experimental.pallas import tpu as pltpu
from jax.sharding import PartitionSpec as P

HD = 64
ROT = 16
BLK = 512
LB = 8
EPSILON = 1e-05
ROPE_BASE = 10000.0
MASKED = -1e30
BF = jnp.bfloat16
F32 = jnp.float32
NN = (((1,), (0,)), ((), ()))
NT = (((1,), (1,)), ((), ()))
TN = (((0,), (0,)), ((), ()))
VMEM = pl.BlockSpec(memory_space=pltpu.VMEM)
SMEM = pl.BlockSpec(memory_space=pltpu.SMEM)
ANY = pl.BlockSpec(memory_space=pl.ANY)
SMALL = pl.CostEstimate(flops=1000, bytes_accessed=1000, transcendentals=0)


def dot(left, right, dims):
    return lax.dot_general(left, right, dims, preferred_element_type=F32)


def block_info(block, long_blocks):
    is_long = block < long_blocks
    place = jnp.where(is_long, block % LB, (block - long_blocks) % 2)
    return is_long, place, block - place


def lane_half(packed, half, upper):
    piece = packed[:, half * HD : (half + 1) * HD]
    zero = jnp.zeros_like(piece)
    return jnp.concatenate([zero, piece] if upper else [piece, zero], axis=1)


def allowed_pairs(place, step, limit):
    key_pos = step * BLK + lax.broadcasted_iota(jnp.int32, (BLK, BLK), 0)
    query_pos = place * BLK + lax.broadcasted_iota(jnp.int32, (BLK, BLK), 1)
    return (key_pos <= query_pos) & (key_pos < limit)


def attn_fwd_kernel(long_blocks, qblk, qlim, kslot, q_ref, kv_ref, ot_ref, lse_ref, o_ref):
    def pack(i, unused):
        packed = q_ref[i, 0]
        for half in range(2):
            slot = 2 * i + half
            is_long, place, first = block_info(qblk[slot], long_blocks)
            limit = qlim[slot]
            queries = lane_half(packed, half, False) * jnp.asarray(0.125, BF)

            def step(j, carry, masked):
                top, total, acc = carry
                rows = pl.ds(pl.multiple_of(kslot[first + j] * BLK, BLK), BLK)
                kv = kv_ref[rows, :]
                scores = dot(kv, queries, NT)
                if masked:
                    scores = jnp.where(allowed_pairs(place, j, limit), scores, MASKED)
                new_top = jnp.maximum(top, jnp.max(scores, axis=0, keepdims=True))
                fade = jnp.exp(top - new_top)
                probs = jnp.exp(scores - new_top)
                total = total * fade + jnp.sum(probs, axis=0, keepdims=True)
                acc = acc * fade + dot(kv, probs.astype(BF), TN)
                return new_top, total, acc

            free = jnp.where(is_long, place, 0)
            carry = (
                jnp.full((1, BLK), MASKED, F32),
                jnp.zeros((1, BLK), F32),
                jnp.zeros((2 * HD, BLK), F32),
            )
            carry = lax.fori_loop(0, free, lambda j, c: step(j, c, False), carry)
            top, total, acc = lax.fori_loop(free, place + 1, lambda j, c: step(j, c, True), carry)
            lse_ref[slot] = top + jnp.log(total)
            ot_ref[i, half * HD : (half + 1) * HD, :] = acc[HD:, :] / total
        o_ref[i] = jnp.transpose(ot_ref[i]).astype(BF)
        return unused

    lax.fori_loop(0, q_ref.shape[0], pack, 0)


def attn_fwd(qblk, qlim, kslot, q, kv, long_blocks):
    n = q.shape[0]
    return pl.pallas_call(
        functools.partial(attn_fwd_kernel, long_blocks),
        out_shape=(
            jax.ShapeDtypeStruct((n, 2 * HD, BLK), F32),
            jax.ShapeDtypeStruct((2 * n, 1, BLK), F32),
            jax.ShapeDtypeStruct((n, BLK, 2 * HD), BF),
        ),
        in_specs=[SMEM, SMEM, SMEM, VMEM, VMEM],
        out_specs=(VMEM, VMEM, VMEM),
        compiler_params=pltpu.CompilerParams(vmem_limit_bytes=60 * 2**20),
        cost_estimate=SMALL,
        name="attn_fwd",
    )(qblk, qlim, kslot, q, kv)


def attn_bwd_kernel(
    long_blocks, qblk, qlim, kslot, q_ref, kv_ref, ot_ref, lse_ref, dq_ref, dkv_ref, acc, dqt
):
    acc[...] = jnp.zeros_like(acc)

    def pack(i, unused):
        q_packed = q_ref[i, 0]
        d_packed = q_ref[i, 1]
        d_turned = jnp.transpose(d_packed.astype(F32))
        for half in range(2):
            slot = 2 * i + half
            is_long, place, first = block_info(qblk[slot], long_blocks)
            limit = qlim[slot]
            queries = lane_half(q_packed, half, False) * jnp.asarray(0.125, BF)
            grads = lane_half(d_packed, half, True)
            both = jnp.concatenate([queries, grads], axis=0)
            lanes = slice(half * HD, (half + 1) * HD)
            delta = jnp.sum(d_turned[lanes] * ot_ref[i, lanes, :], axis=0, keepdims=True)
            lse = lse_ref[slot]

            def step(j, total, masked):
                rows = pl.ds(pl.multiple_of(kslot[first + j] * BLK, BLK), BLK)
                kv = kv_ref[rows, :]
                scores = dot(kv, queries, NT)
                if masked:
                    scores = jnp.where(allowed_pairs(place, j, limit), scores, MASKED)
                probs = jnp.exp(scores - lse)
                ds = (probs * (dot(kv, grads, NT) - delta)).astype(BF)
                acc[rows, :] += dot(jnp.concatenate([ds, probs.astype(BF)], axis=1), both, NN)
                return total + dot(kv, ds, TN)

            free = jnp.where(is_long, place, 0)
            total = lax.fori_loop(
                0, free, lambda j, c: step(j, c, False), jnp.zeros((2 * HD, BLK), F32)
            )
            total = lax.fori_loop(free, place + 1, lambda j, c: step(j, c, True), total)
            dqt[lanes, :] = total[:HD, :] * 0.125
        dq_ref[i] = jnp.transpose(dqt[...]).astype(BF)
        return unused

    lax.fori_loop(0, q_ref.shape[0], pack, 0)

    def finish(i, unused):
        rows = pl.ds(pl.multiple_of(i * BLK, BLK), BLK)
        dkv_ref[rows, :] = acc[rows, :].astype(BF)
        return unused

    lax.fori_loop(0, kv_ref.shape[0] // BLK, finish, 0)


def attn_bwd(qblk, qlim, kslot, q, kv, ot, lse, long_blocks):
    n = q.shape[0]
    return pl.pallas_call(
        functools.partial(attn_bwd_kernel, long_blocks),
        out_shape=(
            jax.ShapeDtypeStruct((n, BLK, 2 * HD), BF),
            jax.ShapeDtypeStruct(kv.shape, BF),
        ),
        in_specs=[SMEM, SMEM, SMEM, VMEM, VMEM, VMEM, VMEM],
        out_specs=(VMEM, VMEM),
        scratch_shapes=[pltpu.VMEM(kv.shape, F32), pltpu.VMEM((2 * HD, BLK), F32)],
        compiler_params=pltpu.CompilerParams(vmem_limit_bytes=60 * 2**20),
        cost_estimate=SMALL,
        name="attn_bwd",
    )(qblk, qlim, kslot, q, kv, ot, lse)


def turn(values, table, copies, paired, sign):
    width = values.shape[1]
    lane = lax.broadcasted_iota(jnp.int32, values.shape, 1) % HD
    partner = jnp.where(
        lane < ROT // 2,
        pltpu.roll(values, width - ROT // 2, 1),
        pltpu.roll(values, ROT // 2, 1),
    )
    cos, sin = table[:, :HD], sign * table[:, HD:]
    cos = jnp.concatenate([cos, jnp.ones_like(cos) if paired else cos], axis=1)
    sin = jnp.concatenate([sin, jnp.zeros_like(sin) if paired else sin], axis=1)
    cos = jnp.concatenate([cos] * copies, axis=1)
    sin = jnp.concatenate([sin] * copies, axis=1)
    return values * cos + partner * sin


def ff_part(main, down, first, x, g, w_ref, h_ref, s_ref, mixed_grad, pause):
    rows, depth = x.shape[1:]
    x = x.reshape(2 * rows, depth)
    g = g.reshape(2 * rows, depth)
    gate_up = dot(x, w_ref[:, first:], NN)
    pause(0)
    gh = dot(g, w_ref[:, :first], NN)
    mixed_grad(gh[:, down:].astype(BF))
    gh = gh[:, :down]
    ends = gate_up[:, 2 * main :]
    gate = jnp.concatenate([gate_up[:, :main], ends], axis=1)
    up = jnp.concatenate([gate_up[:, main : 2 * main], pltpu.roll(ends, HD, 1)], axis=1)
    sig = jax.nn.sigmoid(gate)
    silu = gate * sig
    hidden = (silu * up).astype(BF)
    d_gate = gh * up * sig * (1.0 + gate * (1.0 - sig))
    d_up = gh * silu
    tail = d_gate[:, main:] + pltpu.roll(d_up[:, main:], HD, 1)
    grads = jnp.concatenate(
        [d_gate[:, :main].astype(BF), d_up[:, :main].astype(BF), tail.astype(BF)], axis=1
    )
    h_ref[...] = hidden.reshape(h_ref.shape)
    pause(1)
    s_ref[...] = dot(grads, w_ref[:, first:], NT).astype(BF).reshape(s_ref.shape)
    return grads, hidden


def coords():
    tok, br = lax.axis_index("tok"), lax.axis_index("br")
    return tok // 4, (tok // 2) % 2, tok % 2, br // 4, br % 4


def peer(dy=0, dz=0, dc=0, dl=0, dx=0):
    y, z, c, l, x = coords()
    tok = ((y + dy) % 4) * 4 + ((z + dz) % 2) * 2 + (c + dc) % 2
    return tok, ((l + dl) % 2) * 4 + (x + dx) % 4


class Links:
    def __init__(self, send_sems, recv_sems, local_sems):
        self.sems = (send_sems, recv_sems, local_sems)
        self.sent, self.locals = [], []

    def greet(self, partners):
        barrier = pltpu.get_barrier_semaphore()
        for offsets in partners:
            pl.semaphore_signal(
                barrier, inc=1, device_id=peer(**offsets), device_id_type=pl.DeviceIdType.MESH
            )
        pl.semaphore_wait(barrier, len(partners))

    def copy(self, number, source, target, offsets):
        return pltpu.make_async_remote_copy(
            src_ref=source,
            dst_ref=target,
            send_sem=self.sems[0].at[number],
            recv_sem=self.sems[1].at[number],
            device_id=peer(**offsets),
            device_id_type=pl.DeviceIdType.MESH,
        )

    def send(self, source, target, **offsets):
        copy = self.copy(len(self.sent), source, target, offsets)
        copy.start()
        self.sent.append(copy)
        return len(self.sent) - 1, offsets

    def arrived(self, ticket, place):
        self.copy(ticket[0], place, place, ticket[1]).wait_recv()

    def local(self, source, target):
        copy = pltpu.make_async_copy(source, target, self.sems[2].at[len(self.locals)])
        copy.start()
        self.locals.append([copy, True])
        return len(self.locals) - 1

    def settle(self, number):
        copy, pending = self.locals[number]
        if pending:
            copy.wait()
        self.locals[number][1] = False

    def close(self):
        for number in range(len(self.locals)):
            self.settle(number)
        for copy in self.sent:
            copy.wait_send()


def in_turn(tasks):
    tasks = list(tasks)
    while tasks:
        for task in list(tasks):
            try:
                next(task)
            except StopIteration:
                tasks.remove(task)


def ring_four(links, own, place, axis, landed):
    right = links.send(own, place(0, None), **{axis: 1})
    left = links.send(own, place(0, None), **{axis: -1})
    yield
    links.arrived(right, place(-1, None))
    on_right = links.send(place(-1, 0), place(-1, 0), **{axis: 1})
    landed(-1)
    yield
    links.arrived(left, place(1, None))
    on_left = links.send(place(1, 1), place(1, 1), **{axis: -1})
    landed(1)
    yield
    links.arrived(on_right, place(2, 0))
    links.arrived(on_left, place(2, 1))
    landed(2)


def half_of(ref, part):
    if part is None:
        return ref
    rows = ref.shape[0] // 2
    return ref.at[pl.ds(part * rows, rows)]


def gather_br(links, own, whole):
    unused_y, unused_z, unused_c, l, x = coords()

    def place(dl):
        return lambda dx, part: half_of(whole.at[(l + dl) % 2, (x + dx) % 4], part)

    kept = links.local(own, place(0)(0, None))
    across = links.send(own, place(0)(0, None), dl=1)
    near = ring_four(links, own, place(0), "dx", lambda d: None)
    next(near)
    yield
    links.arrived(across, place(1)(0, None))
    far = ring_four(links, place(1)(0, None), place(1), "dx", lambda d: None)
    next(far)
    for unused in near:
        yield
    for unused in far:
        yield
    links.settle(kept)


def gather_tok(links, own, whole):
    y, z, c, unused_l, unused_x = coords()
    passed = []

    def place(dz, dc=0):
        return lambda dy, part: half_of(
            whole.at[(y + dy) % 4, (z + dz) % 2, (c + dc) % 2], part
        )

    def passer(dz):
        def landed(dy):
            ref = place(dz)(dy, None)
            passed.append((links.send(ref, ref, dc=1), place(dz, 1)(dy, None)))

        return landed

    kept = links.local(own, place(0)(0, None))
    across = links.send(own, place(0)(0, None), dz=1)
    near = ring_four(links, own, place(0), "dy", passer(0))
    next(near)
    passed.append((links.send(own, place(0)(0, None), dc=1), place(0, 1)(0, None)))
    yield
    links.arrived(across, place(1)(0, None))
    far = ring_four(links, place(1)(0, None), place(1), "dy", passer(1))
    next(far)
    passer(1)(0)
    for unused in near:
        yield
    for unused in far:
        yield
    links.settle(kept)
    for ticket, ref in passed:
        links.arrived(ticket, ref)


def add_up(target, sources, rows, finish):
    chunk = 16

    def step(i, unused):
        here = pl.ds(pl.multiple_of(i * chunk, chunk), chunk)
        total = sources[0][here, :].astype(F32)
        for source in sources[1:]:
            total = total + source[here, :].astype(F32)
        target[here, :] = finish(total, here).astype(target.dtype)
        return unused

    lax.fori_loop(0, rows // chunk, step, 0)


def plain(total, here):
    return total


def reduce_heads(links, grads, dq, dq_home, grads_home, mine, near, far, total):
    y, z, c, unused_l, unused_x = coords()
    order = (1, 3, 2, 0)
    held, from_core = {}, {}
    for dz in (1, 0):
        for d in order:
            place = ((y + d) % 4, (z + dz) % 2)
            from_core[d, dz] = links.send(
                grads.at[place[0], place[1], 1 - c], near.at[place[0], place[1]], dc=1
            )
            held[d, dz] = links.local(
                grads.at[place[0], place[1], c], mine.at[place[0], place[1]]
            )
    asked = [links.send(dq.at[(y + d) % 4], dq_home.at[y], dy=d) for d in order[:3]]
    links.local(dq.at[y], dq_home.at[y])
    yield
    rows = mine.shape[2]
    across = {}
    for d in order:
        here = (y + d) % 4
        links.arrived(from_core[d, 1], near.at[here, 1 - z])
        links.settle(held[d, 1])
        add_up(
            mine.at[here, 1 - z], [mine.at[here, 1 - z], near.at[here, 1 - z]], rows, plain
        )
        across[d] = links.send(mine.at[here, 1 - z], far.at[here], dz=1)
        yield
    home = {}
    for d in order:
        here = (y + d) % 4
        links.arrived(from_core[d, 0], near.at[here, z])
        links.settle(held[d, 0])
        links.arrived(across[d], far.at[here])
        add_up(
            total.at[here], [mine.at[here, z], near.at[here, z], far.at[here]], rows, plain
        )
        if d:
            home[d] = links.send(total.at[here], grads_home.at[y], dy=d)
        else:
            links.local(total.at[here], grads_home.at[y])
        yield
    for i, d in enumerate(order[:3]):
        links.arrived(asked[i], dq_home.at[(y - d) % 4])
        links.arrived(home[d], grads_home.at[(y - d) % 4])


class ScatterSpace:
    names = ("pieces", "near", "out", "far", "across", "sums", "side")

    def __init__(self, refs):
        for name, ref in zip(self.names, refs):
            setattr(self, name, ref)

    @staticmethod
    def shapes(rows, depth, half):
        if half == depth:
            sizes = ((2, 4, rows, depth), (3, 2, rows, depth), (rows, depth), (rows, depth))
            return [pltpu.VMEM(size, BF) for size in sizes]
        assert 2 * half == depth
        sizes = (
            (2, 4, rows, depth),
            (3, 2, rows, half),
            (rows, half),
            (rows, half),
            (4, rows, half),
            (4, rows, half),
            (3, rows, half),
        )
        return [pltpu.VMEM(size, BF) for size in sizes]


def scatter_br(links, make, space, target, finish):
    unused_y, unused_z, unused_c, l, x = coords()
    rows, half = space.out.shape
    split = half < target.shape[1]
    first, second = pl.ds(0, half), pl.ds(half, half)
    order = (1, 3, 2, 0)
    direct, folded, onward = {}, {}, {}
    for i, d in enumerate(order):
        there = (x + d) % 4
        make(there)
        if d:
            for dl in (1, 0):
                to = (l + dl) % 2
                direct[dl, i] = links.send(
                    space.pieces.at[to, there, :, first], space.near.at[i, to], dx=d
                )
        if split:
            folded[d] = links.send(
                space.pieces.at[1 - l, there, :, second], space.across.at[there], dl=1
            )
        yield
    for i in range(3):
        links.arrived(direct[1, i], space.near.at[i, 1 - l])
        yield
    mine = space.pieces.at[1 - l, x, :, first]
    add_up(space.out, [mine] + [space.near.at[i, 1 - l] for i in range(3)], rows, plain)
    over = links.send(space.out, space.far, dl=1)
    for i, d in enumerate(order if split else ()):
        there = (x + d) % 4
        links.arrived(folded[d], space.across.at[there])
        own = space.pieces.at[l, there, :, second]
        add_up(space.sums.at[there], [own, space.across.at[there]], rows, plain)
        if d:
            onward[i] = links.send(space.sums.at[there], space.side.at[i], dx=d)
        yield
    for i in range(3):
        links.arrived(direct[0, i], space.near.at[i, l])
    yield
    links.arrived(over, space.far)
    sources = [space.pieces.at[l, x, :, first]] + [space.near.at[i, l] for i in range(3)]
    add_up(target.at[:, first], sources + [space.far], rows, finish(0))
    if not split:
        return
    yield
    for i in range(3):
        links.arrived(onward[i], space.side.at[i])
    sources = [space.sums.at[x]] + [space.side.at[i] for i in range(3)]
    add_up(target.at[:, second], sources, rows, finish(half))


def reduce_tok(links, make, parts, near, side, out, far, target):
    y, z, c, unused_l, unused_x = coords()
    order = (1, 3, 2, 0)
    tickets = {}
    for d in order:
        here = (y + d) % 4
        make(here)
        tickets[d] = links.send(parts.at[here, :, 1 - c], near.at[here], dc=1)
        yield
    rows = out.shape[0]
    sent = {}
    for dz in (1, 0):
        k = (z + dz) % 2
        for i, d in enumerate(order):
            here = (y + d) % 4
            if dz:
                links.arrived(tickets[d], near.at[here])
            own = parts.at[here, k, c]
            add_up(own, [own, near.at[here, k]], rows, plain)
            if d:
                sent[dz, i] = links.send(own, side.at[i, k], dy=d)
            if dz:
                yield
    for i in range(3):
        links.arrived(sent[1, i], side.at[i, 1 - z])
        yield
    add_up(out, [parts.at[y, 1 - z, c]] + [side.at[i, 1 - z] for i in range(3)], rows, plain)
    across = links.send(out, far, dz=1)
    yield
    for i in range(3):
        links.arrived(sent[0, i], side.at[i, z])
    yield
    links.arrived(across, far)
    add_up(target, [parts.at[y, z, c]] + [side.at[i, z] for i in range(3)] + [far], rows, plain)


BR_NEAR = [dict(dl=1), dict(dx=1), dict(dx=-1)]
BR_ALL = BR_NEAR + [dict(dx=2)]
TOK_NEAR = [dict(dz=1), dict(dc=1), dict(dy=1), dict(dy=-1)]
TOK_ALL = TOK_NEAR + [dict(dy=2)]


def comm_call(
    kernel, name, number, args, outs, scratch=(), in_vmem=(), out_vmem=(), in_smem=(), copies=48
):
    return pl.pallas_call(
        kernel,
        out_shape=tuple(outs),
        in_specs=[
            VMEM if i in in_vmem else SMEM if i in in_smem else ANY for i in range(len(args))
        ],
        out_specs=tuple(VMEM if i in out_vmem else ANY for i in range(len(outs))),
        scratch_shapes=list(scratch)
        + [
            pltpu.SemaphoreType.DMA((copies,)),
            pltpu.SemaphoreType.DMA((copies,)),
            pltpu.SemaphoreType.DMA((32,)),
        ],
        compiler_params=pltpu.CompilerParams(
            collective_id=number, has_side_effects=True, vmem_limit_bytes=60 * 2**20
        ),
        cost_estimate=SMALL,
        name=name,
    )(*args)


def table_rows(table, block_map, slot, long_blocks):
    block = block_map[lax.axis_index("tok") * 2 + slot]
    place = jnp.where(block < long_blocks, block % LB, (block - long_blocks) % 2)
    return table[place]


def shift_rows(tokens, gain, bias, shifted):
    rows = tokens.shape[0]
    chunk = 16

    def step(i, unused):
        here = pl.ds(pl.multiple_of(i * chunk, chunk), chunk)
        value = tokens[here, :].astype(F32)
        value = value - jnp.mean(value, axis=-1, keepdims=True)
        scale = lax.rsqrt(jnp.mean(value * value, axis=-1, keepdims=True) + EPSILON)
        shifted[here, :] = (value * scale * gain[...] + bias[...]).astype(BF)
        return unused

    lax.fori_loop(0, rows // chunk, step, 0)


def turned(block):
    return jnp.transpose(block.astype(F32)).astype(BF)


def bias_places(heads, per):
    width = heads * HD
    places = np.zeros((128, 3 * width), np.float32)
    for column in range(3 * width):
        if column < width:
            part, head, lane = 0, column // HD, column % HD
        else:
            pair, lane = divmod(column - width, HD)
            part, head = 1 + pair % 2, pair // 2
        places[(part * heads + head) * per + lane % per, column] = 1.0
    return places


def start_kernel(
    heads,
    main,
    block_map,
    tokens,
    gain,
    bias,
    cot,
    qkv,
    qkv_bias,
    places,
    gate,
    up,
    down,
    out,
    table,
    x_out,
    g_out,
    w_out,
    f_out,
    kv_mine,
    q_heads,
    *rest,
):
    shifted, qkv_shard, ff_shard, held_x, held_w, pairs, queries, held_t = rest[:8]
    links = Links(*rest[8:])
    y, z, c, unused_l, unused_x = coords()
    width = heads * HD
    links.greet(BR_NEAR + TOK_ALL)
    rotary = links.local(table, held_t)
    shift_rows(tokens, gain, bias, shifted)
    rows, depth = tokens.shape
    kv = []
    for head in range(heads):
        lanes = slice(head * HD, (head + 1) * HD)
        kv += [qkv[1, :, lanes], qkv[2, :, lanes]]
    qkv_shard[:, : 3 * width] = jnp.concatenate([qkv[0]] + kv, axis=1)
    line = dot(qkv_bias[...], places[...], NN)
    lane = lax.broadcasted_iota(jnp.int32, line.shape, 1) % HD
    line = jnp.where(lane // (HD // 16) == lax.axis_index("tok"), line, 0.0)[:1]
    lines = [line[:, r * 128 : (r + 1) * 128] for r in range(3 * width // 128)]
    zero = jnp.zeros((qkv_shard.shape[0] - len(lines), 128), F32)
    qkv_shard[:, 3 * width :] = jnp.concatenate(lines + [zero], axis=0).astype(BF)

    def project(half):
        tile = 2 * rows
        here = slice(half * tile, (half + 1) * tile)
        span = held_x[:, 2 * half : 2 * half + 2].reshape(2 * tile, depth)
        corner = held_w[0, 0, 0, :8, 3 * width :].astype(F32)
        for t in range(1, 16):
            corner = corner + held_w[t // 4, t // 2 % 2, t % 2, :8, 3 * width :].astype(F32)
        added = jnp.concatenate([corner[r : r + 1] for r in range(len(lines))], axis=1)
        products = dot(span, held_w[...].reshape(depth, -1)[:, : 3 * width], NN) + added
        parts = []
        for slot in range(2):
            turns = table_rows(held_t, block_map, slot, 2 * LB)[here]
            joined = products[slot * tile : (slot + 1) * tile]
            parts.append(turn(joined[:, :width], turns, heads // 2, False, 1.0).astype(BF))
            kv = turn(joined[:, width:], turns, heads, True, 1.0).astype(BF)
            for head in range(heads):
                pairs[head, slot, here, :] = kv[:, head * 2 * HD : (head + 1) * 2 * HD]
        for head in range(heads):
            lanes = slice(head * HD, (head + 1) * HD)
            queries[head, here, :] = jnp.concatenate(
                [parts[0][:, lanes], parts[1][:, lanes]], axis=1
            )

    def attention():
        tasks = [gather_br(links, shifted, held_x), gather_tok(links, qkv_shard, held_w)]
        while tasks:
            for task in list(tasks):
                try:
                    next(task)
                except StopIteration:
                    tasks.remove(task)
            yield
        links.local(held_x, x_out)
        links.local(held_w, w_out)
        links.settle(rotary)
        for half in range(2):
            project(half)
        sent = [
            (d, links.send(pairs.at[(y + d) % 4], kv_mine.at[y], dy=d)) for d in (1, 3, 2)
        ]
        links.local(pairs.at[y], kv_mine.at[y])
        links.local(queries, q_heads)
        for unused in range(12):
            yield
        for d, ticket in sent:
            links.arrived(ticket, kv_mine.at[(y - d) % 4])

    def feed_forward():
        ff_shard[:, :main] = turned(down[:main, :])
        tail = down.shape[0] - main
        ends = jnp.concatenate([down[main:, :], jnp.zeros((128 - tail, rows), BF)], axis=0)
        ff_shard[:, main : main + 128] = turned(ends)
        at = main + 128
        ff_shard[:, at : at + width] = turned(out[...])
        at += width
        ff_shard[:, at : at + main] = turned(gate[:main, :])
        ff_shard[:, at + main : at + 2 * main] = turned(up[:main, :])
        ends = jnp.concatenate([gate[main:, :], up[main:, :]], axis=0)
        ff_shard[:, at + 2 * main :] = turned(ends)
        yield
        yield from gather_tok(links, ff_shard, f_out)

    def gradient():
        for unused in range(3):
            yield
        yield from gather_br(links, cot, g_out)

    in_turn([attention(), feed_forward(), gradient()])
    links.close()


def start(
    block_map, tokens, gain, bias, cot, qkv, qkv_bias, gate, up, down, out, table, heads, main
):
    rows, depth = tokens.shape
    wrows = qkv.shape[1]
    width = heads * HD
    cols = main + 128 + width + 2 * gate.shape[0]
    whole = jax.ShapeDtypeStruct((2, 4, rows, depth), BF)
    places = jnp.asarray(bias_places(heads, qkv_bias.shape[2]))
    flat = jnp.pad(qkv_bias.reshape(1, -1).astype(F32), ((0, 7), (0, 128 - qkv_bias.size)))
    args = (block_map, tokens, gain, bias, cot, qkv, flat, places, gate, up, down, out, table)
    copies = 72
    shapes = (
        whole,
        whole,
        jax.ShapeDtypeStruct((4, 2, 2, wrows, 3 * width + 128), BF),
        jax.ShapeDtypeStruct((4, 2, 2, wrows, cols), BF),
        jax.ShapeDtypeStruct((heads, 2, BLK, 2 * HD), BF),
        jax.ShapeDtypeStruct((heads, BLK, 2 * HD), BF),
    )
    specs = [SMEM] + [VMEM] * (len(args) - 1)
    specs[4] = specs[12] = ANY
    return pl.pallas_call(
        functools.partial(start_kernel, heads, main),
        out_shape=shapes,
        in_specs=specs,
        out_specs=(ANY,) * len(shapes),
        scratch_shapes=[
            pltpu.VMEM((rows, depth), BF),
            pltpu.VMEM((wrows, 3 * width + 128), BF),
            pltpu.VMEM((wrows, cols), BF),
            pltpu.VMEM(whole.shape, BF),
            pltpu.VMEM(shapes[2].shape, BF),
            pltpu.VMEM(shapes[4].shape, BF),
            pltpu.VMEM(shapes[5].shape, BF),
            pltpu.VMEM(table.shape, F32),
            pltpu.SemaphoreType.DMA((copies,)),
            pltpu.SemaphoreType.DMA((copies,)),
            pltpu.SemaphoreType.DMA((32,)),
        ],
        compiler_params=pltpu.CompilerParams(
            collective_id=0, has_side_effects=True, vmem_limit_bytes=60 * 2**20
        ),
        cost_estimate=SMALL,
        name="start",
    )(*args)


def ff_heads_kernel(
    main,
    down,
    first,
    x_ref,
    g_ref,
    x_strip,
    g_strip,
    weights,
    kv_mine,
    q_heads,
    h_ref,
    s_ref,
    grad_ref,
    asked,
    pairs,
    w_ref,
    held,
    held_hidden,
    outs,
    *sems,
):
    y, z, c, unused_l, unused_x = coords()
    step = pl.program_id(0)
    final = pl.num_programs(0) - 1
    links = Links(*sems)
    order = (1, 3, 2)
    rows = x_ref.shape[1]

    load = pltpu.make_async_copy(weights, w_ref, sems[2].at[0])
    kept = [
        pltpu.make_async_copy(kv_mine, pairs.at[:, z, c], sems[2].at[1]),
        pltpu.make_async_copy(q_heads.at[y], asked.at[y, 0], sems[2].at[2]),
    ]
    kept_out = pltpu.make_async_copy(outs.at[y], asked.at[y, 1], sems[2].at[3])
    number = iter(range(64))

    def plan(source, target, lands, **offsets):
        n = next(number)
        return links.copy(n, source, target, offsets), links.copy(n, lands, lands, offsets)

    def swap(source, k):
        return [
            plan(source.at[(y + d) % 4], asked.at[y, k], asked.at[(y - d) % 4, k], dy=d)
            for d in order
        ]

    far = [plan(kv_mine.at[i], pairs.at[i, z, c], pairs.at[i, 1 - z, c], dz=1) for i in range(4)]
    near = [plan(kv_mine.at[i], pairs.at[i, z, c], pairs.at[i, z, 1 - c], dc=1) for i in range(4)]
    diagonal = [
        plan(pairs.at[i, 1 - z, c], pairs.at[i, 1 - z, c], pairs.at[i, 1 - z, 1 - c], dc=1)
        for i in range(4)
    ]
    asked_q, asked_o = swap(q_heads, 0), swap(outs, 1)

    def cross(i):
        far[i][1].wait_recv()
        diagonal[i][0].start()

    @pl.when(step == 0)
    def _():
        load.start()
        links.greet([dict(dz=1), dict(dc=1), dict(dy=1), dict(dy=2), dict(dy=3)])
        for copy, unused in far + near + asked_q:
            copy.start()
        for copy in kept:
            copy.start()
        load.wait()

    def pause(point):
        @pl.when(step == 1)
        def _():
            cross(point)

    for i in range(2, 4):

        @pl.when(step == i + 1)
        def _():
            cross(i)

    here = pl.ds(pl.multiple_of(jnp.minimum(step, 1) * rows, rows), rows)

    def mixed_grad(value):
        for head in range(outs.shape[0]):
            lanes = slice(head * HD, (head + 1) * HD)
            outs[head, here, :] = jnp.concatenate(
                [value[:rows, lanes], value[rows:, lanes]], axis=1
            )

    @pl.when(step < 2)
    def _():
        grads, hidden = ff_part(
            main, down, first, x_ref[...], g_ref[...], w_ref, h_ref, s_ref, mixed_grad, pause
        )
        held[:, here, :] = grads.reshape(2, rows, -1)
        held_hidden[:, here, :] = hidden.reshape(2, rows, -1)

    @pl.when(step == 1)
    def _():
        for copy, unused in asked_o:
            copy.start()
        kept_out.start()

    @pl.when(step >= 2)
    def _():
        grads = held[...].reshape(-1, held.shape[2])
        hidden = held_hidden[...].reshape(-1, down)
        grad_ref[:, :down] = dot(g_strip[...], hidden, TN).astype(BF)
        grad_ref[:, down:] = dot(x_strip[...], grads, TN).astype(BF)

    @pl.when(step == final)
    def _():
        for copy in kept + [kept_out]:
            copy.wait()
        for unused, landed in near + diagonal + asked_q + asked_o:
            landed.wait_recv()
        for copy, unused in far + near + diagonal + asked_q + asked_o:
            copy.wait_send()


def ff_heads(x, g, w, kv_mine, q_heads, main, down, first):
    depth, cols = w.shape
    heads, unused, span, lanes = kv_mine.shape
    rows = BLK // 2
    both = cols - first
    strip = 512

    def tile(width):
        return pl.BlockSpec((2, rows, width), lambda i: (0, jnp.minimum(i, 1), 0))

    return pl.pallas_call(
        functools.partial(ff_heads_kernel, main, down, first),
        grid=(2 + depth // strip,),
        in_specs=[
            tile(depth),
            tile(depth),
            pl.BlockSpec((2 * BLK, strip), lambda i: (0, jnp.maximum(i - 2, 0))),
            pl.BlockSpec((2 * BLK, strip), lambda i: (0, jnp.maximum(i - 2, 0))),
            ANY,
            ANY,
            ANY,
        ],
        out_specs=(
            tile(down),
            tile(depth),
            pl.BlockSpec((strip, both + down), lambda i: (jnp.maximum(i - 2, 0), 0)),
            ANY,
            ANY,
        ),
        out_shape=(
            jax.ShapeDtypeStruct((2, BLK, down), BF),
            jax.ShapeDtypeStruct((2, BLK, depth), BF),
            jax.ShapeDtypeStruct((depth, both + down), BF),
            jax.ShapeDtypeStruct((4, 2, span, lanes), BF),
            jax.ShapeDtypeStruct((4, 2, 2, 2, span, lanes), BF),
        ),
        scratch_shapes=[
            pltpu.VMEM((depth, cols), BF),
            pltpu.VMEM((2, BLK, both), BF),
            pltpu.VMEM((2, BLK, down), BF),
            pltpu.VMEM(q_heads.shape, BF),
            pltpu.SemaphoreType.DMA((32,)),
            pltpu.SemaphoreType.DMA((32,)),
            pltpu.SemaphoreType.DMA((4,)),
        ],
        compiler_params=pltpu.CompilerParams(
            collective_id=1, has_side_effects=True, vmem_limit_bytes=60 * 2**20
        ),
        cost_estimate=SMALL,
        name="ff_heads",
    )(x, g, x.reshape(2 * BLK, depth), g.reshape(2 * BLK, depth), w, kv_mine, q_heads)


def residual(tokens, first):
    def finish(column):
        def add(value, here):
            at = first + column
            return value + tokens[here, at : at + value.shape[1]].astype(F32)

        return add

    return finish


def home_kernel(
    heads,
    grads,
    dq,
    o_parts,
    hidden,
    weights,
    tokens,
    dq_home,
    grads_home,
    mixed_out,
    result,
    later,
    *rest,
):
    mine, near, far, total, held_w, held_h, held_o, held_later = rest[:8]
    space = ScatterSpace(rest[8:12])
    links = Links(*rest[12:])
    y, unused_z, unused_c, unused_l, unused_x = coords()
    rows, depth = tokens.shape
    kept = held_w.shape[1]
    links.greet(BR_ALL + TOK_ALL)
    loads = [
        links.local(o_parts.at[y], held_o.at[y]),
        links.local(hidden, held_h),
        links.local(weights.at[:, pl.ds(0, kept)], held_w),
    ]
    returned = [
        (d, links.send(o_parts.at[(y + d) % 4], held_o.at[y], dy=d)) for d in (1, 3, 2)
    ]

    def make(there):
        here = pl.ds(pl.multiple_of(there * rows, rows), rows)
        mixed = [
            jnp.concatenate(
                [held_o[head, here, slot * HD : (slot + 1) * HD] for head in range(heads)],
                axis=1,
            )
            for slot in range(2)
        ]
        for slot in range(2):
            mixed_out[slot, here, :] = mixed[slot]
        both = jnp.concatenate(
            [held_h[:, here, :].reshape(2 * rows, -1), jnp.concatenate(mixed, axis=0)], axis=1
        )
        branches = dot(both, held_w[...], NT).astype(BF)
        half = space.pieces.shape[3]
        for slot in range(2):
            piece = branches[slot * rows : (slot + 1) * rows]
            space.pieces[slot, there] = piece[:, :half]
            held_later[slot, there] = piece[:, half:]
        links.local(held_later.at[:, there], later.at[:, there])

    def output():
        yield
        for d, ticket in returned:
            links.arrived(ticket, held_o.at[(y - d) % 4])
        for load in loads:
            links.settle(load)
        yield from scatter_br(links, make, space, result, residual(tokens, 0))

    in_turn(
        [
            reduce_heads(links, grads, dq, dq_home, grads_home, mine, near, far, total),
            output(),
        ]
    )
    links.close()


def heads_home(grads, dq, o_parts, hidden, weights, tokens, heads):
    rows, depth = tokens.shape
    span, lanes = grads.shape[3:]
    width = heads * HD
    kept = hidden.shape[2] + width
    return comm_call(
        functools.partial(home_kernel, heads),
        "heads_home",
        2,
        (grads, dq, o_parts, hidden, weights, tokens),
        (
            jax.ShapeDtypeStruct(dq.shape, BF),
            jax.ShapeDtypeStruct((4, span, lanes), BF),
            jax.ShapeDtypeStruct((2, BLK, width), BF),
            jax.ShapeDtypeStruct((rows, depth // 2), BF),
            jax.ShapeDtypeStruct((2, 4, rows, depth // 2), BF),
        ),
        scratch=[
            pltpu.VMEM((4, 2, span, lanes), BF),
            pltpu.VMEM((4, 2, span, lanes), BF),
            pltpu.VMEM((4, span, lanes), BF),
            pltpu.VMEM((4, span, lanes), BF),
            pltpu.VMEM((depth, kept), BF),
            pltpu.VMEM(hidden.shape, BF),
            pltpu.VMEM(o_parts.shape, BF),
            pltpu.VMEM((2, 4, rows, depth // 2), BF),
        ]
        + ScatterSpace.shapes(rows, depth // 2, depth // 2),
        in_vmem=(5,),
        out_vmem=(2, 3),
        copies=64,
    )


def normal_rows(tokens, normed, scales):
    rows = tokens.shape[0]
    chunk = 16

    def step(i, unused):
        here = pl.ds(pl.multiple_of(i * chunk, chunk), chunk)
        value = tokens[here, :].astype(F32)
        value = value - jnp.mean(value, axis=-1, keepdims=True)
        scale = lax.rsqrt(jnp.mean(value * value, axis=-1, keepdims=True) + EPSILON)
        normed[here, :] = value * scale
        scales[here, :] = jnp.broadcast_to(scale, (chunk, 128))
        return unused

    lax.fori_loop(0, rows // chunk, step, 0)


def turn_back(grads, normed, scales, cot, gain, parts, result):
    rows, depth = normed.shape
    chunk = 16

    def rows_at(i):
        return pl.ds(pl.multiple_of(i * chunk, chunk), chunk)

    def sums(i, carry):
        here = rows_at(i)
        grad = grads[here, :]
        up = (grad * normed[here, :]).reshape(2, 8, depth)
        return carry[0] + up.sum(0), carry[1] + grad.reshape(2, 8, depth).sum(0)

    zero = jnp.zeros((8, depth), F32)
    found = lax.fori_loop(0, rows // chunk, sums, (zero, zero))
    for k in range(2):
        line = jnp.sum(found[k], axis=0, keepdims=True)
        parts[16 * k : 16 * (k + 1), :] = jnp.concatenate(
            [line[:, t * 128 : (t + 1) * 128] for t in range(depth // 128)], axis=0
        )
    yield

    def back(i, unused):
        here = rows_at(i)
        line = normed[here, :]
        grad = grads[here, :] * gain[...]
        slope = jnp.mean(grad * line, axis=-1, keepdims=True)
        grad = grad - jnp.mean(grad, axis=-1, keepdims=True) - line * slope
        result[here, :] = cot[here, :].astype(F32) + scales[here, :1] * grad
        return unused

    lax.fori_loop(0, rows // chunk, back, 0)


BR_PEERS = [dict(dl=i // 4, dx=i % 4) for i in range(1, 8)]
TOK_PEERS = [dict(dy=i // 4, dz=(i // 2) % 2, dc=i % 2) for i in range(1, 16)]


def last_kernel(
    heads,
    dq,
    dkv,
    table,
    x_in,
    g_in,
    m_in,
    w_in,
    s_in,
    tokens,
    cot,
    gain,
    block_map,
    later,
    result,
    qkv_out,
    out_out,
    late_out,
    sides,
    *rest,
):
    held_q, held_kv, held_t, held_x, held_g, held_m, held_w, held_s, gj = rest[:9]
    parts, near, side, out, far, wsum, summed, normed, scales = rest[9:18]
    lines, lines_in, last, last_in = rest[18:22]
    space = ScatterSpace(rest[22:29])
    late = ScatterSpace(rest[29:33])
    links = Links(*rest[33:])
    y, z, c, l, x = coords()
    links.greet(BR_PEERS + TOK_PEERS)
    width = heads * HD
    rows, depth = tokens.shape
    branches = [links.local(later, late.pieces)]
    first = [
        links.local(dq, held_q),
        links.local(dkv, held_kv),
        links.local(table, held_t),
    ]
    second = [
        links.local(x_in, held_x),
        links.local(g_in, held_g),
        links.local(m_in, held_m),
    ]
    third = [links.local(w_in.at[:, pl.ds(0, 3 * width)], held_w), links.local(s_in, held_s)]
    for load in first:
        links.settle(load)
    total = jnp.zeros((1, 3 * width), F32)
    for slot in range(2):
        for half in range(2):
            here = slice(half * BLK // 2, (half + 1) * BLK // 2)
            lanes = slice(slot * HD, (slot + 1) * HD)
            turns = table_rows(held_t, block_map, slot, 2 * LB)[here]
            q = jnp.concatenate([held_q[h, here, lanes] for h in range(heads)], axis=1)
            q = turn(q.astype(F32), turns, heads // 2, False, -1.0).astype(BF)
            kv = jnp.concatenate([held_kv[h, slot, here] for h in range(heads)], axis=1)
            kv = turn(kv.astype(F32), turns, heads, True, -1.0).astype(BF)
            both = jnp.concatenate([q, kv], axis=1)
            gj[slot, here, :] = both
            total += jnp.sum(both.astype(F32), axis=0, keepdims=True)
    line = [total[:, :width]]
    for k in range(2):
        at = [width + (2 * h + k) * HD for h in range(heads)]
        line.append(jnp.concatenate([total[:, a : a + HD] for a in at], axis=1))
    line = jnp.concatenate(line, axis=1)
    bias_sums = jnp.concatenate(
        [line[:, r * 128 : (r + 1) * 128] for r in range(3 * width // 128)], axis=0
    )
    for load in second:
        links.settle(load)
    wrows = parts.shape[3]
    strip = 4 * wrows

    def weights_of(there):
        here = pl.ds(pl.multiple_of(there * strip, strip), strip)
        qkv = dot(held_x[:, here], gj[...].reshape(2 * BLK, 3 * width), TN).astype(BF)
        outs = dot(held_g[:, here], held_m[...], TN).astype(BF)
        for k in range(4):
            at = slice(k * wrows, (k + 1) * wrows)
            parts[there, k // 2, k % 2, :, : 3 * width] = qkv[at]
            parts[there, k // 2, k % 2, :, 3 * width : 4 * width] = outs[at]

    def rows_of(there):
        if third:
            for load in third:
                links.settle(load)
            third.clear()
        here = pl.ds(pl.multiple_of(there * rows, rows), rows)
        both = gj[:, here, :].reshape(2 * rows, 3 * width)
        grads = dot(both, held_w[...], NT)
        for slot in range(2):
            value = grads[slot * rows : (slot + 1) * rows] + held_s[slot, here, :].astype(F32)
            space.pieces[slot, there] = value.astype(BF)

    def loaded(there):
        for load in branches:
            links.settle(load)
        branches.clear()

    def aside():
        for unused in range(5):
            yield
        normal_rows(tokens, normed, scales)

    in_turn(
        [
            reduce_tok(links, weights_of, parts, near, side, out, far, wsum),
            scatter_br(links, rows_of, space, summed, lambda column: plain),
            scatter_br(links, loaded, late, late_out, residual(tokens, depth // 2)),
            aside(),
        ]
    )
    through = turn_back(summed, normed, scales, cot, gain, lines, result)
    next(through)
    tickets = [links.send(lines, lines_in.at[i], **o) for i, o in enumerate(BR_PEERS)]
    for unused in through:
        pass
    total = lines[...]
    for i, ticket in enumerate(tickets):
        links.arrived(ticket, lines_in.at[i])
        total = total + lines_in[i]
    for t in range(16):
        last[t] = jnp.concatenate([total[t : t + 1], total[16 + t : 17 + t], bias_sums], axis=0)
    tickets = []
    for i, o in enumerate(TOK_PEERS):
        there = ((y + o["dy"]) % 4) * 4 + ((z + o["dz"]) % 2) * 2 + (c + o["dc"]) % 2
        tickets.append(links.send(last.at[there], last_in.at[i], **o))
    qkv_out[0] = wsum[:, :width]
    for k in range(2):
        qkv_out[1 + k] = jnp.concatenate(
            [
                wsum[:, width + (2 * h + k) * HD : width + (2 * h + k + 1) * HD]
                for h in range(heads)
            ],
            axis=1,
        )
    out_out[...] = jnp.transpose(wsum[:, 3 * width : 4 * width])
    total = last[y * 4 + z * 2 + c]
    for i, ticket in enumerate(tickets):
        links.arrived(ticket, last_in.at[i])
        total = total + last_in[i]
    sides[...] = total
    links.close()


def last_sums(
    dq, dkv, table, x, g, mixed, w, partial_grad, tokens, cot, gain, block_map, later, heads
):
    rows, depth = tokens.shape
    wrows = depth // 16
    width = heads * HD
    cols = 4 * width
    return comm_call(
        functools.partial(last_kernel, heads),
        "last_sums",
        3,
        (dq, dkv, table, x, g, mixed, w, partial_grad, tokens, cot, gain, block_map, later),
        (
            jax.ShapeDtypeStruct((rows, depth), F32),
            jax.ShapeDtypeStruct((3, wrows, width), F32),
            jax.ShapeDtypeStruct((width, wrows), F32),
            jax.ShapeDtypeStruct((rows, depth // 2), BF),
            jax.ShapeDtypeStruct((8, 128), F32),
        ),
        scratch=[
            pltpu.VMEM(dq.shape, BF),
            pltpu.VMEM(dkv.shape, BF),
            pltpu.VMEM(table.shape, F32),
            pltpu.VMEM(x.shape, BF),
            pltpu.VMEM(g.shape, BF),
            pltpu.VMEM(mixed.shape, BF),
            pltpu.VMEM((depth, 3 * width), BF),
            pltpu.VMEM(partial_grad.shape, BF),
            pltpu.VMEM((2, BLK, 3 * width), BF),
            pltpu.VMEM((4, 2, 2, wrows, cols), BF),
            pltpu.VMEM((4, 2, wrows, cols), BF),
            pltpu.VMEM((3, 2, wrows, cols), BF),
            pltpu.VMEM((wrows, cols), BF),
            pltpu.VMEM((wrows, cols), BF),
            pltpu.VMEM((wrows, cols), F32),
            pltpu.VMEM((rows, depth), F32),
            pltpu.VMEM((rows, depth), F32),
            pltpu.VMEM((rows, 128), F32),
            pltpu.VMEM((32, 128), F32),
            pltpu.VMEM((7, 32, 128), F32),
            pltpu.VMEM((16, 8, 128), F32),
            pltpu.VMEM((15, 8, 128), F32),
        ]
        + ScatterSpace.shapes(rows, depth, depth // 2)
        + ScatterSpace.shapes(rows, depth // 2, depth // 2),
        in_vmem=(8, 9, 10),
        in_smem=(11,),
        out_vmem=(0, 1, 2, 3, 4),
        copies=96,
    )


def finish_kernel(main, grads, first, second, tokens, qkv, out, *outs):
    def lines(start, count):
        return jnp.transpose(grads[:, start : start + count].astype(F32))

    result, tokens_out, qkv_out, out_out, down, gate, up = outs
    half = first.shape[1]
    result[:, :half] = first[...]
    result[:, half:] = second[...]
    tokens_out[...] = tokens[...]
    qkv_out[...] = qkv[...]
    out_out[...] = out[...]
    tail = down.shape[0] - main
    down[:main, :] = lines(0, main)
    down[main:, :] = lines(main, 128)[:tail]
    at = main + 128
    gate[:main, :] = lines(at, main)
    up[:main, :] = lines(at + main, main)
    ends = lines(at + 2 * main, 128)
    gate[main:, :] = ends[:tail]
    up[main:, :] = ends[tail:]


def finish(grads, first, second, tokens, qkv, out, main, hidden_width):
    rows, half = first.shape
    shape = jax.ShapeDtypeStruct((hidden_width, grads.shape[0]), F32)
    return pl.pallas_call(
        functools.partial(finish_kernel, main),
        out_shape=(
            jax.ShapeDtypeStruct((rows, 2 * half), BF),
            jax.ShapeDtypeStruct(tokens.shape, F32),
            jax.ShapeDtypeStruct(qkv.shape, F32),
            jax.ShapeDtypeStruct(out.shape, F32),
        )
        + (shape,) * 3,
        in_specs=[VMEM] * 6,
        out_specs=(VMEM,) * 7,
        cost_estimate=SMALL,
        name="finish",
    )(grads, first, second, tokens, qkv, out)


def rotary_table():
    half = ROT // 2
    frequency = (ROPE_BASE ** (-(np.arange(half) * 2.0 / ROT))).astype(np.float32)
    angles = np.arange(LB * BLK, dtype=np.float32)[:, None] * frequency[None, :]
    cos, sin = np.cos(angles), np.sin(angles)
    one = np.ones((LB * BLK, HD - ROT), np.float32)
    table = np.concatenate([cos, cos, one, -sin, sin, 0.0 * one], axis=1)
    return table.astype(np.float32).reshape(LB, BLK, 2 * HD)


def body(
    tokens,
    norm_gain,
    norm_bias,
    qkv_weight,
    qkv_bias,
    out_weight,
    gate_weight,
    up_weight,
    down_weight,
    cotangent,
    block_map,
    lengths,
):
    tok = lax.axis_index("tok")
    y, z, c = tok // 4, (tok // 2) % 2, tok % 2
    total_blocks = block_map.shape[0]
    long_blocks = total_blocks // 2
    rows = tokens.shape[0]
    depth = tokens.shape[1]
    wrows = qkv_weight.shape[1]
    heads = qkv_bias.shape[1]
    width = heads * HD
    hidden_width = gate_weight.shape[1]
    main = hidden_width // 128 * 128
    tail = hidden_width - main

    down_width = main + 128
    first = down_width + width
    table = jnp.asarray(rotary_table())
    x, grad, qkv_full, ff_full, kv_mine, q_heads = start(
        block_map,
        tokens,
        norm_gain.reshape(1, depth),
        norm_bias.reshape(1, depth),
        cotangent,
        qkv_weight,
        qkv_bias,
        jnp.transpose(gate_weight),
        jnp.transpose(up_weight),
        down_weight,
        out_weight,
        table,
        heads,
        main,
    )
    x = x.reshape(2, BLK, depth)
    grad = grad.reshape(2, BLK, depth)
    qkv_full = qkv_full.reshape(16 * wrows, -1)
    ff_full = ff_full.reshape(16 * wrows, -1)

    slot_table = jnp.arange(total_blocks, dtype=jnp.int32)
    slot_of = jnp.sum(
        jnp.where(block_map[None, :] == slot_table[:, None], slot_table[None, :], 0), axis=1
    )
    key_slot = slot_of.astype(jnp.int32)
    from_tok = jnp.arange(4, dtype=jnp.int32) * 4 + z * 2 + c
    my_queries = jnp.stack([2 * from_tok, 2 * from_tok + 1], axis=1).reshape(-1)
    query_block = jnp.sum(
        jnp.where(my_queries[:, None] == slot_table[None, :], block_map[None, :], 0), axis=1
    ).astype(jnp.int32)
    query_row = jnp.where(
        query_block < long_blocks,
        query_block // LB,
        long_blocks // LB + (query_block - long_blocks) // 2,
    )
    row_table = jnp.arange(lengths.shape[0], dtype=jnp.int32)
    query_limit = jnp.sum(
        jnp.where(query_row[:, None] == row_table[None, :], lengths[None, :], 0), axis=1
    ).astype(jnp.int32)

    hidden, grad_x, grad_ff, qd_all, kv_all = ff_heads(
        x, grad, ff_full, kv_mine, q_heads, main, down_width, first
    )
    kv_all = kv_all.reshape(-1, 2 * HD)
    x = x.reshape(2 * BLK, depth)
    grad = grad.reshape(2 * BLK, depth)
    grad_ff = lax.psum_scatter(grad_ff, "tok", scatter_dimension=0, tiled=True)

    turned, lse, o_parts = attn_fwd(query_block, query_limit, key_slot, qd_all, kv_all, long_blocks)
    dq_parts, dkv_all = attn_bwd(
        query_block, query_limit, key_slot, qd_all, kv_all, turned, lse, long_blocks
    )
    dq_heads, dkv_heads, mixed, first_half, later = heads_home(
        dkv_all.reshape(4, 2, 2, 2 * BLK, 2 * HD), dq_parts, o_parts, hidden, ff_full, tokens, heads
    )
    grad_ff, dq_heads = lax.optimization_barrier((grad_ff, dq_heads))
    grad_tokens, grad_qkv, grad_out, second_half, sides = last_sums(
        dq_heads,
        dkv_heads.reshape(heads, 2, BLK, 2 * HD),
        table,
        x,
        grad,
        mixed.reshape(2 * BLK, width),
        qkv_full,
        grad_x,
        tokens,
        cotangent,
        norm_gain.reshape(1, depth),
        block_map,
        later,
        heads,
    )
    grad_qkv_bias = lax.dynamic_slice_in_dim(
        sides[2:].reshape(3, heads, HD), tok * qkv_bias.shape[2], qkv_bias.shape[2], 2
    )
    result, grad_tokens, grad_qkv, grad_out, grad_down, grad_gate, grad_up = finish(
        grad_ff, first_half, second_half, grad_tokens, grad_qkv, grad_out, main, hidden_width
    )

    sides = lax.dynamic_slice_in_dim(sides[:2], lax.axis_index("br") * 16, 16, 1)
    return (
        result,
        grad_tokens,
        sides[0],
        sides[1],
        grad_qkv,
        grad_qkv_bias,
        grad_out,
        jnp.transpose(grad_gate),
        jnp.transpose(grad_up),
        grad_down,
    )


def solution(mesh):
    in_specs = (
        P(("tok", "br"), None),
        P(),
        P(),
        P(None, "tok", "br"),
        P(None, "br", "tok"),
        P("br", "tok"),
        P("tok", "br"),
        P("tok", "br"),
        P("br", "tok"),
        P(("tok", "br"), None),
        P(),
        P(),
    )
    out_specs = (
        P(("tok", "br"), None),
        P(("tok", "br"), None),
        P(("tok", "br")),
        P(("tok", "br")),
        P(None, "tok", "br"),
        P(None, "br", "tok"),
        P("br", "tok"),
        P("tok", "br"),
        P("tok", "br"),
        P("br", "tok"),
    )
    return jax.shard_map(body, mesh=mesh, in_specs=in_specs, out_specs=out_specs, check_vma=False)
```

```python
import functools

import jax
import jax.numpy as jnp
import numpy as np
from jax import lax
from jax.experimental import pallas as pl
from jax.experimental.pallas import tpu as pltpu
from jax.sharding import PartitionSpec as P

HD = 64
ROT = 16
BLK = 512
LB = 8
EPSILON = 1e-05
ROPE_BASE = 10000.0
MASKED = -1e30
BF = jnp.bfloat16
F32 = jnp.float32
NN = (((1,), (0,)), ((), ()))
NT = (((1,), (1,)), ((), ()))
TN = (((0,), (0,)), ((), ()))
VMEM = pl.BlockSpec(memory_space=pltpu.VMEM)
SMEM = pl.BlockSpec(memory_space=pltpu.SMEM)
ANY = pl.BlockSpec(memory_space=pl.ANY)
SMALL = pl.CostEstimate(flops=1000, bytes_accessed=1000, transcendentals=0)


def dot(left, right, dims):
    return lax.dot_general(left, right, dims, preferred_element_type=F32)


def block_info(block, long_blocks):
    is_long = block < long_blocks
    place = jnp.where(is_long, block % LB, (block - long_blocks) % 2)
    return is_long, place, block - place


def lane_half(packed, half, upper):
    piece = packed[:, half * HD : (half + 1) * HD]
    zero = jnp.zeros_like(piece)
    return jnp.concatenate([zero, piece] if upper else [piece, zero], axis=1)


def allowed_pairs(place, step, limit):
    key_pos = step * BLK + lax.broadcasted_iota(jnp.int32, (BLK, BLK), 0)
    query_pos = place * BLK + lax.broadcasted_iota(jnp.int32, (BLK, BLK), 1)
    return (key_pos <= query_pos) & (key_pos < limit)


def attn_kernel(
    block_map, lengths, q_ref, kv_ref, o_ref, dq_ref, dkv_ref, slot_of, ot, lses, acc, dqt
):
    total_blocks = block_map.shape[0]
    long_blocks = total_blocks // 2
    own = lax.axis_index("tok") % 4

    def note(slot, unused):
        slot_of[block_map[slot]] = slot
        return unused

    lax.fori_loop(0, total_blocks, note, 0)

    def about(i, half):
        block = block_map[2 * (4 * i + own) + half]
        is_long, place, first = block_info(block, long_blocks)
        row = jnp.where(
            is_long, block // LB, long_blocks // LB + (block - long_blocks) // 2
        )
        return is_long, place, first, lengths[row]

    def rows_at(block):
        return pl.ds(pl.multiple_of(slot_of[block] * BLK, BLK), BLK)

    def forward(i, unused):
        packed = q_ref[i, 0]
        for half in range(2):
            is_long, place, first, limit = about(i, half)
            queries = lane_half(packed, half, False) * jnp.asarray(0.125, BF)

            def step(j, carry, masked):
                top, total, summed = carry
                kv = kv_ref[rows_at(first + j), :]
                scores = dot(kv, queries, NT)
                if masked:
                    scores = jnp.where(allowed_pairs(place, j, limit), scores, MASKED)
                new_top = jnp.maximum(top, jnp.max(scores, axis=0, keepdims=True))
                fade = jnp.exp(top - new_top)
                probs = jnp.exp(scores - new_top)
                total = total * fade + jnp.sum(probs, axis=0, keepdims=True)
                summed = summed * fade + dot(kv, probs.astype(BF), TN)
                return new_top, total, summed

            free = jnp.where(is_long, place, 0)
            carry = (
                jnp.full((1, BLK), MASKED, F32),
                jnp.zeros((1, BLK), F32),
                jnp.zeros((2 * HD, BLK), F32),
            )
            carry = lax.fori_loop(0, free, lambda j, c: step(j, c, False), carry)
            top, total, summed = lax.fori_loop(
                free, place + 1, lambda j, c: step(j, c, True), carry
            )
            lses[2 * i + half] = top + jnp.log(total)
            ot[i, half * HD : (half + 1) * HD, :] = summed[HD:, :] / total
        o_ref[i] = jnp.transpose(ot[i]).astype(BF)
        return unused

    lax.fori_loop(0, q_ref.shape[0], forward, 0)
    acc[...] = jnp.zeros_like(acc)

    def backward(i, unused):
        q_packed = q_ref[i, 0]
        d_packed = q_ref[i, 1]
        d_turned = jnp.transpose(d_packed.astype(F32))
        for half in range(2):
            is_long, place, first, limit = about(i, half)
            queries = lane_half(q_packed, half, False) * jnp.asarray(0.125, BF)
            grads = lane_half(d_packed, half, True)
            both = jnp.concatenate([queries, grads], axis=0)
            lanes = slice(half * HD, (half + 1) * HD)
            delta = jnp.sum(d_turned[lanes] * ot[i, lanes, :], axis=0, keepdims=True)
            lse = lses[2 * i + half]

            def step(j, total, masked):
                rows = rows_at(first + j)
                kv = kv_ref[rows, :]
                scores = dot(kv, queries, NT)
                if masked:
                    scores = jnp.where(allowed_pairs(place, j, limit), scores, MASKED)
                probs = jnp.exp(scores - lse)
                ds = (probs * (dot(kv, grads, NT) - delta)).astype(BF)
                acc[rows, :] += dot(jnp.concatenate([ds, probs.astype(BF)], axis=1), both, NN)
                return total + dot(kv, ds, TN)

            free = jnp.where(is_long, place, 0)
            total = lax.fori_loop(
                0, free, lambda j, c: step(j, c, False), jnp.zeros((2 * HD, BLK), F32)
            )
            total = lax.fori_loop(free, place + 1, lambda j, c: step(j, c, True), total)
            dqt[lanes, :] = total[:HD, :] * 0.125
        dq_ref[i] = jnp.transpose(dqt[...]).astype(BF)
        return unused

    lax.fori_loop(0, q_ref.shape[0], backward, 0)

    def finish(i, unused):
        rows = pl.ds(pl.multiple_of(i * BLK, BLK), BLK)
        dkv_ref[rows, :] = acc[rows, :].astype(BF)
        return unused

    lax.fori_loop(0, kv_ref.shape[0] // BLK, finish, 0)


def attention(block_map, lengths, qd, kv):
    n = qd.shape[0]
    shape = jax.ShapeDtypeStruct((n, BLK, 2 * HD), BF)
    return pl.pallas_call(
        attn_kernel,
        out_shape=(shape, shape, jax.ShapeDtypeStruct(kv.shape, BF)),
        in_specs=[SMEM, SMEM, VMEM, VMEM],
        out_specs=(VMEM, VMEM, VMEM),
        scratch_shapes=[
            pltpu.SMEM(block_map.shape, jnp.int32),
            pltpu.VMEM((n, 2 * HD, BLK), F32),
            pltpu.VMEM((2 * n, 1, BLK), F32),
            pltpu.VMEM(kv.shape, F32),
            pltpu.VMEM((2 * HD, BLK), F32),
        ],
        compiler_params=pltpu.CompilerParams(vmem_limit_bytes=60 * 2**20),
        cost_estimate=SMALL,
        name="attention",
    )(block_map, lengths, qd, kv)


def turn(values, table, copies, paired, sign):
    width = values.shape[1]
    lane = lax.broadcasted_iota(jnp.int32, values.shape, 1) % HD
    partner = jnp.where(
        lane < ROT // 2,
        pltpu.roll(values, width - ROT // 2, 1),
        pltpu.roll(values, ROT // 2, 1),
    )
    cos, sin = table[:, :HD], sign * table[:, HD:]
    cos = jnp.concatenate([cos, jnp.ones_like(cos) if paired else cos], axis=1)
    sin = jnp.concatenate([sin, jnp.zeros_like(sin) if paired else sin], axis=1)
    cos = jnp.concatenate([cos] * copies, axis=1)
    sin = jnp.concatenate([sin] * copies, axis=1)
    return values * cos + partner * sin


def ff_part(main, down, first, x, g, w_ref, h_ref, s_ref, mixed_grad, pause):
    rows, depth = x.shape[1:]
    x = x.reshape(2 * rows, depth)
    g = g.reshape(2 * rows, depth)
    gate_up = dot(x, w_ref[:, first:], NN)
    pause(0)
    gh = dot(g, w_ref[:, :first], NN)
    mixed_grad(gh[:, down:].astype(BF))
    gh = gh[:, :down]
    ends = gate_up[:, 2 * main :]
    gate = jnp.concatenate([gate_up[:, :main], ends], axis=1)
    up = jnp.concatenate([gate_up[:, main : 2 * main], pltpu.roll(ends, HD, 1)], axis=1)
    sig = jax.nn.sigmoid(gate)
    silu = gate * sig
    hidden = (silu * up).astype(BF)
    d_gate = gh * up * sig * (1.0 + gate * (1.0 - sig))
    d_up = gh * silu
    tail = d_gate[:, main:] + pltpu.roll(d_up[:, main:], HD, 1)
    grads = jnp.concatenate(
        [d_gate[:, :main].astype(BF), d_up[:, :main].astype(BF), tail.astype(BF)], axis=1
    )
    h_ref[...] = hidden.reshape(h_ref.shape)
    pause(1)
    s_ref[...] = dot(grads, w_ref[:, first:], NT).astype(BF).reshape(s_ref.shape)
    return grads, hidden


def coords():
    tok, br = lax.axis_index("tok"), lax.axis_index("br")
    return tok // 4, (tok // 2) % 2, tok % 2, br // 4, br % 4


def peer(dy=0, dz=0, dc=0, dl=0, dx=0):
    y, z, c, l, x = coords()
    tok = ((y + dy) % 4) * 4 + ((z + dz) % 2) * 2 + (c + dc) % 2
    return tok, ((l + dl) % 2) * 4 + (x + dx) % 4


class Links:
    def __init__(self, send_sems, recv_sems, local_sems):
        self.sems = (send_sems, recv_sems, local_sems)
        self.sent, self.locals = [], []

    def greet(self, partners):
        barrier = pltpu.get_barrier_semaphore()
        for offsets in partners:
            pl.semaphore_signal(
                barrier, inc=1, device_id=peer(**offsets), device_id_type=pl.DeviceIdType.MESH
            )
        pl.semaphore_wait(barrier, len(partners))

    def copy(self, number, source, target, offsets):
        return pltpu.make_async_remote_copy(
            src_ref=source,
            dst_ref=target,
            send_sem=self.sems[0].at[number],
            recv_sem=self.sems[1].at[number],
            device_id=peer(**offsets),
            device_id_type=pl.DeviceIdType.MESH,
        )

    def send(self, source, target, **offsets):
        copy = self.copy(len(self.sent), source, target, offsets)
        copy.start()
        self.sent.append(copy)
        return len(self.sent) - 1, offsets

    def arrived(self, ticket, place):
        self.copy(ticket[0], place, place, ticket[1]).wait_recv()

    def local(self, source, target):
        copy = pltpu.make_async_copy(source, target, self.sems[2].at[len(self.locals)])
        copy.start()
        self.locals.append([copy, True])
        return len(self.locals) - 1

    def settle(self, number):
        copy, pending = self.locals[number]
        if pending:
            copy.wait()
        self.locals[number][1] = False

    def close(self):
        for number in range(len(self.locals)):
            self.settle(number)
        for copy in self.sent:
            copy.wait_send()


def in_turn(tasks):
    tasks = list(tasks)
    while tasks:
        for task in list(tasks):
            try:
                next(task)
            except StopIteration:
                tasks.remove(task)


def ring_four(links, own, place, axis, landed):
    right = links.send(own, place(0, None), **{axis: 1})
    left = links.send(own, place(0, None), **{axis: -1})
    yield
    links.arrived(right, place(-1, None))
    on_right = links.send(place(-1, 0), place(-1, 0), **{axis: 1})
    landed(-1)
    yield
    links.arrived(left, place(1, None))
    on_left = links.send(place(1, 1), place(1, 1), **{axis: -1})
    landed(1)
    yield
    links.arrived(on_right, place(2, 0))
    links.arrived(on_left, place(2, 1))
    landed(2)


def half_of(ref, part):
    if part is None:
        return ref
    rows = ref.shape[0] // 2
    return ref.at[pl.ds(part * rows, rows)]


def gather_br(links, own, whole):
    unused_y, unused_z, unused_c, l, x = coords()

    def place(dl):
        return lambda dx, part: half_of(whole.at[(l + dl) % 2, (x + dx) % 4], part)

    kept = links.local(own, place(0)(0, None))
    across = links.send(own, place(0)(0, None), dl=1)
    near = ring_four(links, own, place(0), "dx", lambda d: None)
    next(near)
    yield
    links.arrived(across, place(1)(0, None))
    far = ring_four(links, place(1)(0, None), place(1), "dx", lambda d: None)
    next(far)
    for unused in near:
        yield
    for unused in far:
        yield
    links.settle(kept)


def gather_tok(links, own, whole):
    y, z, c, unused_l, unused_x = coords()
    passed = []

    def place(dz, dc=0):
        return lambda dy, part: half_of(
            whole.at[(y + dy) % 4, (z + dz) % 2, (c + dc) % 2], part
        )

    def passer(dz):
        def landed(dy):
            ref = place(dz)(dy, None)
            passed.append((links.send(ref, ref, dc=1), place(dz, 1)(dy, None)))

        return landed

    kept = links.local(own, place(0)(0, None))
    across = links.send(own, place(0)(0, None), dz=1)
    near = ring_four(links, own, place(0), "dy", passer(0))
    next(near)
    passed.append((links.send(own, place(0)(0, None), dc=1), place(0, 1)(0, None)))
    yield
    links.arrived(across, place(1)(0, None))
    far = ring_four(links, place(1)(0, None), place(1), "dy", passer(1))
    next(far)
    passer(1)(0)
    for unused in near:
        yield
    for unused in far:
        yield
    links.settle(kept)
    for ticket, ref in passed:
        links.arrived(ticket, ref)


def add_up(target, sources, rows, finish):
    chunk = 16

    def step(i, unused):
        here = pl.ds(pl.multiple_of(i * chunk, chunk), chunk)
        total = sources[0][here, :].astype(F32)
        for source in sources[1:]:
            total = total + source[here, :].astype(F32)
        target[here, :] = finish(total, here).astype(target.dtype)
        return unused

    lax.fori_loop(0, rows // chunk, step, 0)


def plain(total, here):
    return total


def reduce_heads(links, grads, dq, dq_home, grads_home, mine, near, far, total):
    y, z, c, unused_l, unused_x = coords()
    order = (1, 3, 2, 0)
    held, from_core = {}, {}
    for dz in (1, 0):
        for d in order:
            place = ((y + d) % 4, (z + dz) % 2)
            from_core[d, dz] = links.send(
                grads.at[place[0], place[1], 1 - c], near.at[place[0], place[1]], dc=1
            )
            held[d, dz] = links.local(
                grads.at[place[0], place[1], c], mine.at[place[0], place[1]]
            )
    asked = [links.send(dq.at[(y + d) % 4], dq_home.at[y], dy=d) for d in order[:3]]
    links.local(dq.at[y], dq_home.at[y])
    yield
    rows = mine.shape[2]
    across = {}
    for d in order:
        here = (y + d) % 4
        links.arrived(from_core[d, 1], near.at[here, 1 - z])
        links.settle(held[d, 1])
        add_up(
            mine.at[here, 1 - z], [mine.at[here, 1 - z], near.at[here, 1 - z]], rows, plain
        )
        across[d] = links.send(mine.at[here, 1 - z], far.at[here], dz=1)
        yield
    home = {}
    for d in order:
        here = (y + d) % 4
        links.arrived(from_core[d, 0], near.at[here, z])
        links.settle(held[d, 0])
        links.arrived(across[d], far.at[here])
        add_up(
            total.at[here], [mine.at[here, z], near.at[here, z], far.at[here]], rows, plain
        )
        if d:
            home[d] = links.send(total.at[here], grads_home.at[y], dy=d)
        else:
            links.local(total.at[here], grads_home.at[y])
        yield
    for i, d in enumerate(order[:3]):
        links.arrived(asked[i], dq_home.at[(y - d) % 4])
        links.arrived(home[d], grads_home.at[(y - d) % 4])


class ScatterSpace:
    def __init__(self, refs):
        self.pieces, self.ring, self.out, self.far = refs[:4]
        if len(refs) > 4:
            self.across, self.sums, self.last = refs[4:]

    @staticmethod
    def shapes(rows, depth, half):
        def ring(parts, columns):
            return (parts, 2, rows + rows // 2, columns)

        sizes = [(2, 4, rows, depth), ring(2, half), (rows, half), (rows, half)]
        if half < depth:
            assert 2 * half == depth
            sizes += [(4, rows, half), (4, rows, half), ring(1, half)]
        return [pltpu.VMEM(size, BF) for size in sizes]


def ring_sum(links, pieces, ring, total, finish):
    unused_y, unused_z, unused_c, unused_l, x = coords()
    rows = total.shape[0]
    half = rows // 2
    halves = (pl.ds(0, half), pl.ds(half, half))
    passing = pl.ds(rows, half)
    whole = pl.ds(0, rows)
    opposite = pieces((x + 2) % 4)
    steps = (1, -1)
    first = [
        links.send(opposite.at[halves[k]], ring.at[k, passing], dx=steps[k]) for k in range(2)
    ]
    yield
    second = []
    for k in range(2):
        links.arrived(first[k], ring.at[k, passing])
        piece = pieces((x + steps[k]) % 4)
        add_up(
            piece.at[halves[k]], [piece.at[halves[k]], ring.at[k, passing]], half, plain
        )
        second.append(links.send(piece, ring.at[k, whole], dx=steps[k]))
        yield
    for k in range(2):
        links.arrived(second[k], ring.at[k, whole])
    add_up(total, [pieces(x), ring.at[0, whole], ring.at[1, whole]], rows, finish)


def scatter_br(links, make, space, target, finish):
    unused_y, unused_z, unused_c, l, x = coords()
    rows, half = space.out.shape
    split = half < target.shape[1]
    first, second = pl.ds(0, half), pl.ds(half, half)
    order = (2, 1, 3, 0)

    def part(to):
        return lambda there: space.pieces.at[to, there, :, first]

    folded = {}
    outer = ring_sum(links, part(1 - l), space.ring.at[0], space.out, plain)
    for d in order:
        there = (x + d) % 4
        make(there)
        if split:
            folded[d] = links.send(
                space.pieces.at[1 - l, there, :, second], space.across.at[there], dl=1
            )
        if d == 2:
            next(outer)
        yield
    inner = ring_sum(links, part(l), space.ring.at[1], target.at[:, first], finish(0))
    next(inner)
    yield from outer
    over = links.send(space.out, space.far, dl=1)
    next(inner)
    next(inner)
    yield
    rest = []
    for d in order if split else ():
        there = (x + d) % 4
        links.arrived(folded[d], space.across.at[there])
        own = space.pieces.at[l, there, :, second]
        add_up(space.sums.at[there], [own, space.across.at[there]], rows, plain)
        if d == 2:
            late = ring_sum(
                links,
                lambda there: space.sums.at[there],
                space.last.at[0],
                target.at[:, second],
                finish(half),
            )
            next(late)
            rest.append(late)
        yield

    def joined():
        links.arrived(over, space.far)
        mine = space.pieces.at[l, x, :, first]
        add_up(mine, [mine, space.far], rows, plain)
        yield
        yield from inner

    rest.append(joined())
    while rest:
        for task in list(rest):
            try:
                next(task)
            except StopIteration:
                rest.remove(task)
        yield


def reduce_tok(links, make, parts, near, side, out, far, target):
    y, z, c, unused_l, unused_x = coords()
    order = (1, 3, 2, 0)
    tickets = {}
    for d in order:
        here = (y + d) % 4
        make(here)
        tickets[d] = links.send(parts.at[here, :, 1 - c], near.at[here], dc=1)
        yield
    rows = out.shape[0]
    sent = {}
    for dz in (1, 0):
        k = (z + dz) % 2
        for i, d in enumerate(order):
            here = (y + d) % 4
            if dz:
                links.arrived(tickets[d], near.at[here])
            own = parts.at[here, k, c]
            add_up(own, [own, near.at[here, k]], rows, plain)
            if d:
                sent[dz, i] = links.send(own, side.at[i, k], dy=d)
            if dz:
                yield
    for i in range(3):
        links.arrived(sent[1, i], side.at[i, 1 - z])
        yield
    add_up(out, [parts.at[y, 1 - z, c]] + [side.at[i, 1 - z] for i in range(3)], rows, plain)
    across = links.send(out, far, dz=1)
    yield
    for i in range(3):
        links.arrived(sent[0, i], side.at[i, z])
    yield
    links.arrived(across, far)
    add_up(target, [parts.at[y, z, c]] + [side.at[i, z] for i in range(3)] + [far], rows, plain)


BR_NEAR = [dict(dl=1), dict(dx=1), dict(dx=-1)]
BR_ALL = BR_NEAR + [dict(dx=2)]
TOK_NEAR = [dict(dz=1), dict(dc=1), dict(dy=1), dict(dy=-1)]
TOK_ALL = TOK_NEAR + [dict(dy=2)]


def comm_call(
    kernel, name, number, args, outs, scratch=(), in_vmem=(), out_vmem=(), in_smem=(), copies=48
):
    return pl.pallas_call(
        kernel,
        out_shape=tuple(outs),
        in_specs=[
            VMEM if i in in_vmem else SMEM if i in in_smem else ANY for i in range(len(args))
        ],
        out_specs=tuple(VMEM if i in out_vmem else ANY for i in range(len(outs))),
        scratch_shapes=list(scratch)
        + [
            pltpu.SemaphoreType.DMA((copies,)),
            pltpu.SemaphoreType.DMA((copies,)),
            pltpu.SemaphoreType.DMA((32,)),
        ],
        compiler_params=pltpu.CompilerParams(
            collective_id=number, has_side_effects=True, vmem_limit_bytes=60 * 2**20
        ),
        cost_estimate=SMALL,
        name=name,
    )(*args)


def table_rows(table, block_map, slot, long_blocks):
    block = block_map[lax.axis_index("tok") * 2 + slot]
    place = jnp.where(block < long_blocks, block % LB, (block - long_blocks) % 2)
    return table[place]


def shift_rows(tokens, gain, bias, shifted):
    rows = tokens.shape[0]
    chunk = 16

    def step(i, unused):
        here = pl.ds(pl.multiple_of(i * chunk, chunk), chunk)
        value = tokens[here, :].astype(F32)
        value = value - jnp.mean(value, axis=-1, keepdims=True)
        scale = lax.rsqrt(jnp.mean(value * value, axis=-1, keepdims=True) + EPSILON)
        shifted[here, :] = (value * scale * gain[...] + bias[...]).astype(BF)
        return unused

    lax.fori_loop(0, rows // chunk, step, 0)


def turned(block):
    return jnp.transpose(block.astype(F32)).astype(BF)


def bias_places(heads, per):
    width = heads * HD
    places = np.zeros((128, 3 * width), np.float32)
    for column in range(3 * width):
        if column < width:
            part, head, lane = 0, column // HD, column % HD
        else:
            pair, lane = divmod(column - width, HD)
            part, head = 1 + pair % 2, pair // 2
        places[(part * heads + head) * per + lane % per, column] = 1.0
    return places


def start_kernel(
    heads,
    main,
    block_map,
    tokens,
    gain,
    bias,
    cot,
    qkv,
    qkv_bias,
    places,
    gate,
    up,
    down,
    out,
    table,
    x_out,
    g_out,
    w_out,
    f_out,
    kv_mine,
    q_heads,
    *rest,
):
    shifted, qkv_shard, ff_shard, held_x, held_w, pairs, queries, held_t = rest[:8]
    links = Links(*rest[8:])
    y, z, c, unused_l, unused_x = coords()
    width = heads * HD
    links.greet(BR_NEAR + TOK_ALL)
    rotary = links.local(table, held_t)
    shift_rows(tokens, gain, bias, shifted)
    rows, depth = tokens.shape
    kv = []
    for head in range(heads):
        lanes = slice(head * HD, (head + 1) * HD)
        kv += [qkv[1, :, lanes], qkv[2, :, lanes]]
    qkv_shard[:, : 3 * width] = jnp.concatenate([qkv[0]] + kv, axis=1)
    line = dot(qkv_bias[...], places[...], NN)
    lane = lax.broadcasted_iota(jnp.int32, line.shape, 1) % HD
    line = jnp.where(lane // (HD // 16) == lax.axis_index("tok"), line, 0.0)[:1]
    lines = [line[:, r * 128 : (r + 1) * 128] for r in range(3 * width // 128)]
    zero = jnp.zeros((qkv_shard.shape[0] - len(lines), 128), F32)
    qkv_shard[:, 3 * width :] = jnp.concatenate(lines + [zero], axis=0).astype(BF)

    def project(half):
        tile = 2 * rows
        here = slice(half * tile, (half + 1) * tile)
        span = held_x[:, 2 * half : 2 * half + 2].reshape(2 * tile, depth)
        corner = held_w[0, 0, 0, :8, 3 * width :].astype(F32)
        for t in range(1, 16):
            corner = corner + held_w[t // 4, t // 2 % 2, t % 2, :8, 3 * width :].astype(F32)
        added = jnp.concatenate([corner[r : r + 1] for r in range(len(lines))], axis=1)
        products = dot(span, held_w[...].reshape(depth, -1)[:, : 3 * width], NN) + added
        parts = []
        for slot in range(2):
            turns = table_rows(held_t, block_map, slot, 2 * LB)[here]
            joined = products[slot * tile : (slot + 1) * tile]
            parts.append(turn(joined[:, :width], turns, heads // 2, False, 1.0).astype(BF))
            kv = turn(joined[:, width:], turns, heads, True, 1.0).astype(BF)
            for head in range(heads):
                pairs[head, slot, here, :] = kv[:, head * 2 * HD : (head + 1) * 2 * HD]
        for head in range(heads):
            lanes = slice(head * HD, (head + 1) * HD)
            queries[head, here, :] = jnp.concatenate(
                [parts[0][:, lanes], parts[1][:, lanes]], axis=1
            )

    def attention():
        tasks = [gather_br(links, shifted, held_x), gather_tok(links, qkv_shard, held_w)]
        while tasks:
            for task in list(tasks):
                try:
                    next(task)
                except StopIteration:
                    tasks.remove(task)
            yield
        links.local(held_x, x_out)
        links.local(held_w, w_out)
        links.settle(rotary)
        for half in range(2):
            project(half)
        sent = [
            (d, links.send(pairs.at[(y + d) % 4], kv_mine.at[y], dy=d)) for d in (1, 3, 2)
        ]
        links.local(pairs.at[y], kv_mine.at[y])
        links.local(queries, q_heads)
        for unused in range(12):
            yield
        for d, ticket in sent:
            links.arrived(ticket, kv_mine.at[(y - d) % 4])

    def feed_forward():
        ff_shard[:, :main] = turned(down[:main, :])
        tail = down.shape[0] - main
        ends = jnp.concatenate([down[main:, :], jnp.zeros((128 - tail, rows), BF)], axis=0)
        ff_shard[:, main : main + 128] = turned(ends)
        at = main + 128
        ff_shard[:, at : at + width] = turned(out[...])
        at += width
        ff_shard[:, at : at + main] = turned(gate[:main, :])
        ff_shard[:, at + main : at + 2 * main] = turned(up[:main, :])
        ends = jnp.concatenate([gate[main:, :], up[main:, :]], axis=0)
        ff_shard[:, at + 2 * main :] = turned(ends)
        yield
        yield from gather_tok(links, ff_shard, f_out)

    def gradient():
        for unused in range(3):
            yield
        yield from gather_br(links, cot, g_out)

    in_turn([attention(), feed_forward(), gradient()])
    links.close()


def start(
    block_map, tokens, gain, bias, cot, qkv, qkv_bias, gate, up, down, out, table, heads, main
):
    rows, depth = tokens.shape
    wrows = qkv.shape[1]
    width = heads * HD
    cols = main + 128 + width + 2 * gate.shape[0]
    whole = jax.ShapeDtypeStruct((2, 4, rows, depth), BF)
    places = jnp.asarray(bias_places(heads, qkv_bias.shape[2]))
    flat = jnp.pad(qkv_bias.reshape(1, -1).astype(F32), ((0, 7), (0, 128 - qkv_bias.size)))
    args = (block_map, tokens, gain, bias, cot, qkv, flat, places, gate, up, down, out, table)
    copies = 72
    shapes = (
        whole,
        whole,
        jax.ShapeDtypeStruct((4, 2, 2, wrows, 3 * width + 128), BF),
        jax.ShapeDtypeStruct((4, 2, 2, wrows, cols), BF),
        jax.ShapeDtypeStruct((heads, 2, BLK, 2 * HD), BF),
        jax.ShapeDtypeStruct((heads, BLK, 2 * HD), BF),
    )
    specs = [SMEM] + [VMEM] * (len(args) - 1)
    specs[4] = specs[12] = ANY
    return pl.pallas_call(
        functools.partial(start_kernel, heads, main),
        out_shape=shapes,
        in_specs=specs,
        out_specs=(ANY,) * len(shapes),
        scratch_shapes=[
            pltpu.VMEM((rows, depth), BF),
            pltpu.VMEM((wrows, 3 * width + 128), BF),
            pltpu.VMEM((wrows, cols), BF),
            pltpu.VMEM(whole.shape, BF),
            pltpu.VMEM(shapes[2].shape, BF),
            pltpu.VMEM(shapes[4].shape, BF),
            pltpu.VMEM(shapes[5].shape, BF),
            pltpu.VMEM(table.shape, F32),
            pltpu.SemaphoreType.DMA((copies,)),
            pltpu.SemaphoreType.DMA((copies,)),
            pltpu.SemaphoreType.DMA((32,)),
        ],
        compiler_params=pltpu.CompilerParams(
            collective_id=0, has_side_effects=True, vmem_limit_bytes=60 * 2**20
        ),
        cost_estimate=SMALL,
        name="start",
    )(*args)


def ff_heads_kernel(
    main,
    down,
    first,
    x_ref,
    g_ref,
    x_strip,
    g_strip,
    weights,
    kv_mine,
    q_heads,
    h_ref,
    s_ref,
    grad_ref,
    asked,
    pairs,
    w_ref,
    held,
    held_hidden,
    outs,
    *sems,
):
    y, z, c, unused_l, unused_x = coords()
    step = pl.program_id(0)
    final = pl.num_programs(0) - 1
    links = Links(*sems)
    order = (1, 3, 2)
    rows = x_ref.shape[1]

    load = pltpu.make_async_copy(weights, w_ref, sems[2].at[0])
    kept = [
        pltpu.make_async_copy(kv_mine, pairs.at[:, z, c], sems[2].at[1]),
        pltpu.make_async_copy(q_heads.at[y], asked.at[y, 0], sems[2].at[2]),
    ]
    kept_out = pltpu.make_async_copy(outs.at[y], asked.at[y, 1], sems[2].at[3])
    number = iter(range(64))

    def plan(source, target, lands, **offsets):
        n = next(number)
        return links.copy(n, source, target, offsets), links.copy(n, lands, lands, offsets)

    def swap(source, k):
        return [
            plan(source.at[(y + d) % 4], asked.at[y, k], asked.at[(y - d) % 4, k], dy=d)
            for d in order
        ]

    far = [plan(kv_mine.at[i], pairs.at[i, z, c], pairs.at[i, 1 - z, c], dz=1) for i in range(4)]
    near = [plan(kv_mine.at[i], pairs.at[i, z, c], pairs.at[i, z, 1 - c], dc=1) for i in range(4)]
    diagonal = [
        plan(pairs.at[i, 1 - z, c], pairs.at[i, 1 - z, c], pairs.at[i, 1 - z, 1 - c], dc=1)
        for i in range(4)
    ]
    asked_q, asked_o = swap(q_heads, 0), swap(outs, 1)

    def cross(i):
        far[i][1].wait_recv()
        diagonal[i][0].start()

    @pl.when(step == 0)
    def _():
        load.start()
        links.greet([dict(dz=1), dict(dc=1), dict(dy=1), dict(dy=2), dict(dy=3)])
        for copy, unused in far + near + asked_q:
            copy.start()
        for copy in kept:
            copy.start()
        load.wait()

    def pause(point):
        @pl.when(step == 1)
        def _():
            cross(point)

    for i in range(2, 4):

        @pl.when(step == i + 1)
        def _():
            cross(i)

    here = pl.ds(pl.multiple_of(jnp.minimum(step, 1) * rows, rows), rows)

    def mixed_grad(value):
        for head in range(outs.shape[0]):
            lanes = slice(head * HD, (head + 1) * HD)
            outs[head, here, :] = jnp.concatenate(
                [value[:rows, lanes], value[rows:, lanes]], axis=1
            )

    @pl.when(step < 2)
    def _():
        grads, hidden = ff_part(
            main, down, first, x_ref[...], g_ref[...], w_ref, h_ref, s_ref, mixed_grad, pause
        )
        held[:, here, :] = grads.reshape(2, rows, -1)
        held_hidden[:, here, :] = hidden.reshape(2, rows, -1)

    @pl.when(step == 1)
    def _():
        for copy, unused in asked_o:
            copy.start()
        kept_out.start()

    @pl.when(step >= 2)
    def _():
        grads = held[...].reshape(-1, held.shape[2])
        hidden = held_hidden[...].reshape(-1, down)
        grad_ref[:, :down] = dot(g_strip[...], hidden, TN).astype(BF)
        grad_ref[:, down:] = dot(x_strip[...], grads, TN).astype(BF)

    @pl.when(step == final)
    def _():
        for copy in kept + [kept_out]:
            copy.wait()
        for unused, landed in near + diagonal + asked_q + asked_o:
            landed.wait_recv()
        for copy, unused in far + near + diagonal + asked_q + asked_o:
            copy.wait_send()


def ff_heads(x, g, w, kv_mine, q_heads, main, down, first):
    depth, cols = w.shape
    heads, unused, span, lanes = kv_mine.shape
    rows = BLK // 2
    both = cols - first
    strip = 512

    def tile(width):
        return pl.BlockSpec((2, rows, width), lambda i: (0, jnp.minimum(i, 1), 0))

    return pl.pallas_call(
        functools.partial(ff_heads_kernel, main, down, first),
        grid=(2 + depth // strip,),
        in_specs=[
            tile(depth),
            tile(depth),
            pl.BlockSpec((2 * BLK, strip), lambda i: (0, jnp.maximum(i - 2, 0))),
            pl.BlockSpec((2 * BLK, strip), lambda i: (0, jnp.maximum(i - 2, 0))),
            ANY,
            ANY,
            ANY,
        ],
        out_specs=(
            tile(down),
            tile(depth),
            pl.BlockSpec((strip, both + down), lambda i: (jnp.maximum(i - 2, 0), 0)),
            ANY,
            ANY,
        ),
        out_shape=(
            jax.ShapeDtypeStruct((2, BLK, down), BF),
            jax.ShapeDtypeStruct((2, BLK, depth), BF),
            jax.ShapeDtypeStruct((depth, both + down), BF),
            jax.ShapeDtypeStruct((4, 2, span, lanes), BF),
            jax.ShapeDtypeStruct((4, 2, 2, 2, span, lanes), BF),
        ),
        scratch_shapes=[
            pltpu.VMEM((depth, cols), BF),
            pltpu.VMEM((2, BLK, both), BF),
            pltpu.VMEM((2, BLK, down), BF),
            pltpu.VMEM(q_heads.shape, BF),
            pltpu.SemaphoreType.DMA((32,)),
            pltpu.SemaphoreType.DMA((32,)),
            pltpu.SemaphoreType.DMA((4,)),
        ],
        compiler_params=pltpu.CompilerParams(
            collective_id=1, has_side_effects=True, vmem_limit_bytes=60 * 2**20
        ),
        cost_estimate=SMALL,
        name="ff_heads",
    )(x, g, x.reshape(2 * BLK, depth), g.reshape(2 * BLK, depth), w, kv_mine, q_heads)


def residual(tokens):
    def finish(column):
        def add(value, here):
            return value + tokens[here, column : column + value.shape[1]].astype(F32)

        return add

    return finish


def home_kernel(
    heads,
    grads,
    dq,
    o_parts,
    hidden,
    weights,
    tokens,
    dq_home,
    grads_home,
    mixed_out,
    result,
    *rest,
):
    mine, near, far, total, held_w, held_h, held_o = rest[:7]
    space = ScatterSpace(rest[7:11])
    links = Links(*rest[11:])
    y, unused_z, unused_c, unused_l, unused_x = coords()
    rows, depth = tokens.shape
    kept = held_w.shape[1]
    links.greet(BR_NEAR + TOK_ALL)
    loads = [
        links.local(o_parts.at[y], held_o.at[y]),
        links.local(hidden, held_h),
        links.local(weights.at[:, pl.ds(0, kept)], held_w),
    ]
    returned = [
        (d, links.send(o_parts.at[(y + d) % 4], held_o.at[y], dy=d)) for d in (1, 3, 2)
    ]

    def make(there):
        here = pl.ds(pl.multiple_of(there * rows, rows), rows)
        mixed = [
            jnp.concatenate(
                [held_o[head, here, slot * HD : (slot + 1) * HD] for head in range(heads)],
                axis=1,
            )
            for slot in range(2)
        ]
        for slot in range(2):
            mixed_out[slot, here, :] = mixed[slot]
        both = jnp.concatenate(
            [held_h[:, here, :].reshape(2 * rows, -1), jnp.concatenate(mixed, axis=0)], axis=1
        )
        branches = dot(both, held_w[...], NT).astype(BF)
        for slot in range(2):
            space.pieces[slot, there] = branches[slot * rows : (slot + 1) * rows]

    def output():
        yield
        for d, ticket in returned:
            links.arrived(ticket, held_o.at[(y - d) % 4])
        for load in loads:
            links.settle(load)
        yield from scatter_br(links, make, space, result, residual(tokens))

    in_turn(
        [
            reduce_heads(links, grads, dq, dq_home, grads_home, mine, near, far, total),
            output(),
        ]
    )
    links.close()


def heads_home(grads, dq, o_parts, hidden, weights, tokens, heads):
    rows, depth = tokens.shape
    span, lanes = grads.shape[3:]
    width = heads * HD
    kept = hidden.shape[2] + width
    return comm_call(
        functools.partial(home_kernel, heads),
        "heads_home",
        2,
        (grads, dq, o_parts, hidden, weights, tokens),
        (
            jax.ShapeDtypeStruct(dq.shape, BF),
            jax.ShapeDtypeStruct((4, span, lanes), BF),
            jax.ShapeDtypeStruct((2, BLK, width), BF),
            jax.ShapeDtypeStruct((rows, depth), BF),
        ),
        scratch=[
            pltpu.VMEM((4, 2, span, lanes), BF),
            pltpu.VMEM((4, 2, span, lanes), BF),
            pltpu.VMEM((4, span, lanes), BF),
            pltpu.VMEM((4, span, lanes), BF),
            pltpu.VMEM((depth, kept), BF),
            pltpu.VMEM(hidden.shape, BF),
            pltpu.VMEM(o_parts.shape, BF),
        ]
        + ScatterSpace.shapes(rows, depth, depth),
        in_vmem=(5,),
        out_vmem=(2, 3),
        copies=64,
    )


def normal_rows(tokens, normed, scales):
    rows = tokens.shape[0]
    chunk = 16

    def step(i, unused):
        here = pl.ds(pl.multiple_of(i * chunk, chunk), chunk)
        value = tokens[here, :].astype(F32)
        value = value - jnp.mean(value, axis=-1, keepdims=True)
        scale = lax.rsqrt(jnp.mean(value * value, axis=-1, keepdims=True) + EPSILON)
        normed[here, :] = value * scale
        scales[here, :] = jnp.broadcast_to(scale, (chunk, 128))
        return unused

    lax.fori_loop(0, rows // chunk, step, 0)


def turn_back(grads, normed, scales, cot, gain, parts, result):
    rows, depth = normed.shape
    chunk = 16

    def rows_at(i):
        return pl.ds(pl.multiple_of(i * chunk, chunk), chunk)

    def sums(i, carry):
        here = rows_at(i)
        grad = grads[here, :]
        up = (grad * normed[here, :]).reshape(2, 8, depth)
        return carry[0] + up.sum(0), carry[1] + grad.reshape(2, 8, depth).sum(0)

    zero = jnp.zeros((8, depth), F32)
    found = lax.fori_loop(0, rows // chunk, sums, (zero, zero))
    for k in range(2):
        line = jnp.sum(found[k], axis=0, keepdims=True)
        parts[16 * k : 16 * (k + 1), :] = jnp.concatenate(
            [line[:, t * 128 : (t + 1) * 128] for t in range(depth // 128)], axis=0
        )
    yield

    def back(i, unused):
        here = rows_at(i)
        line = normed[here, :]
        grad = grads[here, :] * gain[...]
        slope = jnp.mean(grad * line, axis=-1, keepdims=True)
        grad = grad - jnp.mean(grad, axis=-1, keepdims=True) - line * slope
        result[here, :] = cot[here, :].astype(F32) + scales[here, :1] * grad
        return unused

    lax.fori_loop(0, rows // chunk, back, 0)


BR_PEERS = [dict(dl=i // 4, dx=i % 4) for i in range(1, 8)]
TOK_PEERS = [dict(dy=i // 4, dz=(i // 2) % 2, dc=i % 2) for i in range(1, 16)]


def last_kernel(
    heads,
    dq,
    dkv,
    table,
    x_in,
    g_in,
    m_in,
    w_in,
    s_in,
    tokens,
    cot,
    gain,
    block_map,
    result,
    qkv_out,
    out_out,
    sides,
    *rest,
):
    held_q, held_kv, held_t, held_x, held_g, held_m, held_w, held_s, gj = rest[:9]
    parts, near, side, out, far, wsum, summed, normed, scales = rest[9:18]
    lines, lines_in, last, last_in = rest[18:22]
    space = ScatterSpace(rest[22:29])
    links = Links(*rest[29:])
    y, z, c, l, x = coords()
    links.greet(BR_PEERS + TOK_PEERS)
    width = heads * HD
    rows, depth = tokens.shape
    first = [
        links.local(dq, held_q),
        links.local(dkv, held_kv),
        links.local(table, held_t),
    ]
    second = [
        links.local(x_in, held_x),
        links.local(g_in, held_g),
        links.local(m_in, held_m),
    ]
    third = [links.local(w_in.at[:, pl.ds(0, 3 * width)], held_w), links.local(s_in, held_s)]
    for load in first:
        links.settle(load)
    total = jnp.zeros((1, 3 * width), F32)
    for slot in range(2):
        for half in range(2):
            here = slice(half * BLK // 2, (half + 1) * BLK // 2)
            lanes = slice(slot * HD, (slot + 1) * HD)
            turns = table_rows(held_t, block_map, slot, 2 * LB)[here]
            q = jnp.concatenate([held_q[h, here, lanes] for h in range(heads)], axis=1)
            q = turn(q.astype(F32), turns, heads // 2, False, -1.0).astype(BF)
            kv = jnp.concatenate([held_kv[h, slot, here] for h in range(heads)], axis=1)
            kv = turn(kv.astype(F32), turns, heads, True, -1.0).astype(BF)
            both = jnp.concatenate([q, kv], axis=1)
            gj[slot, here, :] = both
            total += jnp.sum(both.astype(F32), axis=0, keepdims=True)
    line = [total[:, :width]]
    for k in range(2):
        at = [width + (2 * h + k) * HD for h in range(heads)]
        line.append(jnp.concatenate([total[:, a : a + HD] for a in at], axis=1))
    line = jnp.concatenate(line, axis=1)
    bias_sums = jnp.concatenate(
        [line[:, r * 128 : (r + 1) * 128] for r in range(3 * width // 128)], axis=0
    )
    for load in second:
        links.settle(load)
    wrows = parts.shape[3]
    strip = 4 * wrows

    def weights_of(there):
        here = pl.ds(pl.multiple_of(there * strip, strip), strip)
        qkv = dot(held_x[:, here], gj[...].reshape(2 * BLK, 3 * width), TN).astype(BF)
        outs = dot(held_g[:, here], held_m[...], TN).astype(BF)
        for k in range(4):
            at = slice(k * wrows, (k + 1) * wrows)
            parts[there, k // 2, k % 2, :, : 3 * width] = qkv[at]
            parts[there, k // 2, k % 2, :, 3 * width : 4 * width] = outs[at]

    def rows_of(there):
        if third:
            for load in third:
                links.settle(load)
            third.clear()
        here = pl.ds(pl.multiple_of(there * rows, rows), rows)
        both = gj[:, here, :].reshape(2 * rows, 3 * width)
        grads = dot(both, held_w[...], NT)
        for slot in range(2):
            value = grads[slot * rows : (slot + 1) * rows] + held_s[slot, here, :].astype(F32)
            space.pieces[slot, there] = value.astype(BF)

    def shifted():
        yield from scatter_br(links, rows_of, space, summed, lambda column: plain)
        through = turn_back(summed, normed, scales, cot, gain, lines, result)
        next(through)
        near_sums = [links.send(lines, lines_in.at[i], **o) for i, o in enumerate(BR_PEERS)]
        yield
        for unused in through:
            pass
        sums = lines[...]
        for i, ticket in enumerate(near_sums):
            links.arrived(ticket, lines_in.at[i])
            sums = sums + lines_in[i]
        for t in range(16):
            last[t] = jnp.concatenate([sums[t : t + 1], sums[16 + t : 17 + t], bias_sums], axis=0)
        all_sums = []
        for i, o in enumerate(TOK_PEERS):
            there = ((y + o["dy"]) % 4) * 4 + ((z + o["dz"]) % 2) * 2 + (c + o["dc"]) % 2
            all_sums.append(links.send(last.at[there], last_in.at[i], **o))
        yield
        yield
        sums = last[y * 4 + z * 2 + c]
        for i, ticket in enumerate(all_sums):
            links.arrived(ticket, last_in.at[i])
            sums = sums + last_in[i]
        sides[...] = sums

    def weights():
        yield from reduce_tok(links, weights_of, parts, near, side, out, far, wsum)
        qkv_out[0] = wsum[:, :width]
        for k in range(2):
            at = [width + (2 * h + k) * HD for h in range(heads)]
            qkv_out[1 + k] = jnp.concatenate([wsum[:, a : a + HD] for a in at], axis=1)
        out_out[...] = jnp.transpose(wsum[:, 3 * width :])

    def aside():
        for unused in range(5):
            yield
        normal_rows(tokens, normed, scales)

    in_turn([shifted(), weights(), aside()])
    links.close()


def last_sums(
    dq, dkv, table, x, g, mixed, w, partial_grad, tokens, cot, gain, block_map, heads
):
    rows, depth = tokens.shape
    wrows = depth // 16
    width = heads * HD
    cols = 4 * width
    return comm_call(
        functools.partial(last_kernel, heads),
        "last_sums",
        3,
        (dq, dkv, table, x, g, mixed, w, partial_grad, tokens, cot, gain, block_map),
        (
            jax.ShapeDtypeStruct((rows, depth), F32),
            jax.ShapeDtypeStruct((3, wrows, width), F32),
            jax.ShapeDtypeStruct((width, wrows), F32),
            jax.ShapeDtypeStruct((8, 128), F32),
        ),
        scratch=[
            pltpu.VMEM(dq.shape, BF),
            pltpu.VMEM(dkv.shape, BF),
            pltpu.VMEM(table.shape, F32),
            pltpu.VMEM(x.shape, BF),
            pltpu.VMEM(g.shape, BF),
            pltpu.VMEM(mixed.shape, BF),
            pltpu.VMEM((depth, 3 * width), BF),
            pltpu.VMEM(partial_grad.shape, BF),
            pltpu.VMEM((2, BLK, 3 * width), BF),
            pltpu.VMEM((4, 2, 2, wrows, cols), BF),
            pltpu.VMEM((4, 2, wrows, cols), BF),
            pltpu.VMEM((3, 2, wrows, cols), BF),
            pltpu.VMEM((wrows, cols), BF),
            pltpu.VMEM((wrows, cols), BF),
            pltpu.VMEM((wrows, cols), F32),
            pltpu.VMEM((rows, depth), F32),
            pltpu.VMEM((rows, depth), F32),
            pltpu.VMEM((rows, 128), F32),
            pltpu.VMEM((32, 128), F32),
            pltpu.VMEM((7, 32, 128), F32),
            pltpu.VMEM((16, 8, 128), F32),
            pltpu.VMEM((15, 8, 128), F32),
        ]
        + ScatterSpace.shapes(rows, depth, depth // 2),
        in_vmem=(8, 9, 10),
        in_smem=(11,),
        out_vmem=(0, 1, 2, 3),
        copies=96,
    )


def finish_kernel(main, grads, value, tokens, qkv, out, *outs):
    def lines(start, count):
        return jnp.transpose(grads[:, start : start + count].astype(F32))

    result, tokens_out, qkv_out, out_out, down, gate, up = outs
    result[...] = value[...]
    tokens_out[...] = tokens[...]
    qkv_out[...] = qkv[...]
    out_out[...] = out[...]
    tail = down.shape[0] - main
    down[:main, :] = lines(0, main)
    down[main:, :] = lines(main, 128)[:tail]
    at = main + 128
    gate[:main, :] = lines(at, main)
    up[:main, :] = lines(at + main, main)
    ends = lines(at + 2 * main, 128)
    gate[main:, :] = ends[:tail]
    up[main:, :] = ends[tail:]


def finish(grads, value, tokens, qkv, out, main, hidden_width):
    shape = jax.ShapeDtypeStruct((hidden_width, grads.shape[0]), F32)
    return pl.pallas_call(
        functools.partial(finish_kernel, main),
        out_shape=(
            jax.ShapeDtypeStruct(value.shape, BF),
            jax.ShapeDtypeStruct(tokens.shape, F32),
            jax.ShapeDtypeStruct(qkv.shape, F32),
            jax.ShapeDtypeStruct(out.shape, F32),
        )
        + (shape,) * 3,
        in_specs=[VMEM] * 5,
        out_specs=(VMEM,) * 7,
        cost_estimate=SMALL,
        name="finish",
    )(grads, value, tokens, qkv, out)


def rotary_table():
    half = ROT // 2
    frequency = (ROPE_BASE ** (-(np.arange(half) * 2.0 / ROT))).astype(np.float32)
    angles = np.arange(LB * BLK, dtype=np.float32)[:, None] * frequency[None, :]
    cos, sin = np.cos(angles), np.sin(angles)
    one = np.ones((LB * BLK, HD - ROT), np.float32)
    table = np.concatenate([cos, cos, one, -sin, sin, 0.0 * one], axis=1)
    return table.astype(np.float32).reshape(LB, BLK, 2 * HD)


def body(
    tokens,
    norm_gain,
    norm_bias,
    qkv_weight,
    qkv_bias,
    out_weight,
    gate_weight,
    up_weight,
    down_weight,
    cotangent,
    block_map,
    lengths,
):
    tok = lax.axis_index("tok")
    rows = tokens.shape[0]
    depth = tokens.shape[1]
    wrows = qkv_weight.shape[1]
    heads = qkv_bias.shape[1]
    width = heads * HD
    hidden_width = gate_weight.shape[1]
    main = hidden_width // 128 * 128
    tail = hidden_width - main

    down_width = main + 128
    first = down_width + width
    table = jnp.asarray(rotary_table())
    x, grad, qkv_full, ff_full, kv_mine, q_heads = start(
        block_map,
        tokens,
        norm_gain.reshape(1, depth),
        norm_bias.reshape(1, depth),
        cotangent,
        qkv_weight,
        qkv_bias,
        jnp.transpose(gate_weight),
        jnp.transpose(up_weight),
        down_weight,
        out_weight,
        table,
        heads,
        main,
    )
    x = x.reshape(2, BLK, depth)
    grad = grad.reshape(2, BLK, depth)
    qkv_full = qkv_full.reshape(16 * wrows, -1)
    ff_full = ff_full.reshape(16 * wrows, -1)

    hidden, grad_x, grad_ff, qd_all, kv_all = ff_heads(
        x, grad, ff_full, kv_mine, q_heads, main, down_width, first
    )
    kv_all = kv_all.reshape(-1, 2 * HD)
    x = x.reshape(2 * BLK, depth)
    grad = grad.reshape(2 * BLK, depth)
    grad_ff = lax.psum_scatter(grad_ff, "tok", scatter_dimension=0, tiled=True)

    o_parts, dq_parts, dkv_all = attention(block_map, lengths, qd_all, kv_all)
    dq_heads, dkv_heads, mixed, result = heads_home(
        dkv_all.reshape(4, 2, 2, 2 * BLK, 2 * HD), dq_parts, o_parts, hidden, ff_full, tokens, heads
    )
    grad_ff, dq_heads = lax.optimization_barrier((grad_ff, dq_heads))
    grad_tokens, grad_qkv, grad_out, sides = last_sums(
        dq_heads,
        dkv_heads.reshape(heads, 2, BLK, 2 * HD),
        table,
        x,
        grad,
        mixed.reshape(2 * BLK, width),
        qkv_full,
        grad_x,
        tokens,
        cotangent,
        norm_gain.reshape(1, depth),
        block_map,
        heads,
    )
    grad_qkv_bias = lax.dynamic_slice_in_dim(
        sides[2:].reshape(3, heads, HD), tok * qkv_bias.shape[2], qkv_bias.shape[2], 2
    )
    result, grad_tokens, grad_qkv, grad_out, grad_down, grad_gate, grad_up = finish(
        grad_ff, result, grad_tokens, grad_qkv, grad_out, main, hidden_width
    )

    sides = lax.dynamic_slice_in_dim(sides[:2], lax.axis_index("br") * 16, 16, 1)
    return (
        result,
        grad_tokens,
        sides[0],
        sides[1],
        grad_qkv,
        grad_qkv_bias,
        grad_out,
        jnp.transpose(grad_gate),
        jnp.transpose(grad_up),
        grad_down,
    )


def solution(mesh):
    in_specs = (
        P(("tok", "br"), None),
        P(),
        P(),
        P(None, "tok", "br"),
        P(None, "br", "tok"),
        P("br", "tok"),
        P("tok", "br"),
        P("tok", "br"),
        P("br", "tok"),
        P(("tok", "br"), None),
        P(),
        P(),
    )
    out_specs = (
        P(("tok", "br"), None),
        P(("tok", "br"), None),
        P(("tok", "br")),
        P(("tok", "br")),
        P(None, "tok", "br"),
        P(None, "br", "tok"),
        P("br", "tok"),
        P("tok", "br"),
        P("tok", "br"),
        P("br", "tok"),
    )
    return jax.shard_map(body, mesh=mesh, in_specs=in_specs, out_specs=out_specs, check_vma=False)
```

```python
import functools

import jax
import jax.numpy as jnp
import numpy as np
from jax import lax
from jax.experimental import pallas as pl
from jax.experimental.pallas import tpu as pltpu
from jax.sharding import PartitionSpec as P

HD = 64
ROT = 16
BLK = 512
LB = 8
EPSILON = 1e-05
ROPE_BASE = 10000.0
MASKED = -1e30
BF = jnp.bfloat16
F32 = jnp.float32
NN = (((1,), (0,)), ((), ()))
NT = (((1,), (1,)), ((), ()))
TN = (((0,), (0,)), ((), ()))
VMEM = pl.BlockSpec(memory_space=pltpu.VMEM)
SMEM = pl.BlockSpec(memory_space=pltpu.SMEM)
ANY = pl.BlockSpec(memory_space=pl.ANY)
SMALL = pl.CostEstimate(flops=1000, bytes_accessed=1000, transcendentals=0)


def dot(left, right, dims):
    return lax.dot_general(left, right, dims, preferred_element_type=F32)


def block_info(block, long_blocks):
    is_long = block < long_blocks
    place = jnp.where(is_long, block % LB, (block - long_blocks) % 2)
    return is_long, place, block - place


def lane_half(packed, half, upper):
    piece = packed[:, half * HD : (half + 1) * HD]
    zero = jnp.zeros_like(piece)
    return jnp.concatenate([zero, piece] if upper else [piece, zero], axis=1)


def allowed_pairs(place, step, limit):
    key_pos = step * BLK + lax.broadcasted_iota(jnp.int32, (BLK, BLK), 0)
    query_pos = place * BLK + lax.broadcasted_iota(jnp.int32, (BLK, BLK), 1)
    return (key_pos <= query_pos) & (key_pos < limit)


def attn_kernel(
    block_map, lengths, q_ref, kv_ref, o_ref, dq_ref, dkv_ref, slot_of, ot, lses, acc, dqt
):
    total_blocks = block_map.shape[0]
    long_blocks = total_blocks // 2
    own = lax.axis_index("tok") % 4

    def note(slot, unused):
        slot_of[block_map[slot]] = slot
        return unused

    lax.fori_loop(0, total_blocks, note, 0)

    def about(i, half):
        block = block_map[2 * (4 * i + own) + half]
        is_long, place, first = block_info(block, long_blocks)
        row = jnp.where(
            is_long, block // LB, long_blocks // LB + (block - long_blocks) // 2
        )
        return is_long, place, first, lengths[row]

    def rows_at(block):
        return pl.ds(pl.multiple_of(slot_of[block] * BLK, BLK), BLK)

    def forward(i, unused):
        packed = q_ref[i, 0]
        for half in range(2):
            is_long, place, first, limit = about(i, half)
            queries = lane_half(packed, half, False) * jnp.asarray(0.125, BF)

            def step(j, carry, masked):
                top, total, summed = carry
                kv = kv_ref[rows_at(first + j), :]
                scores = dot(kv, queries, NT)
                if masked:
                    scores = jnp.where(allowed_pairs(place, j, limit), scores, MASKED)
                new_top = jnp.maximum(top, jnp.max(scores, axis=0, keepdims=True))
                fade = jnp.exp(top - new_top)
                probs = jnp.exp(scores - new_top)
                total = total * fade + jnp.sum(probs, axis=0, keepdims=True)
                summed = summed * fade + dot(kv, probs.astype(BF), TN)
                return new_top, total, summed

            free = jnp.where(is_long, place, 0)
            carry = (
                jnp.full((1, BLK), MASKED, F32),
                jnp.zeros((1, BLK), F32),
                jnp.zeros((2 * HD, BLK), F32),
            )
            carry = lax.fori_loop(0, free, lambda j, c: step(j, c, False), carry)
            top, total, summed = lax.fori_loop(
                free, place + 1, lambda j, c: step(j, c, True), carry
            )
            lses[2 * i + half] = top + jnp.log(total)
            ot[i, half * HD : (half + 1) * HD, :] = summed[HD:, :] / total
        o_ref[i] = jnp.transpose(ot[i]).astype(BF)
        return unused

    lax.fori_loop(0, q_ref.shape[0], forward, 0)
    acc[...] = jnp.zeros_like(acc)

    def backward(i, unused):
        q_packed = q_ref[i, 0]
        d_packed = q_ref[i, 1]
        d_turned = jnp.transpose(d_packed.astype(F32))
        for half in range(2):
            is_long, place, first, limit = about(i, half)
            queries = lane_half(q_packed, half, False) * jnp.asarray(0.125, BF)
            grads = lane_half(d_packed, half, True)
            both = jnp.concatenate([queries, grads], axis=0)
            lanes = slice(half * HD, (half + 1) * HD)
            delta = jnp.sum(d_turned[lanes] * ot[i, lanes, :], axis=0, keepdims=True)
            lse = lses[2 * i + half]

            def step(j, total, masked):
                rows = rows_at(first + j)
                kv = kv_ref[rows, :]
                scores = dot(kv, queries, NT)
                if masked:
                    scores = jnp.where(allowed_pairs(place, j, limit), scores, MASKED)
                probs = jnp.exp(scores - lse)
                ds = (probs * (dot(kv, grads, NT) - delta)).astype(BF)
                acc[rows, :] += dot(jnp.concatenate([ds, probs.astype(BF)], axis=1), both, NN)
                return total + dot(kv, ds, TN)

            free = jnp.where(is_long, place, 0)
            total = lax.fori_loop(
                0, free, lambda j, c: step(j, c, False), jnp.zeros((2 * HD, BLK), F32)
            )
            total = lax.fori_loop(free, place + 1, lambda j, c: step(j, c, True), total)
            dqt[lanes, :] = total[:HD, :] * 0.125
        dq_ref[i] = jnp.transpose(dqt[...]).astype(BF)
        return unused

    lax.fori_loop(0, q_ref.shape[0], backward, 0)

    def finish(i, unused):
        rows = pl.ds(pl.multiple_of(i * BLK, BLK), BLK)
        dkv_ref[rows, :] = acc[rows, :].astype(BF)
        return unused

    lax.fori_loop(0, kv_ref.shape[0] // BLK, finish, 0)


def attention(block_map, lengths, qd, kv):
    n = qd.shape[0]
    shape = jax.ShapeDtypeStruct((n, BLK, 2 * HD), BF)
    return pl.pallas_call(
        attn_kernel,
        out_shape=(shape, shape, jax.ShapeDtypeStruct(kv.shape, BF)),
        in_specs=[SMEM, SMEM, VMEM, VMEM],
        out_specs=(VMEM, VMEM, VMEM),
        scratch_shapes=[
            pltpu.SMEM(block_map.shape, jnp.int32),
            pltpu.VMEM((n, 2 * HD, BLK), F32),
            pltpu.VMEM((2 * n, 1, BLK), F32),
            pltpu.VMEM(kv.shape, F32),
            pltpu.VMEM((2 * HD, BLK), F32),
        ],
        compiler_params=pltpu.CompilerParams(vmem_limit_bytes=60 * 2**20),
        cost_estimate=SMALL,
        name="attention",
    )(block_map, lengths, qd, kv)


def turn(values, table, copies, paired, sign):
    width = values.shape[1]
    lane = lax.broadcasted_iota(jnp.int32, values.shape, 1) % HD
    partner = jnp.where(
        lane < ROT // 2,
        pltpu.roll(values, width - ROT // 2, 1),
        pltpu.roll(values, ROT // 2, 1),
    )
    cos, sin = table[:, :HD], sign * table[:, HD:]
    cos = jnp.concatenate([cos, jnp.ones_like(cos) if paired else cos], axis=1)
    sin = jnp.concatenate([sin, jnp.zeros_like(sin) if paired else sin], axis=1)
    cos = jnp.concatenate([cos] * copies, axis=1)
    sin = jnp.concatenate([sin] * copies, axis=1)
    return values * cos + partner * sin


def ff_part(main, down, first, x, g, w_ref, h_ref, s_ref, mixed_grad, pause):
    rows, depth = x.shape[1:]
    x = x.reshape(2 * rows, depth)
    g = g.reshape(2 * rows, depth)
    gate_up = dot(x, w_ref[:, first:], NN)
    pause(0)
    gh = dot(g, w_ref[:, :first], NN)
    mixed_grad(gh[:, down:].astype(BF))
    gh = gh[:, :down]
    ends = gate_up[:, 2 * main :]
    gate = jnp.concatenate([gate_up[:, :main], ends], axis=1)
    up = jnp.concatenate([gate_up[:, main : 2 * main], pltpu.roll(ends, HD, 1)], axis=1)
    sig = jax.nn.sigmoid(gate)
    silu = gate * sig
    hidden = (silu * up).astype(BF)
    d_gate = gh * up * sig * (1.0 + gate * (1.0 - sig))
    d_up = gh * silu
    tail = d_gate[:, main:] + pltpu.roll(d_up[:, main:], HD, 1)
    grads = jnp.concatenate(
        [d_gate[:, :main].astype(BF), d_up[:, :main].astype(BF), tail.astype(BF)], axis=1
    )
    h_ref[...] = hidden.reshape(h_ref.shape)
    pause(1)
    s_ref[...] = dot(grads, w_ref[:, first:], NT).astype(BF).reshape(s_ref.shape)
    return grads, hidden


def coords():
    tok, br = lax.axis_index("tok"), lax.axis_index("br")
    return tok // 4, (tok // 2) % 2, tok % 2, br // 4, br % 4


def peer(dy=0, dz=0, dc=0, dl=0, dx=0):
    y, z, c, l, x = coords()
    tok = ((y + dy) % 4) * 4 + ((z + dz) % 2) * 2 + (c + dc) % 2
    return tok, ((l + dl) % 2) * 4 + (x + dx) % 4


class Links:
    def __init__(self, send_sems, recv_sems, local_sems):
        self.sems = (send_sems, recv_sems, local_sems)
        self.sent, self.locals = [], []

    def greet(self, partners):
        barrier = pltpu.get_barrier_semaphore()
        for offsets in partners:
            pl.semaphore_signal(
                barrier, inc=1, device_id=peer(**offsets), device_id_type=pl.DeviceIdType.MESH
            )
        pl.semaphore_wait(barrier, len(partners))

    def copy(self, number, source, target, offsets):
        return pltpu.make_async_remote_copy(
            src_ref=source,
            dst_ref=target,
            send_sem=self.sems[0].at[number],
            recv_sem=self.sems[1].at[number],
            device_id=peer(**offsets),
            device_id_type=pl.DeviceIdType.MESH,
        )

    def send(self, source, target, **offsets):
        copy = self.copy(len(self.sent), source, target, offsets)
        copy.start()
        self.sent.append(copy)
        return len(self.sent) - 1, offsets

    def arrived(self, ticket, place):
        self.copy(ticket[0], place, place, ticket[1]).wait_recv()

    def local(self, source, target):
        copy = pltpu.make_async_copy(source, target, self.sems[2].at[len(self.locals)])
        copy.start()
        self.locals.append([copy, True])
        return len(self.locals) - 1

    def settle(self, number):
        copy, pending = self.locals[number]
        if pending:
            copy.wait()
        self.locals[number][1] = False

    def close(self):
        for number in range(len(self.locals)):
            self.settle(number)
        for copy in self.sent:
            copy.wait_send()


def in_turn(tasks):
    tasks = list(tasks)
    while tasks:
        for task in list(tasks):
            try:
                next(task)
            except StopIteration:
                tasks.remove(task)


def ring_four(links, own, place, axis, landed):
    right = links.send(own, place(0, None), **{axis: 1})
    left = links.send(own, place(0, None), **{axis: -1})
    yield
    links.arrived(right, place(-1, None))
    on_right = links.send(place(-1, 0), place(-1, 0), **{axis: 1})
    landed(-1)
    yield
    links.arrived(left, place(1, None))
    on_left = links.send(place(1, 1), place(1, 1), **{axis: -1})
    landed(1)
    yield
    links.arrived(on_right, place(2, 0))
    links.arrived(on_left, place(2, 1))
    landed(2)


def half_of(ref, part):
    if part is None:
        return ref
    rows = ref.shape[0] // 2
    return ref.at[pl.ds(part * rows, rows)]


def gather_br(links, own, whole):
    unused_y, unused_z, unused_c, l, x = coords()

    def place(dl):
        return lambda dx, part: half_of(whole.at[(l + dl) % 2, (x + dx) % 4], part)

    kept = links.local(own, place(0)(0, None))
    across = links.send(own, place(0)(0, None), dl=1)
    near = ring_four(links, own, place(0), "dx", lambda d: None)
    next(near)
    yield
    links.arrived(across, place(1)(0, None))
    far = ring_four(links, place(1)(0, None), place(1), "dx", lambda d: None)
    next(far)
    for unused in near:
        yield
    for unused in far:
        yield
    links.settle(kept)


def gather_tok(links, own, whole):
    y, z, c, unused_l, unused_x = coords()
    passed = []

    def place(dz, dc=0):
        return lambda dy, part: half_of(
            whole.at[(y + dy) % 4, (z + dz) % 2, (c + dc) % 2], part
        )

    def passer(dz):
        def landed(dy):
            ref = place(dz)(dy, None)
            passed.append((links.send(ref, ref, dc=1), place(dz, 1)(dy, None)))

        return landed

    kept = links.local(own, place(0)(0, None))
    across = links.send(own, place(0)(0, None), dz=1)
    near = ring_four(links, own, place(0), "dy", passer(0))
    next(near)
    passed.append((links.send(own, place(0)(0, None), dc=1), place(0, 1)(0, None)))
    yield
    links.arrived(across, place(1)(0, None))
    far = ring_four(links, place(1)(0, None), place(1), "dy", passer(1))
    next(far)
    passer(1)(0)
    for unused in near:
        yield
    for unused in far:
        yield
    links.settle(kept)
    for ticket, ref in passed:
        links.arrived(ticket, ref)


def add_up(target, sources, rows, finish):
    chunk = 16

    def step(i, unused):
        here = pl.ds(pl.multiple_of(i * chunk, chunk), chunk)
        total = sources[0][here, :].astype(F32)
        for source in sources[1:]:
            total = total + source[here, :].astype(F32)
        target[here, :] = finish(total, here).astype(target.dtype)
        return unused

    lax.fori_loop(0, rows // chunk, step, 0)


def plain(total, here):
    return total


def reduce_heads(links, grads, dq, dq_home, grads_home, mine, near, far, total):
    y, z, c, unused_l, unused_x = coords()
    order = (1, 3, 2, 0)
    held, from_core = {}, {}
    for dz in (1, 0):
        for d in order:
            place = ((y + d) % 4, (z + dz) % 2)
            from_core[d, dz] = links.send(
                grads.at[place[0], place[1], 1 - c], near.at[place[0], place[1]], dc=1
            )
            held[d, dz] = links.local(
                grads.at[place[0], place[1], c], mine.at[place[0], place[1]]
            )
    asked = [links.send(dq.at[(y + d) % 4], dq_home.at[y], dy=d) for d in order[:3]]
    links.local(dq.at[y], dq_home.at[y])
    yield
    rows = mine.shape[2]
    across = {}
    for d in order:
        here = (y + d) % 4
        links.arrived(from_core[d, 1], near.at[here, 1 - z])
        links.settle(held[d, 1])
        add_up(
            mine.at[here, 1 - z], [mine.at[here, 1 - z], near.at[here, 1 - z]], rows, plain
        )
        across[d] = links.send(mine.at[here, 1 - z], far.at[here], dz=1)
        yield
    home = {}
    for d in order:
        here = (y + d) % 4
        links.arrived(from_core[d, 0], near.at[here, z])
        links.settle(held[d, 0])
        links.arrived(across[d], far.at[here])
        add_up(
            total.at[here], [mine.at[here, z], near.at[here, z], far.at[here]], rows, plain
        )
        if d:
            home[d] = links.send(total.at[here], grads_home.at[y], dy=d)
        else:
            links.local(total.at[here], grads_home.at[y])
        yield
    for i, d in enumerate(order[:3]):
        links.arrived(asked[i], dq_home.at[(y - d) % 4])
        links.arrived(home[d], grads_home.at[(y - d) % 4])


class ScatterSpace:
    def __init__(self, refs):
        self.pieces, self.ring, self.out, self.far = refs[:4]
        if len(refs) > 4:
            self.across, self.sums, self.last = refs[4:]

    @staticmethod
    def shapes(rows, depth, half):
        def ring(parts, columns):
            return (parts, 2, rows + rows // 2, columns)

        sizes = [(2, 4, rows, depth), ring(2, half), (rows, half), (rows, half)]
        rest = depth - half
        if rest:
            sizes += [(4, rows, rest), (4, rows, rest), ring(1, rest)]
        return [pltpu.VMEM(size, BF) for size in sizes]


def ring_sum(links, pieces, ring, total, finish):
    unused_y, unused_z, unused_c, unused_l, x = coords()
    rows = total.shape[0]
    half = rows // 2
    halves = (pl.ds(0, half), pl.ds(half, half))
    passing = pl.ds(rows, half)
    whole = pl.ds(0, rows)
    opposite = pieces((x + 2) % 4)
    steps = (1, -1)
    first = [
        links.send(opposite.at[halves[k]], ring.at[k, passing], dx=steps[k]) for k in range(2)
    ]
    yield
    second = []
    for k in range(2):
        links.arrived(first[k], ring.at[k, passing])
        piece = pieces((x + steps[k]) % 4)
        add_up(
            piece.at[halves[k]], [piece.at[halves[k]], ring.at[k, passing]], half, plain
        )
        second.append(links.send(piece, ring.at[k, whole], dx=steps[k]))
        yield
    for k in range(2):
        links.arrived(second[k], ring.at[k, whole])
    add_up(total, [pieces(x), ring.at[0, whole], ring.at[1, whole]], rows, finish)


def scatter_br(links, make, space, target, finish):
    unused_y, unused_z, unused_c, l, x = coords()
    rows, half = space.out.shape
    split = half < target.shape[1]
    first, second = pl.ds(0, half), pl.ds(half, target.shape[1] - half)
    order = (2, 1, 3, 0)

    def part(to):
        return lambda there: space.pieces.at[to, there, :, first]

    folded = {}
    outer = ring_sum(links, part(1 - l), space.ring.at[0], space.out, plain)
    for d in order:
        there = (x + d) % 4
        make(there)
        if split:
            folded[d] = links.send(
                space.pieces.at[1 - l, there, :, second], space.across.at[there], dl=1
            )
        if d == 2:
            next(outer)
        yield
    inner = ring_sum(links, part(l), space.ring.at[1], target.at[:, first], finish(0))
    next(inner)
    yield from outer
    over = links.send(space.out, space.far, dl=1)
    next(inner)
    next(inner)
    yield
    rest = []
    for d in order if split else ():
        there = (x + d) % 4
        links.arrived(folded[d], space.across.at[there])
        own = space.pieces.at[l, there, :, second]
        add_up(space.sums.at[there], [own, space.across.at[there]], rows, plain)
        if d == 2:
            late = ring_sum(
                links,
                lambda there: space.sums.at[there],
                space.last.at[0],
                target.at[:, second],
                finish(half),
            )
            next(late)
            rest.append(late)
        yield

    def joined():
        links.arrived(over, space.far)
        mine = space.pieces.at[l, x, :, first]
        add_up(mine, [mine, space.far], rows, plain)
        yield
        yield from inner

    rest.append(joined())
    while rest:
        for task in list(rest):
            try:
                next(task)
            except StopIteration:
                rest.remove(task)
        yield


def reduce_tok(links, make, parts, near, side, out, far, target):
    y, z, c, unused_l, unused_x = coords()
    order = (1, 3, 2, 0)
    tickets = {}
    for d in order:
        here = (y + d) % 4
        make(here)
        tickets[d] = links.send(parts.at[here, :, 1 - c], near.at[here], dc=1)
        yield
    rows = out.shape[0]
    sent = {}
    for dz in (1, 0):
        k = (z + dz) % 2
        for i, d in enumerate(order):
            here = (y + d) % 4
            if dz:
                links.arrived(tickets[d], near.at[here])
            own = parts.at[here, k, c]
            add_up(own, [own, near.at[here, k]], rows, plain)
            if d:
                sent[dz, i] = links.send(own, side.at[i, k], dy=d)
            if dz:
                yield
    for i in range(3):
        links.arrived(sent[1, i], side.at[i, 1 - z])
        yield
    add_up(out, [parts.at[y, 1 - z, c]] + [side.at[i, 1 - z] for i in range(3)], rows, plain)
    across = links.send(out, far, dz=1)
    yield
    for i in range(3):
        links.arrived(sent[0, i], side.at[i, z])
    yield
    links.arrived(across, far)
    add_up(target, [parts.at[y, z, c]] + [side.at[i, z] for i in range(3)] + [far], rows, plain)


BR_NEAR = [dict(dl=1), dict(dx=1), dict(dx=-1)]
BR_ALL = BR_NEAR + [dict(dx=2)]
TOK_NEAR = [dict(dz=1), dict(dc=1), dict(dy=1), dict(dy=-1)]
TOK_ALL = TOK_NEAR + [dict(dy=2)]


def comm_call(
    kernel, name, number, args, outs, scratch=(), in_vmem=(), out_vmem=(), in_smem=(), copies=48
):
    return pl.pallas_call(
        kernel,
        out_shape=tuple(outs),
        in_specs=[
            VMEM if i in in_vmem else SMEM if i in in_smem else ANY for i in range(len(args))
        ],
        out_specs=tuple(VMEM if i in out_vmem else ANY for i in range(len(outs))),
        scratch_shapes=list(scratch)
        + [
            pltpu.SemaphoreType.DMA((copies,)),
            pltpu.SemaphoreType.DMA((copies,)),
            pltpu.SemaphoreType.DMA((32,)),
        ],
        compiler_params=pltpu.CompilerParams(
            collective_id=number, has_side_effects=True, vmem_limit_bytes=60 * 2**20
        ),
        cost_estimate=SMALL,
        name=name,
    )(*args)


def table_rows(table, block_map, slot, here):
    block = block_map[lax.axis_index("tok") * 2 + slot]
    long_blocks = 2 * LB
    place = jnp.where(block < long_blocks, block % LB, (block - long_blocks) % 2)
    return table[place, here, :]


def shift_rows(tokens, gain, bias, shifted):
    rows = tokens.shape[0]
    chunk = 16

    def step(i, unused):
        here = pl.ds(pl.multiple_of(i * chunk, chunk), chunk)
        value = tokens[here, :].astype(F32)
        value = value - jnp.mean(value, axis=-1, keepdims=True)
        scale = lax.rsqrt(jnp.mean(value * value, axis=-1, keepdims=True) + EPSILON)
        shifted[here, :] = (value * scale * gain[...] + bias[...]).astype(BF)
        return unused

    lax.fori_loop(0, rows // chunk, step, 0)


def turned(block):
    return jnp.transpose(block.astype(F32)).astype(BF)


def bias_places(heads, per):
    width = heads * HD
    places = np.zeros((128, 3 * width), np.float32)
    for column in range(3 * width):
        if column < width:
            part, head, lane = 0, column // HD, column % HD
        else:
            pair, lane = divmod(column - width, HD)
            part, head = 1 + pair % 2, pair // 2
        places[(part * heads + head) * per + lane % per, column] = 1.0
    return places


def start_kernel(
    heads,
    main,
    block_map,
    tokens,
    gain,
    bias,
    cot,
    qkv,
    qkv_bias,
    places,
    gate,
    up,
    down,
    out,
    table,
    x_out,
    g_out,
    w_out,
    f_out,
    kv_mine,
    q_heads,
    *rest,
):
    shifted, qkv_shard, ff_shard, held_x, held_w, pairs, queries, held_t = rest[:8]
    links = Links(*rest[8:])
    y, z, c, unused_l, unused_x = coords()
    width = heads * HD
    links.greet(BR_NEAR + TOK_ALL)
    rotary = links.local(table, held_t)
    shift_rows(tokens, gain, bias, shifted)
    rows, depth = tokens.shape
    kv = []
    for head in range(heads):
        lanes = slice(head * HD, (head + 1) * HD)
        kv += [qkv[1, :, lanes], qkv[2, :, lanes]]
    qkv_shard[:, : 3 * width] = jnp.concatenate([qkv[0]] + kv, axis=1)
    line = dot(qkv_bias[...], places[...], NN)
    lane = lax.broadcasted_iota(jnp.int32, line.shape, 1) % HD
    line = jnp.where(lane // (HD // 16) == lax.axis_index("tok"), line, 0.0)[:1]
    lines = [line[:, r * 128 : (r + 1) * 128] for r in range(3 * width // 128)]
    zero = jnp.zeros((qkv_shard.shape[0] - len(lines), 128), F32)
    qkv_shard[:, 3 * width :] = jnp.concatenate(lines + [zero], axis=0).astype(BF)

    def project(half):
        tile = 2 * rows
        here = slice(half * tile, (half + 1) * tile)
        span = held_x[:, 2 * half : 2 * half + 2].reshape(2 * tile, depth)
        corner = held_w[0, 0, 0, :8, 3 * width :].astype(F32)
        for t in range(1, 16):
            corner = corner + held_w[t // 4, t // 2 % 2, t % 2, :8, 3 * width :].astype(F32)
        added = jnp.concatenate([corner[r : r + 1] for r in range(len(lines))], axis=1)
        products = dot(span, held_w[...].reshape(depth, -1)[:, : 3 * width], NN) + added
        parts = []
        for slot in range(2):
            turns = table_rows(held_t, block_map, slot, here)
            joined = products[slot * tile : (slot + 1) * tile]
            parts.append(turn(joined[:, :width], turns, heads // 2, False, 1.0).astype(BF))
            kv = turn(joined[:, width:], turns, heads, True, 1.0).astype(BF)
            for head in range(heads):
                pairs[head, slot, here, :] = kv[:, head * 2 * HD : (head + 1) * 2 * HD]
        for head in range(heads):
            lanes = slice(head * HD, (head + 1) * HD)
            queries[head, here, :] = jnp.concatenate(
                [parts[0][:, lanes], parts[1][:, lanes]], axis=1
            )

    def attention():
        tasks = [gather_br(links, shifted, held_x), gather_tok(links, qkv_shard, held_w)]
        while tasks:
            for task in list(tasks):
                try:
                    next(task)
                except StopIteration:
                    tasks.remove(task)
            yield
        links.local(held_x, x_out)
        links.local(held_w, w_out)
        links.settle(rotary)
        for half in range(2):
            project(half)
            yield
        sent = [
            (d, links.send(pairs.at[(y + d) % 4], kv_mine.at[y], dy=d)) for d in (1, 3, 2)
        ]
        links.local(pairs.at[y], kv_mine.at[y])
        links.local(queries, q_heads)
        for unused in range(12):
            yield
        for d, ticket in sent:
            links.arrived(ticket, kv_mine.at[(y - d) % 4])

    def feed_forward():
        ff_shard[:, :main] = turned(down[:main, :])
        tail = down.shape[0] - main
        ends = jnp.concatenate([down[main:, :], jnp.zeros((128 - tail, rows), BF)], axis=0)
        ff_shard[:, main : main + 128] = turned(ends)
        at = main + 128
        ff_shard[:, at : at + width] = turned(out[...])
        at += width
        ff_shard[:, at : at + main] = turned(gate[:main, :])
        ff_shard[:, at + main : at + 2 * main] = turned(up[:main, :])
        ends = jnp.concatenate([gate[main:, :], up[main:, :]], axis=0)
        ff_shard[:, at + 2 * main :] = turned(ends)
        yield
        yield from gather_tok(links, ff_shard, f_out)

    def gradient():
        for unused in range(3):
            yield
        yield from gather_br(links, cot, g_out)

    in_turn([attention(), feed_forward(), gradient()])
    links.close()


def start(
    block_map, tokens, gain, bias, cot, qkv, qkv_bias, gate, up, down, out, table, heads, main
):
    rows, depth = tokens.shape
    wrows = qkv.shape[1]
    width = heads * HD
    cols = main + 128 + width + 2 * gate.shape[0]
    whole = jax.ShapeDtypeStruct((2, 4, rows, depth), BF)
    places = jnp.asarray(bias_places(heads, qkv_bias.shape[2]))
    flat = jnp.pad(qkv_bias.reshape(1, -1).astype(F32), ((0, 7), (0, 128 - qkv_bias.size)))
    args = (block_map, tokens, gain, bias, cot, qkv, flat, places, gate, up, down, out, table)
    copies = 72
    shapes = (
        whole,
        whole,
        jax.ShapeDtypeStruct((4, 2, 2, wrows, 3 * width + 128), BF),
        jax.ShapeDtypeStruct((4, 2, 2, wrows, cols), BF),
        jax.ShapeDtypeStruct((heads, 2, BLK, 2 * HD), BF),
        jax.ShapeDtypeStruct((heads, BLK, 2 * HD), BF),
    )
    specs = [SMEM] + [VMEM] * (len(args) - 1)
    specs[4] = specs[12] = ANY
    return pl.pallas_call(
        functools.partial(start_kernel, heads, main),
        out_shape=shapes,
        in_specs=specs,
        out_specs=(ANY,) * len(shapes),
        scratch_shapes=[
            pltpu.VMEM((rows, depth), BF),
            pltpu.VMEM((wrows, 3 * width + 128), BF),
            pltpu.VMEM((wrows, cols), BF),
            pltpu.VMEM(whole.shape, BF),
            pltpu.VMEM(shapes[2].shape, BF),
            pltpu.VMEM(shapes[4].shape, BF),
            pltpu.VMEM(shapes[5].shape, BF),
            pltpu.VMEM(table.shape, F32),
            pltpu.SemaphoreType.DMA((copies,)),
            pltpu.SemaphoreType.DMA((copies,)),
            pltpu.SemaphoreType.DMA((32,)),
        ],
        compiler_params=pltpu.CompilerParams(
            collective_id=0, has_side_effects=True, vmem_limit_bytes=60 * 2**20
        ),
        cost_estimate=SMALL,
        name="start",
    )(*args)


def ff_heads_kernel(
    main,
    down,
    first,
    x_ref,
    g_ref,
    x_strip,
    g_strip,
    weights,
    kv_mine,
    q_heads,
    h_ref,
    s_ref,
    grad_ref,
    asked,
    pairs,
    w_ref,
    held,
    held_hidden,
    outs,
    *sems,
):
    y, z, c, unused_l, unused_x = coords()
    step = pl.program_id(0)
    final = pl.num_programs(0) - 1
    links = Links(*sems)
    order = (1, 3, 2)
    rows = x_ref.shape[1]

    loads = [
        pltpu.make_async_copy(weights.at[:, part], w_ref.at[:, part], sems[2].at[n])
        for n, part in ((0, pl.ds(first, w_ref.shape[1] - first)), (4, pl.ds(0, first)))
    ]
    kept = [
        pltpu.make_async_copy(kv_mine, pairs.at[:, z, c], sems[2].at[1]),
        pltpu.make_async_copy(q_heads.at[y], asked.at[y, 0], sems[2].at[2]),
    ]
    kept_out = pltpu.make_async_copy(outs.at[y], asked.at[y, 1], sems[2].at[3])
    number = iter(range(64))

    def plan(source, target, lands, **offsets):
        n = next(number)
        return links.copy(n, source, target, offsets), links.copy(n, lands, lands, offsets)

    def swap(source, k):
        return [
            plan(source.at[(y + d) % 4], asked.at[y, k], asked.at[(y - d) % 4, k], dy=d)
            for d in order
        ]

    far = [plan(kv_mine.at[i], pairs.at[i, z, c], pairs.at[i, 1 - z, c], dz=1) for i in range(4)]
    near = [plan(kv_mine.at[i], pairs.at[i, z, c], pairs.at[i, z, 1 - c], dc=1) for i in range(4)]
    diagonal = [
        plan(pairs.at[i, 1 - z, c], pairs.at[i, 1 - z, c], pairs.at[i, 1 - z, 1 - c], dc=1)
        for i in range(4)
    ]
    asked_q, asked_o = swap(q_heads, 0), swap(outs, 1)

    def cross(i):
        far[i][1].wait_recv()
        diagonal[i][0].start()

    @pl.when(step == 0)
    def _():
        for load in loads:
            load.start()
        links.greet([dict(dz=1), dict(dc=1), dict(dy=1), dict(dy=2), dict(dy=3)])
        for copy, unused in far + near + asked_q:
            copy.start()
        for copy in kept:
            copy.start()
        loads[0].wait()

    def pause(point):
        if point == 0:

            @pl.when(step == 0)
            def _():
                loads[1].wait()

        @pl.when(step == 1)
        def _():
            cross(point)

    for i in range(2, 4):

        @pl.when(step == i + 1)
        def _():
            cross(i)

    here = pl.ds(pl.multiple_of(jnp.minimum(step, 1) * rows, rows), rows)

    def mixed_grad(value):
        for head in range(outs.shape[0]):
            lanes = slice(head * HD, (head + 1) * HD)
            outs[head, here, :] = jnp.concatenate(
                [value[:rows, lanes], value[rows:, lanes]], axis=1
            )

    @pl.when(step < 2)
    def _():
        grads, hidden = ff_part(
            main, down, first, x_ref[...], g_ref[...], w_ref, h_ref, s_ref, mixed_grad, pause
        )
        held[:, here, :] = grads.reshape(2, rows, -1)
        held_hidden[:, here, :] = hidden.reshape(2, rows, -1)

    @pl.when(step == 1)
    def _():
        for copy, unused in asked_o:
            copy.start()
        kept_out.start()

    @pl.when(step >= 2)
    def _():
        grads = held[...].reshape(-1, held.shape[2])
        hidden = held_hidden[...].reshape(-1, down)
        grad_ref[:, :down] = dot(g_strip[...], hidden, TN).astype(BF)
        grad_ref[:, down:] = dot(x_strip[...], grads, TN).astype(BF)

    @pl.when(step == final)
    def _():
        for copy in kept + [kept_out]:
            copy.wait()
        for unused, landed in near + diagonal + asked_q + asked_o:
            landed.wait_recv()
        for copy, unused in far + near + diagonal + asked_q + asked_o:
            copy.wait_send()


def ff_heads(x, g, w, kv_mine, q_heads, main, down, first):
    depth, cols = w.shape
    heads, unused, span, lanes = kv_mine.shape
    rows = BLK // 2
    both = cols - first
    strip = 512

    def tile(width):
        return pl.BlockSpec((2, rows, width), lambda i: (0, jnp.minimum(i, 1), 0))

    return pl.pallas_call(
        functools.partial(ff_heads_kernel, main, down, first),
        grid=(2 + depth // strip,),
        in_specs=[
            tile(depth),
            tile(depth),
            pl.BlockSpec((2 * BLK, strip), lambda i: (0, jnp.maximum(i - 2, 0))),
            pl.BlockSpec((2 * BLK, strip), lambda i: (0, jnp.maximum(i - 2, 0))),
            ANY,
            ANY,
            ANY,
        ],
        out_specs=(
            tile(down),
            tile(depth),
            pl.BlockSpec((strip, both + down), lambda i: (jnp.maximum(i - 2, 0), 0)),
            ANY,
            ANY,
        ),
        out_shape=(
            jax.ShapeDtypeStruct((2, BLK, down), BF),
            jax.ShapeDtypeStruct((2, BLK, depth), BF),
            jax.ShapeDtypeStruct((depth, both + down), BF),
            jax.ShapeDtypeStruct((4, 2, span, lanes), BF),
            jax.ShapeDtypeStruct((4, 2, 2, 2, span, lanes), BF),
        ),
        scratch_shapes=[
            pltpu.VMEM((depth, cols), BF),
            pltpu.VMEM((2, BLK, both), BF),
            pltpu.VMEM((2, BLK, down), BF),
            pltpu.VMEM(q_heads.shape, BF),
            pltpu.SemaphoreType.DMA((32,)),
            pltpu.SemaphoreType.DMA((32,)),
            pltpu.SemaphoreType.DMA((5,)),
        ],
        compiler_params=pltpu.CompilerParams(
            collective_id=1, has_side_effects=True, vmem_limit_bytes=60 * 2**20
        ),
        cost_estimate=SMALL,
        name="ff_heads",
    )(x, g, x.reshape(2 * BLK, depth), g.reshape(2 * BLK, depth), w, kv_mine, q_heads)


def residual(tokens):
    def finish(column):
        def add(value, here):
            return value + tokens[here, column : column + value.shape[1]].astype(F32)

        return add

    return finish


def home_kernel(
    heads,
    grads,
    dq,
    o_parts,
    hidden,
    weights,
    tokens,
    dq_home,
    grads_home,
    mixed_out,
    result,
    *rest,
):
    mine, near, far, total, held_w, held_h, held_o = rest[:7]
    space = ScatterSpace(rest[7:11])
    links = Links(*rest[11:])
    y, unused_z, unused_c, unused_l, unused_x = coords()
    rows, depth = tokens.shape
    kept = held_w.shape[1]
    links.greet(BR_NEAR + TOK_ALL)
    loads = [
        links.local(o_parts.at[y], held_o.at[y]),
        links.local(hidden, held_h),
        links.local(weights.at[:, pl.ds(0, kept)], held_w),
    ]
    returned = [
        (d, links.send(o_parts.at[(y + d) % 4], held_o.at[y], dy=d)) for d in (1, 3, 2)
    ]

    def make(there):
        here = pl.ds(pl.multiple_of(there * rows, rows), rows)
        mixed = [
            jnp.concatenate(
                [held_o[head, here, slot * HD : (slot + 1) * HD] for head in range(heads)],
                axis=1,
            )
            for slot in range(2)
        ]
        for slot in range(2):
            mixed_out[slot, here, :] = mixed[slot]
        both = jnp.concatenate(
            [held_h[:, here, :].reshape(2 * rows, -1), jnp.concatenate(mixed, axis=0)], axis=1
        )
        branches = dot(both, held_w[...], NT).astype(BF)
        for slot in range(2):
            space.pieces[slot, there] = branches[slot * rows : (slot + 1) * rows]

    def output():
        yield
        for d, ticket in returned:
            links.arrived(ticket, held_o.at[(y - d) % 4])
        for load in loads:
            links.settle(load)
        yield from scatter_br(links, make, space, result, residual(tokens))

    in_turn(
        [
            reduce_heads(links, grads, dq, dq_home, grads_home, mine, near, far, total),
            output(),
        ]
    )
    links.close()


def heads_home(grads, dq, o_parts, hidden, weights, tokens, heads):
    rows, depth = tokens.shape
    span, lanes = grads.shape[3:]
    width = heads * HD
    kept = hidden.shape[2] + width
    return comm_call(
        functools.partial(home_kernel, heads),
        "heads_home",
        2,
        (grads, dq, o_parts, hidden, weights, tokens),
        (
            jax.ShapeDtypeStruct(dq.shape, BF),
            jax.ShapeDtypeStruct((4, span, lanes), BF),
            jax.ShapeDtypeStruct((2, BLK, width), BF),
            jax.ShapeDtypeStruct((rows, depth), BF),
        ),
        scratch=[
            pltpu.VMEM((4, 2, span, lanes), BF),
            pltpu.VMEM((4, 2, span, lanes), BF),
            pltpu.VMEM((4, span, lanes), BF),
            pltpu.VMEM((4, span, lanes), BF),
            pltpu.VMEM((depth, kept), BF),
            pltpu.VMEM(hidden.shape, BF),
            pltpu.VMEM(o_parts.shape, BF),
        ]
        + ScatterSpace.shapes(rows, depth, depth),
        in_vmem=(5,),
        out_vmem=(2, 3),
        copies=64,
    )


def normal_rows(tokens, normed, scales):
    rows = tokens.shape[0]
    chunk = 16

    def step(i, unused):
        here = pl.ds(pl.multiple_of(i * chunk, chunk), chunk)
        value = tokens[here, :].astype(F32)
        value = value - jnp.mean(value, axis=-1, keepdims=True)
        scale = lax.rsqrt(jnp.mean(value * value, axis=-1, keepdims=True) + EPSILON)
        normed[here, :] = value * scale
        scales[here, :] = jnp.broadcast_to(scale, (chunk, 128))
        return unused

    lax.fori_loop(0, rows // chunk, step, 0)


def turn_back(grads, normed, scales, cot, gain, parts, result):
    rows, depth = normed.shape
    chunk = 16

    def rows_at(i):
        return pl.ds(pl.multiple_of(i * chunk, chunk), chunk)

    def sums(i, carry):
        here = rows_at(i)
        grad = grads[here, :]
        up = (grad * normed[here, :]).reshape(2, 8, depth)
        return carry[0] + up.sum(0), carry[1] + grad.reshape(2, 8, depth).sum(0)

    zero = jnp.zeros((8, depth), F32)
    found = lax.fori_loop(0, rows // chunk, sums, (zero, zero))
    for k in range(2):
        line = jnp.sum(found[k], axis=0, keepdims=True)
        parts[16 * k : 16 * (k + 1), :] = jnp.concatenate(
            [line[:, t * 128 : (t + 1) * 128] for t in range(depth // 128)], axis=0
        )
    yield

    def back(i, unused):
        here = rows_at(i)
        line = normed[here, :]
        grad = grads[here, :] * gain[...]
        slope = jnp.mean(grad * line, axis=-1, keepdims=True)
        grad = grad - jnp.mean(grad, axis=-1, keepdims=True) - line * slope
        result[here, :] = cot[here, :].astype(F32) + scales[here, :1] * grad
        return unused

    middle = rows // chunk // 2
    lax.fori_loop(0, middle, back, 0)
    yield
    lax.fori_loop(middle, 2 * middle, back, 0)


BR_PEERS = [dict(dl=i // 4, dx=i % 4) for i in range(1, 8)]
TOK_PEERS = [dict(dy=i // 4, dz=(i // 2) % 2, dc=i % 2) for i in range(1, 16)]


def last_kernel(
    heads,
    dq,
    dkv,
    table,
    x_in,
    g_in,
    m_in,
    w_in,
    s_in,
    tokens,
    cot,
    gain,
    block_map,
    result,
    qkv_out,
    out_out,
    sides,
    *rest,
):
    held_q, held_kv, held_t, held_x, held_g, held_m, held_w, held_s, gj = rest[:9]
    parts, near, side, out, far, wsum, summed, normed, scales = rest[9:18]
    lines, lines_in, last, last_in, bias_acc = rest[18:23]
    space = ScatterSpace(rest[23:30])
    links = Links(*rest[30:])
    y, z, c, l, x = coords()
    links.greet(BR_PEERS + TOK_PEERS)
    width = heads * HD
    rows, depth = tokens.shape
    first = [
        links.local(dq, held_q),
        links.local(dkv, held_kv),
        links.local(table, held_t),
    ]
    third = [links.local(w_in.at[:, pl.ds(0, 3 * width)], held_w), links.local(s_in, held_s)]
    second = [
        links.local(x_in, held_x),
        links.local(g_in, held_g),
        links.local(m_in, held_m),
    ]
    wrows = parts.shape[3]
    strip = 4 * wrows
    bias_acc[...] = jnp.zeros_like(bias_acc)

    def settle(loads):
        for load in loads:
            links.settle(load)
        loads.clear()

    def turn_rows(here):
        for slot in range(2):
            lanes = slice(slot * HD, (slot + 1) * HD)
            turns = table_rows(held_t, block_map, slot, here)
            q = jnp.concatenate([held_q[h, here, lanes] for h in range(heads)], axis=1)
            q = turn(q.astype(F32), turns, heads // 2, False, -1.0).astype(BF)
            kv = jnp.concatenate([held_kv[h, slot, here, :] for h in range(heads)], axis=1)
            kv = turn(kv.astype(F32), turns, heads, True, -1.0).astype(BF)
            both = jnp.concatenate([q, kv], axis=1)
            gj[slot, here, :] = both
            bias_acc[...] += jnp.sum(
                both.astype(F32).reshape(rows // 8, 8, 3 * width), axis=0
            )

    def bias_lines():
        total = jnp.sum(bias_acc[...], axis=0, keepdims=True)
        line = [total[:, :width]]
        for k in range(2):
            at = [width + (2 * h + k) * HD for h in range(heads)]
            line.append(jnp.concatenate([total[:, a : a + HD] for a in at], axis=1))
        line = jnp.concatenate(line, axis=1)
        return jnp.concatenate(
            [line[:, r * 128 : (r + 1) * 128] for r in range(3 * width // 128)], axis=0
        )

    def weights_of(there):
        settle(second)
        here = pl.ds(pl.multiple_of(there * strip, strip), strip)
        qkv = dot(held_x[:, here], gj[...].reshape(2 * BLK, 3 * width), TN).astype(BF)
        outs = dot(held_g[:, here], held_m[...], TN).astype(BF)
        for k in range(4):
            at = slice(k * wrows, (k + 1) * wrows)
            parts[there, k // 2, k % 2, :, : 3 * width] = qkv[at]
            parts[there, k // 2, k % 2, :, 3 * width : 4 * width] = outs[at]

    def rows_of(there):
        settle(first)
        here = pl.ds(pl.multiple_of(there * rows, rows), rows)
        turn_rows(here)
        settle(third)
        both = gj[:, here, :].reshape(2 * rows, 3 * width)
        grads = dot(both, held_w[...], NT)
        for slot in range(2):
            value = grads[slot * rows : (slot + 1) * rows] + held_s[slot, here, :].astype(F32)
            space.pieces[slot, there] = value.astype(BF)

    def shifted():
        yield from scatter_br(links, rows_of, space, summed, lambda column: plain)
        through = turn_back(summed, normed, scales, cot, gain, lines, result)
        next(through)
        near_sums = [links.send(lines, lines_in.at[i], **o) for i, o in enumerate(BR_PEERS)]
        yield
        next(through)
        bias_sums = bias_lines()
        sums = lines[...]
        for i, ticket in enumerate(near_sums):
            links.arrived(ticket, lines_in.at[i])
            sums = sums + lines_in[i]
        for t in range(16):
            last[t] = jnp.concatenate([sums[t : t + 1], sums[16 + t : 17 + t], bias_sums], axis=0)
        all_sums = []
        for i, o in enumerate(TOK_PEERS):
            there = ((y + o["dy"]) % 4) * 4 + ((z + o["dz"]) % 2) * 2 + (c + o["dc"]) % 2
            all_sums.append(links.send(last.at[there], last_in.at[i], **o))
        yield
        for unused in through:
            pass
        yield
        sums = last[y * 4 + z * 2 + c]
        for i, ticket in enumerate(all_sums):
            links.arrived(ticket, last_in.at[i])
            sums = sums + last_in[i]
        sides[...] = sums

    def weights():
        for unused in range(4):
            yield
        yield from reduce_tok(links, weights_of, parts, near, side, out, far, wsum)
        qkv_out[0] = wsum[:, :width]
        for k in range(2):
            at = [width + (2 * h + k) * HD for h in range(heads)]
            qkv_out[1 + k] = jnp.concatenate([wsum[:, a : a + HD] for a in at], axis=1)
        out_out[...] = jnp.transpose(wsum[:, 3 * width :])

    def aside():
        for unused in range(5):
            yield
        normal_rows(tokens, normed, scales)

    in_turn([shifted(), weights(), aside()])
    links.close()


def last_sums(
    dq, dkv, table, x, g, mixed, w, partial_grad, tokens, cot, gain, block_map, heads
):
    rows, depth = tokens.shape
    wrows = depth // 16
    width = heads * HD
    cols = 4 * width
    return comm_call(
        functools.partial(last_kernel, heads),
        "last_sums",
        3,
        (dq, dkv, table, x, g, mixed, w, partial_grad, tokens, cot, gain, block_map),
        (
            jax.ShapeDtypeStruct((rows, depth), F32),
            jax.ShapeDtypeStruct((3, wrows, width), F32),
            jax.ShapeDtypeStruct((width, wrows), F32),
            jax.ShapeDtypeStruct((8, 128), F32),
        ),
        scratch=[
            pltpu.VMEM(dq.shape, BF),
            pltpu.VMEM(dkv.shape, BF),
            pltpu.VMEM(table.shape, F32),
            pltpu.VMEM(x.shape, BF),
            pltpu.VMEM(g.shape, BF),
            pltpu.VMEM(mixed.shape, BF),
            pltpu.VMEM((depth, 3 * width), BF),
            pltpu.VMEM(partial_grad.shape, BF),
            pltpu.VMEM((2, BLK, 3 * width), BF),
            pltpu.VMEM((4, 2, 2, wrows, cols), BF),
            pltpu.VMEM((4, 2, wrows, cols), BF),
            pltpu.VMEM((3, 2, wrows, cols), BF),
            pltpu.VMEM((wrows, cols), BF),
            pltpu.VMEM((wrows, cols), BF),
            pltpu.VMEM((wrows, cols), F32),
            pltpu.VMEM((rows, depth), F32),
            pltpu.VMEM((rows, depth), F32),
            pltpu.VMEM((rows, 128), F32),
            pltpu.VMEM((32, 128), F32),
            pltpu.VMEM((7, 32, 128), F32),
            pltpu.VMEM((16, 8, 128), F32),
            pltpu.VMEM((15, 8, 128), F32),
            pltpu.VMEM((8, 3 * width), F32),
        ]
        + ScatterSpace.shapes(rows, depth, depth // 4 * 3),
        in_vmem=(8, 9, 10),
        in_smem=(11,),
        out_vmem=(0, 1, 2, 3),
        copies=96,
    )


def finish_kernel(main, grads, value, tokens, qkv, out, *outs):
    def lines(start, count):
        return jnp.transpose(grads[:, start : start + count].astype(F32))

    result, tokens_out, qkv_out, out_out, down, gate, up = outs
    result[...] = value[...]
    tokens_out[...] = tokens[...]
    qkv_out[...] = qkv[...]
    out_out[...] = out[...]
    tail = down.shape[0] - main
    down[:main, :] = lines(0, main)
    down[main:, :] = lines(main, 128)[:tail]
    at = main + 128
    gate[:main, :] = lines(at, main)
    up[:main, :] = lines(at + main, main)
    ends = lines(at + 2 * main, 128)
    gate[main:, :] = ends[:tail]
    up[main:, :] = ends[tail:]


def finish(grads, value, tokens, qkv, out, main, hidden_width):
    shape = jax.ShapeDtypeStruct((hidden_width, grads.shape[0]), F32)
    return pl.pallas_call(
        functools.partial(finish_kernel, main),
        out_shape=(
            jax.ShapeDtypeStruct(value.shape, BF),
            jax.ShapeDtypeStruct(tokens.shape, F32),
            jax.ShapeDtypeStruct(qkv.shape, F32),
            jax.ShapeDtypeStruct(out.shape, F32),
        )
        + (shape,) * 3,
        in_specs=[VMEM] * 5,
        out_specs=(VMEM,) * 7,
        cost_estimate=SMALL,
        name="finish",
    )(grads, value, tokens, qkv, out)


def rotary_table():
    half = ROT // 2
    frequency = (ROPE_BASE ** (-(np.arange(half) * 2.0 / ROT))).astype(np.float32)
    angles = np.arange(LB * BLK, dtype=np.float32)[:, None] * frequency[None, :]
    cos, sin = np.cos(angles), np.sin(angles)
    one = np.ones((LB * BLK, HD - ROT), np.float32)
    table = np.concatenate([cos, cos, one, -sin, sin, 0.0 * one], axis=1)
    return table.astype(np.float32).reshape(LB, BLK, 2 * HD)


def body(
    tokens,
    norm_gain,
    norm_bias,
    qkv_weight,
    qkv_bias,
    out_weight,
    gate_weight,
    up_weight,
    down_weight,
    cotangent,
    block_map,
    lengths,
):
    tok = lax.axis_index("tok")
    rows = tokens.shape[0]
    depth = tokens.shape[1]
    wrows = qkv_weight.shape[1]
    heads = qkv_bias.shape[1]
    width = heads * HD
    hidden_width = gate_weight.shape[1]
    main = hidden_width // 128 * 128
    tail = hidden_width - main

    down_width = main + 128
    first = down_width + width
    table = jnp.asarray(rotary_table())
    x, grad, qkv_full, ff_full, kv_mine, q_heads = start(
        block_map,
        tokens,
        norm_gain.reshape(1, depth),
        norm_bias.reshape(1, depth),
        cotangent,
        qkv_weight,
        qkv_bias,
        jnp.transpose(gate_weight),
        jnp.transpose(up_weight),
        down_weight,
        out_weight,
        table,
        heads,
        main,
    )
    x = x.reshape(2, BLK, depth)
    grad = grad.reshape(2, BLK, depth)
    qkv_full = qkv_full.reshape(16 * wrows, -1)
    ff_full = ff_full.reshape(16 * wrows, -1)

    hidden, grad_x, grad_ff, qd_all, kv_all = ff_heads(
        x, grad, ff_full, kv_mine, q_heads, main, down_width, first
    )
    kv_all = kv_all.reshape(-1, 2 * HD)
    x = x.reshape(2 * BLK, depth)
    grad = grad.reshape(2 * BLK, depth)
    grad_ff = lax.psum_scatter(grad_ff, "tok", scatter_dimension=0, tiled=True)

    o_parts, dq_parts, dkv_all = attention(block_map, lengths, qd_all, kv_all)
    dq_heads, dkv_heads, mixed, result = heads_home(
        dkv_all.reshape(4, 2, 2, 2 * BLK, 2 * HD), dq_parts, o_parts, hidden, ff_full, tokens, heads
    )
    grad_tokens, grad_qkv, grad_out, sides = last_sums(
        dq_heads,
        dkv_heads.reshape(heads, 2, BLK, 2 * HD),
        table,
        x,
        grad,
        mixed.reshape(2 * BLK, width),
        qkv_full,
        grad_x,
        tokens,
        cotangent,
        norm_gain.reshape(1, depth),
        block_map,
        heads,
    )
    grad_qkv_bias = lax.dynamic_slice_in_dim(
        sides[2:].reshape(3, heads, HD), tok * qkv_bias.shape[2], qkv_bias.shape[2], 2
    )
    grad_ff, grad_tokens = lax.optimization_barrier((grad_ff, grad_tokens))
    result, grad_tokens, grad_qkv, grad_out, grad_down, grad_gate, grad_up = finish(
        grad_ff, result, grad_tokens, grad_qkv, grad_out, main, hidden_width
    )

    sides = lax.dynamic_slice_in_dim(sides[:2], lax.axis_index("br") * 16, 16, 1)
    return (
        result,
        grad_tokens,
        sides[0],
        sides[1],
        grad_qkv,
        grad_qkv_bias,
        grad_out,
        jnp.transpose(grad_gate),
        jnp.transpose(grad_up),
        grad_down,
    )


def solution(mesh):
    in_specs = (
        P(("tok", "br"), None),
        P(),
        P(),
        P(None, "tok", "br"),
        P(None, "br", "tok"),
        P("br", "tok"),
        P("tok", "br"),
        P("tok", "br"),
        P("br", "tok"),
        P(("tok", "br"), None),
        P(),
        P(),
    )
    out_specs = (
        P(("tok", "br"), None),
        P(("tok", "br"), None),
        P(("tok", "br")),
        P(("tok", "br")),
        P(None, "tok", "br"),
        P(None, "br", "tok"),
        P("br", "tok"),
        P("tok", "br"),
        P("tok", "br"),
        P("br", "tok"),
    )
    return jax.shard_map(body, mesh=mesh, in_specs=in_specs, out_specs=out_specs, check_vma=False)
```

```python
import functools

import jax
import jax.numpy as jnp
import numpy as np
from jax import lax
from jax.experimental import pallas as pl
from jax.experimental.pallas import tpu as pltpu
from jax.sharding import PartitionSpec as P

HD = 64
ROT = 16
BLK = 512
LB = 8
EPSILON = 1e-05
ROPE_BASE = 10000.0
MASKED = -1e30
BF = jnp.bfloat16
F32 = jnp.float32
NN = (((1,), (0,)), ((), ()))
NT = (((1,), (1,)), ((), ()))
TN = (((0,), (0,)), ((), ()))
VMEM = pl.BlockSpec(memory_space=pltpu.VMEM)
SMEM = pl.BlockSpec(memory_space=pltpu.SMEM)
ANY = pl.BlockSpec(memory_space=pl.ANY)
SMALL = pl.CostEstimate(flops=1000, bytes_accessed=1000, transcendentals=0)


def dot(left, right, dims):
    return lax.dot_general(left, right, dims, preferred_element_type=F32)


def block_info(block, long_blocks):
    is_long = block < long_blocks
    place = jnp.where(is_long, block % LB, (block - long_blocks) % 2)
    return is_long, place, block - place


def lane_half(packed, half, upper):
    piece = packed[:, half * HD : (half + 1) * HD]
    zero = jnp.zeros_like(piece)
    return jnp.concatenate([zero, piece] if upper else [piece, zero], axis=1)


def allowed_pairs(place, step, limit):
    key_pos = step * BLK + lax.broadcasted_iota(jnp.int32, (BLK, BLK), 0)
    query_pos = place * BLK + lax.broadcasted_iota(jnp.int32, (BLK, BLK), 1)
    return (key_pos <= query_pos) & (key_pos < limit)


def attn_kernel(
    block_map, lengths, q_ref, kv_ref, o_ref, dq_ref, dkv_ref, slot_of, ot, lses, acc, dqt
):
    total_blocks = block_map.shape[0]
    long_blocks = total_blocks // 2
    own = lax.axis_index("tok") % 4

    def note(slot, unused):
        slot_of[block_map[slot]] = slot
        return unused

    lax.fori_loop(0, total_blocks, note, 0)

    def about(i, half):
        block = block_map[2 * (4 * i + own) + half]
        is_long, place, first = block_info(block, long_blocks)
        row = jnp.where(
            is_long, block // LB, long_blocks // LB + (block - long_blocks) // 2
        )
        return is_long, place, first, lengths[row]

    def rows_at(block):
        return pl.ds(pl.multiple_of(slot_of[block] * BLK, BLK), BLK)

    def forward(i, unused):
        packed = q_ref[i, 0]
        for half in range(2):
            is_long, place, first, limit = about(i, half)
            queries = lane_half(packed, half, False) * jnp.asarray(0.125, BF)

            def step(j, carry, masked):
                top, total, summed = carry
                kv = kv_ref[rows_at(first + j), :]
                scores = dot(kv, queries, NT)
                if masked:
                    scores = jnp.where(allowed_pairs(place, j, limit), scores, MASKED)
                new_top = jnp.maximum(top, jnp.max(scores, axis=0, keepdims=True))
                fade = jnp.exp(top - new_top)
                probs = jnp.exp(scores - new_top)
                total = total * fade + jnp.sum(probs, axis=0, keepdims=True)
                summed = summed * fade + dot(kv, probs.astype(BF), TN)
                return new_top, total, summed

            free = jnp.where(is_long, place, 0)
            carry = (
                jnp.full((1, BLK), MASKED, F32),
                jnp.zeros((1, BLK), F32),
                jnp.zeros((2 * HD, BLK), F32),
            )
            carry = lax.fori_loop(0, free, lambda j, c: step(j, c, False), carry)
            top, total, summed = lax.fori_loop(
                free, place + 1, lambda j, c: step(j, c, True), carry
            )
            lses[2 * i + half] = top + jnp.log(total)
            ot[i, half * HD : (half + 1) * HD, :] = summed[HD:, :] / total
        o_ref[i] = jnp.transpose(ot[i]).astype(BF)
        return unused

    lax.fori_loop(0, q_ref.shape[0], forward, 0)
    acc[...] = jnp.zeros_like(acc)

    def backward(i, unused):
        q_packed = q_ref[i, 0]
        d_packed = q_ref[i, 1]
        d_turned = jnp.transpose(d_packed.astype(F32))
        for half in range(2):
            is_long, place, first, limit = about(i, half)
            queries = lane_half(q_packed, half, False) * jnp.asarray(0.125, BF)
            grads = lane_half(d_packed, half, True)
            both = jnp.concatenate([queries, grads], axis=0)
            lanes = slice(half * HD, (half + 1) * HD)
            delta = jnp.sum(d_turned[lanes] * ot[i, lanes, :], axis=0, keepdims=True)
            lse = lses[2 * i + half]

            def step(j, total, masked):
                rows = rows_at(first + j)
                kv = kv_ref[rows, :]
                scores = dot(kv, queries, NT)
                if masked:
                    scores = jnp.where(allowed_pairs(place, j, limit), scores, MASKED)
                probs = jnp.exp(scores - lse)
                ds = (probs * (dot(kv, grads, NT) - delta)).astype(BF)
                acc[rows, :] += dot(jnp.concatenate([ds, probs.astype(BF)], axis=1), both, NN)
                return total + dot(kv, ds, TN)

            free = jnp.where(is_long, place, 0)
            total = lax.fori_loop(
                0, free, lambda j, c: step(j, c, False), jnp.zeros((2 * HD, BLK), F32)
            )
            total = lax.fori_loop(free, place + 1, lambda j, c: step(j, c, True), total)
            dqt[lanes, :] = total[:HD, :] * 0.125
        dq_ref[i] = jnp.transpose(dqt[...]).astype(BF)
        return unused

    lax.fori_loop(0, q_ref.shape[0], backward, 0)

    def finish(i, unused):
        rows = pl.ds(pl.multiple_of(i * BLK, BLK), BLK)
        dkv_ref[rows, :] = acc[rows, :].astype(BF)
        return unused

    lax.fori_loop(0, kv_ref.shape[0] // BLK, finish, 0)


def attention(block_map, lengths, qd, kv):
    n = qd.shape[0]
    shape = jax.ShapeDtypeStruct((n, BLK, 2 * HD), BF)
    return pl.pallas_call(
        attn_kernel,
        out_shape=(shape, shape, jax.ShapeDtypeStruct(kv.shape, BF)),
        in_specs=[SMEM, SMEM, VMEM, VMEM],
        out_specs=(VMEM, VMEM, VMEM),
        scratch_shapes=[
            pltpu.SMEM(block_map.shape, jnp.int32),
            pltpu.VMEM((n, 2 * HD, BLK), F32),
            pltpu.VMEM((2 * n, 1, BLK), F32),
            pltpu.VMEM(kv.shape, F32),
            pltpu.VMEM((2 * HD, BLK), F32),
        ],
        compiler_params=pltpu.CompilerParams(vmem_limit_bytes=60 * 2**20),
        cost_estimate=SMALL,
        name="attention",
    )(block_map, lengths, qd, kv)


def turn(values, table, copies, paired, sign):
    width = values.shape[1]
    lane = lax.broadcasted_iota(jnp.int32, values.shape, 1) % HD
    partner = jnp.where(
        lane < ROT // 2,
        pltpu.roll(values, width - ROT // 2, 1),
        pltpu.roll(values, ROT // 2, 1),
    )
    cos, sin = table[:, :HD], sign * table[:, HD:]
    cos = jnp.concatenate([cos, jnp.ones_like(cos) if paired else cos], axis=1)
    sin = jnp.concatenate([sin, jnp.zeros_like(sin) if paired else sin], axis=1)
    cos = jnp.concatenate([cos] * copies, axis=1)
    sin = jnp.concatenate([sin] * copies, axis=1)
    return values * cos + partner * sin


def ff_part(main, down, first, x, g, w_ref, h_ref, a_ref, mixed_grad, pause):
    rows, depth = x.shape[1:]
    x = x.reshape(2 * rows, depth)
    g = g.reshape(2 * rows, depth)
    gate_up = dot(x, w_ref[:, first:], NN)
    pause(0)
    gh = dot(g, w_ref[:, :first], NN)
    mixed_grad(gh[:, down:].astype(BF))
    gh = gh[:, :down]
    ends = gate_up[:, 2 * main :]
    gate = jnp.concatenate([gate_up[:, :main], ends], axis=1)
    up = jnp.concatenate([gate_up[:, main : 2 * main], pltpu.roll(ends, HD, 1)], axis=1)
    sig = jax.nn.sigmoid(gate)
    silu = gate * sig
    hidden = (silu * up).astype(BF)
    d_gate = gh * up * sig * (1.0 + gate * (1.0 - sig))
    d_up = gh * silu
    tail = d_gate[:, main:] + pltpu.roll(d_up[:, main:], HD, 1)
    grads = jnp.concatenate(
        [d_gate[:, :main].astype(BF), d_up[:, :main].astype(BF), tail.astype(BF)], axis=1
    )
    h_ref[...] = hidden.reshape(h_ref.shape)
    pause(1)
    a_ref[...] = grads.reshape(a_ref.shape)
    return grads, hidden


def coords():
    tok, br = lax.axis_index("tok"), lax.axis_index("br")
    return tok // 4, (tok // 2) % 2, tok % 2, br // 4, br % 4


def peer(dy=0, dz=0, dc=0, dl=0, dx=0):
    y, z, c, l, x = coords()
    tok = ((y + dy) % 4) * 4 + ((z + dz) % 2) * 2 + (c + dc) % 2
    return tok, ((l + dl) % 2) * 4 + (x + dx) % 4


class Links:
    def __init__(self, send_sems, recv_sems, local_sems):
        self.sems = (send_sems, recv_sems, local_sems)
        self.sent, self.locals = [], []

    def greet(self, partners):
        barrier = pltpu.get_barrier_semaphore()
        for offsets in partners:
            pl.semaphore_signal(
                barrier, inc=1, device_id=peer(**offsets), device_id_type=pl.DeviceIdType.MESH
            )
        pl.semaphore_wait(barrier, len(partners))

    def copy(self, number, source, target, offsets):
        return pltpu.make_async_remote_copy(
            src_ref=source,
            dst_ref=target,
            send_sem=self.sems[0].at[number],
            recv_sem=self.sems[1].at[number],
            device_id=peer(**offsets),
            device_id_type=pl.DeviceIdType.MESH,
        )

    def send(self, source, target, **offsets):
        copy = self.copy(len(self.sent), source, target, offsets)
        copy.start()
        self.sent.append(copy)
        return len(self.sent) - 1, offsets

    def arrived(self, ticket, place):
        self.copy(ticket[0], place, place, ticket[1]).wait_recv()

    def local(self, source, target):
        copy = pltpu.make_async_copy(source, target, self.sems[2].at[len(self.locals)])
        copy.start()
        self.locals.append([copy, True])
        return len(self.locals) - 1

    def settle(self, number):
        copy, pending = self.locals[number]
        if pending:
            copy.wait()
        self.locals[number][1] = False

    def close(self):
        for number in range(len(self.locals)):
            self.settle(number)
        for copy in self.sent:
            copy.wait_send()


def in_turn(tasks):
    tasks = list(tasks)
    while tasks:
        for task in list(tasks):
            try:
                next(task)
            except StopIteration:
                tasks.remove(task)


def ring_four(links, own, place, axis, landed):
    right = links.send(own, place(0, None), **{axis: 1})
    left = links.send(own, place(0, None), **{axis: -1})
    yield
    links.arrived(right, place(-1, None))
    on_right = links.send(place(-1, 0), place(-1, 0), **{axis: 1})
    landed(-1)
    yield
    links.arrived(left, place(1, None))
    on_left = links.send(place(1, 1), place(1, 1), **{axis: -1})
    landed(1)
    yield
    links.arrived(on_right, place(2, 0))
    links.arrived(on_left, place(2, 1))
    landed(2)


def half_of(ref, part):
    if part is None:
        return ref
    rows = ref.shape[0] // 2
    return ref.at[pl.ds(part * rows, rows)]


def gather_br(links, own, whole):
    unused_y, unused_z, unused_c, l, x = coords()

    def place(dl):
        return lambda dx, part: half_of(whole.at[(l + dl) % 2, (x + dx) % 4], part)

    kept = links.local(own, place(0)(0, None))
    across = links.send(own, place(0)(0, None), dl=1)
    near = ring_four(links, own, place(0), "dx", lambda d: None)
    next(near)
    yield
    links.arrived(across, place(1)(0, None))
    far = ring_four(links, place(1)(0, None), place(1), "dx", lambda d: None)
    next(far)
    for unused in near:
        yield
    for unused in far:
        yield
    links.settle(kept)


def gather_tok(links, own, whole):
    y, z, c, unused_l, unused_x = coords()
    passed = []

    def place(dz, dc=0):
        return lambda dy, part: half_of(
            whole.at[(y + dy) % 4, (z + dz) % 2, (c + dc) % 2], part
        )

    def passer(dz):
        def landed(dy):
            ref = place(dz)(dy, None)
            passed.append((links.send(ref, ref, dc=1), place(dz, 1)(dy, None)))

        return landed

    kept = links.local(own, place(0)(0, None))
    across = links.send(own, place(0)(0, None), dz=1)
    near = ring_four(links, own, place(0), "dy", passer(0))
    next(near)
    passed.append((links.send(own, place(0)(0, None), dc=1), place(0, 1)(0, None)))
    yield
    links.arrived(across, place(1)(0, None))
    far = ring_four(links, place(1)(0, None), place(1), "dy", passer(1))
    next(far)
    passer(1)(0)
    for unused in near:
        yield
    for unused in far:
        yield
    links.settle(kept)
    for ticket, ref in passed:
        links.arrived(ticket, ref)


def add_up(target, sources, rows, finish):
    chunk = 16

    def step(i, unused):
        here = pl.ds(pl.multiple_of(i * chunk, chunk), chunk)
        total = sources[0][here, :].astype(F32)
        for source in sources[1:]:
            total = total + source[here, :].astype(F32)
        target[here, :] = finish(total, here).astype(target.dtype)
        return unused

    lax.fori_loop(0, rows // chunk, step, 0)


def plain(total, here):
    return total


def reduce_heads(links, grads, dq, dq_home, grads_home, mine, near, far, total):
    y, z, c, unused_l, unused_x = coords()
    order = (1, 3, 2, 0)
    held, from_core = {}, {}
    for dz in (1, 0):
        for d in order:
            place = ((y + d) % 4, (z + dz) % 2)
            from_core[d, dz] = links.send(
                grads.at[place[0], place[1], 1 - c], near.at[place[0], place[1]], dc=1
            )
            held[d, dz] = links.local(
                grads.at[place[0], place[1], c], mine.at[place[0], place[1]]
            )
    asked = [links.send(dq.at[(y + d) % 4], dq_home.at[y], dy=d) for d in order[:3]]
    links.local(dq.at[y], dq_home.at[y])
    yield
    rows = mine.shape[2]
    across = {}
    for d in order:
        here = (y + d) % 4
        links.arrived(from_core[d, 1], near.at[here, 1 - z])
        links.settle(held[d, 1])
        add_up(
            mine.at[here, 1 - z], [mine.at[here, 1 - z], near.at[here, 1 - z]], rows, plain
        )
        across[d] = links.send(mine.at[here, 1 - z], far.at[here], dz=1)
        yield
    home = {}
    for d in order:
        here = (y + d) % 4
        links.arrived(from_core[d, 0], near.at[here, z])
        links.settle(held[d, 0])
        links.arrived(across[d], far.at[here])
        add_up(
            total.at[here], [mine.at[here, z], near.at[here, z], far.at[here]], rows, plain
        )
        if d:
            home[d] = links.send(total.at[here], grads_home.at[y], dy=d)
        else:
            links.local(total.at[here], grads_home.at[y])
        yield
    for i, d in enumerate(order[:3]):
        links.arrived(asked[i], dq_home.at[(y - d) % 4])
        links.arrived(home[d], grads_home.at[(y - d) % 4])


class ScatterSpace:
    def __init__(self, refs):
        self.pieces, self.ring, self.out, self.far = refs[:4]
        if len(refs) > 4:
            self.across, self.sums, self.last = refs[4:]

    @staticmethod
    def shapes(rows, depth, half):
        def ring(parts, columns):
            return (parts, 2, rows + rows // 2, columns)

        sizes = [(2, 4, rows, depth), ring(2, half), (rows, half), (rows, half)]
        rest = depth - half
        if rest:
            sizes += [(4, rows, rest), (4, rows, rest), ring(1, rest)]
        return [pltpu.VMEM(size, BF) for size in sizes]


def ring_sum(links, pieces, ring, total, finish):
    unused_y, unused_z, unused_c, unused_l, x = coords()
    rows = total.shape[0]
    half = rows // 2
    halves = (pl.ds(0, half), pl.ds(half, half))
    passing = pl.ds(rows, half)
    whole = pl.ds(0, rows)
    opposite = pieces((x + 2) % 4)
    steps = (1, -1)
    first = [
        links.send(opposite.at[halves[k]], ring.at[k, passing], dx=steps[k]) for k in range(2)
    ]
    yield
    second = []
    for k in range(2):
        links.arrived(first[k], ring.at[k, passing])
        piece = pieces((x + steps[k]) % 4)
        add_up(
            piece.at[halves[k]], [piece.at[halves[k]], ring.at[k, passing]], half, plain
        )
        second.append(links.send(piece, ring.at[k, whole], dx=steps[k]))
        yield
    for k in range(2):
        links.arrived(second[k], ring.at[k, whole])
    add_up(total, [pieces(x), ring.at[0, whole], ring.at[1, whole]], rows, finish)


def scatter_br(links, make, space, target, finish):
    unused_y, unused_z, unused_c, l, x = coords()
    rows, half = space.out.shape
    split = half < target.shape[1]
    first, second = pl.ds(0, half), pl.ds(half, target.shape[1] - half)
    order = (2, 1, 3, 0)

    def part(to):
        return lambda there: space.pieces.at[to, there, :, first]

    folded = {}
    outer = ring_sum(links, part(1 - l), space.ring.at[0], space.out, plain)
    for d in order:
        there = (x + d) % 4
        make(there)
        if split:
            folded[d] = links.send(
                space.pieces.at[1 - l, there, :, second], space.across.at[there], dl=1
            )
        if d == 2:
            next(outer)
        yield
    inner = ring_sum(links, part(l), space.ring.at[1], target.at[:, first], finish(0))
    next(inner)
    yield from outer
    over = links.send(space.out, space.far, dl=1)
    next(inner)
    next(inner)
    yield
    rest = []
    for d in order if split else ():
        there = (x + d) % 4
        links.arrived(folded[d], space.across.at[there])
        own = space.pieces.at[l, there, :, second]
        add_up(space.sums.at[there], [own, space.across.at[there]], rows, plain)
        if d == 2:
            late = ring_sum(
                links,
                lambda there: space.sums.at[there],
                space.last.at[0],
                target.at[:, second],
                finish(half),
            )
            next(late)
            rest.append(late)
        yield

    def joined():
        links.arrived(over, space.far)
        mine = space.pieces.at[l, x, :, first]
        add_up(mine, [mine, space.far], rows, plain)
        yield
        yield from inner

    rest.append(joined())
    while rest:
        for task in list(rest):
            try:
                next(task)
            except StopIteration:
                rest.remove(task)
        yield


def reduce_tok(links, make, parts, near, side, out, far, target):
    y, z, c, unused_l, unused_x = coords()
    order = (1, 3, 2, 0)
    tickets = {}
    for d in order:
        here = (y + d) % 4
        make(here)
        tickets[d] = links.send(parts.at[here, :, 1 - c], near.at[here], dc=1)
        yield
    rows = out.shape[0]
    sent = {}
    for dz in (1, 0):
        k = (z + dz) % 2
        for i, d in enumerate(order):
            here = (y + d) % 4
            if dz:
                links.arrived(tickets[d], near.at[here])
            own = parts.at[here, k, c]
            add_up(own, [own, near.at[here, k]], rows, plain)
            if d:
                sent[dz, i] = links.send(own, side.at[i, k], dy=d)
            if dz:
                yield
    for i in range(3):
        links.arrived(sent[1, i], side.at[i, 1 - z])
        yield
    add_up(out, [parts.at[y, 1 - z, c]] + [side.at[i, 1 - z] for i in range(3)], rows, plain)
    across = links.send(out, far, dz=1)
    yield
    for i in range(3):
        links.arrived(sent[0, i], side.at[i, z])
    yield
    links.arrived(across, far)
    add_up(target, [parts.at[y, z, c]] + [side.at[i, z] for i in range(3)] + [far], rows, plain)


BR_NEAR = [dict(dl=1), dict(dx=1), dict(dx=-1)]
BR_ALL = BR_NEAR + [dict(dx=2)]
TOK_NEAR = [dict(dz=1), dict(dc=1), dict(dy=1), dict(dy=-1)]
TOK_ALL = TOK_NEAR + [dict(dy=2)]


def comm_call(
    kernel, name, number, args, outs, scratch=(), in_vmem=(), out_vmem=(), in_smem=(), copies=48
):
    return pl.pallas_call(
        kernel,
        out_shape=tuple(outs),
        in_specs=[
            VMEM if i in in_vmem else SMEM if i in in_smem else ANY for i in range(len(args))
        ],
        out_specs=tuple(VMEM if i in out_vmem else ANY for i in range(len(outs))),
        scratch_shapes=list(scratch)
        + [
            pltpu.SemaphoreType.DMA((copies,)),
            pltpu.SemaphoreType.DMA((copies,)),
            pltpu.SemaphoreType.DMA((32,)),
        ],
        compiler_params=pltpu.CompilerParams(
            collective_id=number, has_side_effects=True, vmem_limit_bytes=60 * 2**20
        ),
        cost_estimate=SMALL,
        name=name,
    )(*args)


def table_rows(table, block_map, slot, here):
    block = block_map[lax.axis_index("tok") * 2 + slot]
    long_blocks = 2 * LB
    place = jnp.where(block < long_blocks, block % LB, (block - long_blocks) % 2)
    return table[place, here, :]


def shift_rows(tokens, gain, bias, shifted):
    rows = tokens.shape[0]
    chunk = 16

    def step(i, unused):
        here = pl.ds(pl.multiple_of(i * chunk, chunk), chunk)
        value = tokens[here, :].astype(F32)
        value = value - jnp.mean(value, axis=-1, keepdims=True)
        scale = lax.rsqrt(jnp.mean(value * value, axis=-1, keepdims=True) + EPSILON)
        shifted[here, :] = (value * scale * gain[...] + bias[...]).astype(BF)
        return unused

    lax.fori_loop(0, rows // chunk, step, 0)


def turned(block):
    return jnp.transpose(block.astype(F32)).astype(BF)


def bias_places(heads, per):
    width = heads * HD
    places = np.zeros((128, 3 * width), np.float32)
    for column in range(3 * width):
        if column < width:
            part, head, lane = 0, column // HD, column % HD
        else:
            pair, lane = divmod(column - width, HD)
            part, head = 1 + pair % 2, pair // 2
        places[(part * heads + head) * per + lane % per, column] = 1.0
    return places


def start_kernel(
    heads,
    main,
    block_map,
    tokens,
    gain,
    bias,
    cot,
    qkv,
    qkv_bias,
    places,
    gate,
    up,
    down,
    out,
    table,
    x_out,
    g_out,
    w_out,
    f_out,
    kv_mine,
    q_heads,
    *rest,
):
    shifted, qkv_shard, ff_shard, held_x, held_w, pairs, queries, held_t = rest[:8]
    links = Links(*rest[8:])
    y, z, c, unused_l, unused_x = coords()
    width = heads * HD
    links.greet(BR_NEAR + TOK_ALL)
    rotary = links.local(table, held_t)
    shift_rows(tokens, gain, bias, shifted)
    rows, depth = tokens.shape
    kv = []
    for head in range(heads):
        lanes = slice(head * HD, (head + 1) * HD)
        kv += [qkv[1, :, lanes], qkv[2, :, lanes]]
    qkv_shard[:, : 3 * width] = jnp.concatenate([qkv[0]] + kv, axis=1)
    line = dot(qkv_bias[...], places[...], NN)
    lane = lax.broadcasted_iota(jnp.int32, line.shape, 1) % HD
    line = jnp.where(lane // (HD // 16) == lax.axis_index("tok"), line, 0.0)[:1]
    lines = [line[:, r * 128 : (r + 1) * 128] for r in range(3 * width // 128)]
    zero = jnp.zeros((qkv_shard.shape[0] - len(lines), 128), F32)
    qkv_shard[:, 3 * width :] = jnp.concatenate(lines + [zero], axis=0).astype(BF)

    def project(half):
        tile = 2 * rows
        here = slice(half * tile, (half + 1) * tile)
        span = held_x[:, 2 * half : 2 * half + 2].reshape(2 * tile, depth)
        corner = held_w[0, 0, 0, :8, 3 * width :].astype(F32)
        for t in range(1, 16):
            corner = corner + held_w[t // 4, t // 2 % 2, t % 2, :8, 3 * width :].astype(F32)
        added = jnp.concatenate([corner[r : r + 1] for r in range(len(lines))], axis=1)
        products = dot(span, held_w[...].reshape(depth, -1)[:, : 3 * width], NN) + added
        parts = []
        for slot in range(2):
            turns = table_rows(held_t, block_map, slot, here)
            joined = products[slot * tile : (slot + 1) * tile]
            parts.append(turn(joined[:, :width], turns, heads // 2, False, 1.0).astype(BF))
            kv = turn(joined[:, width:], turns, heads, True, 1.0).astype(BF)
            for head in range(heads):
                pairs[head, slot, here, :] = kv[:, head * 2 * HD : (head + 1) * 2 * HD]
        for head in range(heads):
            lanes = slice(head * HD, (head + 1) * HD)
            queries[head, here, :] = jnp.concatenate(
                [parts[0][:, lanes], parts[1][:, lanes]], axis=1
            )

    def attention():
        tasks = [gather_br(links, shifted, held_x), gather_tok(links, qkv_shard, held_w)]
        while tasks:
            for task in list(tasks):
                try:
                    next(task)
                except StopIteration:
                    tasks.remove(task)
            yield
        links.local(held_x, x_out)
        links.local(held_w, w_out)
        links.settle(rotary)
        for half in range(2):
            project(half)
        sent = [
            (d, links.send(pairs.at[(y + d) % 4], kv_mine.at[y], dy=d)) for d in (1, 3, 2)
        ]
        links.local(pairs.at[y], kv_mine.at[y])
        links.local(queries, q_heads)
        for unused in range(12):
            yield
        for d, ticket in sent:
            links.arrived(ticket, kv_mine.at[(y - d) % 4])

    def feed_forward():
        ff_shard[:, :main] = turned(down[:main, :])
        tail = down.shape[0] - main
        ends = jnp.concatenate([down[main:, :], jnp.zeros((128 - tail, rows), BF)], axis=0)
        ff_shard[:, main : main + 128] = turned(ends)
        at = main + 128
        ff_shard[:, at : at + width] = turned(out[...])
        at += width
        ff_shard[:, at : at + main] = turned(gate[:main, :])
        ff_shard[:, at + main : at + 2 * main] = turned(up[:main, :])
        ends = jnp.concatenate([gate[main:, :], up[main:, :]], axis=0)
        ff_shard[:, at + 2 * main :] = turned(ends)
        yield
        yield from gather_tok(links, ff_shard, f_out)

    def gradient():
        for unused in range(3):
            yield
        yield from gather_br(links, cot, g_out)

    in_turn([attention(), feed_forward(), gradient()])
    links.close()


def start(
    block_map, tokens, gain, bias, cot, qkv, qkv_bias, gate, up, down, out, table, heads, main
):
    rows, depth = tokens.shape
    wrows = qkv.shape[1]
    width = heads * HD
    cols = main + 128 + width + 2 * gate.shape[0]
    whole = jax.ShapeDtypeStruct((2, 4, rows, depth), BF)
    places = jnp.asarray(bias_places(heads, qkv_bias.shape[2]))
    flat = jnp.pad(qkv_bias.reshape(1, -1).astype(F32), ((0, 7), (0, 128 - qkv_bias.size)))
    args = (block_map, tokens, gain, bias, cot, qkv, flat, places, gate, up, down, out, table)
    copies = 72
    shapes = (
        whole,
        whole,
        jax.ShapeDtypeStruct((4, 2, 2, wrows, 3 * width + 128), BF),
        jax.ShapeDtypeStruct((4, 2, 2, wrows, cols), BF),
        jax.ShapeDtypeStruct((heads, 2, BLK, 2 * HD), BF),
        jax.ShapeDtypeStruct((heads, BLK, 2 * HD), BF),
    )
    specs = [SMEM] + [VMEM] * (len(args) - 1)
    specs[4] = specs[12] = ANY
    return pl.pallas_call(
        functools.partial(start_kernel, heads, main),
        out_shape=shapes,
        in_specs=specs,
        out_specs=(ANY,) * len(shapes),
        scratch_shapes=[
            pltpu.VMEM((rows, depth), BF),
            pltpu.VMEM((wrows, 3 * width + 128), BF),
            pltpu.VMEM((wrows, cols), BF),
            pltpu.VMEM(whole.shape, BF),
            pltpu.VMEM(shapes[2].shape, BF),
            pltpu.VMEM(shapes[4].shape, BF),
            pltpu.VMEM(shapes[5].shape, BF),
            pltpu.VMEM(table.shape, F32),
            pltpu.SemaphoreType.DMA((copies,)),
            pltpu.SemaphoreType.DMA((copies,)),
            pltpu.SemaphoreType.DMA((32,)),
        ],
        compiler_params=pltpu.CompilerParams(
            collective_id=0, has_side_effects=True, vmem_limit_bytes=60 * 2**20
        ),
        cost_estimate=SMALL,
        name="start",
    )(*args)


def ff_heads_kernel(
    main,
    down,
    first,
    x_ref,
    g_ref,
    x_strip,
    g_strip,
    weights,
    kv_mine,
    q_heads,
    h_ref,
    a_ref,
    grad_ref,
    asked,
    pairs,
    w_ref,
    held,
    held_hidden,
    outs,
    *sems,
):
    y, z, c, unused_l, unused_x = coords()
    step = pl.program_id(0)
    final = pl.num_programs(0) - 1
    links = Links(*sems)
    order = (1, 3, 2)
    rows = x_ref.shape[1]

    loads = [
        pltpu.make_async_copy(weights.at[:, part], w_ref.at[:, part], sems[2].at[n])
        for n, part in ((0, pl.ds(first, w_ref.shape[1] - first)), (4, pl.ds(0, first)))
    ]
    kept = [
        pltpu.make_async_copy(kv_mine, pairs.at[:, z, c], sems[2].at[1]),
        pltpu.make_async_copy(q_heads.at[y], asked.at[y, 0], sems[2].at[2]),
    ]
    kept_out = pltpu.make_async_copy(outs.at[y], asked.at[y, 1], sems[2].at[3])
    number = iter(range(64))

    def plan(source, target, lands, **offsets):
        n = next(number)
        return links.copy(n, source, target, offsets), links.copy(n, lands, lands, offsets)

    def swap(source, k):
        return [
            plan(source.at[(y + d) % 4], asked.at[y, k], asked.at[(y - d) % 4, k], dy=d)
            for d in order
        ]

    far = [plan(kv_mine.at[i], pairs.at[i, z, c], pairs.at[i, 1 - z, c], dz=1) for i in range(4)]
    near = [plan(kv_mine.at[i], pairs.at[i, z, c], pairs.at[i, z, 1 - c], dc=1) for i in range(4)]
    diagonal = [
        plan(pairs.at[i, 1 - z, c], pairs.at[i, 1 - z, c], pairs.at[i, 1 - z, 1 - c], dc=1)
        for i in range(4)
    ]
    asked_q, asked_o = swap(q_heads, 0), swap(outs, 1)

    def cross(i):
        far[i][1].wait_recv()
        diagonal[i][0].start()

    @pl.when(step == 0)
    def _():
        for load in loads:
            load.start()
        links.greet([dict(dz=1), dict(dc=1), dict(dy=1), dict(dy=2), dict(dy=3)])
        for copy, unused in far + near + asked_q:
            copy.start()
        for copy in kept:
            copy.start()
        loads[0].wait()

    def pause(point):
        if point == 0:

            @pl.when(step == 0)
            def _():
                loads[1].wait()

        @pl.when(step == 1)
        def _():
            cross(point)

    for i in range(2, 4):

        @pl.when(step == i + 1)
        def _():
            cross(i)

    here = pl.ds(pl.multiple_of(jnp.minimum(step, 1) * rows, rows), rows)

    def mixed_grad(value):
        for head in range(outs.shape[0]):
            lanes = slice(head * HD, (head + 1) * HD)
            outs[head, here, :] = jnp.concatenate(
                [value[:rows, lanes], value[rows:, lanes]], axis=1
            )

    @pl.when(step < 2)
    def _():
        grads, hidden = ff_part(
            main, down, first, x_ref[...], g_ref[...], w_ref, h_ref, a_ref, mixed_grad, pause
        )
        held[:, here, :] = grads.reshape(2, rows, -1)
        held_hidden[:, here, :] = hidden.reshape(2, rows, -1)

    @pl.when(step == 1)
    def _():
        for copy, unused in asked_o:
            copy.start()
        kept_out.start()

    @pl.when(step >= 2)
    def _():
        grads = held[...].reshape(-1, held.shape[2])
        hidden = held_hidden[...].reshape(-1, down)
        grad_ref[:, :down] = dot(g_strip[...], hidden, TN).astype(BF)
        grad_ref[:, down:] = dot(x_strip[...], grads, TN).astype(BF)

    @pl.when(step == final)
    def _():
        for copy in kept + [kept_out]:
            copy.wait()
        for unused, landed in near + diagonal + asked_q + asked_o:
            landed.wait_recv()
        for copy, unused in far + near + diagonal + asked_q + asked_o:
            copy.wait_send()


def ff_heads(x, g, w, kv_mine, q_heads, main, down, first):
    depth, cols = w.shape
    heads, unused, span, lanes = kv_mine.shape
    rows = BLK // 2
    both = cols - first
    strip = 512

    def tile(width):
        return pl.BlockSpec((2, rows, width), lambda i: (0, jnp.minimum(i, 1), 0))

    return pl.pallas_call(
        functools.partial(ff_heads_kernel, main, down, first),
        grid=(2 + depth // strip,),
        in_specs=[
            tile(depth),
            tile(depth),
            pl.BlockSpec((2 * BLK, strip), lambda i: (0, jnp.maximum(i - 2, 0))),
            pl.BlockSpec((2 * BLK, strip), lambda i: (0, jnp.maximum(i - 2, 0))),
            ANY,
            ANY,
            ANY,
        ],
        out_specs=(
            tile(down),
            tile(both),
            pl.BlockSpec((strip, both + down), lambda i: (jnp.maximum(i - 2, 0), 0)),
            ANY,
            ANY,
        ),
        out_shape=(
            jax.ShapeDtypeStruct((2, BLK, down), BF),
            jax.ShapeDtypeStruct((2, BLK, both), BF),
            jax.ShapeDtypeStruct((depth, both + down), BF),
            jax.ShapeDtypeStruct((4, 2, span, lanes), BF),
            jax.ShapeDtypeStruct((4, 2, 2, 2, span, lanes), BF),
        ),
        scratch_shapes=[
            pltpu.VMEM((depth, cols), BF),
            pltpu.VMEM((2, BLK, both), BF),
            pltpu.VMEM((2, BLK, down), BF),
            pltpu.VMEM(q_heads.shape, BF),
            pltpu.SemaphoreType.DMA((32,)),
            pltpu.SemaphoreType.DMA((32,)),
            pltpu.SemaphoreType.DMA((5,)),
        ],
        compiler_params=pltpu.CompilerParams(
            collective_id=1, has_side_effects=True, vmem_limit_bytes=60 * 2**20
        ),
        cost_estimate=SMALL,
        name="ff_heads",
    )(x, g, x.reshape(2 * BLK, depth), g.reshape(2 * BLK, depth), w, kv_mine, q_heads)


def residual(tokens):
    def finish(column):
        def add(value, here):
            return value + tokens[here, column : column + value.shape[1]].astype(F32)

        return add

    return finish


def home_kernel(
    heads,
    grads,
    dq,
    o_parts,
    hidden,
    grad_both,
    weights,
    tokens,
    dq_home,
    grads_home,
    mixed_out,
    result,
    grad_x,
    *rest,
):
    mine, near, far, total, held_w, held_h, held_o, held_wa, held_a, held_x = rest[:10]
    space = ScatterSpace(rest[10:14])
    links = Links(*rest[14:])
    y, unused_z, unused_c, unused_l, unused_x = coords()
    rows, depth = tokens.shape
    kept = held_w.shape[1]
    links.greet(BR_NEAR + TOK_ALL)
    loads = [
        links.local(o_parts.at[y], held_o.at[y]),
        links.local(hidden, held_h),
        links.local(weights.at[:, pl.ds(0, kept)], held_w),
    ]
    later = [
        links.local(weights.at[:, pl.ds(kept, held_wa.shape[1])], held_wa),
        links.local(grad_both, held_a),
    ]
    returned = [
        (d, links.send(o_parts.at[(y + d) % 4], held_o.at[y], dy=d)) for d in (1, 3, 2)
    ]

    def make(there):
        here = pl.ds(pl.multiple_of(there * rows, rows), rows)
        mixed = [
            jnp.concatenate(
                [held_o[head, here, slot * HD : (slot + 1) * HD] for head in range(heads)],
                axis=1,
            )
            for slot in range(2)
        ]
        for slot in range(2):
            mixed_out[slot, here, :] = mixed[slot]
        both = jnp.concatenate(
            [held_h[:, here, :].reshape(2 * rows, -1), jnp.concatenate(mixed, axis=0)], axis=1
        )
        branches = dot(both, held_w[...], NT).astype(BF)
        for slot in range(2):
            space.pieces[slot, there] = branches[slot * rows : (slot + 1) * rows]

    def output():
        yield
        for d, ticket in returned:
            links.arrived(ticket, held_o.at[(y - d) % 4])
        for load in loads:
            links.settle(load)
        yield from scatter_br(links, make, space, result, residual(tokens))

    def gradient():
        for unused in range(5):
            yield
        for load in later:
            links.settle(load)
        for tile in range(4):
            here = slice(tile * rows, (tile + 1) * rows)
            part = held_a[:, here, :].reshape(2 * rows, -1)
            held_x[:, here, :] = dot(part, held_wa[...], NT).astype(BF).reshape(2, rows, depth)
            span = pl.ds(tile * rows, rows)
            links.local(held_x.at[:, span], grad_x.at[:, span])
            yield

    in_turn(
        [
            gradient(),
            reduce_heads(links, grads, dq, dq_home, grads_home, mine, near, far, total),
            output(),
        ]
    )
    links.close()


def heads_home(grads, dq, o_parts, hidden, grad_both, weights, tokens, heads):
    rows, depth = tokens.shape
    span, lanes = grads.shape[3:]
    width = heads * HD
    kept = hidden.shape[2] + width
    return comm_call(
        functools.partial(home_kernel, heads),
        "heads_home",
        2,
        (grads, dq, o_parts, hidden, grad_both, weights, tokens),
        (
            jax.ShapeDtypeStruct(dq.shape, BF),
            jax.ShapeDtypeStruct((4, span, lanes), BF),
            jax.ShapeDtypeStruct((2, BLK, width), BF),
            jax.ShapeDtypeStruct((rows, depth), BF),
            jax.ShapeDtypeStruct((2, BLK, depth), BF),
        ),
        scratch=[
            pltpu.VMEM((4, 2, span, lanes), BF),
            pltpu.VMEM((4, 2, span, lanes), BF),
            pltpu.VMEM((4, span, lanes), BF),
            pltpu.VMEM((4, span, lanes), BF),
            pltpu.VMEM((depth, kept), BF),
            pltpu.VMEM(hidden.shape, BF),
            pltpu.VMEM(o_parts.shape, BF),
            pltpu.VMEM((depth, grad_both.shape[2]), BF),
            pltpu.VMEM(grad_both.shape, BF),
            pltpu.VMEM((2, BLK, depth), BF),
        ]
        + ScatterSpace.shapes(rows, depth, depth),
        in_vmem=(6,),
        out_vmem=(2, 3),
        copies=64,
    )


def normal_rows(tokens, normed, scales):
    rows = tokens.shape[0]
    chunk = 16

    def step(i, unused):
        here = pl.ds(pl.multiple_of(i * chunk, chunk), chunk)
        value = tokens[here, :].astype(F32)
        value = value - jnp.mean(value, axis=-1, keepdims=True)
        scale = lax.rsqrt(jnp.mean(value * value, axis=-1, keepdims=True) + EPSILON)
        normed[here, :] = value * scale
        scales[here, :] = jnp.broadcast_to(scale, (chunk, 128))
        return unused

    lax.fori_loop(0, rows // chunk, step, 0)


def turn_back(grads, normed, scales, cot, gain, parts, result):
    rows, depth = normed.shape
    chunk = 16

    def rows_at(i):
        return pl.ds(pl.multiple_of(i * chunk, chunk), chunk)

    def sums(i, carry):
        here = rows_at(i)
        grad = grads[here, :]
        up = (grad * normed[here, :]).reshape(2, 8, depth)
        return carry[0] + up.sum(0), carry[1] + grad.reshape(2, 8, depth).sum(0)

    zero = jnp.zeros((8, depth), F32)
    found = lax.fori_loop(0, rows // chunk, sums, (zero, zero))
    for k in range(2):
        line = jnp.sum(found[k], axis=0, keepdims=True)
        parts[16 * k : 16 * (k + 1), :] = jnp.concatenate(
            [line[:, t * 128 : (t + 1) * 128] for t in range(depth // 128)], axis=0
        )
    yield

    def back(i, unused):
        here = rows_at(i)
        line = normed[here, :]
        grad = grads[here, :] * gain[...]
        slope = jnp.mean(grad * line, axis=-1, keepdims=True)
        grad = grad - jnp.mean(grad, axis=-1, keepdims=True) - line * slope
        result[here, :] = cot[here, :].astype(F32) + scales[here, :1] * grad
        return unused

    middle = rows // chunk // 2
    lax.fori_loop(0, middle, back, 0)
    yield
    lax.fori_loop(middle, 2 * middle, back, 0)


BR_PEERS = [dict(dl=i // 4, dx=i % 4) for i in range(1, 8)]
TOK_PEERS = [dict(dy=i // 4, dz=(i // 2) % 2, dc=i % 2) for i in range(1, 16)]


def last_kernel(
    heads,
    dq,
    dkv,
    table,
    x_in,
    g_in,
    m_in,
    w_in,
    s_in,
    tokens,
    cot,
    gain,
    block_map,
    result,
    qkv_out,
    out_out,
    sides,
    *rest,
):
    held_q, held_kv, held_t, held_x, held_g, held_m, held_w, held_s, gj = rest[:9]
    parts, near, side, out, far, wsum, summed, normed, scales = rest[9:18]
    lines, lines_in, last, last_in, bias_acc = rest[18:23]
    space = ScatterSpace(rest[23:30])
    links = Links(*rest[30:])
    y, z, c, l, x = coords()
    links.greet(BR_PEERS + TOK_PEERS)
    width = heads * HD
    rows, depth = tokens.shape
    first = [
        links.local(dq, held_q),
        links.local(dkv, held_kv),
        links.local(table, held_t),
    ]
    third = [links.local(w_in.at[:, pl.ds(0, 3 * width)], held_w), links.local(s_in, held_s)]
    second = [
        links.local(x_in, held_x),
        links.local(g_in, held_g),
        links.local(m_in, held_m),
    ]
    wrows = parts.shape[3]
    strip = 4 * wrows
    bias_acc[...] = jnp.zeros_like(bias_acc)

    def settle(loads):
        for load in loads:
            links.settle(load)
        loads.clear()

    def turn_rows(here):
        for slot in range(2):
            lanes = slice(slot * HD, (slot + 1) * HD)
            turns = table_rows(held_t, block_map, slot, here)
            q = jnp.concatenate([held_q[h, here, lanes] for h in range(heads)], axis=1)
            q = turn(q.astype(F32), turns, heads // 2, False, -1.0).astype(BF)
            kv = jnp.concatenate([held_kv[h, slot, here, :] for h in range(heads)], axis=1)
            kv = turn(kv.astype(F32), turns, heads, True, -1.0).astype(BF)
            both = jnp.concatenate([q, kv], axis=1)
            gj[slot, here, :] = both
            bias_acc[...] += jnp.sum(
                both.astype(F32).reshape(rows // 8, 8, 3 * width), axis=0
            )

    def bias_lines():
        total = jnp.sum(bias_acc[...], axis=0, keepdims=True)
        line = [total[:, :width]]
        for k in range(2):
            at = [width + (2 * h + k) * HD for h in range(heads)]
            line.append(jnp.concatenate([total[:, a : a + HD] for a in at], axis=1))
        line = jnp.concatenate(line, axis=1)
        return jnp.concatenate(
            [line[:, r * 128 : (r + 1) * 128] for r in range(3 * width // 128)], axis=0
        )

    def weights_of(there):
        settle(second)
        here = pl.ds(pl.multiple_of(there * strip, strip), strip)
        qkv = dot(held_x[:, here], gj[...].reshape(2 * BLK, 3 * width), TN).astype(BF)
        outs = dot(held_g[:, here], held_m[...], TN).astype(BF)
        for k in range(4):
            at = slice(k * wrows, (k + 1) * wrows)
            parts[there, k // 2, k % 2, :, : 3 * width] = qkv[at]
            parts[there, k // 2, k % 2, :, 3 * width : 4 * width] = outs[at]

    def rows_of(there):
        settle(first)
        here = pl.ds(pl.multiple_of(there * rows, rows), rows)
        turn_rows(here)
        settle(third)
        both = gj[:, here, :].reshape(2 * rows, 3 * width)
        grads = dot(both, held_w[...], NT)
        for slot in range(2):
            value = grads[slot * rows : (slot + 1) * rows] + held_s[slot, here, :].astype(F32)
            space.pieces[slot, there] = value.astype(BF)

    def shifted():
        yield from scatter_br(links, rows_of, space, summed, lambda column: plain)
        through = turn_back(summed, normed, scales, cot, gain, lines, result)
        next(through)
        near_sums = [links.send(lines, lines_in.at[i], **o) for i, o in enumerate(BR_PEERS)]
        yield
        next(through)
        bias_sums = bias_lines()
        sums = lines[...]
        for i, ticket in enumerate(near_sums):
            links.arrived(ticket, lines_in.at[i])
            sums = sums + lines_in[i]
        for t in range(16):
            last[t] = jnp.concatenate([sums[t : t + 1], sums[16 + t : 17 + t], bias_sums], axis=0)
        all_sums = []
        for i, o in enumerate(TOK_PEERS):
            there = ((y + o["dy"]) % 4) * 4 + ((z + o["dz"]) % 2) * 2 + (c + o["dc"]) % 2
            all_sums.append(links.send(last.at[there], last_in.at[i], **o))
        yield
        for unused in through:
            pass
        yield
        sums = last[y * 4 + z * 2 + c]
        for i, ticket in enumerate(all_sums):
            links.arrived(ticket, last_in.at[i])
            sums = sums + last_in[i]
        sides[...] = sums

    def weights():
        for unused in range(4):
            yield
        yield from reduce_tok(links, weights_of, parts, near, side, out, far, wsum)
        qkv_out[0] = wsum[:, :width]
        for k in range(2):
            at = [width + (2 * h + k) * HD for h in range(heads)]
            qkv_out[1 + k] = jnp.concatenate([wsum[:, a : a + HD] for a in at], axis=1)
        out_out[...] = jnp.transpose(wsum[:, 3 * width :])

    def aside():
        for unused in range(5):
            yield
        normal_rows(tokens, normed, scales)

    in_turn([shifted(), weights(), aside()])
    links.close()


def last_sums(
    dq, dkv, table, x, g, mixed, w, partial_grad, tokens, cot, gain, block_map, heads
):
    rows, depth = tokens.shape
    wrows = depth // 16
    width = heads * HD
    cols = 4 * width
    return comm_call(
        functools.partial(last_kernel, heads),
        "last_sums",
        3,
        (dq, dkv, table, x, g, mixed, w, partial_grad, tokens, cot, gain, block_map),
        (
            jax.ShapeDtypeStruct((rows, depth), F32),
            jax.ShapeDtypeStruct((3, wrows, width), F32),
            jax.ShapeDtypeStruct((width, wrows), F32),
            jax.ShapeDtypeStruct((8, 128), F32),
        ),
        scratch=[
            pltpu.VMEM(dq.shape, BF),
            pltpu.VMEM(dkv.shape, BF),
            pltpu.VMEM(table.shape, F32),
            pltpu.VMEM(x.shape, BF),
            pltpu.VMEM(g.shape, BF),
            pltpu.VMEM(mixed.shape, BF),
            pltpu.VMEM((depth, 3 * width), BF),
            pltpu.VMEM(partial_grad.shape, BF),
            pltpu.VMEM((2, BLK, 3 * width), BF),
            pltpu.VMEM((4, 2, 2, wrows, cols), BF),
            pltpu.VMEM((4, 2, wrows, cols), BF),
            pltpu.VMEM((3, 2, wrows, cols), BF),
            pltpu.VMEM((wrows, cols), BF),
            pltpu.VMEM((wrows, cols), BF),
            pltpu.VMEM((wrows, cols), F32),
            pltpu.VMEM((rows, depth), F32),
            pltpu.VMEM((rows, depth), F32),
            pltpu.VMEM((rows, 128), F32),
            pltpu.VMEM((32, 128), F32),
            pltpu.VMEM((7, 32, 128), F32),
            pltpu.VMEM((16, 8, 128), F32),
            pltpu.VMEM((15, 8, 128), F32),
            pltpu.VMEM((8, 3 * width), F32),
        ]
        + ScatterSpace.shapes(rows, depth, depth // 4 * 3),
        in_vmem=(8, 9, 10),
        in_smem=(11,),
        out_vmem=(0, 1, 2, 3),
        copies=96,
    )


def finish_kernel(main, grads, value, tokens, qkv, out, *outs):
    def lines(start, count):
        return jnp.transpose(grads[:, start : start + count].astype(F32))

    result, tokens_out, qkv_out, out_out, down, gate, up = outs
    result[...] = value[...]
    tokens_out[...] = tokens[...]
    qkv_out[...] = qkv[...]
    out_out[...] = out[...]
    tail = down.shape[0] - main
    down[:main, :] = lines(0, main)
    down[main:, :] = lines(main, 128)[:tail]
    at = main + 128
    gate[:main, :] = lines(at, main)
    up[:main, :] = lines(at + main, main)
    ends = lines(at + 2 * main, 128)
    gate[main:, :] = ends[:tail]
    up[main:, :] = ends[tail:]


def finish(grads, value, tokens, qkv, out, main, hidden_width):
    shape = jax.ShapeDtypeStruct((hidden_width, grads.shape[0]), F32)
    return pl.pallas_call(
        functools.partial(finish_kernel, main),
        out_shape=(
            jax.ShapeDtypeStruct(value.shape, BF),
            jax.ShapeDtypeStruct(tokens.shape, F32),
            jax.ShapeDtypeStruct(qkv.shape, F32),
            jax.ShapeDtypeStruct(out.shape, F32),
        )
        + (shape,) * 3,
        in_specs=[VMEM] * 5,
        out_specs=(VMEM,) * 7,
        cost_estimate=SMALL,
        name="finish",
    )(grads, value, tokens, qkv, out)


def rotary_table():
    half = ROT // 2
    frequency = (ROPE_BASE ** (-(np.arange(half) * 2.0 / ROT))).astype(np.float32)
    angles = np.arange(LB * BLK, dtype=np.float32)[:, None] * frequency[None, :]
    cos, sin = np.cos(angles), np.sin(angles)
    one = np.ones((LB * BLK, HD - ROT), np.float32)
    table = np.concatenate([cos, cos, one, -sin, sin, 0.0 * one], axis=1)
    return table.astype(np.float32).reshape(LB, BLK, 2 * HD)


def body(
    tokens,
    norm_gain,
    norm_bias,
    qkv_weight,
    qkv_bias,
    out_weight,
    gate_weight,
    up_weight,
    down_weight,
    cotangent,
    block_map,
    lengths,
):
    tok = lax.axis_index("tok")
    rows = tokens.shape[0]
    depth = tokens.shape[1]
    wrows = qkv_weight.shape[1]
    heads = qkv_bias.shape[1]
    width = heads * HD
    hidden_width = gate_weight.shape[1]
    main = hidden_width // 128 * 128
    tail = hidden_width - main

    down_width = main + 128
    first = down_width + width
    table = jnp.asarray(rotary_table())
    x, grad, qkv_full, ff_full, kv_mine, q_heads = start(
        block_map,
        tokens,
        norm_gain.reshape(1, depth),
        norm_bias.reshape(1, depth),
        cotangent,
        qkv_weight,
        qkv_bias,
        jnp.transpose(gate_weight),
        jnp.transpose(up_weight),
        down_weight,
        out_weight,
        table,
        heads,
        main,
    )
    x = x.reshape(2, BLK, depth)
    grad = grad.reshape(2, BLK, depth)
    qkv_full = qkv_full.reshape(16 * wrows, -1)
    ff_full = ff_full.reshape(16 * wrows, -1)

    hidden, grad_both, grad_ff, qd_all, kv_all = ff_heads(
        x, grad, ff_full, kv_mine, q_heads, main, down_width, first
    )
    kv_all = kv_all.reshape(-1, 2 * HD)
    x = x.reshape(2 * BLK, depth)
    grad = grad.reshape(2 * BLK, depth)
    grad_ff = lax.psum_scatter(grad_ff, "tok", scatter_dimension=0, tiled=True)

    o_parts, dq_parts, dkv_all = attention(block_map, lengths, qd_all, kv_all)
    dq_heads, dkv_heads, mixed, result, grad_x = heads_home(
        dkv_all.reshape(4, 2, 2, 2 * BLK, 2 * HD),
        dq_parts,
        o_parts,
        hidden,
        grad_both,
        ff_full,
        tokens,
        heads,
    )
    grad_tokens, grad_qkv, grad_out, sides = last_sums(
        dq_heads,
        dkv_heads.reshape(heads, 2, BLK, 2 * HD),
        table,
        x,
        grad,
        mixed.reshape(2 * BLK, width),
        qkv_full,
        grad_x,
        tokens,
        cotangent,
        norm_gain.reshape(1, depth),
        block_map,
        heads,
    )
    grad_qkv_bias = lax.dynamic_slice_in_dim(
        sides[2:].reshape(3, heads, HD), tok * qkv_bias.shape[2], qkv_bias.shape[2], 2
    )
    grad_ff, grad_tokens = lax.optimization_barrier((grad_ff, grad_tokens))
    result, grad_tokens, grad_qkv, grad_out, grad_down, grad_gate, grad_up = finish(
        grad_ff, result, grad_tokens, grad_qkv, grad_out, main, hidden_width
    )

    sides = lax.dynamic_slice_in_dim(sides[:2], lax.axis_index("br") * 16, 16, 1)
    return (
        result,
        grad_tokens,
        sides[0],
        sides[1],
        grad_qkv,
        grad_qkv_bias,
        grad_out,
        jnp.transpose(grad_gate),
        jnp.transpose(grad_up),
        grad_down,
    )


def solution(mesh):
    in_specs = (
        P(("tok", "br"), None),
        P(),
        P(),
        P(None, "tok", "br"),
        P(None, "br", "tok"),
        P("br", "tok"),
        P("tok", "br"),
        P("tok", "br"),
        P("br", "tok"),
        P(("tok", "br"), None),
        P(),
        P(),
    )
    out_specs = (
        P(("tok", "br"), None),
        P(("tok", "br"), None),
        P(("tok", "br")),
        P(("tok", "br")),
        P(None, "tok", "br"),
        P(None, "br", "tok"),
        P("br", "tok"),
        P("tok", "br"),
        P("tok", "br"),
        P("br", "tok"),
    )
    return jax.shard_map(body, mesh=mesh, in_specs=in_specs, out_specs=out_specs, check_vma=False)
```

```python
import functools

import jax
import jax.numpy as jnp
import numpy as np
from jax import lax
from jax.experimental import pallas as pl
from jax.experimental.pallas import tpu as pltpu
from jax.sharding import PartitionSpec as P

HD = 64
ROT = 16
BLK = 512
LB = 8
EPSILON = 1e-05
ROPE_BASE = 10000.0
MASKED = -1e30
BF = jnp.bfloat16
F32 = jnp.float32
NN = (((1,), (0,)), ((), ()))
NT = (((1,), (1,)), ((), ()))
TN = (((0,), (0,)), ((), ()))
VMEM = pl.BlockSpec(memory_space=pltpu.VMEM)
SMEM = pl.BlockSpec(memory_space=pltpu.SMEM)
ANY = pl.BlockSpec(memory_space=pl.ANY)
SMALL = pl.CostEstimate(flops=1000, bytes_accessed=1000, transcendentals=0)


def dot(left, right, dims):
    return lax.dot_general(left, right, dims, preferred_element_type=F32)


def block_info(block, long_blocks):
    is_long = block < long_blocks
    place = jnp.where(is_long, block % LB, (block - long_blocks) % 2)
    return is_long, place, block - place


def lane_half(packed, half, upper):
    piece = packed[:, half * HD : (half + 1) * HD]
    zero = jnp.zeros_like(piece)
    return jnp.concatenate([zero, piece] if upper else [piece, zero], axis=1)


def allowed_pairs(place, step, limit):
    key_pos = step * BLK + lax.broadcasted_iota(jnp.int32, (BLK, BLK), 0)
    query_pos = place * BLK + lax.broadcasted_iota(jnp.int32, (BLK, BLK), 1)
    return (key_pos <= query_pos) & (key_pos < limit)


def attn_kernel(
    block_map, lengths, q_ref, kv_ref, o_ref, dq_ref, dkv_ref, slot_of, ot, lses, acc, dqt
):
    total_blocks = block_map.shape[0]
    long_blocks = total_blocks // 2
    own = lax.axis_index("tok") % 4

    def note(slot, unused):
        slot_of[block_map[slot]] = slot
        return unused

    lax.fori_loop(0, total_blocks, note, 0)

    def about(i, half):
        block = block_map[2 * (4 * i + own) + half]
        is_long, place, first = block_info(block, long_blocks)
        row = jnp.where(
            is_long, block // LB, long_blocks // LB + (block - long_blocks) // 2
        )
        return is_long, place, first, lengths[row]

    def rows_at(block):
        return pl.ds(pl.multiple_of(slot_of[block] * BLK, BLK), BLK)

    def forward(i, unused):
        packed = q_ref[i, 0]
        for half in range(2):
            is_long, place, first, limit = about(i, half)
            queries = lane_half(packed, half, False) * jnp.asarray(0.125, BF)

            def step(j, carry, masked):
                top, total, summed = carry
                kv = kv_ref[rows_at(first + j), :]
                scores = dot(kv, queries, NT)
                if masked:
                    scores = jnp.where(allowed_pairs(place, j, limit), scores, MASKED)
                new_top = jnp.maximum(top, jnp.max(scores, axis=0, keepdims=True))
                fade = jnp.exp(top - new_top)
                probs = jnp.exp(scores - new_top)
                total = total * fade + jnp.sum(probs, axis=0, keepdims=True)
                summed = summed * fade + dot(kv, probs.astype(BF), TN)
                return new_top, total, summed

            free = jnp.where(is_long, place, 0)
            carry = (
                jnp.full((1, BLK), MASKED, F32),
                jnp.zeros((1, BLK), F32),
                jnp.zeros((2 * HD, BLK), F32),
            )
            carry = lax.fori_loop(0, free, lambda j, c: step(j, c, False), carry)
            top, total, summed = lax.fori_loop(
                free, place + 1, lambda j, c: step(j, c, True), carry
            )
            lses[2 * i + half] = top + jnp.log(total)
            ot[i, half * HD : (half + 1) * HD, :] = summed[HD:, :] / total
        o_ref[i] = jnp.transpose(ot[i]).astype(BF)
        return unused

    lax.fori_loop(0, q_ref.shape[0], forward, 0)
    acc[...] = jnp.zeros_like(acc)

    def backward(i, unused):
        q_packed = q_ref[i, 0]
        d_packed = q_ref[i, 1]
        d_turned = jnp.transpose(d_packed.astype(F32))
        for half in range(2):
            is_long, place, first, limit = about(i, half)
            queries = lane_half(q_packed, half, False) * jnp.asarray(0.125, BF)
            grads = lane_half(d_packed, half, True)
            both = jnp.concatenate([queries, grads], axis=0)
            lanes = slice(half * HD, (half + 1) * HD)
            delta = jnp.sum(d_turned[lanes] * ot[i, lanes, :], axis=0, keepdims=True)
            lse = lses[2 * i + half]

            def step(j, total, masked):
                rows = rows_at(first + j)
                kv = kv_ref[rows, :]
                scores = dot(kv, queries, NT)
                if masked:
                    scores = jnp.where(allowed_pairs(place, j, limit), scores, MASKED)
                probs = jnp.exp(scores - lse)
                ds = (probs * (dot(kv, grads, NT) - delta)).astype(BF)
                acc[rows, :] += dot(jnp.concatenate([ds, probs.astype(BF)], axis=1), both, NN)
                return total + dot(kv, ds, TN)

            free = jnp.where(is_long, place, 0)
            total = lax.fori_loop(
                0, free, lambda j, c: step(j, c, False), jnp.zeros((2 * HD, BLK), F32)
            )
            total = lax.fori_loop(free, place + 1, lambda j, c: step(j, c, True), total)
            dqt[lanes, :] = total[:HD, :] * 0.125
        dq_ref[i] = jnp.transpose(dqt[...]).astype(BF)
        return unused

    lax.fori_loop(0, q_ref.shape[0], backward, 0)

    def finish(i, unused):
        rows = pl.ds(pl.multiple_of(i * BLK, BLK), BLK)
        dkv_ref[rows, :] = acc[rows, :].astype(BF)
        return unused

    lax.fori_loop(0, kv_ref.shape[0] // BLK, finish, 0)


def attention(block_map, lengths, qd, kv):
    n = qd.shape[0]
    shape = jax.ShapeDtypeStruct((n, BLK, 2 * HD), BF)
    return pl.pallas_call(
        attn_kernel,
        out_shape=(shape, shape, jax.ShapeDtypeStruct(kv.shape, BF)),
        in_specs=[SMEM, SMEM, VMEM, VMEM],
        out_specs=(VMEM, VMEM, VMEM),
        scratch_shapes=[
            pltpu.SMEM(block_map.shape, jnp.int32),
            pltpu.VMEM((n, 2 * HD, BLK), F32),
            pltpu.VMEM((2 * n, 1, BLK), F32),
            pltpu.VMEM(kv.shape, F32),
            pltpu.VMEM((2 * HD, BLK), F32),
        ],
        compiler_params=pltpu.CompilerParams(vmem_limit_bytes=60 * 2**20),
        cost_estimate=SMALL,
        name="attention",
    )(block_map, lengths, qd, kv)


def turn(values, table, copies, paired, sign):
    width = values.shape[1]
    lane = lax.broadcasted_iota(jnp.int32, values.shape, 1) % HD
    partner = jnp.where(
        lane < ROT // 2,
        pltpu.roll(values, width - ROT // 2, 1),
        pltpu.roll(values, ROT // 2, 1),
    )
    cos, sin = table[:, :HD], sign * table[:, HD:]
    cos = jnp.concatenate([cos, jnp.ones_like(cos) if paired else cos], axis=1)
    sin = jnp.concatenate([sin, jnp.zeros_like(sin) if paired else sin], axis=1)
    cos = jnp.concatenate([cos] * copies, axis=1)
    sin = jnp.concatenate([sin] * copies, axis=1)
    return values * cos + partner * sin


def ff_part(main, down, first, x, g, w_ref, h_ref, a_ref, mixed_grad, pause):
    rows, depth = x.shape[1:]
    x = x.reshape(2 * rows, depth)
    g = g.reshape(2 * rows, depth)
    gate_up = dot(x, w_ref[:, first:], NN)
    pause(0)
    gh = dot(g, w_ref[:, :first], NN)
    mixed_grad(gh[:, down:].astype(BF))
    gh = gh[:, :down]
    ends = gate_up[:, 2 * main :]
    gate = jnp.concatenate([gate_up[:, :main], ends], axis=1)
    up = jnp.concatenate([gate_up[:, main : 2 * main], pltpu.roll(ends, HD, 1)], axis=1)
    sig = jax.nn.sigmoid(gate)
    silu = gate * sig
    hidden = (silu * up).astype(BF)
    d_gate = gh * up * sig * (1.0 + gate * (1.0 - sig))
    d_up = gh * silu
    tail = d_gate[:, main:] + pltpu.roll(d_up[:, main:], HD, 1)
    grads = jnp.concatenate(
        [d_gate[:, :main].astype(BF), d_up[:, :main].astype(BF), tail.astype(BF)], axis=1
    )
    h_ref[...] = hidden.reshape(h_ref.shape)
    pause(1)
    a_ref[...] = grads.reshape(a_ref.shape)
    return grads, hidden


def coords():
    tok, br = lax.axis_index("tok"), lax.axis_index("br")
    return tok // 4, (tok // 2) % 2, tok % 2, br // 4, br % 4


def peer(dy=0, dz=0, dc=0, dl=0, dx=0):
    y, z, c, l, x = coords()
    tok = ((y + dy) % 4) * 4 + ((z + dz) % 2) * 2 + (c + dc) % 2
    return tok, ((l + dl) % 2) * 4 + (x + dx) % 4


class Links:
    def __init__(self, send_sems, recv_sems, local_sems):
        self.sems = (send_sems, recv_sems, local_sems)
        self.sent, self.locals = [], []

    def greet(self, partners):
        barrier = pltpu.get_barrier_semaphore()
        for offsets in partners:
            pl.semaphore_signal(
                barrier, inc=1, device_id=peer(**offsets), device_id_type=pl.DeviceIdType.MESH
            )
        pl.semaphore_wait(barrier, len(partners))

    def copy(self, number, source, target, offsets):
        return pltpu.make_async_remote_copy(
            src_ref=source,
            dst_ref=target,
            send_sem=self.sems[0].at[number],
            recv_sem=self.sems[1].at[number],
            device_id=peer(**offsets),
            device_id_type=pl.DeviceIdType.MESH,
        )

    def send(self, source, target, **offsets):
        copy = self.copy(len(self.sent), source, target, offsets)
        copy.start()
        self.sent.append(copy)
        return len(self.sent) - 1, offsets

    def arrived(self, ticket, place):
        self.copy(ticket[0], place, place, ticket[1]).wait_recv()

    def local(self, source, target):
        copy = pltpu.make_async_copy(source, target, self.sems[2].at[len(self.locals)])
        copy.start()
        self.locals.append([copy, True])
        return len(self.locals) - 1

    def settle(self, number):
        copy, pending = self.locals[number]
        if pending:
            copy.wait()
        self.locals[number][1] = False

    def close(self):
        for number in range(len(self.locals)):
            self.settle(number)
        for copy in self.sent:
            copy.wait_send()


def in_turn(tasks):
    tasks = list(tasks)
    while tasks:
        for task in list(tasks):
            try:
                next(task)
            except StopIteration:
                tasks.remove(task)


def ring_four(links, own, place, axis, landed):
    right = links.send(own, place(0, None), **{axis: 1})
    left = links.send(own, place(0, None), **{axis: -1})
    yield
    links.arrived(right, place(-1, None))
    on_right = links.send(place(-1, 0), place(-1, 0), **{axis: 1})
    landed(-1)
    yield
    links.arrived(left, place(1, None))
    on_left = links.send(place(1, 1), place(1, 1), **{axis: -1})
    landed(1)
    yield
    links.arrived(on_right, place(2, 0))
    links.arrived(on_left, place(2, 1))
    landed(2)


def half_of(ref, part):
    if part is None:
        return ref
    rows = ref.shape[0] // 2
    return ref.at[pl.ds(part * rows, rows)]


def gather_br(links, own, whole):
    unused_y, unused_z, unused_c, l, x = coords()

    def place(dl):
        return lambda dx, part: half_of(whole.at[(l + dl) % 2, (x + dx) % 4], part)

    kept = links.local(own, place(0)(0, None))
    across = links.send(own, place(0)(0, None), dl=1)
    near = ring_four(links, own, place(0), "dx", lambda d: None)
    next(near)
    yield
    links.arrived(across, place(1)(0, None))
    far = ring_four(links, place(1)(0, None), place(1), "dx", lambda d: None)
    next(far)
    for unused in near:
        yield
    for unused in far:
        yield
    links.settle(kept)


def gather_tok(links, own, whole):
    y, z, c, unused_l, unused_x = coords()
    passed = []

    def place(dz, dc=0):
        return lambda dy, part: half_of(
            whole.at[(y + dy) % 4, (z + dz) % 2, (c + dc) % 2], part
        )

    def passer(dz):
        def landed(dy):
            ref = place(dz)(dy, None)
            passed.append((links.send(ref, ref, dc=1), place(dz, 1)(dy, None)))

        return landed

    kept = links.local(own, place(0)(0, None))
    across = links.send(own, place(0)(0, None), dz=1)
    near = ring_four(links, own, place(0), "dy", passer(0))
    next(near)
    passed.append((links.send(own, place(0)(0, None), dc=1), place(0, 1)(0, None)))
    yield
    links.arrived(across, place(1)(0, None))
    far = ring_four(links, place(1)(0, None), place(1), "dy", passer(1))
    next(far)
    passer(1)(0)
    for unused in near:
        yield
    for unused in far:
        yield
    links.settle(kept)
    for ticket, ref in passed:
        links.arrived(ticket, ref)


def add_up(target, sources, rows, finish):
    chunk = 16

    def step(i, unused):
        here = pl.ds(pl.multiple_of(i * chunk, chunk), chunk)
        total = sources[0][here, :].astype(F32)
        for source in sources[1:]:
            total = total + source[here, :].astype(F32)
        target[here, :] = finish(total, here).astype(target.dtype)
        return unused

    lax.fori_loop(0, rows // chunk, step, 0)


def plain(total, here):
    return total


def reduce_heads(links, grads, dq, dq_home, grads_home, mine, near, far, total):
    y, z, c, unused_l, unused_x = coords()
    order = (1, 3, 2, 0)
    held, from_core = {}, {}
    for dz in (1, 0):
        for d in order:
            place = ((y + d) % 4, (z + dz) % 2)
            from_core[d, dz] = links.send(
                grads.at[place[0], place[1], 1 - c], near.at[place[0], place[1]], dc=1
            )
            held[d, dz] = links.local(
                grads.at[place[0], place[1], c], mine.at[place[0], place[1]]
            )
    asked = [links.send(dq.at[(y + d) % 4], dq_home.at[y], dy=d) for d in order[:3]]
    links.local(dq.at[y], dq_home.at[y])
    yield
    rows = mine.shape[2]
    across = {}
    for d in order:
        here = (y + d) % 4
        links.arrived(from_core[d, 1], near.at[here, 1 - z])
        links.settle(held[d, 1])
        add_up(
            mine.at[here, 1 - z], [mine.at[here, 1 - z], near.at[here, 1 - z]], rows, plain
        )
        across[d] = links.send(mine.at[here, 1 - z], far.at[here], dz=1)
        yield
    home = {}
    for d in order:
        here = (y + d) % 4
        links.arrived(from_core[d, 0], near.at[here, z])
        links.settle(held[d, 0])
        links.arrived(across[d], far.at[here])
        add_up(
            total.at[here], [mine.at[here, z], near.at[here, z], far.at[here]], rows, plain
        )
        if d:
            home[d] = links.send(total.at[here], grads_home.at[y], dy=d)
        else:
            links.local(total.at[here], grads_home.at[y])
        yield
    for i, d in enumerate(order[:3]):
        links.arrived(asked[i], dq_home.at[(y - d) % 4])
        links.arrived(home[d], grads_home.at[(y - d) % 4])


class ScatterSpace:
    def __init__(self, refs):
        self.pieces, self.ring, self.out, self.far = refs[:4]
        if len(refs) > 4:
            self.across, self.sums, self.last = refs[4:]

    @staticmethod
    def shapes(rows, depth, half):
        def ring(parts, columns):
            return (parts, 2, rows + rows // 2, columns)

        sizes = [(2, 4, rows, depth), ring(2, half), (rows, half), (rows, half)]
        rest = depth - half
        if rest:
            sizes += [(4, rows, rest), (4, rows, rest), ring(1, rest)]
        return [pltpu.VMEM(size, BF) for size in sizes]


def ring_sum(links, pieces, ring, total, finish):
    unused_y, unused_z, unused_c, unused_l, x = coords()
    rows = total.shape[0]
    half = rows // 2
    halves = (pl.ds(0, half), pl.ds(half, half))
    passing = pl.ds(rows, half)
    whole = pl.ds(0, rows)
    opposite = pieces((x + 2) % 4)
    steps = (1, -1)
    first = [
        links.send(opposite.at[halves[k]], ring.at[k, passing], dx=steps[k]) for k in range(2)
    ]
    yield
    second = []
    for k in range(2):
        links.arrived(first[k], ring.at[k, passing])
        piece = pieces((x + steps[k]) % 4)
        add_up(
            piece.at[halves[k]], [piece.at[halves[k]], ring.at[k, passing]], half, plain
        )
        second.append(links.send(piece, ring.at[k, whole], dx=steps[k]))
        yield
    for k in range(2):
        links.arrived(second[k], ring.at[k, whole])
    add_up(total, [pieces(x), ring.at[0, whole], ring.at[1, whole]], rows, finish)


def scatter_br(links, make, space, target, finish):
    unused_y, unused_z, unused_c, l, x = coords()
    rows, half = space.out.shape
    split = half < target.shape[1]
    first, second = pl.ds(0, half), pl.ds(half, target.shape[1] - half)
    order = (2, 1, 3, 0)

    def part(to):
        return lambda there: space.pieces.at[to, there, :, first]

    folded = {}
    outer = ring_sum(links, part(1 - l), space.ring.at[0], space.out, plain)
    for d in order:
        there = (x + d) % 4
        make(there)
        if split:
            folded[d] = links.send(
                space.pieces.at[1 - l, there, :, second], space.across.at[there], dl=1
            )
        if d == 2:
            next(outer)
        yield
    inner = ring_sum(links, part(l), space.ring.at[1], target.at[:, first], finish(0))
    next(inner)
    yield from outer
    over = links.send(space.out, space.far, dl=1)
    next(inner)
    next(inner)
    yield
    rest = []
    for d in order if split else ():
        there = (x + d) % 4
        links.arrived(folded[d], space.across.at[there])
        own = space.pieces.at[l, there, :, second]
        add_up(space.sums.at[there], [own, space.across.at[there]], rows, plain)
        if d == 2:
            late = ring_sum(
                links,
                lambda there: space.sums.at[there],
                space.last.at[0],
                target.at[:, second],
                finish(half),
            )
            next(late)
            rest.append(late)
        yield

    def joined():
        links.arrived(over, space.far)
        mine = space.pieces.at[l, x, :, first]
        add_up(mine, [mine, space.far], rows, plain)
        yield
        yield from inner

    rest.append(joined())
    while rest:
        for task in list(rest):
            try:
                next(task)
            except StopIteration:
                rest.remove(task)
        yield


def reduce_tok(links, make, parts, near, side, out, far, target):
    y, z, c, unused_l, unused_x = coords()
    order = (1, 3, 2, 0)
    tickets = {}
    for d in order:
        here = (y + d) % 4
        make(here)
        tickets[d] = links.send(parts.at[here, :, 1 - c], near.at[here], dc=1)
        yield
    rows = out.shape[0]
    sent = {}
    for dz in (1, 0):
        k = (z + dz) % 2
        for i, d in enumerate(order):
            here = (y + d) % 4
            if dz:
                links.arrived(tickets[d], near.at[here])
            own = parts.at[here, k, c]
            add_up(own, [own, near.at[here, k]], rows, plain)
            if d:
                sent[dz, i] = links.send(own, side.at[i, k], dy=d)
            if dz:
                yield
    for i in range(3):
        links.arrived(sent[1, i], side.at[i, 1 - z])
        yield
    add_up(out, [parts.at[y, 1 - z, c]] + [side.at[i, 1 - z] for i in range(3)], rows, plain)
    across = links.send(out, far, dz=1)
    yield
    for i in range(3):
        links.arrived(sent[0, i], side.at[i, z])
    yield
    links.arrived(across, far)
    add_up(target, [parts.at[y, z, c]] + [side.at[i, z] for i in range(3)] + [far], rows, plain)


BR_NEAR = [dict(dl=1), dict(dx=1), dict(dx=-1)]
BR_ALL = BR_NEAR + [dict(dx=2)]
TOK_NEAR = [dict(dz=1), dict(dc=1), dict(dy=1), dict(dy=-1)]
TOK_ALL = TOK_NEAR + [dict(dy=2)]


def comm_call(
    kernel, name, number, args, outs, scratch=(), in_vmem=(), out_vmem=(), in_smem=(), copies=48
):
    return pl.pallas_call(
        kernel,
        out_shape=tuple(outs),
        in_specs=[
            VMEM if i in in_vmem else SMEM if i in in_smem else ANY for i in range(len(args))
        ],
        out_specs=tuple(VMEM if i in out_vmem else ANY for i in range(len(outs))),
        scratch_shapes=list(scratch)
        + [
            pltpu.SemaphoreType.DMA((copies,)),
            pltpu.SemaphoreType.DMA((copies,)),
            pltpu.SemaphoreType.DMA((32,)),
        ],
        compiler_params=pltpu.CompilerParams(
            collective_id=number, has_side_effects=True, vmem_limit_bytes=60 * 2**20
        ),
        cost_estimate=SMALL,
        name=name,
    )(*args)


def table_rows(table, block_map, slot, here):
    block = block_map[lax.axis_index("tok") * 2 + slot]
    long_blocks = 2 * LB
    place = jnp.where(block < long_blocks, block % LB, (block - long_blocks) % 2)
    return table[place, here, :]


def shift_rows(tokens, gain, bias, shifted):
    rows = tokens.shape[0]
    chunk = 16

    def step(i, unused):
        here = pl.ds(pl.multiple_of(i * chunk, chunk), chunk)
        value = tokens[here, :].astype(F32)
        value = value - jnp.mean(value, axis=-1, keepdims=True)
        scale = lax.rsqrt(jnp.mean(value * value, axis=-1, keepdims=True) + EPSILON)
        shifted[here, :] = (value * scale * gain[...] + bias[...]).astype(BF)
        return unused

    lax.fori_loop(0, rows // chunk, step, 0)


def turned(block):
    return jnp.transpose(block.astype(F32)).astype(BF)


def bias_places(heads, per):
    width = heads * HD
    places = np.zeros((128, 3 * width), np.float32)
    for column in range(3 * width):
        if column < width:
            part, head, lane = 0, column // HD, column % HD
        else:
            pair, lane = divmod(column - width, HD)
            part, head = 1 + pair % 2, pair // 2
        places[(part * heads + head) * per + lane % per, column] = 1.0
    return places


def start_kernel(
    heads,
    main,
    block_map,
    tokens,
    gain,
    bias,
    cot,
    qkv,
    qkv_bias,
    places,
    gate,
    up,
    down,
    out,
    table,
    x_out,
    g_out,
    w_out,
    f_out,
    kv_mine,
    q_heads,
    *rest,
):
    shifted, qkv_shard, ff_shard, held_x, held_w, pairs, queries, held_t = rest[:8]
    links = Links(*rest[8:])
    y, z, c, unused_l, unused_x = coords()
    width = heads * HD
    links.greet(BR_NEAR + TOK_ALL)
    rotary = links.local(table, held_t)
    shift_rows(tokens, gain, bias, shifted)
    rows, depth = tokens.shape
    kv = []
    for head in range(heads):
        lanes = slice(head * HD, (head + 1) * HD)
        kv += [qkv[1, :, lanes], qkv[2, :, lanes]]
    qkv_shard[:, : 3 * width] = jnp.concatenate([qkv[0]] + kv, axis=1)
    line = dot(qkv_bias[...], places[...], NN)
    lane = lax.broadcasted_iota(jnp.int32, line.shape, 1) % HD
    line = jnp.where(lane // (HD // 16) == lax.axis_index("tok"), line, 0.0)[:1]
    lines = [line[:, r * 128 : (r + 1) * 128] for r in range(3 * width // 128)]
    zero = jnp.zeros((qkv_shard.shape[0] - len(lines), 128), F32)
    qkv_shard[:, 3 * width :] = jnp.concatenate(lines + [zero], axis=0).astype(BF)

    def project(half):
        tile = 2 * rows
        here = slice(half * tile, (half + 1) * tile)
        span = held_x[:, 2 * half : 2 * half + 2].reshape(2 * tile, depth)
        corner = held_w[0, 0, 0, :8, 3 * width :].astype(F32)
        for t in range(1, 16):
            corner = corner + held_w[t // 4, t // 2 % 2, t % 2, :8, 3 * width :].astype(F32)
        added = jnp.concatenate([corner[r : r + 1] for r in range(len(lines))], axis=1)
        products = dot(span, held_w[...].reshape(depth, -1)[:, : 3 * width], NN) + added
        parts = []
        for slot in range(2):
            turns = table_rows(held_t, block_map, slot, here)
            joined = products[slot * tile : (slot + 1) * tile]
            parts.append(turn(joined[:, :width], turns, heads // 2, False, 1.0).astype(BF))
            kv = turn(joined[:, width:], turns, heads, True, 1.0).astype(BF)
            for head in range(heads):
                pairs[head, slot, here, :] = kv[:, head * 2 * HD : (head + 1) * 2 * HD]
        for head in range(heads):
            lanes = slice(head * HD, (head + 1) * HD)
            queries[head, here, :] = jnp.concatenate(
                [parts[0][:, lanes], parts[1][:, lanes]], axis=1
            )

    def attention():
        tasks = [gather_br(links, shifted, held_x), gather_tok(links, qkv_shard, held_w)]
        while tasks:
            for task in list(tasks):
                try:
                    next(task)
                except StopIteration:
                    tasks.remove(task)
            yield
        links.local(held_x, x_out)
        links.local(held_w, w_out)
        links.settle(rotary)
        for half in range(2):
            project(half)
        sent = [
            (d, links.send(pairs.at[(y + d) % 4], kv_mine.at[y], dy=d)) for d in (1, 3, 2)
        ]
        links.local(pairs.at[y], kv_mine.at[y])
        links.local(queries, q_heads)
        for unused in range(12):
            yield
        for d, ticket in sent:
            links.arrived(ticket, kv_mine.at[(y - d) % 4])

    def feed_forward():
        ff_shard[:, :main] = turned(down[:main, :])
        tail = down.shape[0] - main
        ends = jnp.concatenate([down[main:, :], jnp.zeros((128 - tail, rows), BF)], axis=0)
        ff_shard[:, main : main + 128] = turned(ends)
        at = main + 128
        ff_shard[:, at : at + width] = turned(out[...])
        at += width
        ff_shard[:, at : at + main] = turned(gate[:main, :])
        ff_shard[:, at + main : at + 2 * main] = turned(up[:main, :])
        ends = jnp.concatenate([gate[main:, :], up[main:, :]], axis=0)
        ff_shard[:, at + 2 * main :] = turned(ends)
        yield
        yield from gather_tok(links, ff_shard, f_out)

    def gradient():
        for unused in range(3):
            yield
        yield from gather_br(links, cot, g_out)

    in_turn([attention(), feed_forward(), gradient()])
    links.close()


def start(
    block_map, tokens, gain, bias, cot, qkv, qkv_bias, gate, up, down, out, table, heads, main
):
    rows, depth = tokens.shape
    wrows = qkv.shape[1]
    width = heads * HD
    cols = main + 128 + width + 2 * gate.shape[0]
    whole = jax.ShapeDtypeStruct((2, 4, rows, depth), BF)
    places = jnp.asarray(bias_places(heads, qkv_bias.shape[2]))
    flat = jnp.pad(qkv_bias.reshape(1, -1).astype(F32), ((0, 7), (0, 128 - qkv_bias.size)))
    args = (block_map, tokens, gain, bias, cot, qkv, flat, places, gate, up, down, out, table)
    copies = 72
    shapes = (
        whole,
        whole,
        jax.ShapeDtypeStruct((4, 2, 2, wrows, 3 * width + 128), BF),
        jax.ShapeDtypeStruct((4, 2, 2, wrows, cols), BF),
        jax.ShapeDtypeStruct((heads, 2, BLK, 2 * HD), BF),
        jax.ShapeDtypeStruct((heads, BLK, 2 * HD), BF),
    )
    specs = [SMEM] + [VMEM] * (len(args) - 1)
    specs[12] = ANY
    return pl.pallas_call(
        functools.partial(start_kernel, heads, main),
        out_shape=shapes,
        in_specs=specs,
        out_specs=(ANY,) * len(shapes),
        scratch_shapes=[
            pltpu.VMEM((rows, depth), BF),
            pltpu.VMEM((wrows, 3 * width + 128), BF),
            pltpu.VMEM((wrows, cols), BF),
            pltpu.VMEM(whole.shape, BF),
            pltpu.VMEM(shapes[2].shape, BF),
            pltpu.VMEM(shapes[4].shape, BF),
            pltpu.VMEM(shapes[5].shape, BF),
            pltpu.VMEM(table.shape, F32),
            pltpu.SemaphoreType.DMA((copies,)),
            pltpu.SemaphoreType.DMA((copies,)),
            pltpu.SemaphoreType.DMA((32,)),
        ],
        compiler_params=pltpu.CompilerParams(
            collective_id=0, has_side_effects=True, vmem_limit_bytes=60 * 2**20
        ),
        cost_estimate=SMALL,
        name="start",
    )(*args)


def ff_heads_kernel(
    main,
    down,
    first,
    x_ref,
    g_ref,
    x_strip,
    g_strip,
    weights,
    kv_mine,
    q_heads,
    h_ref,
    a_ref,
    grad_ref,
    asked,
    pairs,
    w_ref,
    held,
    held_hidden,
    outs,
    own_kv,
    own_q,
    *sems,
):
    y, z, c, unused_l, unused_x = coords()
    step = pl.program_id(0)
    final = pl.num_programs(0) - 1
    links = Links(*sems)
    order = (1, 3, 2)
    rows = x_ref.shape[1]

    loads = [
        pltpu.make_async_copy(weights.at[:, part], w_ref.at[:, part], sems[2].at[n])
        for n, part in ((0, pl.ds(first, w_ref.shape[1] - first)), (4, pl.ds(0, first)))
    ]
    taken = [
        pltpu.make_async_copy(kv_mine, own_kv, sems[2].at[1]),
        pltpu.make_async_copy(q_heads.at[y], own_q, sems[2].at[2]),
    ]
    kept = [
        pltpu.make_async_copy(own_kv, pairs.at[:, z, c], sems[2].at[5]),
        pltpu.make_async_copy(own_q, asked.at[y, 0], sems[2].at[6]),
    ]
    kept_out = pltpu.make_async_copy(outs.at[y], asked.at[y, 1], sems[2].at[3])
    number = iter(range(64))

    def plan(source, target, lands, **offsets):
        n = next(number)
        return links.copy(n, source, target, offsets), links.copy(n, lands, lands, offsets)

    def swap(source, k):
        return [
            plan(source.at[(y + d) % 4], asked.at[y, k], asked.at[(y - d) % 4, k], dy=d)
            for d in order
        ]

    far = [plan(kv_mine.at[i], pairs.at[i, z, c], pairs.at[i, 1 - z, c], dz=1) for i in range(4)]
    near = [plan(kv_mine.at[i], pairs.at[i, z, c], pairs.at[i, z, 1 - c], dc=1) for i in range(4)]
    diagonal = [
        plan(pairs.at[i, 1 - z, c], pairs.at[i, 1 - z, c], pairs.at[i, 1 - z, 1 - c], dc=1)
        for i in range(4)
    ]
    asked_q, asked_o = swap(q_heads, 0), swap(outs, 1)

    def cross(i):
        far[i][1].wait_recv()
        diagonal[i][0].start()

    @pl.when(step == 0)
    def _():
        for load in loads:
            load.start()
        links.greet([dict(dz=1), dict(dc=1), dict(dy=1), dict(dy=2), dict(dy=3)])
        for copy, unused in far + near + asked_q:
            copy.start()
        for copy in taken:
            copy.start()
        loads[0].wait()

    @pl.when(step == 1)
    def _():
        for copy in taken:
            copy.wait()
        for copy in kept:
            copy.start()

    def pause(point):
        if point == 0:

            @pl.when(step == 0)
            def _():
                loads[1].wait()

    for i in range(2):

        @pl.when(step == 3 + i)
        def _():
            cross(2 * i)
            cross(2 * i + 1)

    here = pl.ds(pl.multiple_of(jnp.minimum(step, 1) * rows, rows), rows)

    def mixed_grad(value):
        for head in range(outs.shape[0]):
            lanes = slice(head * HD, (head + 1) * HD)
            outs[head, here, :] = jnp.concatenate(
                [value[:rows, lanes], value[rows:, lanes]], axis=1
            )

    @pl.when(step < 2)
    def _():
        grads, hidden = ff_part(
            main, down, first, x_ref[...], g_ref[...], w_ref, h_ref, a_ref, mixed_grad, pause
        )
        held[:, here, :] = grads.reshape(2, rows, -1)
        held_hidden[:, here, :] = hidden.reshape(2, rows, -1)

    @pl.when(step == 1)
    def _():
        for copy, unused in asked_o:
            copy.start()
        kept_out.start()

    @pl.when(step >= 2)
    def _():
        grads = held[...].reshape(-1, held.shape[2])
        hidden = held_hidden[...].reshape(-1, down)
        grad_ref[:, :down] = dot(g_strip[...], hidden, TN).astype(BF)
        grad_ref[:, down:] = dot(x_strip[...], grads, TN).astype(BF)

    @pl.when(step == final)
    def _():
        for copy in kept + [kept_out]:
            copy.wait()
        for unused, landed in near + diagonal + asked_q + asked_o:
            landed.wait_recv()
        for copy, unused in far + near + diagonal + asked_q + asked_o:
            copy.wait_send()


def ff_heads(x, g, w, kv_mine, q_heads, main, down, first):
    depth, cols = w.shape
    heads, unused, span, lanes = kv_mine.shape
    rows = BLK // 2
    both = cols - first
    strip = 512

    def tile(width):
        return pl.BlockSpec((2, rows, width), lambda i: (0, jnp.minimum(i, 1), 0))

    return pl.pallas_call(
        functools.partial(ff_heads_kernel, main, down, first),
        grid=(2 + depth // strip,),
        in_specs=[
            tile(depth),
            tile(depth),
            pl.BlockSpec((2 * BLK, strip), lambda i: (0, jnp.maximum(i - 2, 0))),
            pl.BlockSpec((2 * BLK, strip), lambda i: (0, jnp.maximum(i - 2, 0))),
            ANY,
            ANY,
            ANY,
        ],
        out_specs=(
            tile(down),
            tile(both),
            pl.BlockSpec((strip, both + down), lambda i: (jnp.maximum(i - 2, 0), 0)),
            ANY,
            ANY,
        ),
        out_shape=(
            jax.ShapeDtypeStruct((2, BLK, down), BF),
            jax.ShapeDtypeStruct((2, BLK, both), BF),
            jax.ShapeDtypeStruct((depth, both + down), BF),
            jax.ShapeDtypeStruct((4, 2, span, lanes), BF),
            jax.ShapeDtypeStruct((4, 2, 2, 2, span, lanes), BF),
        ),
        scratch_shapes=[
            pltpu.VMEM((depth, cols), BF),
            pltpu.VMEM((2, BLK, both), BF),
            pltpu.VMEM((2, BLK, down), BF),
            pltpu.VMEM(q_heads.shape, BF),
            pltpu.VMEM(kv_mine.shape, BF),
            pltpu.VMEM(q_heads.shape[1:], BF),
            pltpu.SemaphoreType.DMA((32,)),
            pltpu.SemaphoreType.DMA((32,)),
            pltpu.SemaphoreType.DMA((7,)),
        ],
        compiler_params=pltpu.CompilerParams(
            collective_id=1, has_side_effects=True, vmem_limit_bytes=60 * 2**20
        ),
        cost_estimate=SMALL,
        name="ff_heads",
    )(x, g, x.reshape(2 * BLK, depth), g.reshape(2 * BLK, depth), w, kv_mine, q_heads)


def residual(tokens):
    def finish(column):
        def add(value, here):
            return value + tokens[here, column : column + value.shape[1]].astype(F32)

        return add

    return finish


def home_kernel(
    heads,
    grads,
    dq,
    o_parts,
    hidden,
    grad_both,
    weights,
    tokens,
    dq_home,
    grads_home,
    mixed_out,
    result,
    grad_x,
    *rest,
):
    mine, near, far, total, held_w, held_h, held_o, held_wa, held_a, held_x = rest[:10]
    space = ScatterSpace(rest[10:14])
    links = Links(*rest[14:])
    y, unused_z, unused_c, unused_l, unused_x = coords()
    rows, depth = tokens.shape
    kept = held_w.shape[1]
    links.greet(BR_NEAR + TOK_ALL)
    loads = [
        links.local(o_parts.at[y], held_o.at[y]),
        links.local(hidden, held_h),
        links.local(weights.at[:, pl.ds(0, kept)], held_w),
    ]
    later = [
        links.local(weights.at[:, pl.ds(kept, held_wa.shape[1])], held_wa),
        links.local(grad_both, held_a),
    ]
    returned = [
        (d, links.send(o_parts.at[(y + d) % 4], held_o.at[y], dy=d)) for d in (1, 3, 2)
    ]

    def make(there):
        here = pl.ds(pl.multiple_of(there * rows, rows), rows)
        mixed = [
            jnp.concatenate(
                [held_o[head, here, slot * HD : (slot + 1) * HD] for head in range(heads)],
                axis=1,
            )
            for slot in range(2)
        ]
        for slot in range(2):
            mixed_out[slot, here, :] = mixed[slot]
        both = jnp.concatenate(
            [held_h[:, here, :].reshape(2 * rows, -1), jnp.concatenate(mixed, axis=0)], axis=1
        )
        branches = dot(both, held_w[...], NT).astype(BF)
        for slot in range(2):
            space.pieces[slot, there] = branches[slot * rows : (slot + 1) * rows]

    def output():
        yield
        for d, ticket in returned:
            links.arrived(ticket, held_o.at[(y - d) % 4])
        for load in loads:
            links.settle(load)
        yield from scatter_br(links, make, space, result, residual(tokens))

    def gradient():
        for unused in range(5):
            yield
        for load in later:
            links.settle(load)
        for tile in range(4):
            here = slice(tile * rows, (tile + 1) * rows)
            part = held_a[:, here, :].reshape(2 * rows, -1)
            held_x[:, here, :] = dot(part, held_wa[...], NT).astype(BF).reshape(2, rows, depth)
            span = pl.ds(tile * rows, rows)
            links.local(held_x.at[:, span], grad_x.at[:, span])
            yield

    in_turn(
        [
            gradient(),
            reduce_heads(links, grads, dq, dq_home, grads_home, mine, near, far, total),
            output(),
        ]
    )
    links.close()


def heads_home(grads, dq, o_parts, hidden, grad_both, weights, tokens, heads):
    rows, depth = tokens.shape
    span, lanes = grads.shape[3:]
    width = heads * HD
    kept = hidden.shape[2] + width
    return comm_call(
        functools.partial(home_kernel, heads),
        "heads_home",
        2,
        (grads, dq, o_parts, hidden, grad_both, weights, tokens),
        (
            jax.ShapeDtypeStruct(dq.shape, BF),
            jax.ShapeDtypeStruct((4, span, lanes), BF),
            jax.ShapeDtypeStruct((2, BLK, width), BF),
            jax.ShapeDtypeStruct((rows, depth), BF),
            jax.ShapeDtypeStruct((2, BLK, depth), BF),
        ),
        scratch=[
            pltpu.VMEM((4, 2, span, lanes), BF),
            pltpu.VMEM((4, 2, span, lanes), BF),
            pltpu.VMEM((4, span, lanes), BF),
            pltpu.VMEM((4, span, lanes), BF),
            pltpu.VMEM((depth, kept), BF),
            pltpu.VMEM(hidden.shape, BF),
            pltpu.VMEM(o_parts.shape, BF),
            pltpu.VMEM((depth, grad_both.shape[2]), BF),
            pltpu.VMEM(grad_both.shape, BF),
            pltpu.VMEM((2, BLK, depth), BF),
        ]
        + ScatterSpace.shapes(rows, depth, depth),
        in_vmem=(1, 6),
        out_vmem=(2, 3),
        copies=64,
    )


def normal_rows(tokens, normed, scales):
    rows = tokens.shape[0]
    chunk = 16

    def step(i, unused):
        here = pl.ds(pl.multiple_of(i * chunk, chunk), chunk)
        value = tokens[here, :].astype(F32)
        value = value - jnp.mean(value, axis=-1, keepdims=True)
        scale = lax.rsqrt(jnp.mean(value * value, axis=-1, keepdims=True) + EPSILON)
        normed[here, :] = value * scale
        scales[here, :] = jnp.broadcast_to(scale, (chunk, 128))
        return unused

    lax.fori_loop(0, rows // chunk, step, 0)


def turn_back(grads, normed, scales, cot, gain, parts, result):
    rows, depth = normed.shape
    chunk = 16

    def rows_at(i):
        return pl.ds(pl.multiple_of(i * chunk, chunk), chunk)

    def sums(i, carry):
        here = rows_at(i)
        grad = grads[here, :]
        up = (grad * normed[here, :]).reshape(2, 8, depth)
        return carry[0] + up.sum(0), carry[1] + grad.reshape(2, 8, depth).sum(0)

    zero = jnp.zeros((8, depth), F32)
    found = lax.fori_loop(0, rows // chunk, sums, (zero, zero))
    for k in range(2):
        line = jnp.sum(found[k], axis=0, keepdims=True)
        parts[16 * k : 16 * (k + 1), :] = jnp.concatenate(
            [line[:, t * 128 : (t + 1) * 128] for t in range(depth // 128)], axis=0
        )
    yield

    def back(i, unused):
        here = rows_at(i)
        line = normed[here, :]
        grad = grads[here, :] * gain[...]
        slope = jnp.mean(grad * line, axis=-1, keepdims=True)
        grad = grad - jnp.mean(grad, axis=-1, keepdims=True) - line * slope
        result[here, :] = cot[here, :].astype(F32) + scales[here, :1] * grad
        return unused

    middle = rows // chunk // 2
    lax.fori_loop(0, middle, back, 0)
    yield
    lax.fori_loop(middle, 2 * middle, back, 0)


BR_PEERS = [dict(dl=i // 4, dx=i % 4) for i in range(1, 8)]
TOK_PEERS = [dict(dy=i // 4, dz=(i // 2) % 2, dc=i % 2) for i in range(1, 16)]


def last_kernel(
    heads,
    dq,
    dkv,
    table,
    x_in,
    g_in,
    m_in,
    w_in,
    s_in,
    tokens,
    cot,
    gain,
    block_map,
    result,
    qkv_out,
    out_out,
    sides,
    *rest,
):
    held_q, held_kv, held_t, held_x, held_g, held_m, held_w, held_s, gj = rest[:9]
    parts, near, side, out, far, wsum, summed, normed, scales = rest[9:18]
    lines, lines_in, last, last_in, bias_acc = rest[18:23]
    space = ScatterSpace(rest[23:30])
    links = Links(*rest[30:])
    y, z, c, l, x = coords()
    links.greet(BR_PEERS + TOK_PEERS)
    width = heads * HD
    rows, depth = tokens.shape
    first = [
        links.local(dq, held_q),
        links.local(dkv, held_kv),
        links.local(table, held_t),
    ]
    third = [links.local(w_in.at[:, pl.ds(0, 3 * width)], held_w), links.local(s_in, held_s)]
    second = [
        links.local(x_in, held_x),
        links.local(g_in, held_g),
        links.local(m_in, held_m),
    ]
    wrows = parts.shape[3]
    strip = 4 * wrows
    bias_acc[...] = jnp.zeros_like(bias_acc)

    def settle(loads):
        for load in loads:
            links.settle(load)
        loads.clear()

    def turn_rows(here):
        for slot in range(2):
            lanes = slice(slot * HD, (slot + 1) * HD)
            turns = table_rows(held_t, block_map, slot, here)
            q = jnp.concatenate([held_q[h, here, lanes] for h in range(heads)], axis=1)
            q = turn(q.astype(F32), turns, heads // 2, False, -1.0).astype(BF)
            kv = jnp.concatenate([held_kv[h, slot, here, :] for h in range(heads)], axis=1)
            kv = turn(kv.astype(F32), turns, heads, True, -1.0).astype(BF)
            both = jnp.concatenate([q, kv], axis=1)
            gj[slot, here, :] = both
            bias_acc[...] += jnp.sum(
                both.astype(F32).reshape(rows // 8, 8, 3 * width), axis=0
            )

    def bias_lines():
        total = jnp.sum(bias_acc[...], axis=0, keepdims=True)
        line = [total[:, :width]]
        for k in range(2):
            at = [width + (2 * h + k) * HD for h in range(heads)]
            line.append(jnp.concatenate([total[:, a : a + HD] for a in at], axis=1))
        line = jnp.concatenate(line, axis=1)
        return jnp.concatenate(
            [line[:, r * 128 : (r + 1) * 128] for r in range(3 * width // 128)], axis=0
        )

    def weights_of(there):
        settle(second)
        here = pl.ds(pl.multiple_of(there * strip, strip), strip)
        qkv = dot(held_x[:, here], gj[...].reshape(2 * BLK, 3 * width), TN).astype(BF)
        outs = dot(held_g[:, here], held_m[...], TN).astype(BF)
        for k in range(4):
            at = slice(k * wrows, (k + 1) * wrows)
            parts[there, k // 2, k % 2, :, : 3 * width] = qkv[at]
            parts[there, k // 2, k % 2, :, 3 * width : 4 * width] = outs[at]

    def rows_of(there):
        settle(first)
        here = pl.ds(pl.multiple_of(there * rows, rows), rows)
        turn_rows(here)
        settle(third)
        both = gj[:, here, :].reshape(2 * rows, 3 * width)
        grads = dot(both, held_w[...], NT)
        for slot in range(2):
            value = grads[slot * rows : (slot + 1) * rows] + held_s[slot, here, :].astype(F32)
            space.pieces[slot, there] = value.astype(BF)

    def shifted():
        yield from scatter_br(links, rows_of, space, summed, lambda column: plain)
        through = turn_back(summed, normed, scales, cot, gain, lines, result)
        next(through)
        near_sums = [links.send(lines, lines_in.at[i], **o) for i, o in enumerate(BR_PEERS)]
        yield
        next(through)
        bias_sums = bias_lines()
        sums = lines[...]
        for i, ticket in enumerate(near_sums):
            links.arrived(ticket, lines_in.at[i])
            sums = sums + lines_in[i]
        for t in range(16):
            last[t] = jnp.concatenate([sums[t : t + 1], sums[16 + t : 17 + t], bias_sums], axis=0)
        all_sums = []
        for i, o in enumerate(TOK_PEERS):
            there = ((y + o["dy"]) % 4) * 4 + ((z + o["dz"]) % 2) * 2 + (c + o["dc"]) % 2
            all_sums.append(links.send(last.at[there], last_in.at[i], **o))
        yield
        for unused in through:
            pass
        yield
        sums = last[y * 4 + z * 2 + c]
        for i, ticket in enumerate(all_sums):
            links.arrived(ticket, last_in.at[i])
            sums = sums + last_in[i]
        sides[...] = sums

    def weights():
        for unused in range(4):
            yield
        yield from reduce_tok(links, weights_of, parts, near, side, out, far, wsum)
        qkv_out[0] = wsum[:, :width]
        for k in range(2):
            at = [width + (2 * h + k) * HD for h in range(heads)]
            qkv_out[1 + k] = jnp.concatenate([wsum[:, a : a + HD] for a in at], axis=1)
        out_out[...] = jnp.transpose(wsum[:, 3 * width :])

    def aside():
        for unused in range(5):
            yield
        normal_rows(tokens, normed, scales)

    in_turn([shifted(), weights(), aside()])
    links.close()


def last_sums(
    dq, dkv, table, x, g, mixed, w, partial_grad, tokens, cot, gain, block_map, heads
):
    rows, depth = tokens.shape
    wrows = depth // 16
    width = heads * HD
    cols = 4 * width
    return comm_call(
        functools.partial(last_kernel, heads),
        "last_sums",
        3,
        (dq, dkv, table, x, g, mixed, w, partial_grad, tokens, cot, gain, block_map),
        (
            jax.ShapeDtypeStruct((rows, depth), F32),
            jax.ShapeDtypeStruct((3, wrows, width), F32),
            jax.ShapeDtypeStruct((width, wrows), F32),
            jax.ShapeDtypeStruct((8, 128), F32),
        ),
        scratch=[
            pltpu.VMEM(dq.shape, BF),
            pltpu.VMEM(dkv.shape, BF),
            pltpu.VMEM(table.shape, F32),
            pltpu.VMEM(x.shape, BF),
            pltpu.VMEM(g.shape, BF),
            pltpu.VMEM(mixed.shape, BF),
            pltpu.VMEM((depth, 3 * width), BF),
            pltpu.VMEM(partial_grad.shape, BF),
            pltpu.VMEM((2, BLK, 3 * width), BF),
            pltpu.VMEM((4, 2, 2, wrows, cols), BF),
            pltpu.VMEM((4, 2, wrows, cols), BF),
            pltpu.VMEM((3, 2, wrows, cols), BF),
            pltpu.VMEM((wrows, cols), BF),
            pltpu.VMEM((wrows, cols), BF),
            pltpu.VMEM((wrows, cols), F32),
            pltpu.VMEM((rows, depth), F32),
            pltpu.VMEM((rows, depth), F32),
            pltpu.VMEM((rows, 128), F32),
            pltpu.VMEM((32, 128), F32),
            pltpu.VMEM((7, 32, 128), F32),
            pltpu.VMEM((16, 8, 128), F32),
            pltpu.VMEM((15, 8, 128), F32),
            pltpu.VMEM((8, 3 * width), F32),
        ]
        + ScatterSpace.shapes(rows, depth, depth // 4 * 3),
        in_vmem=(8, 9, 10),
        in_smem=(11,),
        out_vmem=(0, 1, 2, 3),
        copies=96,
    )


def finish_kernel(main, grads, value, tokens, qkv, out, *outs):
    def lines(start, count):
        return jnp.transpose(grads[:, start : start + count].astype(F32))

    result, tokens_out, qkv_out, out_out, down, gate, up = outs
    result[...] = value[...]
    tokens_out[...] = tokens[...]
    qkv_out[...] = qkv[...]
    out_out[...] = out[...]
    tail = down.shape[0] - main
    down[:main, :] = lines(0, main)
    down[main:, :] = lines(main, 128)[:tail]
    at = main + 128
    gate[:main, :] = lines(at, main)
    up[:main, :] = lines(at + main, main)
    ends = lines(at + 2 * main, 128)
    gate[main:, :] = ends[:tail]
    up[main:, :] = ends[tail:]


def finish(grads, value, tokens, qkv, out, main, hidden_width):
    shape = jax.ShapeDtypeStruct((hidden_width, grads.shape[0]), F32)
    return pl.pallas_call(
        functools.partial(finish_kernel, main),
        out_shape=(
            jax.ShapeDtypeStruct(value.shape, BF),
            jax.ShapeDtypeStruct(tokens.shape, F32),
            jax.ShapeDtypeStruct(qkv.shape, F32),
            jax.ShapeDtypeStruct(out.shape, F32),
        )
        + (shape,) * 3,
        in_specs=[VMEM] * 5,
        out_specs=(VMEM,) * 7,
        cost_estimate=SMALL,
        name="finish",
    )(grads, value, tokens, qkv, out)


def rotary_table():
    half = ROT // 2
    frequency = (ROPE_BASE ** (-(np.arange(half) * 2.0 / ROT))).astype(np.float32)
    angles = np.arange(LB * BLK, dtype=np.float32)[:, None] * frequency[None, :]
    cos, sin = np.cos(angles), np.sin(angles)
    one = np.ones((LB * BLK, HD - ROT), np.float32)
    table = np.concatenate([cos, cos, one, -sin, sin, 0.0 * one], axis=1)
    return table.astype(np.float32).reshape(LB, BLK, 2 * HD)


def body(
    tokens,
    norm_gain,
    norm_bias,
    qkv_weight,
    qkv_bias,
    out_weight,
    gate_weight,
    up_weight,
    down_weight,
    cotangent,
    block_map,
    lengths,
):
    tok = lax.axis_index("tok")
    rows = tokens.shape[0]
    depth = tokens.shape[1]
    wrows = qkv_weight.shape[1]
    heads = qkv_bias.shape[1]
    width = heads * HD
    hidden_width = gate_weight.shape[1]
    main = hidden_width // 128 * 128
    tail = hidden_width - main

    down_width = main + 128
    first = down_width + width
    table = jnp.asarray(rotary_table())
    x, grad, qkv_full, ff_full, kv_mine, q_heads = start(
        block_map,
        tokens,
        norm_gain.reshape(1, depth),
        norm_bias.reshape(1, depth),
        cotangent,
        qkv_weight,
        qkv_bias,
        jnp.transpose(gate_weight),
        jnp.transpose(up_weight),
        down_weight,
        out_weight,
        table,
        heads,
        main,
    )
    x = x.reshape(2, BLK, depth)
    grad = grad.reshape(2, BLK, depth)
    qkv_full = qkv_full.reshape(16 * wrows, -1)
    ff_full = ff_full.reshape(16 * wrows, -1)

    hidden, grad_both, grad_ff, qd_all, kv_all = ff_heads(
        x, grad, ff_full, kv_mine, q_heads, main, down_width, first
    )
    kv_all = kv_all.reshape(-1, 2 * HD)
    x = x.reshape(2 * BLK, depth)
    grad = grad.reshape(2 * BLK, depth)
    grad_ff = lax.psum_scatter(grad_ff, "tok", scatter_dimension=0, tiled=True)

    o_parts, dq_parts, dkv_all = attention(block_map, lengths, qd_all, kv_all)
    dq_heads, dkv_heads, mixed, result, grad_x = heads_home(
        dkv_all.reshape(4, 2, 2, 2 * BLK, 2 * HD),
        dq_parts,
        o_parts,
        hidden,
        grad_both,
        ff_full,
        tokens,
        heads,
    )
    grad_tokens, grad_qkv, grad_out, sides = last_sums(
        dq_heads,
        dkv_heads.reshape(heads, 2, BLK, 2 * HD),
        table,
        x,
        grad,
        mixed.reshape(2 * BLK, width),
        qkv_full,
        grad_x,
        tokens,
        cotangent,
        norm_gain.reshape(1, depth),
        block_map,
        heads,
    )
    grad_qkv_bias = lax.dynamic_slice_in_dim(
        sides[2:].reshape(3, heads, HD), tok * qkv_bias.shape[2], qkv_bias.shape[2], 2
    )
    grad_ff, grad_tokens = lax.optimization_barrier((grad_ff, grad_tokens))
    result, grad_tokens, grad_qkv, grad_out, grad_down, grad_gate, grad_up = finish(
        grad_ff, result, grad_tokens, grad_qkv, grad_out, main, hidden_width
    )

    sides = lax.dynamic_slice_in_dim(sides[:2], lax.axis_index("br") * 16, 16, 1)
    return (
        result,
        grad_tokens,
        sides[0],
        sides[1],
        grad_qkv,
        grad_qkv_bias,
        grad_out,
        jnp.transpose(grad_gate),
        jnp.transpose(grad_up),
        grad_down,
    )


def solution(mesh):
    in_specs = (
        P(("tok", "br"), None),
        P(),
        P(),
        P(None, "tok", "br"),
        P(None, "br", "tok"),
        P("br", "tok"),
        P("tok", "br"),
        P("tok", "br"),
        P("br", "tok"),
        P(("tok", "br"), None),
        P(),
        P(),
    )
    out_specs = (
        P(("tok", "br"), None),
        P(("tok", "br"), None),
        P(("tok", "br")),
        P(("tok", "br")),
        P(None, "tok", "br"),
        P(None, "br", "tok"),
        P("br", "tok"),
        P("tok", "br"),
        P("tok", "br"),
        P("br", "tok"),
    )
    return jax.shard_map(body, mesh=mesh, in_specs=in_specs, out_specs=out_specs, check_vma=False)
```

```python
import functools

import jax
import jax.numpy as jnp
import numpy as np
from jax import lax
from jax.experimental import pallas as pl
from jax.experimental.pallas import tpu as pltpu
from jax.sharding import PartitionSpec as P

HD = 64
ROT = 16
BLK = 512
LB = 8
EPSILON = 1e-05
ROPE_BASE = 10000.0
MASKED = -1e30
BF = jnp.bfloat16
F32 = jnp.float32
NN = (((1,), (0,)), ((), ()))
NT = (((1,), (1,)), ((), ()))
TN = (((0,), (0,)), ((), ()))
VMEM = pl.BlockSpec(memory_space=pltpu.VMEM)
SMEM = pl.BlockSpec(memory_space=pltpu.SMEM)
ANY = pl.BlockSpec(memory_space=pl.ANY)
SMALL = pl.CostEstimate(flops=1000, bytes_accessed=1000, transcendentals=0)


def dot(left, right, dims):
    return lax.dot_general(left, right, dims, preferred_element_type=F32)


def block_info(block, long_blocks):
    is_long = block < long_blocks
    place = jnp.where(is_long, block % LB, (block - long_blocks) % 2)
    return is_long, place, block - place


def lane_half(packed, half, upper):
    piece = packed[:, half * HD : (half + 1) * HD]
    zero = jnp.zeros_like(piece)
    return jnp.concatenate([zero, piece] if upper else [piece, zero], axis=1)


def allowed_pairs(place, step, limit):
    key_pos = step * BLK + lax.broadcasted_iota(jnp.int32, (BLK, BLK), 0)
    query_pos = place * BLK + lax.broadcasted_iota(jnp.int32, (BLK, BLK), 1)
    return (key_pos <= query_pos) & (key_pos < limit)


def attn_kernel(
    block_map,
    lengths,
    q_ref,
    kv_in,
    o_ref,
    dq_ref,
    dkv_out,
    slot_of,
    kv_ref,
    ot,
    lses,
    acc,
    dqt,
    load_sem,
    store_sems,
):
    load = pltpu.make_async_copy(kv_in, kv_ref, load_sem.at[0])
    load.start()
    acc[...] = jnp.zeros_like(acc)
    total_blocks = block_map.shape[0]
    long_blocks = total_blocks // 2
    own = lax.axis_index("tok") % 4

    def note(slot, unused):
        slot_of[block_map[slot]] = slot
        return unused

    lax.fori_loop(0, total_blocks, note, 0)
    load.wait()

    def about(i, half):
        block = block_map[2 * (4 * i + own) + half]
        is_long, place, first = block_info(block, long_blocks)
        row = jnp.where(
            is_long, block // LB, long_blocks // LB + (block - long_blocks) // 2
        )
        return is_long, place, first, lengths[row]

    def rows_at(block):
        return pl.ds(pl.multiple_of(slot_of[block] * BLK, BLK), BLK)

    def forward(i, unused):
        packed = q_ref[i, 0]
        for half in range(2):
            is_long, place, first, limit = about(i, half)
            queries = lane_half(packed, half, False) * jnp.asarray(0.125, BF)

            def step(j, carry, masked):
                top, total, summed = carry
                kv = kv_ref[rows_at(first + j), :]
                scores = dot(kv, queries, NT)
                if masked:
                    scores = jnp.where(allowed_pairs(place, j, limit), scores, MASKED)
                new_top = jnp.maximum(top, jnp.max(scores, axis=0, keepdims=True))
                fade = jnp.exp(top - new_top)
                probs = jnp.exp(scores - new_top)
                total = total * fade + jnp.sum(probs, axis=0, keepdims=True)
                summed = summed * fade + dot(kv, probs.astype(BF), TN)
                return new_top, total, summed

            free = jnp.where(is_long, place, 0)
            carry = (
                jnp.full((1, BLK), MASKED, F32),
                jnp.zeros((1, BLK), F32),
                jnp.zeros((2 * HD, BLK), F32),
            )
            carry = lax.fori_loop(0, free, lambda j, c: step(j, c, False), carry)
            top, total, summed = lax.fori_loop(
                free, place + 1, lambda j, c: step(j, c, True), carry
            )
            lses[2 * i + half] = top + jnp.log(total)
            ot[i, half * HD : (half + 1) * HD, :] = summed[HD:, :] / total
        o_ref[i] = jnp.transpose(ot[i]).astype(BF)
        return unused

    lax.fori_loop(0, q_ref.shape[0], forward, 0)

    def backward(i, unused):
        q_packed = q_ref[i, 0]
        d_packed = q_ref[i, 1]
        d_turned = jnp.transpose(d_packed.astype(F32))
        for half in range(2):
            is_long, place, first, limit = about(i, half)
            queries = lane_half(q_packed, half, False) * jnp.asarray(0.125, BF)
            grads = lane_half(d_packed, half, True)
            both = jnp.concatenate([queries, grads], axis=0)
            lanes = slice(half * HD, (half + 1) * HD)
            delta = jnp.sum(d_turned[lanes] * ot[i, lanes, :], axis=0, keepdims=True)
            lse = lses[2 * i + half]

            def step(j, total, masked):
                rows = rows_at(first + j)
                kv = kv_ref[rows, :]
                scores = dot(kv, queries, NT)
                if masked:
                    scores = jnp.where(allowed_pairs(place, j, limit), scores, MASKED)
                probs = jnp.exp(scores - lse)
                ds = (probs * (dot(kv, grads, NT) - delta)).astype(BF)
                acc[rows, :] += dot(jnp.concatenate([ds, probs.astype(BF)], axis=1), both, NN)
                return total + dot(kv, ds, TN)

            free = jnp.where(is_long, place, 0)
            total = lax.fori_loop(
                0, free, lambda j, c: step(j, c, False), jnp.zeros((2 * HD, BLK), F32)
            )
            total = lax.fori_loop(free, place + 1, lambda j, c: step(j, c, True), total)
            dqt[lanes, :] = total[:HD, :] * 0.125
        dq_ref[i] = jnp.transpose(dqt[...]).astype(BF)
        return unused

    lax.fori_loop(0, q_ref.shape[0], backward, 0)

    def store(i):
        rows = pl.ds(pl.multiple_of(i * BLK, BLK), BLK)
        return rows, pltpu.make_async_copy(
            kv_ref.at[rows], dkv_out.at[rows], store_sems.at[i]
        )

    def finish(i, unused):
        rows, copy = store(i)
        kv_ref[rows, :] = acc[rows, :].astype(BF)
        copy.start()
        return unused

    def stored(i, unused):
        store(i)[1].wait()
        return unused

    lax.fori_loop(0, total_blocks, finish, 0)
    lax.fori_loop(0, total_blocks, stored, 0)


def attention(block_map, lengths, qd, kv):
    n = qd.shape[0]
    shape = jax.ShapeDtypeStruct((n, BLK, 2 * HD), BF)
    return pl.pallas_call(
        attn_kernel,
        out_shape=(shape, shape, jax.ShapeDtypeStruct(kv.shape, BF)),
        in_specs=[SMEM, SMEM, VMEM, ANY],
        out_specs=(VMEM, VMEM, ANY),
        scratch_shapes=[
            pltpu.SMEM(block_map.shape, jnp.int32),
            pltpu.VMEM(kv.shape, BF),
            pltpu.VMEM((n, 2 * HD, BLK), F32),
            pltpu.VMEM((2 * n, 1, BLK), F32),
            pltpu.VMEM(kv.shape, F32),
            pltpu.VMEM((2 * HD, BLK), F32),
            pltpu.SemaphoreType.DMA((1,)),
            pltpu.SemaphoreType.DMA(block_map.shape),
        ],
        compiler_params=pltpu.CompilerParams(vmem_limit_bytes=60 * 2**20),
        cost_estimate=SMALL,
        name="attention",
    )(block_map, lengths, qd, kv)


def turn(values, table, copies, paired, sign):
    width = values.shape[1]
    lane = lax.broadcasted_iota(jnp.int32, values.shape, 1) % HD
    partner = jnp.where(
        lane < ROT // 2,
        pltpu.roll(values, width - ROT // 2, 1),
        pltpu.roll(values, ROT // 2, 1),
    )
    cos, sin = table[:, :HD], sign * table[:, HD:]
    cos = jnp.concatenate([cos, jnp.ones_like(cos) if paired else cos], axis=1)
    sin = jnp.concatenate([sin, jnp.zeros_like(sin) if paired else sin], axis=1)
    cos = jnp.concatenate([cos] * copies, axis=1)
    sin = jnp.concatenate([sin] * copies, axis=1)
    return values * cos + partner * sin


def ff_part(main, down, first, x, g, w_ref, h_ref, a_ref, mixed_grad, pause):
    rows, depth = x.shape[1:]
    x = x.reshape(2 * rows, depth)
    g = g.reshape(2 * rows, depth)
    gate_up = dot(x, w_ref[:, first:], NN)
    pause(0)
    gh = dot(g, w_ref[:, :first], NN)
    mixed_grad(gh[:, down:].astype(BF))
    gh = gh[:, :down]
    ends = gate_up[:, 2 * main :]
    gate = jnp.concatenate([gate_up[:, :main], ends], axis=1)
    up = jnp.concatenate([gate_up[:, main : 2 * main], pltpu.roll(ends, HD, 1)], axis=1)
    sig = jax.nn.sigmoid(gate)
    silu = gate * sig
    hidden = (silu * up).astype(BF)
    d_gate = gh * up * sig * (1.0 + gate * (1.0 - sig))
    d_up = gh * silu
    tail = d_gate[:, main:] + pltpu.roll(d_up[:, main:], HD, 1)
    grads = jnp.concatenate(
        [d_gate[:, :main].astype(BF), d_up[:, :main].astype(BF), tail.astype(BF)], axis=1
    )
    h_ref[...] = hidden.reshape(h_ref.shape)
    pause(1)
    a_ref[...] = grads.reshape(a_ref.shape)
    return grads, hidden


def coords():
    tok, br = lax.axis_index("tok"), lax.axis_index("br")
    return tok // 4, (tok // 2) % 2, tok % 2, br // 4, br % 4


def peer(dy=0, dz=0, dc=0, dl=0, dx=0):
    y, z, c, l, x = coords()
    tok = ((y + dy) % 4) * 4 + ((z + dz) % 2) * 2 + (c + dc) % 2
    return tok, ((l + dl) % 2) * 4 + (x + dx) % 4


class Links:
    def __init__(self, send_sems, recv_sems, local_sems):
        self.sems = (send_sems, recv_sems, local_sems)
        self.sent, self.locals = [], []

    def greet(self, partners):
        barrier = pltpu.get_barrier_semaphore()
        for offsets in partners:
            pl.semaphore_signal(
                barrier, inc=1, device_id=peer(**offsets), device_id_type=pl.DeviceIdType.MESH
            )
        pl.semaphore_wait(barrier, len(partners))

    def copy(self, number, source, target, offsets):
        return pltpu.make_async_remote_copy(
            src_ref=source,
            dst_ref=target,
            send_sem=self.sems[0].at[number],
            recv_sem=self.sems[1].at[number],
            device_id=peer(**offsets),
            device_id_type=pl.DeviceIdType.MESH,
        )

    def send(self, source, target, **offsets):
        copy = self.copy(len(self.sent), source, target, offsets)
        copy.start()
        self.sent.append(copy)
        return len(self.sent) - 1, offsets

    def arrived(self, ticket, place):
        self.copy(ticket[0], place, place, ticket[1]).wait_recv()

    def local(self, source, target):
        copy = pltpu.make_async_copy(source, target, self.sems[2].at[len(self.locals)])
        copy.start()
        self.locals.append([copy, True])
        return len(self.locals) - 1

    def settle(self, number):
        copy, pending = self.locals[number]
        if pending:
            copy.wait()
        self.locals[number][1] = False

    def close(self):
        for number in range(len(self.locals)):
            self.settle(number)
        for copy in self.sent:
            copy.wait_send()


def in_turn(tasks):
    tasks = list(tasks)
    while tasks:
        for task in list(tasks):
            try:
                next(task)
            except StopIteration:
                tasks.remove(task)


def ring_four(links, own, place, axis, landed):
    right = links.send(own, place(0, None), **{axis: 1})
    left = links.send(own, place(0, None), **{axis: -1})
    yield
    links.arrived(right, place(-1, None))
    on_right = links.send(place(-1, 0), place(-1, 0), **{axis: 1})
    landed(-1)
    yield
    links.arrived(left, place(1, None))
    on_left = links.send(place(1, 1), place(1, 1), **{axis: -1})
    landed(1)
    yield
    links.arrived(on_right, place(2, 0))
    links.arrived(on_left, place(2, 1))
    landed(2)


def half_of(ref, part):
    if part is None:
        return ref
    rows = ref.shape[0] // 2
    return ref.at[pl.ds(part * rows, rows)]


def gather_br(links, own, whole):
    unused_y, unused_z, unused_c, l, x = coords()

    def place(dl):
        return lambda dx, part: half_of(whole.at[(l + dl) % 2, (x + dx) % 4], part)

    kept = links.local(own, place(0)(0, None))
    across = links.send(own, place(0)(0, None), dl=1)
    near = ring_four(links, own, place(0), "dx", lambda d: None)
    next(near)
    yield
    links.arrived(across, place(1)(0, None))
    far = ring_four(links, place(1)(0, None), place(1), "dx", lambda d: None)
    next(far)
    for unused in near:
        yield
    for unused in far:
        yield
    links.settle(kept)


def gather_tok(links, own, whole):
    y, z, c, unused_l, unused_x = coords()
    passed = []

    def place(dz, dc=0):
        return lambda dy, part: half_of(
            whole.at[(y + dy) % 4, (z + dz) % 2, (c + dc) % 2], part
        )

    def passer(dz):
        def landed(dy):
            ref = place(dz)(dy, None)
            passed.append((links.send(ref, ref, dc=1), place(dz, 1)(dy, None)))

        return landed

    kept = links.local(own, place(0)(0, None))
    across = links.send(own, place(0)(0, None), dz=1)
    near = ring_four(links, own, place(0), "dy", passer(0))
    next(near)
    passed.append((links.send(own, place(0)(0, None), dc=1), place(0, 1)(0, None)))
    yield
    links.arrived(across, place(1)(0, None))
    far = ring_four(links, place(1)(0, None), place(1), "dy", passer(1))
    next(far)
    passer(1)(0)
    for unused in near:
        yield
    for unused in far:
        yield
    links.settle(kept)
    for ticket, ref in passed:
        links.arrived(ticket, ref)


def add_up(target, sources, rows, finish):
    chunk = 16

    def step(i, unused):
        here = pl.ds(pl.multiple_of(i * chunk, chunk), chunk)
        total = sources[0][here, :].astype(F32)
        for source in sources[1:]:
            total = total + source[here, :].astype(F32)
        target[here, :] = finish(total, here).astype(target.dtype)
        return unused

    lax.fori_loop(0, rows // chunk, step, 0)


def plain(total, here):
    return total


def reduce_heads(links, grads, dq, dq_home, grads_home, mine, near, far, total):
    y, z, c, unused_l, unused_x = coords()
    order = (1, 3, 2, 0)
    held, from_core = {}, {}
    for dz in (1, 0):
        for d in order:
            place = ((y + d) % 4, (z + dz) % 2)
            from_core[d, dz] = links.send(
                grads.at[place[0], place[1], 1 - c], near.at[place[0], place[1]], dc=1
            )
            held[d, dz] = links.local(
                grads.at[place[0], place[1], c], mine.at[place[0], place[1]]
            )
    asked = [links.send(dq.at[(y + d) % 4], dq_home.at[y], dy=d) for d in order[:3]]
    links.local(dq.at[y], dq_home.at[y])
    yield
    rows = mine.shape[2]
    across = {}
    for d in order:
        here = (y + d) % 4
        links.arrived(from_core[d, 1], near.at[here, 1 - z])
        links.settle(held[d, 1])
        add_up(
            mine.at[here, 1 - z], [mine.at[here, 1 - z], near.at[here, 1 - z]], rows, plain
        )
        across[d] = links.send(mine.at[here, 1 - z], far.at[here], dz=1)
        yield
    home = {}
    for d in order:
        here = (y + d) % 4
        links.arrived(from_core[d, 0], near.at[here, z])
        links.settle(held[d, 0])
        links.arrived(across[d], far.at[here])
        add_up(
            total.at[here], [mine.at[here, z], near.at[here, z], far.at[here]], rows, plain
        )
        if d:
            home[d] = links.send(total.at[here], grads_home.at[y], dy=d)
        else:
            links.local(total.at[here], grads_home.at[y])
        yield
    for i, d in enumerate(order[:3]):
        links.arrived(asked[i], dq_home.at[(y - d) % 4])
        links.arrived(home[d], grads_home.at[(y - d) % 4])


class ScatterSpace:
    def __init__(self, refs):
        self.pieces, self.ring, self.out, self.far = refs[:4]
        if len(refs) > 4:
            self.across, self.sums, self.last = refs[4:]

    @staticmethod
    def shapes(rows, depth, half):
        def ring(parts, columns):
            return (parts, 2, rows + rows // 2, columns)

        sizes = [(2, 4, rows, depth), ring(2, half), (rows, half), (rows, half)]
        rest = depth - half
        if rest:
            sizes += [(4, rows, rest), (4, rows, rest), ring(1, rest)]
        return [pltpu.VMEM(size, BF) for size in sizes]


def ring_sum(links, pieces, ring, total, finish):
    unused_y, unused_z, unused_c, unused_l, x = coords()
    rows = total.shape[0]
    half = rows // 2
    halves = (pl.ds(0, half), pl.ds(half, half))
    passing = pl.ds(rows, half)
    whole = pl.ds(0, rows)
    opposite = pieces((x + 2) % 4)
    steps = (1, -1)
    first = [
        links.send(opposite.at[halves[k]], ring.at[k, passing], dx=steps[k]) for k in range(2)
    ]
    yield
    second = []
    for k in range(2):
        links.arrived(first[k], ring.at[k, passing])
        piece = pieces((x + steps[k]) % 4)
        add_up(
            piece.at[halves[k]], [piece.at[halves[k]], ring.at[k, passing]], half, plain
        )
        second.append(links.send(piece, ring.at[k, whole], dx=steps[k]))
        yield
    for k in range(2):
        links.arrived(second[k], ring.at[k, whole])
    add_up(total, [pieces(x), ring.at[0, whole], ring.at[1, whole]], rows, finish)


def scatter_br(links, make, space, target, finish):
    unused_y, unused_z, unused_c, l, x = coords()
    rows, half = space.out.shape
    split = half < target.shape[1]
    first, second = pl.ds(0, half), pl.ds(half, target.shape[1] - half)
    order = (2, 1, 3, 0)

    def part(to):
        return lambda there: space.pieces.at[to, there, :, first]

    folded = {}
    outer = ring_sum(links, part(1 - l), space.ring.at[0], space.out, plain)
    for d in order:
        there = (x + d) % 4
        make(there)
        if split:
            folded[d] = links.send(
                space.pieces.at[1 - l, there, :, second], space.across.at[there], dl=1
            )
        if d == 2:
            next(outer)
        yield
    inner = ring_sum(links, part(l), space.ring.at[1], target.at[:, first], finish(0))
    next(inner)
    yield from outer
    over = links.send(space.out, space.far, dl=1)
    next(inner)
    next(inner)
    yield
    rest = []
    for d in order if split else ():
        there = (x + d) % 4
        links.arrived(folded[d], space.across.at[there])
        own = space.pieces.at[l, there, :, second]
        add_up(space.sums.at[there], [own, space.across.at[there]], rows, plain)
        if d == 2:
            late = ring_sum(
                links,
                lambda there: space.sums.at[there],
                space.last.at[0],
                target.at[:, second],
                finish(half),
            )
            next(late)
            rest.append(late)
        yield

    def joined():
        links.arrived(over, space.far)
        mine = space.pieces.at[l, x, :, first]
        add_up(mine, [mine, space.far], rows, plain)
        yield
        yield from inner

    rest.append(joined())
    while rest:
        for task in list(rest):
            try:
                next(task)
            except StopIteration:
                rest.remove(task)
        yield


def reduce_tok(links, make, parts, near, side, out, far, target):
    y, z, c, unused_l, unused_x = coords()
    order = (1, 3, 2, 0)
    tickets = {}
    for d in order:
        here = (y + d) % 4
        make(here)
        tickets[d] = links.send(parts.at[here, :, 1 - c], near.at[here], dc=1)
        yield
    rows = out.shape[0]
    sent = {}
    for dz in (1, 0):
        k = (z + dz) % 2
        for i, d in enumerate(order):
            here = (y + d) % 4
            if dz:
                links.arrived(tickets[d], near.at[here])
            own = parts.at[here, k, c]
            add_up(own, [own, near.at[here, k]], rows, plain)
            if d:
                sent[dz, i] = links.send(own, side.at[i, k], dy=d)
            if dz:
                yield
    for i in range(3):
        links.arrived(sent[1, i], side.at[i, 1 - z])
        yield
    add_up(out, [parts.at[y, 1 - z, c]] + [side.at[i, 1 - z] for i in range(3)], rows, plain)
    across = links.send(out, far, dz=1)
    yield
    for i in range(3):
        links.arrived(sent[0, i], side.at[i, z])
    yield
    links.arrived(across, far)
    add_up(target, [parts.at[y, z, c]] + [side.at[i, z] for i in range(3)] + [far], rows, plain)


BR_NEAR = [dict(dl=1), dict(dx=1), dict(dx=-1)]
BR_ALL = BR_NEAR + [dict(dx=2)]
TOK_NEAR = [dict(dz=1), dict(dc=1), dict(dy=1), dict(dy=-1)]
TOK_ALL = TOK_NEAR + [dict(dy=2)]


def comm_call(
    kernel, name, number, args, outs, scratch=(), in_vmem=(), out_vmem=(), in_smem=(), copies=48
):
    return pl.pallas_call(
        kernel,
        out_shape=tuple(outs),
        in_specs=[
            VMEM if i in in_vmem else SMEM if i in in_smem else ANY for i in range(len(args))
        ],
        out_specs=tuple(VMEM if i in out_vmem else ANY for i in range(len(outs))),
        scratch_shapes=list(scratch)
        + [
            pltpu.SemaphoreType.DMA((copies,)),
            pltpu.SemaphoreType.DMA((copies,)),
            pltpu.SemaphoreType.DMA((32,)),
        ],
        compiler_params=pltpu.CompilerParams(
            collective_id=number, has_side_effects=True, vmem_limit_bytes=60 * 2**20
        ),
        cost_estimate=SMALL,
        name=name,
    )(*args)


def table_rows(table, block_map, slot, here):
    block = block_map[lax.axis_index("tok") * 2 + slot]
    long_blocks = 2 * LB
    place = jnp.where(block < long_blocks, block % LB, (block - long_blocks) % 2)
    return table[place, here, :]


def shift_rows(tokens, gain, bias, shifted):
    rows = tokens.shape[0]
    chunk = 16

    def step(i, unused):
        here = pl.ds(pl.multiple_of(i * chunk, chunk), chunk)
        value = tokens[here, :].astype(F32)
        value = value - jnp.mean(value, axis=-1, keepdims=True)
        scale = lax.rsqrt(jnp.mean(value * value, axis=-1, keepdims=True) + EPSILON)
        shifted[here, :] = (value * scale * gain[...] + bias[...]).astype(BF)
        return unused

    lax.fori_loop(0, rows // chunk, step, 0)


def turned(block):
    return jnp.transpose(block.astype(F32)).astype(BF)


def bias_places(heads, per):
    width = heads * HD
    places = np.zeros((128, 3 * width), np.float32)
    for column in range(3 * width):
        if column < width:
            part, head, lane = 0, column // HD, column % HD
        else:
            pair, lane = divmod(column - width, HD)
            part, head = 1 + pair % 2, pair // 2
        places[(part * heads + head) * per + lane % per, column] = 1.0
    return places


def start_kernel(
    heads,
    main,
    block_map,
    tokens,
    gain,
    bias,
    cot,
    qkv,
    qkv_bias,
    places,
    gate,
    up,
    down,
    out,
    table,
    x_out,
    g_out,
    w_out,
    f_out,
    kv_mine,
    q_heads,
    *rest,
):
    shifted, qkv_shard, ff_shard, held_x, held_w, pairs, queries, held_t = rest[:8]
    links = Links(*rest[8:])
    y, z, c, unused_l, unused_x = coords()
    width = heads * HD
    links.greet(BR_NEAR + TOK_ALL)
    rotary = links.local(table, held_t)
    shift_rows(tokens, gain, bias, shifted)
    rows, depth = tokens.shape
    kv = []
    for head in range(heads):
        lanes = slice(head * HD, (head + 1) * HD)
        kv += [qkv[1, :, lanes], qkv[2, :, lanes]]
    qkv_shard[:, : 3 * width] = jnp.concatenate([qkv[0]] + kv, axis=1)
    line = dot(qkv_bias[...], places[...], NN)
    lane = lax.broadcasted_iota(jnp.int32, line.shape, 1) % HD
    line = jnp.where(lane // (HD // 16) == lax.axis_index("tok"), line, 0.0)[:1]
    lines = [line[:, r * 128 : (r + 1) * 128] for r in range(3 * width // 128)]
    zero = jnp.zeros((qkv_shard.shape[0] - len(lines), 128), F32)
    qkv_shard[:, 3 * width :] = jnp.concatenate(lines + [zero], axis=0).astype(BF)

    def project(half):
        tile = 2 * rows
        here = slice(half * tile, (half + 1) * tile)
        span = held_x[:, 2 * half : 2 * half + 2].reshape(2 * tile, depth)
        corner = held_w[0, 0, 0, :8, 3 * width :].astype(F32)
        for t in range(1, 16):
            corner = corner + held_w[t // 4, t // 2 % 2, t % 2, :8, 3 * width :].astype(F32)
        added = jnp.concatenate([corner[r : r + 1] for r in range(len(lines))], axis=1)
        products = dot(span, held_w[...].reshape(depth, -1)[:, : 3 * width], NN) + added
        parts = []
        for slot in range(2):
            turns = table_rows(held_t, block_map, slot, here)
            joined = products[slot * tile : (slot + 1) * tile]
            parts.append(turn(joined[:, :width], turns, heads // 2, False, 1.0).astype(BF))
            kv = turn(joined[:, width:], turns, heads, True, 1.0).astype(BF)
            for head in range(heads):
                pairs[head, slot, here, :] = kv[:, head * 2 * HD : (head + 1) * 2 * HD]
        for head in range(heads):
            lanes = slice(head * HD, (head + 1) * HD)
            queries[head, here, :] = jnp.concatenate(
                [parts[0][:, lanes], parts[1][:, lanes]], axis=1
            )

    def attention():
        tasks = [gather_tok(links, qkv_shard, held_w), gather_br(links, shifted, held_x)]
        while tasks:
            for task in list(tasks):
                try:
                    next(task)
                except StopIteration:
                    tasks.remove(task)
            yield
        links.local(held_x, x_out)
        links.local(held_w, w_out)
        links.settle(rotary)
        for half in range(2):
            project(half)
        sent = [
            (d, links.send(pairs.at[(y + d) % 4], kv_mine.at[y], dy=d)) for d in (1, 3, 2)
        ]
        links.local(pairs.at[y], kv_mine.at[y])
        links.local(queries, q_heads)
        for unused in range(12):
            yield
        for d, ticket in sent:
            links.arrived(ticket, kv_mine.at[(y - d) % 4])

    def feed_forward():
        ff_shard[:, :main] = turned(down[:main, :])
        tail = down.shape[0] - main
        ends = jnp.concatenate([down[main:, :], jnp.zeros((128 - tail, rows), BF)], axis=0)
        ff_shard[:, main : main + 128] = turned(ends)
        at = main + 128
        ff_shard[:, at : at + width] = turned(out[...])
        at += width
        ff_shard[:, at : at + main] = turned(gate[:main, :])
        ff_shard[:, at + main : at + 2 * main] = turned(up[:main, :])
        ends = jnp.concatenate([gate[main:, :], up[main:, :]], axis=0)
        ff_shard[:, at + 2 * main :] = turned(ends)
        yield
        yield from gather_tok(links, ff_shard, f_out)

    def gradient():
        for unused in range(3):
            yield
        yield from gather_br(links, cot, g_out)

    in_turn([attention(), feed_forward(), gradient()])
    links.close()


def start(
    block_map, tokens, gain, bias, cot, qkv, qkv_bias, gate, up, down, out, table, heads, main
):
    rows, depth = tokens.shape
    wrows = qkv.shape[1]
    width = heads * HD
    cols = main + 128 + width + 2 * gate.shape[0]
    whole = jax.ShapeDtypeStruct((2, 4, rows, depth), BF)
    places = jnp.asarray(bias_places(heads, qkv_bias.shape[2]))
    flat = jnp.pad(qkv_bias.reshape(1, -1).astype(F32), ((0, 7), (0, 128 - qkv_bias.size)))
    args = (block_map, tokens, gain, bias, cot, qkv, flat, places, gate, up, down, out, table)
    copies = 72
    shapes = (
        whole,
        whole,
        jax.ShapeDtypeStruct((4, 2, 2, wrows, 3 * width + 128), BF),
        jax.ShapeDtypeStruct((4, 2, 2, wrows, cols), BF),
        jax.ShapeDtypeStruct((heads, 2, BLK, 2 * HD), BF),
        jax.ShapeDtypeStruct((heads, BLK, 2 * HD), BF),
    )
    specs = [SMEM] + [VMEM] * (len(args) - 1)
    specs[12] = ANY
    return pl.pallas_call(
        functools.partial(start_kernel, heads, main),
        out_shape=shapes,
        in_specs=specs,
        out_specs=(ANY,) * len(shapes),
        scratch_shapes=[
            pltpu.VMEM((rows, depth), BF),
            pltpu.VMEM((wrows, 3 * width + 128), BF),
            pltpu.VMEM((wrows, cols), BF),
            pltpu.VMEM(whole.shape, BF),
            pltpu.VMEM(shapes[2].shape, BF),
            pltpu.VMEM(shapes[4].shape, BF),
            pltpu.VMEM(shapes[5].shape, BF),
            pltpu.VMEM(table.shape, F32),
            pltpu.SemaphoreType.DMA((copies,)),
            pltpu.SemaphoreType.DMA((copies,)),
            pltpu.SemaphoreType.DMA((32,)),
        ],
        compiler_params=pltpu.CompilerParams(
            collective_id=0, has_side_effects=True, vmem_limit_bytes=60 * 2**20
        ),
        cost_estimate=SMALL,
        name="start",
    )(*args)


def ff_heads_kernel(
    main,
    down,
    first,
    x_ref,
    g_ref,
    x_strip,
    g_strip,
    weights,
    kv_mine,
    q_heads,
    h_ref,
    a_ref,
    grad_ref,
    asked,
    pairs,
    w_ref,
    held,
    held_hidden,
    outs,
    own_kv,
    own_q,
    *sems,
):
    y, z, c, unused_l, unused_x = coords()
    step = pl.program_id(0)
    final = pl.num_programs(0) - 1
    links = Links(*sems)
    order = (1, 3, 2)
    rows = x_ref.shape[1]

    loads = [
        pltpu.make_async_copy(weights.at[:, part], w_ref.at[:, part], sems[2].at[n])
        for n, part in ((0, pl.ds(first, w_ref.shape[1] - first)), (4, pl.ds(0, first)))
    ]
    taken = [
        pltpu.make_async_copy(kv_mine, own_kv, sems[2].at[1]),
        pltpu.make_async_copy(q_heads.at[y], own_q, sems[2].at[2]),
    ]
    kept = [
        pltpu.make_async_copy(own_kv, pairs.at[:, z, c], sems[2].at[5]),
        pltpu.make_async_copy(own_q, asked.at[y, 0], sems[2].at[6]),
    ]
    kept_out = pltpu.make_async_copy(outs.at[y], asked.at[y, 1], sems[2].at[3])
    number = iter(range(64))

    def plan(source, target, lands, **offsets):
        n = next(number)
        return links.copy(n, source, target, offsets), links.copy(n, lands, lands, offsets)

    def swap(source, k):
        return [
            plan(source.at[(y + d) % 4], asked.at[y, k], asked.at[(y - d) % 4, k], dy=d)
            for d in order
        ]

    far = [plan(kv_mine.at[i], pairs.at[i, z, c], pairs.at[i, 1 - z, c], dz=1) for i in range(4)]
    near = [plan(kv_mine.at[i], pairs.at[i, z, c], pairs.at[i, z, 1 - c], dc=1) for i in range(4)]
    diagonal = [
        plan(pairs.at[i, 1 - z, c], pairs.at[i, 1 - z, c], pairs.at[i, 1 - z, 1 - c], dc=1)
        for i in range(4)
    ]
    asked_q, asked_o = swap(q_heads, 0), swap(outs, 1)

    def cross(i):
        far[i][1].wait_recv()
        diagonal[i][0].start()

    @pl.when(step == 0)
    def _():
        for load in loads:
            load.start()
        links.greet([dict(dz=1), dict(dc=1), dict(dy=1), dict(dy=2), dict(dy=3)])
        for copy, unused in far + near + asked_q:
            copy.start()
        for copy in taken:
            copy.start()
        loads[0].wait()

    @pl.when(step == 1)
    def _():
        for copy in taken:
            copy.wait()
        for copy in kept:
            copy.start()

    def pause(point):
        if point == 0:

            @pl.when(step == 0)
            def _():
                loads[1].wait()

    for i in range(2):

        @pl.when(step == 3 + i)
        def _():
            cross(2 * i)
            cross(2 * i + 1)

    here = pl.ds(pl.multiple_of(jnp.minimum(step, 1) * rows, rows), rows)

    def mixed_grad(value):
        for head in range(outs.shape[0]):
            lanes = slice(head * HD, (head + 1) * HD)
            outs[head, here, :] = jnp.concatenate(
                [value[:rows, lanes], value[rows:, lanes]], axis=1
            )

    @pl.when(step < 2)
    def _():
        grads, hidden = ff_part(
            main, down, first, x_ref[...], g_ref[...], w_ref, h_ref, a_ref, mixed_grad, pause
        )
        held[:, here, :] = grads.reshape(2, rows, -1)
        held_hidden[:, here, :] = hidden.reshape(2, rows, -1)

    @pl.when(step == 1)
    def _():
        for copy, unused in asked_o:
            copy.start()
        kept_out.start()

    @pl.when(step >= 2)
    def _():
        grads = held[...].reshape(-1, held.shape[2])
        hidden = held_hidden[...].reshape(-1, down)
        grad_ref[:, :down] = dot(g_strip[...], hidden, TN).astype(BF)
        grad_ref[:, down:] = dot(x_strip[...], grads, TN).astype(BF)

    @pl.when(step == final)
    def _():
        for copy in kept + [kept_out]:
            copy.wait()
        for unused, landed in near + diagonal + asked_q + asked_o:
            landed.wait_recv()
        for copy, unused in far + near + diagonal + asked_q + asked_o:
            copy.wait_send()


def ff_heads(x, g, w, kv_mine, q_heads, main, down, first):
    depth, cols = w.shape
    heads, unused, span, lanes = kv_mine.shape
    rows = BLK // 2
    both = cols - first
    strip = 512

    def tile(width):
        return pl.BlockSpec((2, rows, width), lambda i: (0, jnp.minimum(i, 1), 0))

    return pl.pallas_call(
        functools.partial(ff_heads_kernel, main, down, first),
        grid=(2 + depth // strip,),
        in_specs=[
            tile(depth),
            tile(depth),
            pl.BlockSpec((2 * BLK, strip), lambda i: (0, jnp.maximum(i - 2, 0))),
            pl.BlockSpec((2 * BLK, strip), lambda i: (0, jnp.maximum(i - 2, 0))),
            ANY,
            ANY,
            ANY,
        ],
        out_specs=(
            tile(down),
            tile(both),
            pl.BlockSpec((strip, both + down), lambda i: (jnp.maximum(i - 2, 0), 0)),
            ANY,
            ANY,
        ),
        out_shape=(
            jax.ShapeDtypeStruct((2, BLK, down), BF),
            jax.ShapeDtypeStruct((2, BLK, both), BF),
            jax.ShapeDtypeStruct((depth, both + down), BF),
            jax.ShapeDtypeStruct((4, 2, span, lanes), BF),
            jax.ShapeDtypeStruct((4, 2, 2, 2, span, lanes), BF),
        ),
        scratch_shapes=[
            pltpu.VMEM((depth, cols), BF),
            pltpu.VMEM((2, BLK, both), BF),
            pltpu.VMEM((2, BLK, down), BF),
            pltpu.VMEM(q_heads.shape, BF),
            pltpu.VMEM(kv_mine.shape, BF),
            pltpu.VMEM(q_heads.shape[1:], BF),
            pltpu.SemaphoreType.DMA((32,)),
            pltpu.SemaphoreType.DMA((32,)),
            pltpu.SemaphoreType.DMA((7,)),
        ],
        compiler_params=pltpu.CompilerParams(
            collective_id=1, has_side_effects=True, vmem_limit_bytes=60 * 2**20
        ),
        cost_estimate=SMALL,
        name="ff_heads",
    )(x, g, x.reshape(2 * BLK, depth), g.reshape(2 * BLK, depth), w, kv_mine, q_heads)


def residual(tokens):
    def finish(column):
        def add(value, here):
            return value + tokens[here, column : column + value.shape[1]].astype(F32)

        return add

    return finish


def home_kernel(
    heads,
    grads,
    dq,
    o_parts,
    hidden,
    grad_both,
    weights,
    tokens,
    dq_home,
    grads_home,
    mixed_out,
    result,
    grad_x,
    *rest,
):
    mine, near, far, total, held_w, held_h, held_o, held_wa, held_a, held_x = rest[:10]
    space = ScatterSpace(rest[10:14])
    links = Links(*rest[14:])
    y, unused_z, unused_c, unused_l, unused_x = coords()
    rows, depth = tokens.shape
    kept = held_w.shape[1]
    links.greet(BR_NEAR + TOK_ALL)
    loads = [
        links.local(o_parts.at[y], held_o.at[y]),
        links.local(hidden, held_h),
        links.local(weights.at[:, pl.ds(0, kept)], held_w),
    ]
    later = [
        links.local(weights.at[:, pl.ds(kept, held_wa.shape[1])], held_wa),
        links.local(grad_both, held_a),
    ]
    returned = [
        (d, links.send(o_parts.at[(y + d) % 4], held_o.at[y], dy=d)) for d in (1, 3, 2)
    ]

    def make(there):
        here = pl.ds(pl.multiple_of(there * rows, rows), rows)
        mixed = [
            jnp.concatenate(
                [held_o[head, here, slot * HD : (slot + 1) * HD] for head in range(heads)],
                axis=1,
            )
            for slot in range(2)
        ]
        for slot in range(2):
            mixed_out[slot, here, :] = mixed[slot]
        both = jnp.concatenate(
            [held_h[:, here, :].reshape(2 * rows, -1), jnp.concatenate(mixed, axis=0)], axis=1
        )
        branches = dot(both, held_w[...], NT).astype(BF)
        for slot in range(2):
            space.pieces[slot, there] = branches[slot * rows : (slot + 1) * rows]

    def output():
        yield
        for d, ticket in returned:
            links.arrived(ticket, held_o.at[(y - d) % 4])
        for load in loads:
            links.settle(load)
        yield from scatter_br(links, make, space, result, residual(tokens))

    def gradient():
        for unused in range(5):
            yield
        for load in later:
            links.settle(load)
        for tile in range(4):
            here = slice(tile * rows, (tile + 1) * rows)
            part = held_a[:, here, :].reshape(2 * rows, -1)
            held_x[:, here, :] = dot(part, held_wa[...], NT).astype(BF).reshape(2, rows, depth)
            span = pl.ds(tile * rows, rows)
            links.local(held_x.at[:, span], grad_x.at[:, span])
            yield

    in_turn(
        [
            gradient(),
            reduce_heads(links, grads, dq, dq_home, grads_home, mine, near, far, total),
            output(),
        ]
    )
    links.close()


def heads_home(grads, dq, o_parts, hidden, grad_both, weights, tokens, heads):
    rows, depth = tokens.shape
    span, lanes = grads.shape[3:]
    width = heads * HD
    kept = hidden.shape[2] + width
    return comm_call(
        functools.partial(home_kernel, heads),
        "heads_home",
        2,
        (grads, dq, o_parts, hidden, grad_both, weights, tokens),
        (
            jax.ShapeDtypeStruct(dq.shape, BF),
            jax.ShapeDtypeStruct((4, span, lanes), BF),
            jax.ShapeDtypeStruct((2, BLK, width), BF),
            jax.ShapeDtypeStruct((rows, depth), BF),
            jax.ShapeDtypeStruct((2, BLK, depth), BF),
        ),
        scratch=[
            pltpu.VMEM((4, 2, span, lanes), BF),
            pltpu.VMEM((4, 2, span, lanes), BF),
            pltpu.VMEM((4, span, lanes), BF),
            pltpu.VMEM((4, span, lanes), BF),
            pltpu.VMEM((depth, kept), BF),
            pltpu.VMEM(hidden.shape, BF),
            pltpu.VMEM(o_parts.shape, BF),
            pltpu.VMEM((depth, grad_both.shape[2]), BF),
            pltpu.VMEM(grad_both.shape, BF),
            pltpu.VMEM((2, BLK, depth), BF),
        ]
        + ScatterSpace.shapes(rows, depth, depth),
        in_vmem=(1, 6),
        out_vmem=(2, 3),
        copies=64,
    )


def normal_rows(tokens, normed, scales):
    rows = tokens.shape[0]
    chunk = 16

    def step(i, unused):
        here = pl.ds(pl.multiple_of(i * chunk, chunk), chunk)
        value = tokens[here, :].astype(F32)
        value = value - jnp.mean(value, axis=-1, keepdims=True)
        scale = lax.rsqrt(jnp.mean(value * value, axis=-1, keepdims=True) + EPSILON)
        normed[here, :] = value * scale
        scales[here, :] = jnp.broadcast_to(scale, (chunk, 128))
        return unused

    lax.fori_loop(0, rows // chunk, step, 0)


def turn_back(grads, normed, scales, cot, gain, parts, result):
    rows, depth = normed.shape
    chunk = 16

    def rows_at(i):
        return pl.ds(pl.multiple_of(i * chunk, chunk), chunk)

    def sums(i, carry):
        here = rows_at(i)
        grad = grads[here, :]
        up = (grad * normed[here, :]).reshape(2, 8, depth)
        return carry[0] + up.sum(0), carry[1] + grad.reshape(2, 8, depth).sum(0)

    zero = jnp.zeros((8, depth), F32)
    found = lax.fori_loop(0, rows // chunk, sums, (zero, zero))
    for k in range(2):
        line = jnp.sum(found[k], axis=0, keepdims=True)
        parts[16 * k : 16 * (k + 1), :] = jnp.concatenate(
            [line[:, t * 128 : (t + 1) * 128] for t in range(depth // 128)], axis=0
        )
    yield

    def back(i, unused):
        here = rows_at(i)
        line = normed[here, :]
        grad = grads[here, :] * gain[...]
        slope = jnp.mean(grad * line, axis=-1, keepdims=True)
        grad = grad - jnp.mean(grad, axis=-1, keepdims=True) - line * slope
        result[here, :] = cot[here, :].astype(F32) + scales[here, :1] * grad
        return unused

    middle = rows // chunk // 2
    lax.fori_loop(0, middle, back, 0)
    yield
    lax.fori_loop(middle, 2 * middle, back, 0)


BR_PEERS = [dict(dl=i // 4, dx=i % 4) for i in range(1, 8)]
TOK_PEERS = [dict(dy=i // 4, dz=(i // 2) % 2, dc=i % 2) for i in range(1, 16)]


def last_kernel(
    heads,
    dq,
    dkv,
    table,
    x_in,
    g_in,
    m_in,
    w_in,
    s_in,
    tokens,
    cot,
    gain,
    block_map,
    result,
    qkv_out,
    out_out,
    sides,
    *rest,
):
    held_q, held_kv, held_t, held_x, held_g, held_m, held_w, held_s, gj = rest[:9]
    parts, near, side, out, far, wsum, summed, normed, scales = rest[9:18]
    lines, lines_in, last, last_in, bias_acc = rest[18:23]
    space = ScatterSpace(rest[23:30])
    links = Links(*rest[30:])
    y, z, c, l, x = coords()
    links.greet(BR_PEERS + TOK_PEERS)
    width = heads * HD
    rows, depth = tokens.shape
    first = [
        links.local(dq, held_q),
        links.local(dkv, held_kv),
        links.local(table, held_t),
    ]
    third = [links.local(w_in.at[:, pl.ds(0, 3 * width)], held_w), links.local(s_in, held_s)]
    second = [
        links.local(x_in, held_x),
        links.local(g_in, held_g),
        links.local(m_in, held_m),
    ]
    wrows = parts.shape[3]
    strip = 4 * wrows
    bias_acc[...] = jnp.zeros_like(bias_acc)

    def settle(loads):
        for load in loads:
            links.settle(load)
        loads.clear()

    def turn_rows(here):
        for slot in range(2):
            lanes = slice(slot * HD, (slot + 1) * HD)
            turns = table_rows(held_t, block_map, slot, here)
            q = jnp.concatenate([held_q[h, here, lanes] for h in range(heads)], axis=1)
            q = turn(q.astype(F32), turns, heads // 2, False, -1.0).astype(BF)
            kv = jnp.concatenate([held_kv[h, slot, here, :] for h in range(heads)], axis=1)
            kv = turn(kv.astype(F32), turns, heads, True, -1.0).astype(BF)
            both = jnp.concatenate([q, kv], axis=1)
            gj[slot, here, :] = both
            bias_acc[...] += jnp.sum(
                both.astype(F32).reshape(rows // 8, 8, 3 * width), axis=0
            )

    def bias_lines():
        total = jnp.sum(bias_acc[...], axis=0, keepdims=True)
        line = [total[:, :width]]
        for k in range(2):
            at = [width + (2 * h + k) * HD for h in range(heads)]
            line.append(jnp.concatenate([total[:, a : a + HD] for a in at], axis=1))
        line = jnp.concatenate(line, axis=1)
        return jnp.concatenate(
            [line[:, r * 128 : (r + 1) * 128] for r in range(3 * width // 128)], axis=0
        )

    def weights_of(there):
        settle(second)
        here = pl.ds(pl.multiple_of(there * strip, strip), strip)
        qkv = dot(held_x[:, here], gj[...].reshape(2 * BLK, 3 * width), TN).astype(BF)
        outs = dot(held_g[:, here], held_m[...], TN).astype(BF)
        for k in range(4):
            at = slice(k * wrows, (k + 1) * wrows)
            parts[there, k // 2, k % 2, :, : 3 * width] = qkv[at]
            parts[there, k // 2, k % 2, :, 3 * width : 4 * width] = outs[at]

    def rows_of(there):
        settle(first)
        here = pl.ds(pl.multiple_of(there * rows, rows), rows)
        turn_rows(here)
        settle(third)
        both = gj[:, here, :].reshape(2 * rows, 3 * width)
        grads = dot(both, held_w[...], NT)
        for slot in range(2):
            value = grads[slot * rows : (slot + 1) * rows] + held_s[slot, here, :].astype(F32)
            space.pieces[slot, there] = value.astype(BF)

    def shifted():
        yield from scatter_br(links, rows_of, space, summed, lambda column: plain)
        through = turn_back(summed, normed, scales, cot, gain, lines, result)
        next(through)
        near_sums = [links.send(lines, lines_in.at[i], **o) for i, o in enumerate(BR_PEERS)]
        yield
        next(through)
        bias_sums = bias_lines()
        sums = lines[...]
        for i, ticket in enumerate(near_sums):
            links.arrived(ticket, lines_in.at[i])
            sums = sums + lines_in[i]
        for t in range(16):
            last[t] = jnp.concatenate([sums[t : t + 1], sums[16 + t : 17 + t], bias_sums], axis=0)
        all_sums = []
        for i, o in enumerate(TOK_PEERS):
            there = ((y + o["dy"]) % 4) * 4 + ((z + o["dz"]) % 2) * 2 + (c + o["dc"]) % 2
            all_sums.append(links.send(last.at[there], last_in.at[i], **o))
        yield
        for unused in through:
            pass
        yield
        sums = last[y * 4 + z * 2 + c]
        for i, ticket in enumerate(all_sums):
            links.arrived(ticket, last_in.at[i])
            sums = sums + last_in[i]
        sides[...] = sums

    def weights():
        for unused in range(4):
            yield
        yield from reduce_tok(links, weights_of, parts, near, side, out, far, wsum)
        qkv_out[0] = wsum[:, :width]
        for k in range(2):
            at = [width + (2 * h + k) * HD for h in range(heads)]
            qkv_out[1 + k] = jnp.concatenate([wsum[:, a : a + HD] for a in at], axis=1)
        out_out[...] = jnp.transpose(wsum[:, 3 * width :])

    def aside():
        for unused in range(5):
            yield
        normal_rows(tokens, normed, scales)

    in_turn([shifted(), weights(), aside()])
    links.close()


def last_sums(
    dq, dkv, table, x, g, mixed, w, partial_grad, tokens, cot, gain, block_map, heads
):
    rows, depth = tokens.shape
    wrows = depth // 16
    width = heads * HD
    cols = 4 * width
    return comm_call(
        functools.partial(last_kernel, heads),
        "last_sums",
        3,
        (dq, dkv, table, x, g, mixed, w, partial_grad, tokens, cot, gain, block_map),
        (
            jax.ShapeDtypeStruct((rows, depth), F32),
            jax.ShapeDtypeStruct((3, wrows, width), F32),
            jax.ShapeDtypeStruct((width, wrows), F32),
            jax.ShapeDtypeStruct((8, 128), F32),
        ),
        scratch=[
            pltpu.VMEM(dq.shape, BF),
            pltpu.VMEM(dkv.shape, BF),
            pltpu.VMEM(table.shape, F32),
            pltpu.VMEM(x.shape, BF),
            pltpu.VMEM(g.shape, BF),
            pltpu.VMEM(mixed.shape, BF),
            pltpu.VMEM((depth, 3 * width), BF),
            pltpu.VMEM(partial_grad.shape, BF),
            pltpu.VMEM((2, BLK, 3 * width), BF),
            pltpu.VMEM((4, 2, 2, wrows, cols), BF),
            pltpu.VMEM((4, 2, wrows, cols), BF),
            pltpu.VMEM((3, 2, wrows, cols), BF),
            pltpu.VMEM((wrows, cols), BF),
            pltpu.VMEM((wrows, cols), BF),
            pltpu.VMEM((wrows, cols), F32),
            pltpu.VMEM((rows, depth), F32),
            pltpu.VMEM((rows, depth), F32),
            pltpu.VMEM((rows, 128), F32),
            pltpu.VMEM((32, 128), F32),
            pltpu.VMEM((7, 32, 128), F32),
            pltpu.VMEM((16, 8, 128), F32),
            pltpu.VMEM((15, 8, 128), F32),
            pltpu.VMEM((8, 3 * width), F32),
        ]
        + ScatterSpace.shapes(rows, depth, depth // 4 * 3),
        in_vmem=(8, 9, 10),
        in_smem=(11,),
        out_vmem=(0, 1, 2, 3),
        copies=96,
    )


def finish_kernel(main, grads, value, tokens, qkv, out, *outs):
    def lines(start, count):
        return jnp.transpose(grads[:, start : start + count].astype(F32))

    result, tokens_out, qkv_out, out_out, down, gate, up = outs
    result[...] = value[...]
    tokens_out[...] = tokens[...]
    qkv_out[...] = qkv[...]
    out_out[...] = out[...]
    tail = down.shape[0] - main
    down[:main, :] = lines(0, main)
    down[main:, :] = lines(main, 128)[:tail]
    at = main + 128
    gate[:main, :] = lines(at, main)
    up[:main, :] = lines(at + main, main)
    ends = lines(at + 2 * main, 128)
    gate[main:, :] = ends[:tail]
    up[main:, :] = ends[tail:]


def finish(grads, value, tokens, qkv, out, main, hidden_width):
    shape = jax.ShapeDtypeStruct((hidden_width, grads.shape[0]), F32)
    return pl.pallas_call(
        functools.partial(finish_kernel, main),
        out_shape=(
            jax.ShapeDtypeStruct(value.shape, BF),
            jax.ShapeDtypeStruct(tokens.shape, F32),
            jax.ShapeDtypeStruct(qkv.shape, F32),
            jax.ShapeDtypeStruct(out.shape, F32),
        )
        + (shape,) * 3,
        in_specs=[VMEM] * 5,
        out_specs=(VMEM,) * 7,
        cost_estimate=SMALL,
        name="finish",
    )(grads, value, tokens, qkv, out)


def rotary_table():
    half = ROT // 2
    frequency = (ROPE_BASE ** (-(np.arange(half) * 2.0 / ROT))).astype(np.float32)
    angles = np.arange(LB * BLK, dtype=np.float32)[:, None] * frequency[None, :]
    cos, sin = np.cos(angles), np.sin(angles)
    one = np.ones((LB * BLK, HD - ROT), np.float32)
    table = np.concatenate([cos, cos, one, -sin, sin, 0.0 * one], axis=1)
    return table.astype(np.float32).reshape(LB, BLK, 2 * HD)


def body(
    tokens,
    norm_gain,
    norm_bias,
    qkv_weight,
    qkv_bias,
    out_weight,
    gate_weight,
    up_weight,
    down_weight,
    cotangent,
    block_map,
    lengths,
):
    tok = lax.axis_index("tok")
    rows = tokens.shape[0]
    depth = tokens.shape[1]
    wrows = qkv_weight.shape[1]
    heads = qkv_bias.shape[1]
    width = heads * HD
    hidden_width = gate_weight.shape[1]
    main = hidden_width // 128 * 128
    tail = hidden_width - main

    down_width = main + 128
    first = down_width + width
    table = jnp.asarray(rotary_table())
    x, grad, qkv_full, ff_full, kv_mine, q_heads = start(
        block_map,
        tokens,
        norm_gain.reshape(1, depth),
        norm_bias.reshape(1, depth),
        cotangent,
        qkv_weight,
        qkv_bias,
        jnp.transpose(gate_weight),
        jnp.transpose(up_weight),
        down_weight,
        out_weight,
        table,
        heads,
        main,
    )
    x = x.reshape(2, BLK, depth)
    grad = grad.reshape(2, BLK, depth)
    qkv_full = qkv_full.reshape(16 * wrows, -1)
    ff_full = ff_full.reshape(16 * wrows, -1)

    hidden, grad_both, grad_ff, qd_all, kv_all = ff_heads(
        x, grad, ff_full, kv_mine, q_heads, main, down_width, first
    )
    kv_all = kv_all.reshape(-1, 2 * HD)
    x = x.reshape(2 * BLK, depth)
    grad = grad.reshape(2 * BLK, depth)
    grad_ff = lax.psum_scatter(grad_ff, "tok", scatter_dimension=0, tiled=True)

    o_parts, dq_parts, dkv_all = attention(block_map, lengths, qd_all, kv_all)
    dq_heads, dkv_heads, mixed, result, grad_x = heads_home(
        dkv_all.reshape(4, 2, 2, 2 * BLK, 2 * HD),
        dq_parts,
        o_parts,
        hidden,
        grad_both,
        ff_full,
        tokens,
        heads,
    )
    grad_tokens, grad_qkv, grad_out, sides = last_sums(
        dq_heads,
        dkv_heads.reshape(heads, 2, BLK, 2 * HD),
        table,
        x,
        grad,
        mixed.reshape(2 * BLK, width),
        qkv_full,
        grad_x,
        tokens,
        cotangent,
        norm_gain.reshape(1, depth),
        block_map,
        heads,
    )
    grad_qkv_bias = lax.dynamic_slice_in_dim(
        sides[2:].reshape(3, heads, HD), tok * qkv_bias.shape[2], qkv_bias.shape[2], 2
    )
    grad_ff, grad_tokens = lax.optimization_barrier((grad_ff, grad_tokens))
    result, grad_tokens, grad_qkv, grad_out, grad_down, grad_gate, grad_up = finish(
        grad_ff, result, grad_tokens, grad_qkv, grad_out, main, hidden_width
    )

    sides = lax.dynamic_slice_in_dim(sides[:2], lax.axis_index("br") * 16, 16, 1)
    return (
        result,
        grad_tokens,
        sides[0],
        sides[1],
        grad_qkv,
        grad_qkv_bias,
        grad_out,
        jnp.transpose(grad_gate),
        jnp.transpose(grad_up),
        grad_down,
    )


def solution(mesh):
    in_specs = (
        P(("tok", "br"), None),
        P(),
        P(),
        P(None, "tok", "br"),
        P(None, "br", "tok"),
        P("br", "tok"),
        P("tok", "br"),
        P("tok", "br"),
        P("br", "tok"),
        P(("tok", "br"), None),
        P(),
        P(),
    )
    out_specs = (
        P(("tok", "br"), None),
        P(("tok", "br"), None),
        P(("tok", "br")),
        P(("tok", "br")),
        P(None, "tok", "br"),
        P(None, "br", "tok"),
        P("br", "tok"),
        P("tok", "br"),
        P("tok", "br"),
        P("br", "tok"),
    )
    return jax.shard_map(body, mesh=mesh, in_specs=in_specs, out_specs=out_specs, check_vma=False)
```
